32 devices in a mesh: expert: 16 (over z, y, x), tensor: 2 (over core).
Axes of the slice: x: 2, y: 2, z: 4, core: 2. Of those that a mesh axis runs over, the one named last changes fastest.
Arguments:
- tokens: bfloat16 [4096, 2048], P('expert'), may hold values from -6 to 6
- lengths: int32 [16, 4], P('expert'), may hold values from 1 to 128, 256 in all within a row
- routes: int32 [4096, 6], P('expert'), may hold values from 0 to 15, all different within a row; in each aligned block of 256 rows (0 to 255, 256 to 511, ...) at most 128 rows name the same one
- gain_attn: bfloat16 [2048], P('expert'), may hold values from 0.5 to 1.5
- w_query: bfloat16 [2048, 2048], P('expert', 'tensor'), may hold values from -0.125 to 0.125
- w_key: bfloat16 [2048, 2048], P('expert', 'tensor'), may hold values from -0.125 to 0.125
- w_value: bfloat16 [2048, 2048], P('expert', 'tensor'), may hold values from -0.125 to 0.125
- w_out: bfloat16 [2048, 2048], P('tensor', 'expert'), may hold values from -0.5 to 0.5
- gain_ffn: bfloat16 [2048], P('expert'), may hold values from 0.5 to 1.5
- w_router: bfloat16 [2048, 16], P('expert'), may hold values from -0.0625 to 0.0625
- routed_gate_weight: bfloat16 [16, 2048, 1408], P('expert', None, 'tensor'), may hold values from -0.125 to 0.125
- routed_up_weight: bfloat16 [16, 2048, 1408], P('expert', None, 'tensor'), may hold values from -0.125 to 0.125
- w_down: bfloat16 [16, 1408, 2048], P('expert', 'tensor'), may hold values from -0.625 to 0.625
- w_shared_gate: bfloat16 [2048, 2816], P('expert', 'tensor'), may hold values from -0.125 to 0.125
- w_shared_up: bfloat16 [2048, 2816], P('expert', 'tensor'), may hold values from -0.125 to 0.125
- w_shared_down: bfloat16 [2816, 2048], P('tensor', 'expert'), may hold values from -0.15625 to 0.15625
- out_grad: bfloat16 [4096, 2048], P('expert'), may hold values from -6 to 6
Outputs:
- output: bfloat16 [4096, 2048], P('expert')
- input_grad: bfloat16 [4096, 2048], P('expert')
- gain_attn_grad: float32 [2048], P('expert')
- query_grad: float32 [2048, 2048], P('expert', 'tensor')
- key_grad: float32 [2048, 2048], P('expert', 'tensor')
- value_grad: float32 [2048, 2048], P('expert', 'tensor')
- out_proj_grad: float32 [2048, 2048], P('tensor', 'expert')
- gain_ffn_grad: float32 [2048], P('expert')
- router_grad: float32 [2048, 16], P('expert')
- gate_grad: float32 [16, 2048, 1408], P('expert', None, 'tensor')
- routed_up_gradient: float32 [16, 2048, 1408], P('expert', None, 'tensor')
- down_grad: float32 [16, 1408, 2048], P('expert', 'tensor')
- shared_gate_grad: float32 [2048, 2816], P('expert', 'tensor')
- shared_up_grad: float32 [2048, 2816], P('expert', 'tensor')
- shared_down_grad: float32 [2816, 2048], P('tensor', 'expert')
The draws below stay inside these ranges and needn't reach their ends.
Inputs may be any that keep to these rules, and one draw needn't show every extreme that they name: `routes`: each row names 6 different experts. Among the rows of one index of expert no expert is named by more than 128 rows, a bound that some block reaches. `lengths`: each row sums to 256, and its longest entry is exactly 128.
All inputs are finite; a program needn't handle non-finite values.
Results may differ from the reference program's by a relative error of at most 0.025.
Values may be sent and summed in bfloat16 or wider, within the bound.
A program may use at most 320 MiB of HBM per device.

```python
import math
from functools import partial
import jax
import jax.numpy as jnp
import numpy as np
from jax import lax

D = 2048
HEADS = 16
HEAD_DIM = 128
FF_EXP = 1408
SHARED_FF = 2816
TOP = 6
TOK_DEV = 256
SEQ_DEV = 4
LONGEST = 128
GROUPS = 16
EXPERTS = 16
CAP = 128
TOKENS = 4096


def block_levels(own_key, shape, cuts, low, high):
    level, own = 1.0, jax.random.fold_in(own_key, 6)
    for dim, shards_of in cuts:
        steps = jnp.exp(jax.random.uniform(jax.random.fold_in(own, dim), (shards_of,), jnp.float32, low / len(cuts), high / len(cuts)))
        level = level * jnp.repeat(steps, shape[dim] // shards_of).reshape([-1 if axis == dim else 1 for axis in range(len(shape))])
    return level


def profile(count, total, bound, slope):
    weights = [(1 << 20) // math.isqrt(rank ** slope) + 1 for rank in range(2, count + 1)]
    surplus, given = total - bound - (count - 1), [1] * (count - 1)
    while surplus > 0:
        free = [i for i in range(count - 1) if given[i] < bound]
        pool, remaining = sum([weights[i] for i in free]), surplus
        for i in free:
            addition = min(bound - given[i], max(1, remaining * weights[i] // pool), surplus)
            given[i] = given[i] + addition
            surplus = surplus - addition
    return np.array([bound] + given)


def ragged(rng, number_of, total, bound, slope):
    if number_of == 2:
        one = jax.random.randint(rng, (), max(1, total - bound), min(bound, total - 1) + 1)
        return jnp.stack([one, total - one])
    sizes = jnp.asarray(profile(number_of, total, bound, slope), jnp.int32)
    pairs = (number_of - 1) // 2
    source_of, receiver = sizes[1:1 + 2 * pairs:2], sizes[2:2 + 2 * pairs:2]
    margin = jnp.minimum(source_of - 1, bound - receiver)
    moved = jax.random.randint(jax.random.fold_in(rng, 1), (pairs,), 0, 1 << 20) % (margin + 1)
    sizes = sizes.at[1:1 + 2 * pairs:2].set(source_of - moved).at[2:2 + 2 * pairs:2].set(receiver + moved)
    return sizes[jax.random.permutation(jax.random.fold_in(rng, 2), number_of)]


def shared_out(stream_key, own, number, rows, number_of, top, limit, lean):
    order = jax.random.permutation(stream_key, number_of)
    heavy_load, ordinary = load_shares(number_of, rows * top, limit, lean, True), load_shares(number_of, rows * top, limit, lean, False)
    places = jnp.arange(number_of)

    def named(sizes, offset_by):
        used = int((sizes > 0).sum())
        fixed = max(1, used // 4)
        moved = fixed + (places - fixed + offset_by * (used - fixed)) % max(1, number_of - fixed)
        return jnp.zeros((number_of,), jnp.int32).at[order[jnp.where(places < fixed, places, moved)]].set(jnp.asarray(sizes, jnp.int32))

    sizes = jnp.where(number % 4 == 0, named(heavy_load, number // 4), named(ordinary, number - number // 4 - 1))
    mixed = jax.random.permutation(jax.random.fold_in(own, 3), number_of)
    donor, sink = mixed[0:number_of // 2 * 2:2], mixed[1:number_of // 2 * 2:2]
    room = jnp.minimum(sizes[donor] - 1, limit - sizes[sink]) // 2
    room = jnp.where((donor == order[0]) | (sink == order[0]) | (sizes[sink] == 0), 0, jnp.maximum(room, 0))
    moved = jax.random.randint(jax.random.fold_in(own, 4), (number_of // 2,), 0, 1 << 20) % (room + 1)
    sizes = sizes.at[donor].add(-moved).at[sink].add(moved)
    labels = jnp.searchsorted(jnp.cumsum(sizes), jnp.arange(rows * top), side="right").astype(jnp.int32)
    grid = labels.reshape(top, rows).T
    grid = grid[jax.random.permutation(jax.random.fold_in(own, 1), rows)]
    offset_by = jax.random.randint(jax.random.fold_in(own, 2), (rows, 1), 0, top)
    return jnp.take_along_axis(grid, (jnp.arange(top)[None, :] + offset_by) % top, axis=1)


def load_shares(number_of, total, limit, slope, full):
    loads = [(1 << 20) // math.isqrt(grade ** slope) + 1 for grade in range(1, number_of + 1)]
    largest = limit if full else min(limit, max(-(-total // number_of), total * loads[0] // sum(loads)))
    least = 1 if total - largest >= number_of - 1 else 0
    holding, spare = [largest] + [least] * (number_of - 1), total - largest - least * (number_of - 1)
    while spare > 0:
        free = [i for i in range(1, number_of) if holding[i] < largest] or [i for i in range(1, number_of) if holding[i] < limit]
        mass, budget = sum([loads[i] for i in free]), spare
        for i in free:
            extra = min(limit - holding[i], max(1, budget * loads[i] // mass), spare)
            holding[i] = holding[i] + extra
            spare = spare - extra
    return np.array(holding)


def bell_draw(own_key, extent, spread, bound, split=(), held_as=jnp.bfloat16):
    entries = jax.random.normal(own_key, extent, jnp.float32) * spread
    if len(split) > 0:
        entries = block_levels(own_key, extent, split, -0.22, 0.18) * entries
    return jnp.clip(entries, min=-bound, max=bound).astype(held_as)


def setup_inputs(seed: int = 0) -> dict:
    seeds = jax.random.split(jax.random.key(seed), 18)
    tokens = bell_draw(seeds[0], (TOKENS, D), 1.0, 6.0, ((0, 16),))
    lengths = jax.vmap(lambda own: ragged(own, SEQ_DEV, TOK_DEV, LONGEST, 2))(jax.random.split(seeds[1], GROUPS)).reshape((GROUPS, SEQ_DEV)).astype(jnp.int32)
    routes_keys = jax.random.split(jax.random.fold_in(seeds[2], 1), TOKENS // TOK_DEV)
    routes_turns = jax.random.permutation(jax.random.fold_in(seeds[2], 3), TOKENS // TOK_DEV)
    routes = jax.vmap(lambda own, number: shared_out(jax.random.fold_in(seeds[2], 2), own, number, TOK_DEV, EXPERTS, TOP, CAP, 1))(routes_keys, routes_turns).reshape((TOKENS, TOP))
    gain_attn = jnp.clip(1.0 + 0.1 * jax.random.normal(seeds[3], (D,), jnp.float32), 0.5, 1.5).astype(jnp.bfloat16)
    w_query = bell_draw(seeds[4], (D, HEADS * HEAD_DIM), D ** -0.5, 0.125, ((0, 16), (1, 2)))
    w_key = bell_draw(seeds[5], (D, HEADS * HEAD_DIM), D ** -0.5, 0.125, ((0, 16), (1, 2)))
    w_value = bell_draw(seeds[6], (D, HEADS * HEAD_DIM), D ** -0.5, 0.125, ((0, 16), (1, 2)))
    w_out = bell_draw(seeds[7], (HEADS * HEAD_DIM, D), (HEADS * HEAD_DIM // 16) ** -0.5, 0.5, ((0, 2), (1, 16)))
    gain_ffn = jnp.clip(1.0 + 0.1 * jax.random.normal(seeds[8], (D,), jnp.float32), 0.5, 1.5).astype(jnp.bfloat16)
    w_router = bell_draw(seeds[9], (D, EXPERTS), (4 * D) ** -0.5, 0.0625, ((0, 16),))
    routed_gate_weight = bell_draw(seeds[10], (EXPERTS, D, FF_EXP), D ** -0.5, 0.125, ((0, 16), (2, 2)))
    routed_up_weight = bell_draw(seeds[11], (EXPERTS, D, FF_EXP), D ** -0.5, 0.125, ((0, 16), (2, 2)))
    w_down = bell_draw(seeds[12], (EXPERTS, FF_EXP, D), (FF_EXP // 16) ** -0.5, 0.625, ((0, 16), (1, 2)))
    w_shared_gate = bell_draw(seeds[13], (D, SHARED_FF), D ** -0.5, 0.125, ((0, 16), (1, 2)))
    w_shared_up = bell_draw(seeds[14], (D, SHARED_FF), D ** -0.5, 0.125, ((0, 16), (1, 2)))
    w_shared_down = bell_draw(seeds[15], (SHARED_FF, D), (SHARED_FF // 2) ** -0.5, 0.15625, ((0, 2), (1, 16)))
    out_grad = bell_draw(seeds[16], (TOKENS, D), 1.0, 6.0, ((0, 16),))
    return dict(tokens=tokens, lengths=lengths, routes=routes, gain_attn=gain_attn, w_query=w_query, w_key=w_key, w_value=w_value, w_out=w_out, gain_ffn=gain_ffn, w_router=w_router, routed_gate_weight=routed_gate_weight, routed_up_weight=routed_up_weight, w_down=w_down, w_shared_gate=w_shared_gate, w_shared_up=w_shared_up, w_shared_down=w_shared_down, out_grad=out_grad)


@jax.custom_vjp
def low(v):
    return lax.optimization_barrier(v.astype(jnp.bfloat16)).astype(jnp.float32)

@jax.custom_vjp
def low_back(v):
    return v

def low_keep(v):
    return (low(v), None)

def low_pass(kept, grad):
    return (grad,)

def back_keep(v):
    return (v, None)

def back_low(kept, grad):
    return (low(grad),)
low.defvjp(low_keep, low_pass)
low_back.defvjp(back_keep, back_low)
eps = 1e-06
highest = lax.Precision.HIGHEST
floor_score = -1e+30

def product(left, right):
    return jnp.dot(left, right, precision=highest)

def rms_norm(values, gains):
    scale = lax.rsqrt(lax.optimization_barrier(jnp.mean(values * values, axis=-1, keepdims=True)) + eps)
    return values * scale * gains

def rotary(values, positions):
    half = values.shape[-1] // 2
    inverse = 10000.0 ** (-2.0 * jnp.arange(half, dtype=jnp.float32) / values.shape[-1])
    angles = positions.astype(jnp.float32)[:, None] * inverse[None, :]
    cosine = jnp.cos(angles)[:, None, :]
    sine = jnp.sin(angles)[:, None, :]
    first = values[..., :half]
    second = values[..., half:]
    return jnp.concatenate([first * cosine - second * sine, second * cosine + first * sine], axis=-1)

def sequence_tables(lengths_row, tok_rows):
    ends = jnp.cumsum(lengths_row)
    starts = ends - lengths_row
    places = jnp.arange(tok_rows, dtype=jnp.int32)
    segment = lax.optimization_barrier(jnp.sum((places[:, None] >= ends[None, :]).astype(jnp.int32), axis=1))
    member = segment[:, None] == jnp.arange(lengths_row.shape[0], dtype=jnp.int32)[None, :]
    first = lax.optimization_barrier(jnp.sum(jnp.where(member, starts[None, :], 0), axis=1))
    return (segment, places - first)

def slot_places(routes_dev, experts, capacity):
    flat = routes_dev.reshape(-1)
    onehot = (flat[:, None] == jnp.arange(experts, dtype=jnp.int32)[None, :]).astype(jnp.int32)
    before = jnp.cumsum(onehot, axis=0) - onehot
    return flat * capacity + lax.optimization_barrier(jnp.sum(before * onehot, axis=1))

def expert_rows(padded, source, gate_weight, up_weight, down_weight):
    rows = padded[source]
    gate = low_back(product(rows, gate_weight))
    upper = low_back(product(rows, up_weight))
    return low_back(product(low(jax.nn.silu(gate) * upper), down_weight))

def layer(params, lengths, routes):
    tokens, gain_attn, w_query, w_key, w_value, w_out, gain_ffn, w_router, routed_gate_weight, routed_up_weight, w_down, w_shared_gate, w_shared_up, w_shared_down = params
    experts = w_router.shape[1]
    capacity = min(TOK_DEV, TOK_DEV * TOP * 4 // (3 * experts))
    groups = TOKENS // TOK_DEV
    segments, positions = jax.vmap(partial(sequence_tables, tok_rows=TOK_DEV))(lengths)
    normed_one = low(rms_norm(tokens, gain_attn))
    scale = HEAD_DIM ** (-0.5)
    head_shape = (TOK_DEV, HEADS, HEAD_DIM)

    def attend(items):
        block, segment, position = items
        q_lin = low_back(product(block, w_query)).reshape(head_shape)
        k_lin = low_back(product(block, w_key)).reshape(head_shape)
        valued = low(low_back(product(block, w_value))).reshape(head_shape)
        query = low(rotary(q_lin, position))
        keyed = low(rotary(k_lin, position))
        scores = low_back(jnp.einsum('qhd,khd->hqk', query, keyed, precision=highest) * scale)
        places = jnp.arange(TOK_DEV, dtype=jnp.int32)
        allowed = (segment[:, None] == segment[None, :]) & (places[None, :] <= places[:, None])
        scores = jnp.where(allowed[None], scores, floor_score)
        probs = low(jax.nn.softmax(scores, axis=-1))
        heads_out = jnp.einsum('hqk,khd->qhd', probs, valued, precision=highest).reshape(TOK_DEV, HEADS * HEAD_DIM)
        return low_back(product(low(low_back(heads_out)), w_out))
    attention = lax.map(jax.checkpoint(attend), (normed_one.reshape(groups, TOK_DEV, D), segments, positions)).reshape(TOKENS, D)
    hidden = tokens + attention
    normed_two = low(rms_norm(hidden, gain_ffn))
    logits = product(normed_two, w_router)
    gates = jax.nn.softmax(jnp.take_along_axis(logits, routes, axis=1), axis=-1)
    sh_gate = low_back(product(normed_two, w_shared_gate))
    sh_up = low_back(product(normed_two, w_shared_up))
    shared = product(low(jax.nn.silu(sh_gate) * sh_up), w_shared_down)
    places = jax.vmap(partial(slot_places, experts=experts, capacity=capacity))(routes.reshape(groups, TOK_DEV, TOP))
    token_ids = jnp.arange(TOKENS, dtype=jnp.int32).reshape(groups, TOK_DEV)
    pair_tokens = jnp.repeat(token_ids, TOP, axis=1)

    def fill_slots(place_row, token_row, gate_row):
        source = jnp.full((experts * capacity,), TOKENS, jnp.int32).at[place_row].set(token_row)
        weight = jnp.zeros((experts * capacity,), jnp.float32).at[place_row].set(gate_row)
        return (source, weight)
    sources, slot_gates = jax.vmap(fill_slots)(places, pair_tokens, gates.reshape(groups, TOK_DEV * TOP))
    sources = sources.reshape(groups, experts, capacity).transpose(1, 0, 2).reshape(experts, groups * capacity)
    slot_gates = slot_gates.reshape(groups, experts, capacity).transpose(1, 0, 2).reshape(experts, groups * capacity)
    padded = jnp.concatenate([normed_two, jnp.zeros((1, D), jnp.float32)], axis=0)
    checked = jax.checkpoint(expert_rows)

    def expert_step(total, items):
        source, weight_rows, gate_weight, up_weight, down_weight = items
        result = checked(padded, source, gate_weight, up_weight, down_weight)
        return (total.at[source].add(weight_rows[:, None] * result), None)
    routed, unused = lax.scan(expert_step, jnp.zeros((TOKENS + 1, D), jnp.float32), (sources, slot_gates, routed_gate_weight, routed_up_weight, w_down))
    return hidden + routed[:TOKENS] + shared

def reference(tokens, lengths, routes, gain_attn, w_query, w_key, w_value, w_out, gain_ffn, w_router, routed_gate_weight, routed_up_weight, w_down, w_shared_gate, w_shared_up, w_shared_down, out_grad):
    params = (tokens.astype(jnp.float32), gain_attn.astype(jnp.float32), w_query.astype(jnp.float32), w_key.astype(jnp.float32), w_value.astype(jnp.float32), w_out.astype(jnp.float32), gain_ffn.astype(jnp.float32), w_router.astype(jnp.float32), routed_gate_weight.astype(jnp.float32), routed_up_weight.astype(jnp.float32), w_down.astype(jnp.float32), w_shared_gate.astype(jnp.float32), w_shared_up.astype(jnp.float32), w_shared_down.astype(jnp.float32))
    output, pullback = jax.vjp(partial(layer, lengths=lengths, routes=routes), params)
    grads, = pullback(out_grad.astype(jnp.float32))
    return (output.astype(jnp.bfloat16), grads[0].astype(jnp.bfloat16), grads[1], grads[2], grads[3], grads[4], grads[5], grads[6], grads[7], grads[8], grads[9], grads[10], grads[11], grads[12], grads[13])
```

```python
import functools

import jax
import jax.numpy as jnp
from jax import lax
from jax.experimental import pallas as pl
from jax.experimental.pallas import tpu as pltpu
from jax.sharding import PartitionSpec as P

HEAD_DIM = 128
TOP = 6
MESH = pl.DeviceIdType.MESH
ANY = pl.BlockSpec(memory_space=pl.ANY)

bf16 = jnp.bfloat16
f32 = jnp.float32
eps = 1e-06
highest = lax.Precision.HIGHEST
floor_score = -1e30


class Place:
    def __init__(self, sems, count, cores):
        self.sems, self.used = sems, 0
        self.count, self.cores = count, cores
        self.e = lax.axis_index("expert")
        self.t = lax.axis_index("tensor")
        self.quad = lax.rem(self.e, 4)
        self.far = lax.div(self.e, 4)

    def take(self, number):
        first = self.used
        self.used = first + number
        return first

    def ring(self, distance):
        return lax.rem(self.t + distance, self.cores)

    def copy(self, src, dst, out_sem, in_sem, e, t):
        return pltpu.make_async_remote_copy(
            src_ref=src,
            dst_ref=dst,
            send_sem=self.sems.at[out_sem],
            recv_sem=self.sems.at[in_sem],
            device_id={"expert": e, "tensor": t},
            device_id_type=MESH,
        )

    def send(self, src, dst, out_sem, in_sem, e, t):
        move = self.copy(src, dst, out_sem, in_sem, e, t)
        move.start()
        return move

    def arrived(self, landing, in_sem):
        self.copy(landing, landing, in_sem, in_sem, self.e, self.t).wait_recv()

    def keep(self, src, dst):
        move = pltpu.make_async_copy(src, dst, self.sems.at[self.take(1)])
        move.start()
        return move

    def meet(self):
        barrier = pltpu.get_barrier_semaphore()
        for step in range(1, self.count):
            pl.semaphore_signal(
                barrier,
                inc=1,
                device_id={"expert": lax.rem(self.e + step, self.count), "tensor": self.t},
                device_id_type=MESH,
            )
        for step in range(1, self.cores):
            pl.semaphore_signal(
                barrier,
                inc=1,
                device_id={"expert": self.e, "tensor": self.ring(step)},
                device_id_type=MESH,
            )
        pl.semaphore_wait(barrier, self.count + self.cores - 2)


class Block:
    def __init__(self, place, members):
        self.place, self.deep = place, members // 4
        self.rank = lax.rem(place.far, self.deep)
        self.start = place.far - self.rank

    def flips(self, order):
        high, low = lax.div(self.place.quad, 2), lax.rem(self.place.quad, 2)
        one = high + (low - high) * order
        two = low + (high - low) * order
        return (2 - order) * (1 - 2 * one), (1 + order) * (1 - 2 * two)

    def slot(self, k, i, j, order):
        one, two = self.flips(order)
        return lax.rem(self.rank + k, self.deep) * 4 + self.place.quad + i * one + j * two

    def own(self):
        return self.rank * 4 + self.place.quad

    def device(self, slot):
        return self.start * 4 + slot


def gather(place, members, mine, whole, view, halves):
    block = Block(place, members)
    deep, e, t = block.deep, place.e, place.t
    order = lax.rem(t, 2)
    cores = place.cores if halves else 1
    s1, r1 = place.take(deep), place.take(deep)
    s2, r2 = place.take(deep), place.take(deep)
    s3, r3 = place.take(2 * deep), place.take(2 * deep)
    s4, r4 = place.take(4 * deep * cores), place.take(4 * deep * cores)
    own = block.own()
    one, two = block.flips(order)
    sent, kept = [], place.keep(whole[0], whole[1](own))
    for j in range(1, deep):
        target = block.device(lax.rem(block.rank + j, deep) * 4 + place.quad)
        sent.append(place.send(mine, view(own, t), s1 + j, r1 + j, target, t))
    sent.append(place.send(mine, view(own, t), s2, r2, e + one, t))
    sent.append(place.send(mine, view(own, t), s3, r3, e + two, t))
    yield

    def share(k, i, j):
        slot = block.slot(k, i, j, order)
        for d in range(1, cores):
            at = ((d - 1) * deep + k) * 4 + i * 2 + j
            sent.append(place.send(view(slot, t), view(slot, t), s4 + at, r4 + at, e, place.ring(d)))

    for k in range(deep):
        slot = block.slot(k, 0, 0, order)
        if k > 0:
            place.arrived(view(slot, t), r1 + deep - k)
            sent.append(place.send(view(slot, t), view(slot, t), s2 + k, r2 + k, e + one, t))
            sent.append(place.send(view(slot, t), view(slot, t), s3 + 2 * k, r3 + 2 * k, e + two, t))
            share(k, 0, 0)
            yield
        slot = block.slot(k, 1, 0, order)
        place.arrived(view(slot, t), r2 + k)
        sent.append(place.send(view(slot, t), view(slot, t), s3 + 2 * k + 1, r3 + 2 * k + 1, e + two, t))
        share(k, 1, 0)
        yield
    for k in range(deep):
        for i in range(2):
            place.arrived(view(block.slot(k, i, 1, order), t), r3 + 2 * k + i)
            share(k, i, 1)
            yield
    for d in range(1, cores):
        source = place.ring(cores - d)
        for k in range(deep):
            for i in range(2):
                for j in range(2):
                    if k + i + j > 0:
                        at = ((d - 1) * deep + k) * 4 + i * 2 + j
                        place.arrived(view(block.slot(k, i, j, lax.rem(source, 2)), source), r4 + at)
    for move in sent:
        move.wait_send()
    kept.wait()


def add_up(target, sources, rows, columns):
    step = max(16, min(rows, 16384 // columns // 16 * 16))

    def body(at, carry):
        piece = pl.ds(pl.multiple_of(at * step, step), step)
        total = sources[0][piece, :].astype(f32)
        for other in sources[1:]:
            total = total + other[piece, :].astype(f32)
        target[piece, :] = total.astype(target.dtype)
        return carry

    lax.fori_loop(0, rows // step, body, 0)


def scatter(place, members, partial, mine, landings, final, view, shape, halves):
    block = Block(place, members)
    deep, e, t = block.deep, place.e, place.t
    rows, columns = shape
    order = 1 - lax.rem(t, 2)
    cores = place.cores if halves else 1
    land0, land1, land2, land3 = landings
    s0, r0 = place.take(4 * deep * cores), place.take(4 * deep * cores)
    s1, r1 = place.take(2 * deep), place.take(2 * deep)
    s2, r2 = place.take(deep), place.take(deep)
    s3, r3 = place.take(deep), place.take(deep)
    s4, r4 = place.take(cores), place.take(cores)
    walk = list(range(1, deep)) + [0]
    turns = [(k, 1, 1) for k in walk]
    for k in walk:
        turns += [(k, 1, 0), (k, 0, 1)]
    turns += [(k, 0, 0) for k in walk]
    one, two = block.flips(order)
    sent, loads = [], {}
    for k, i, j in turns:
        at = k * 4 + i * 2 + j
        for d in range(1, cores):
            target = place.ring(d)
            slot = block.slot(k, i, j, 1 - lax.rem(target, 2))
            place_at = (d - 1) * deep * 4 + at
            sent.append(
                place.send(partial(slot, target), land0.at[place_at], s0 + place_at, r0 + place_at, e, target)
            )
        slot = block.slot(k, i, j, order)
        loads[k, i, j] = place.keep(partial(slot, t), mine.at[slot])
    yield
    for k, i, j in turns:
        at = k * 4 + i * 2 + j
        slot = block.slot(k, i, j, order)
        loads[k, i, j].wait()
        terms = [mine.at[slot]]
        for d in range(1, cores):
            place_at = (d - 1) * deep * 4 + at
            place.arrived(land0.at[place_at], r0 + place_at)
            terms.append(land0.at[place_at])
        if i == 0:
            place.arrived(land1.at[2 * k + j], r1 + 2 * k + j)
            terms.append(land1.at[2 * k + j])
            if j == 0:
                place.arrived(land2.at[k], r2 + k)
                terms.append(land2.at[k])
                if k == 0:
                    for far in range(1, deep):
                        place.arrived(land3.at[far], r3 + far)
                        terms.append(land3.at[far])
        target = final if k + i + j == 0 else mine.at[slot]
        if len(terms) > 1 or k + i + j == 0:
            add_up(target, terms, rows, columns)
        if i == 1:
            sent.append(place.send(mine.at[slot], land1.at[2 * k + j], s1 + 2 * k + j, r1 + 2 * k + j, e + one, t))
        elif j == 1:
            sent.append(place.send(mine.at[slot], land2.at[k], s2 + k, r2 + k, e + two, t))
        elif k > 0:
            peer = block.device(lax.rem(block.rank + k, deep) * 4 + place.quad)
            sent.append(place.send(mine.at[slot], land3.at[k], s3 + k, r3 + k, peer, t))
        yield
    kept = place.keep(final, view(t))
    for d in range(1, cores):
        sent.append(place.send(final, view(t), s4 + d, r4 + d, e, place.ring(d)))
    yield
    for d in range(1, cores):
        place.arrived(view(place.ring(cores - d)), r4 + d)
    for move in sent:
        move.wait_send()
    kept.wait()


def scatter_scratch(members, cores, rows, columns):
    deep = members // 4
    return [
        pltpu.VMEM((members, rows, columns), bf16),
        pltpu.VMEM((max(1, (cores - 1) * members), rows if cores > 1 else 16, columns), bf16),
        pltpu.VMEM((2 * deep, rows, columns), bf16),
        pltpu.VMEM((deep, rows, columns), bf16),
        pltpu.VMEM((deep, rows, columns), bf16),
        pltpu.VMEM((rows, columns), bf16),
    ]


def exchange(place, members, source, landing):
    e, t = place.e, place.t
    own = lax.rem(e, members)
    base = e - own
    sends, arrivals = place.take(members), place.take(members)
    sent = []
    for d in range(1, members):
        target = lax.rem(own + d, members)
        sent.append(place.send(source(target), landing(own), sends + d, arrivals + d, base + target, t))
    kept = place.keep(source(own), landing(own))
    yield
    for d in range(1, members):
        place.arrived(landing(lax.rem(own + members - d, members)), arrivals + d)
    for move in sent:
        move.wait_send()
    kept.wait()


def both(place, members, source, landing, part):
    yield from exchange(place, members, source, lambda slot: landing(place.t, slot))
    sends, arrivals = place.take(place.cores), place.take(place.cores)
    sent = []
    for d in range(1, place.cores):
        mine = part(place.t)
        sent.append(place.send(mine, mine, sends + d, arrivals + d, place.e, place.ring(d)))
    yield
    for d in range(1, place.cores):
        place.arrived(part(place.ring(place.cores - d)), arrivals + d)
    for move in sent:
        move.wait_send()


def run(tasks):
    tasks = list(tasks)
    while tasks:
        left = []
        for task in tasks:
            try:
                next(task)
                left.append(task)
            except StopIteration:
                pass
        tasks = left


def transfer(name, number, mesh, body, ins, outs, scratch=(), semaphores=256, vmem=None):
    count, cores = mesh.shape["expert"], mesh.shape["tensor"]
    semaphores = semaphores * max(1, count * cores // 32)

    def kernel(*refs):
        given = refs[: len(ins)]
        made = refs[len(ins) : len(ins) + len(outs)]
        room = refs[len(ins) + len(outs) : -1]
        place = Place(refs[-1], count, cores)
        place.meet()
        run(body(place, given, made, room))
        assert place.used <= semaphores, place.used

    size = sum(x.size * x.dtype.itemsize for x in list(ins) + list(outs))
    return pl.pallas_call(
        kernel,
        name=name,
        out_shape=[jax.ShapeDtypeStruct(shape, dtype) for shape, dtype in outs_of(outs)],
        in_specs=[ANY] * len(ins),
        out_specs=[ANY] * len(outs),
        scratch_shapes=list(scratch) + [pltpu.SemaphoreType.DMA((semaphores,))],
        cost_estimate=pl.CostEstimate(flops=0, bytes_accessed=size, transcendentals=0),
        compiler_params=pltpu.CompilerParams(
            collective_id=number, has_side_effects=True, vmem_limit_bytes=vmem
        ),
    )(*ins)


def outs_of(outs):
    return [(x.shape, x.dtype) for x in outs]


def like(shape, dtype=bf16):
    return jax.ShapeDtypeStruct(shape, dtype)


def part_view(ref, rows, columns):
    def view(slot, core):
        at = 0 if isinstance(slot, int) else pl.multiple_of(slot * rows, rows)
        return ref.at[pl.ds(at, rows), pl.ds(pl.multiple_of(core * columns, columns), columns)]

    return view


def rotary(values, cosine, sine):
    half = values.shape[-1] // 2
    first = values[..., :half]
    second = values[..., half:]
    return jnp.concatenate([first * cosine - second * sine, second * cosine + first * sine], axis=-1)


def rotary_back(grads, cosine, sine):
    half = grads.shape[-1] // 2
    first = grads[..., :half]
    second = grads[..., half:]
    return jnp.concatenate([first * cosine + second * sine, second * cosine - first * sine], axis=-1)


def sequence_tables(lengths_rows, tok_rows):
    ends = jnp.cumsum(lengths_rows, axis=1)
    starts = ends - lengths_rows
    places = jnp.arange(tok_rows, dtype=jnp.int32)
    segment = jnp.sum((places[None, :, None] >= ends[:, None, :]).astype(jnp.int32), axis=2)
    member = segment[:, :, None] == jnp.arange(lengths_rows.shape[1], dtype=jnp.int32)[None, None, :]
    first = jnp.sum(jnp.where(member, starts[:, None, :], 0), axis=2)
    return segment, places[None, :] - first


def silu_parts(values):
    sigmoid_value = jax.nn.sigmoid(values)
    return values * sigmoid_value, sigmoid_value * (1.0 + values * (1.0 - sigmoid_value))


def mm(form, left, right):
    return jnp.einsum(form, left, right, preferred_element_type=f32)


def up_to(value, step):
    return -(-value // step) * step


def local(
    mesh,
    tokens,
    lengths,
    routes,
    gain_attn,
    w_query,
    w_key,
    w_value,
    w_out,
    gain_ffn,
    w_router,
    routed_gate_weight,
    routed_up_weight,
    w_down,
    w_shared_gate,
    w_shared_up,
    w_shared_down,
    out_grad,
):
    count, cores = mesh.shape["expert"], mesh.shape["tensor"]
    rows, width = tokens.shape
    part = width // cores
    deep = w_query.shape[0]
    experts = w_router.shape[1]
    heads = w_query.shape[1] // HEAD_DIM
    capacity = min(rows, rows * TOP * 4 // (3 * count))
    hidden_units = w_shared_gate.shape[1] // count
    scale = HEAD_DIM ** (-0.5)
    e = lax.axis_index("expert")
    t = lax.axis_index("tensor")
    chunk = heads * rows

    expert_ids = jnp.arange(experts, dtype=jnp.int32)
    choose = jnp.any(routes[:, :, None] == expert_ids[None, None, :], axis=1)
    mask_t = choose.T.astype(bf16)
    vectors = jnp.concatenate(
        [
            w_router.T,
            gain_attn[None],
            gain_ffn[None],
            jnp.pad(lengths.astype(bf16), ((0, 0), (0, deep - lengths.shape[1]))),
        ],
        axis=0,
    )
    head_rows = up_to(vectors.shape[0], 16)
    vectors = jnp.pad(vectors, ((0, head_rows - vectors.shape[0]), (0, 0)))
    pieces = rows // deep
    mask_rows = mask_t.reshape(experts * pieces, deep)
    small = jnp.concatenate([vectors, mask_rows], axis=0)
    small_rows = up_to(small.shape[0], 16)
    small = jnp.pad(small, ((0, small_rows - small.shape[0]), (0, 0)))

    def by_head(weight):
        return weight.reshape(deep, heads, HEAD_DIM).transpose(1, 0, 2)

    w_heads = jnp.concatenate([by_head(w_query), by_head(w_key), by_head(w_value)], axis=2)

    def first_body(place, given, made, room):
        tok, wh, sm = given
        tok_all, wh_all, sm_all = made
        view = part_view(tok_all, rows, part)
        yield exchange(place, count, lambda s: sm, lambda s: sm_all.at[s])
        yield gather(
            place,
            heads,
            tok.at[:, pl.ds(pl.multiple_of(place.t * part, part), part)],
            (tok, lambda s: tok_all.at[pl.ds(pl.multiple_of(s * rows, rows), rows), :]),
            view,
            True,
        )
        yield exchange(place, count, lambda s: wh.at[lax.rem(s, heads)], lambda s: wh_all.at[s])

    tok_chunk, w_qkv, small_all = transfer(
        "gather_tokens",
        0,
        mesh,
        first_body,
        (tokens, w_heads, small),
        (like((chunk, width)), like((count, deep, 3 * HEAD_DIM)), like((count, small_rows, deep))),
    )
    w_qkv = w_qkv.reshape(width, 3 * HEAD_DIM)

    router_full = small_all[:, :experts].transpose(1, 0, 2).reshape(experts, width)
    attn_gain = small_all[:, experts].reshape(width).astype(f32)
    ffn_gain = small_all[:, experts + 1].reshape(width).astype(f32)
    lengths_all = small_all[:, experts + 2, : lengths.shape[1]].astype(f32).astype(jnp.int32)
    masks = small_all[:, head_rows : head_rows + experts * pieces].reshape(count, experts, rows)

    member = e % heads
    lengths_chunk = lax.dynamic_slice_in_dim(lengths_all, e - member, heads, axis=0)
    segment, positions = sequence_tables(lengths_chunk, rows)
    half = HEAD_DIM // 2
    inverse = 10000.0 ** (-2.0 * jnp.arange(half, dtype=f32) / HEAD_DIM)
    angles = positions.astype(f32)[:, :, None] * inverse[None, None, :]
    cosine, sine = jnp.cos(angles), jnp.sin(angles)

    tok32 = tok_chunk.astype(f32)
    rstd_chunk = lax.rsqrt(jnp.mean(tok32 * tok32, axis=-1, keepdims=True) + eps)
    xn_chunk = (tok32 * rstd_chunk * attn_gain).astype(bf16)
    qkv = jnp.dot(xn_chunk, w_qkv, preferred_element_type=f32).reshape(heads, rows, 3 * HEAD_DIM)
    query = rotary(qkv[..., :HEAD_DIM], cosine, sine).astype(bf16)
    keyed = rotary(qkv[..., HEAD_DIM : 2 * HEAD_DIM], cosine, sine).astype(bf16)
    valued = qkv[..., 2 * HEAD_DIM :].astype(bf16)
    places = jnp.arange(rows, dtype=jnp.int32)
    allowed = (segment[:, :, None] == segment[:, None, :]) & (places[None, :] <= places[:, None])[None]
    scores = jnp.where(allowed, mm("gqd,gkd->gqk", query, keyed) * scale, floor_score)
    top_score = jnp.max(scores, axis=-1, keepdims=True)
    raised = jnp.exp(scores - top_score)
    probs = raised / jnp.sum(raised, axis=-1, keepdims=True)
    probs_low = probs.astype(bf16)
    head_out = mm("gqk,gkd->gqd", probs_low, valued).astype(bf16)

    shared_pack = jnp.concatenate(
        [
            w_shared_gate.T.reshape(count, hidden_units, deep),
            w_shared_up.T.reshape(count, hidden_units, deep),
            w_shared_down.reshape(count, hidden_units, deep),
        ],
        axis=1,
    )
    pack_rows = up_to(3 * hidden_units, 16)
    shared_pack = jnp.pad(shared_pack, ((0, 0), (0, pack_rows - 3 * hidden_units), (0, 0)))
    out_rows = w_out.shape[0]

    def second_body(place, given, made, room):
        ho, og, wo, sp = given
        ho_all, og_all, wo_all, sp_all = made
        yield exchange(place, heads, lambda s: ho.at[s], lambda s: ho_all.at[s])
        yield gather(
            place,
            count,
            og.at[:, pl.ds(pl.multiple_of(place.t * part, part), part)],
            (og, lambda s: og_all.at[pl.ds(pl.multiple_of(s * rows, rows), rows), :]),
            part_view(og_all, rows, part),
            True,
        )
        yield gather(place, count, wo, (wo, lambda s: wo_all.at[s]), lambda s, c: wo_all.at[s], False)
        yield exchange(place, count, lambda s: sp.at[s], lambda s: sp_all.at[s])

    heads_own, grad_all, w_out_all, shared_all = transfer(
        "gather_inputs",
        1,
        mesh,
        second_body,
        (head_out, out_grad, w_out, shared_pack),
        (
            like((heads, rows, HEAD_DIM)),
            like((count * rows, width)),
            like((count, out_rows, deep)),
            like((count, pack_rows, deep)),
        ),
        semaphores=400,
    )
    heads_out = heads_own.transpose(1, 0, 2).reshape(rows, heads * HEAD_DIM)
    out_full = w_out_all.transpose(1, 0, 2).reshape(out_rows, width)
    shared_cut = shared_all[:, : 3 * hidden_units].transpose(1, 0, 2).reshape(3 * hidden_units, width)
    sh_in = shared_cut[: 2 * hidden_units]
    sh_down = shared_cut[2 * hidden_units :]

    attention = lax.psum(
        jnp.dot(heads_out, out_full, preferred_element_type=f32).astype(bf16), "tensor"
    ).astype(f32)
    inputs = tokens.astype(f32)
    hidden = inputs + attention
    rstd_two = lax.rsqrt(jnp.mean(hidden * hidden, axis=-1, keepdims=True) + eps)
    xn_two = (hidden * rstd_two * ffn_gain).astype(bf16)
    logits = mm("td,ed->te", xn_two, router_full)
    top_logit = jnp.max(jnp.where(choose, logits, floor_score), axis=1, keepdims=True)
    lifted = jnp.where(choose, jnp.exp(jnp.where(choose, logits - top_logit, 0.0)), 0.0)
    gates = lifted / jnp.sum(lifted, axis=1, keepdims=True)

    def third_body(place, given, made, room):
        xn, gt = given
        xn_all, gt_all = made
        yield gather(
            place,
            count,
            xn.at[:, pl.ds(pl.multiple_of(place.t * part, part), part)],
            (xn, lambda s: xn_all.at[pl.ds(pl.multiple_of(s * rows, rows), rows), :]),
            part_view(xn_all, rows, part),
            True,
        )
        yield exchange(place, count, lambda s: gt, lambda s: gt_all.at[s])

    xn_all, gates_all = transfer(
        "gather_rows",
        2,
        mesh,
        third_body,
        (xn_two, gates.T),
        (like((count * rows, width)), like((count, experts, rows), f32)),
    )

    own_mask = lax.dynamic_index_in_dim(masks, e, axis=1, keepdims=False).astype(f32)
    own_gate = lax.dynamic_index_in_dim(gates_all, e, axis=1, keepdims=False)
    position = (jnp.cumsum(own_mask, axis=1) - own_mask).astype(jnp.int32)
    slots = jnp.arange(capacity, dtype=jnp.int32)
    chosen = (position[:, None, :] == slots[None, :, None]) & (own_mask[:, None, :] > 0.5)
    onehot = chosen.astype(bf16)
    slot_gate = jnp.sum(jnp.where(chosen, own_gate[:, None, :], 0.0), axis=2)
    gate_column = slot_gate.reshape(count * capacity, 1)
    gate_weight, up_weight, down_weight = routed_gate_weight[0], routed_up_weight[0], w_down[0]

    received = mm("gst,gtd->gsd", onehot, xn_all.reshape(count, rows, width)).astype(bf16)
    received = received.reshape(count * capacity, width)
    grad_rows = mm("gst,gtd->gsd", onehot, grad_all.reshape(count, rows, width))
    grad_rows = grad_rows.reshape(count * capacity, width)
    gated_grad = (gate_column * grad_rows).astype(bf16)

    exp_gate = jnp.dot(received, gate_weight, preferred_element_type=f32)
    exp_up = jnp.dot(received, up_weight, preferred_element_type=f32)
    exp_silu, exp_slope = silu_parts(exp_gate)
    exp_act = (exp_silu * exp_up).astype(bf16)
    exp_out = jnp.dot(exp_act, down_weight, preferred_element_type=f32)
    slot_dots = jnp.sum(grad_rows * exp_out, axis=1).reshape(count, capacity)
    token_dots = jnp.sum(jnp.where(chosen, slot_dots[:, :, None], 0.0), axis=1)
    exp_low = (gate_column * exp_out).astype(bf16).reshape(count, capacity, width)

    sh_both = mm("td,hd->th", xn_all, sh_in)
    sh_gate, sh_up = sh_both[:, :hidden_units], sh_both[:, hidden_units:]
    sh_silu, sh_slope = silu_parts(sh_gate)
    sh_act = (sh_silu * sh_up).astype(bf16)
    forward_part = (
        mm("gst,gsd->gtd", onehot, exp_low).reshape(count * rows, width)
        + jnp.dot(sh_act, sh_down, preferred_element_type=f32)
    ).astype(bf16)

    def fourth_body(place, given, made, room):
        fp, td = given
        mixed, dots = made
        mixed_view = part_view(mixed, rows, part)
        yield scatter(
            place,
            count,
            part_view(fp, rows, part),
            room[0],
            room[1:5],
            room[5],
            lambda c: mixed_view(0, c),
            (rows, part),
            True,
        )
        yield both(place, count, lambda s: td.at[s], lambda c, s: dots.at[c, s], lambda c: dots.at[c])

    dots_sent = jnp.pad(token_dots[:, None, :], ((0, 0), (0, 7), (0, 0)))
    mixture, dots_all = transfer(
        "scatter_output",
        3,
        mesh,
        fourth_body,
        (forward_part, dots_sent),
        (like((rows, width)), like((cores, count, 8, rows), f32)),
        scatter_scratch(count, cores, rows, part),
        vmem=56 * 2**20,
    )
    output = (hidden + mixture.astype(f32)).astype(bf16)

    gate_total = jnp.sum(dots_all[:, :, 0, :], axis=0).T
    weighted_dots = jnp.sum(gates * gate_total, axis=1, keepdims=True)
    grad_logits = gates * (gate_total - weighted_dots)

    act_grad = mm("rd,fd->rf", gated_grad, down_weight)
    gate_back = (act_grad * exp_up * exp_slope).astype(bf16)
    up_back = (act_grad * exp_silu).astype(bf16)
    back_rows = (mm("rf,df->rd", gate_back, gate_weight) + mm("rf,df->rd", up_back, up_weight)).astype(bf16)
    grad_shact = mm("td,fd->tf", grad_all, sh_down)
    back_shared = jnp.concatenate(
        [(grad_shact * sh_up * sh_slope).astype(bf16), (grad_shact * sh_silu).astype(bf16)], axis=1
    )
    backward_part = (
        mm("gst,gsd->gtd", onehot, back_rows.reshape(count, capacity, width)).reshape(count * rows, width)
        + jnp.dot(back_shared, sh_in, preferred_element_type=f32)
    ).astype(bf16)

    def fifth_body(place, given, made, room):
        bp, gl = given
        summed, logit_all = made
        summed_view = part_view(summed, rows, part)
        yield scatter(
            place,
            count,
            part_view(bp, rows, part),
            room[0],
            room[1:5],
            room[5],
            lambda c: summed_view(0, c),
            (rows, part),
            True,
        )
        yield exchange(place, count, lambda s: gl, lambda s: logit_all.at[s])

    summed_back, logits_all = transfer(
        "scatter_back",
        4,
        mesh,
        fifth_body,
        (backward_part, grad_logits.T),
        (like((rows, width)), like((count, experts, rows), f32)),
        scatter_scratch(count, cores, rows, part),
        vmem=56 * 2**20,
    )

    down_grad = mm("rf,rd->fd", exp_act, gated_grad)
    gate_grad = mm("rd,rf->df", received, gate_back)
    up_grad = mm("rd,rf->df", received, up_back)
    shared_grads = jnp.concatenate(
        [mm("tf,td->fd", back_shared, xn_all).astype(bf16), mm("tf,td->fd", sh_act, grad_all).astype(bf16)],
        axis=0,
    )
    shared_grads = shared_grads.reshape(3 * hidden_units, count, deep).transpose(1, 0, 2)
    shared_grads = jnp.pad(shared_grads, ((0, 0), (0, pack_rows - 3 * hidden_units), (0, 0)))
    xn_columns = lax.dynamic_slice_in_dim(xn_all, e * deep, deep, axis=1).astype(f32).reshape(count, rows, deep)
    router_grad = jnp.einsum("gtd,get->de", xn_columns, logits_all, precision=highest)

    cotangent = out_grad.astype(f32)
    grad_two = summed_back.astype(f32) + jnp.einsum(
        "te,ed->td", grad_logits, router_full.astype(f32), precision=highest
    )
    scaled = grad_two * ffn_gain
    inner = jnp.mean(scaled * hidden, axis=-1, keepdims=True)
    grad_hidden = cotangent + rstd_two * scaled - hidden * (rstd_two * rstd_two * rstd_two) * inner
    ffn_gain_part = jnp.sum(grad_two * hidden * rstd_two, axis=0)
    grad_branch = grad_hidden.astype(bf16)
    grad_heads = mm("td,cd->tc", grad_branch, out_full).astype(bf16)
    grad_heads = grad_heads.reshape(rows, heads, HEAD_DIM).transpose(1, 0, 2)
    out_proj_part = mm("tc,td->cd", heads_out, grad_branch).astype(bf16)
    out_proj_part = out_proj_part.reshape(out_rows, count, deep).transpose(1, 0, 2)

    def sixth_body(place, given, made, room):
        yield exchange(place, heads, lambda s: given[0].at[s], lambda s: made[0].at[s])

    (grad_head,) = transfer(
        "exchange_heads",
        5,
        mesh,
        sixth_body,
        (grad_heads,),
        (like((heads, rows, HEAD_DIM)),),
    )

    grad_value = mm("gqk,gqd->gkd", probs_low, grad_head)
    grad_probs = mm("gqd,gkd->gqk", grad_head, valued)
    weighted = jnp.sum(probs * grad_probs, axis=-1, keepdims=True)
    grad_scores = (probs * (grad_probs - weighted)).astype(bf16)
    grad_query = mm("gqk,gkd->gqd", grad_scores, keyed) * scale
    grad_key = mm("gqk,gqd->gkd", grad_scores, query) * scale
    grad_qkv = jnp.concatenate(
        [
            rotary_back(grad_query, cosine, sine).astype(bf16),
            rotary_back(grad_key, cosine, sine).astype(bf16),
            grad_value.astype(bf16),
        ],
        axis=2,
    ).reshape(chunk, 3 * HEAD_DIM)
    qkv_grad = mm("td,tc->dc", xn_chunk, grad_qkv).astype(bf16).reshape(count, deep, 3 * HEAD_DIM)
    grad_one_part = mm("tc,dc->td", grad_qkv, w_qkv)
    attn_gain_part = jnp.sum(grad_one_part * tok32 * rstd_chunk, axis=0)

    def spread(vector):
        return jnp.pad(vector.reshape(count, 1, deep), ((0, 0), (0, 7), (0, 0)))

    def seventh_body(place, given, made, room):
        gp, qg, op, sg, ag, fg = given
        one, qg_all, op_sum, sg_all, ag_all, fg_all = made
        one_view = part_view(one, rows, part)
        yield scatter(
            place,
            heads,
            part_view(gp, rows, part),
            room[0],
            room[1:5],
            room[5],
            lambda c: one_view(0, c),
            (rows, part),
            True,
        )
        yield scatter(
            place,
            count,
            lambda s, c: op.at[s],
            room[6],
            room[7:11],
            room[11],
            lambda c: op_sum,
            (out_rows, deep),
            False,
        )
        yield both(place, count, lambda s: ag.at[s], lambda c, s: ag_all.at[c, s], lambda c: ag_all.at[c])
        yield exchange(place, count, lambda s: fg.at[s], lambda s: fg_all.at[s])
        yield exchange(place, count, lambda s: qg.at[s], lambda s: qg_all.at[s])
        yield exchange(place, count, lambda s: sg.at[s], lambda s: sg_all.at[s])

    grad_one, qkv_all, out_proj_sum, shared_back, attn_gains, ffn_gains = transfer(
        "scatter_grads",
        6,
        mesh,
        seventh_body,
        (
            grad_one_part.astype(bf16),
            qkv_grad,
            out_proj_part,
            shared_grads,
            spread(attn_gain_part),
            spread(ffn_gain_part),
        ),
        (
            like((rows, width)),
            like((count, deep, 3 * HEAD_DIM)),
            like((out_rows, deep)),
            like((count, pack_rows, deep)),
            like((cores, count, 8, deep), f32),
            like((count, 8, deep), f32),
        ),
        scatter_scratch(heads, cores, rows, part) + scatter_scratch(count, 1, out_rows, deep),
        semaphores=600,
        vmem=56 * 2**20,
    )

    grad_one = grad_one.astype(f32)
    rstd_one = lax.rsqrt(jnp.mean(inputs * inputs, axis=-1, keepdims=True) + eps)
    scaled_one = grad_one * attn_gain
    inner_one = jnp.mean(scaled_one * inputs, axis=-1, keepdims=True)
    input_grad = (
        grad_hidden + rstd_one * scaled_one - inputs * (rstd_one * rstd_one * rstd_one) * inner_one
    ).astype(bf16)
    qkv_sum = jnp.sum(qkv_all.reshape(count // heads, heads, deep, 3 * HEAD_DIM).astype(f32), axis=0)
    qkv_sum = qkv_sum.transpose(1, 0, 2)

    def of_heads(which):
        return qkv_sum[:, :, which * HEAD_DIM : (which + 1) * HEAD_DIM].reshape(deep, heads * HEAD_DIM)

    def of_shared(which):
        return shared_back[:, which * hidden_units : (which + 1) * hidden_units].reshape(-1, deep).astype(f32)

    return (
        output,
        input_grad,
        jnp.sum(attn_gains[:, :, 0, :], axis=(0, 1)),
        of_heads(0),
        of_heads(1),
        of_heads(2),
        out_proj_sum.astype(f32),
        jnp.sum(ffn_gains[:, 0, :], axis=0),
        router_grad,
        gate_grad[None],
        up_grad[None],
        down_grad[None],
        of_shared(0).T,
        of_shared(1).T,
        of_shared(2),
    )


def solution(mesh):
    in_specs = (
        P("expert", None),
        P("expert", None),
        P("expert", None),
        P("expert"),
        P("expert", "tensor"),
        P("expert", "tensor"),
        P("expert", "tensor"),
        P("tensor", "expert"),
        P("expert"),
        P("expert", None),
        P("expert", None, "tensor"),
        P("expert", None, "tensor"),
        P("expert", "tensor", None),
        P("expert", "tensor"),
        P("expert", "tensor"),
        P("tensor", "expert"),
        P("expert", None),
    )
    out_specs = (
        P("expert", None),
        P("expert", None),
        P("expert"),
        P("expert", "tensor"),
        P("expert", "tensor"),
        P("expert", "tensor"),
        P("tensor", "expert"),
        P("expert"),
        P("expert", None),
        P("expert", None, "tensor"),
        P("expert", None, "tensor"),
        P("expert", "tensor", None),
        P("expert", "tensor"),
        P("expert", "tensor"),
        P("tensor", "expert"),
    )
    return jax.shard_map(
        functools.partial(local, mesh), mesh=mesh, in_specs=in_specs, out_specs=out_specs, check_vma=False
    )
```

```python
import functools

import jax
import jax.numpy as jnp
from jax import lax
from jax.experimental import pallas as pl
from jax.experimental.pallas import tpu as pltpu
from jax.sharding import PartitionSpec as P

HEAD_DIM = 128
TOP = 6
MESH = pl.DeviceIdType.MESH
ANY = pl.BlockSpec(memory_space=pl.ANY)

bf16 = jnp.bfloat16
f32 = jnp.float32
eps = 1e-06
highest = lax.Precision.HIGHEST
floor_score = -1e30


class Place:
    def __init__(self, sems, count, cores):
        self.sems, self.used = sems, 0
        self.count, self.cores = count, cores
        self.e = lax.axis_index("expert")
        self.t = lax.axis_index("tensor")
        self.quad = lax.rem(self.e, 4)
        self.far = lax.div(self.e, 4)

    def take(self, number):
        first = self.used
        self.used = first + number
        return first

    def ring(self, distance):
        return lax.rem(self.t + distance, self.cores)

    def copy(self, src, dst, out_sem, in_sem, e, t):
        return pltpu.make_async_remote_copy(
            src_ref=src,
            dst_ref=dst,
            send_sem=self.sems.at[out_sem],
            recv_sem=self.sems.at[in_sem],
            device_id={"expert": e, "tensor": t},
            device_id_type=MESH,
        )

    def send(self, src, dst, out_sem, in_sem, e, t):
        move = self.copy(src, dst, out_sem, in_sem, e, t)
        move.start()
        return move

    def arrived(self, landing, in_sem):
        self.copy(landing, landing, in_sem, in_sem, self.e, self.t).wait_recv()

    def keep(self, src, dst):
        move = pltpu.make_async_copy(src, dst, self.sems.at[self.take(1)])
        move.start()
        return move

    def meet(self):
        barrier = pltpu.get_barrier_semaphore()
        for step in range(1, self.count):
            pl.semaphore_signal(
                barrier,
                inc=1,
                device_id={"expert": lax.rem(self.e + step, self.count), "tensor": self.t},
                device_id_type=MESH,
            )
        for step in range(1, self.cores):
            pl.semaphore_signal(
                barrier,
                inc=1,
                device_id={"expert": self.e, "tensor": self.ring(step)},
                device_id_type=MESH,
            )
        pl.semaphore_wait(barrier, self.count + self.cores - 2)


class Block:
    def __init__(self, place, members):
        self.place, self.deep = place, members // 4
        self.rank = lax.rem(place.far, self.deep)
        self.start = place.far - self.rank

    def flips(self, order):
        high, low = lax.div(self.place.quad, 2), lax.rem(self.place.quad, 2)
        one = high + (low - high) * order
        two = low + (high - low) * order
        return (2 - order) * (1 - 2 * one), (1 + order) * (1 - 2 * two)

    def slot(self, k, i, j, order):
        one, two = self.flips(order)
        return lax.rem(self.rank + k, self.deep) * 4 + self.place.quad + i * one + j * two

    def own(self):
        return self.rank * 4 + self.place.quad

    def device(self, slot):
        return self.start * 4 + slot


def when(condition, action):
    if condition is None:
        action()
    else:
        pl.when(condition)(action)


def gather(place, members, mine, whole, view, halves, pieces=1):
    block = Block(place, members)
    deep, e, t, rank = block.deep, place.e, place.t, block.rank
    order = lax.rem(t, 2)
    cores = place.cores if halves else 1
    spots = 2 * deep - 1

    def lots(number):
        return place.take(number * pieces)

    zs, zr = lots(spots + 1), lots(spots)
    s2, r2 = lots(spots), lots(spots)
    s3, r3 = lots(2 * spots), lots(2 * spots)
    s4, r4 = lots(4 * spots * (cores - 1)), lots(4 * spots * (cores - 1))
    one, two = block.flips(order)
    own = block.own()
    sent, kept = [], place.keep(whole[0], whole[1](own))
    line = [(0, 0)] + [(d, way) for d in range(1, deep) for way in (1, -1)]

    def index(d, way):
        return 0 if d == 0 else 2 * d - (1 if way > 0 else 0)

    def valid(d, way):
        return None if d == 0 else (rank >= d if way > 0 else rank < deep - d)

    def slot_of(d, way, i, j, order=order):
        one, two = block.flips(order)
        return (rank - way * d) * 4 + place.quad + i * one + j * two

    ends = {1: (rank < deep - 1, 4), -1: (rank >= 1, -4)}

    def onward(d, way, p):
        condition, step = ends[way]
        if d > 0:
            condition = jnp.logical_and(condition, valid(d, way))
        v = index(d, way)
        out = 1 + v if d > 0 else (0 if way > 0 else 1)
        source = view(slot_of(d, way, 0, 0), t, p) if d > 0 else mine(p)
        landing = view(slot_of(d, way, 0, 0), t, p)
        move = place.copy(source, landing, zs + out * pieces + p, zr + index(d + 1, way) * pieces + p, e + step, t)
        sent.append((condition, move))
        when(condition, move.start)

    def pass_on(source, landing, condition, out, into, number, p, target):
        move = place.copy(source, landing, out + number * pieces + p, into + number * pieces + p, target, t)
        sent.append((condition, move))
        return move

    def share(d, way, i, j, p):
        moves = []
        ref = view(slot_of(d, way, i, j), t, p)
        for far in range(1, cores):
            at = (((far - 1) * spots + index(d, way)) * 4 + i * 2 + j) * pieces + p
            move = place.copy(ref, ref, s4 + at, r4 + at, e, place.ring(far))
            sent.append((valid(d, way), move))
            moves.append(move)
        return moves

    def start(moves):
        for move in moves:
            move.start()

    for p in range(pieces):
        if deep > 1:
            onward(0, 1, p)
            onward(0, -1, p)
        pass_on(mine(p), view(own, t, p), None, s2, r2, 0, p, e + one).start()
        pass_on(mine(p), view(own, t, p), None, s3, r3, 0, p, e + two).start()
        yield

    def from_line(d, way, p):
        ref = view(slot_of(d, way, 0, 0), t, p)
        v, condition = index(d, way), valid(d, way)
        when(condition, lambda: place.arrived(ref, zr + v * pieces + p))
        if d < deep - 1:
            onward(d, way, p)
        moves = [
            pass_on(ref, ref, condition, s2, r2, v, p, e + one),
            pass_on(ref, ref, condition, s3, r3, 2 * v, p, e + two),
        ] + share(d, way, 0, 0, p)
        when(condition, lambda: start(moves))

    def from_one(d, way, p):
        ref = view(slot_of(d, way, 1, 0), t, p)
        v, condition = index(d, way), valid(d, way)
        moves = [pass_on(ref, ref, condition, s3, r3, 2 * v + 1, p, e + two)] + share(d, way, 1, 0, p)

        def act():
            place.arrived(ref, r2 + v * pieces + p)
            start(moves)

        when(condition, act)

    def from_two(d, way, i, p):
        ref = view(slot_of(d, way, i, 1), t, p)
        v, condition = index(d, way), valid(d, way)
        moves = share(d, way, i, 1, p)

        def act():
            place.arrived(ref, r3 + (2 * v + i) * pieces + p)
            start(moves)

        when(condition, act)

    for d in range(1, deep + 1):
        for p in range(pieces):
            for way in (1, -1) if d > 1 else (1,):
                from_one(d - 1, way if d > 1 else 0, p)
            if d < deep:
                for way in (1, -1):
                    from_line(d, way, p)
            yield
    for d, way in line:
        for i in range(2):
            for p in range(pieces):
                from_two(d, way, i, p)
        yield
    for far in range(1, cores):
        source = place.ring(cores - far)
        for d, way in line:
            for i in range(2):
                for j in range(2):
                    if d + i + j > 0:
                        for p in range(pieces):
                            at = (((far - 1) * spots + index(d, way)) * 4 + i * 2 + j) * pieces + p
                            ref = view(slot_of(d, way, i, j, lax.rem(source, 2)), source, p)
                            when(valid(d, way), functools.partial(place.arrived, ref, r4 + at))
    for condition, move in sent:
        when(condition, move.wait_send)
    kept.wait()


def add_up(target, sources, rows, columns):
    step = max(16, min(rows, 16384 // columns // 16 * 16))

    def body(at, carry):
        piece = pl.ds(pl.multiple_of(at * step, step), step)
        total = sources[0][piece, :].astype(f32)
        for other in sources[1:]:
            total = total + other[piece, :].astype(f32)
        target[piece, :] = total.astype(target.dtype)
        return carry

    lax.fori_loop(0, rows // step, body, 0)


class Product:
    def __init__(self, place, left, varied, fixed, rooms, members, rows, columns):
        self.place, self.left, self.varied = place, left, varied
        self.lhs, self.rhs = rooms
        self.rows, self.columns = rows, columns
        self.lead = 0 if varied is None else varied.shape[0] // members
        self.waits, self.turn = {}, 0
        self.setup = []
        for buffer in range(self.rhs.shape[0]):
            self.setup.append(place.keep(fixed, self.rhs.at[buffer, pl.ds(self.lead, fixed.shape[0]), :]))

    def fetch(self, turn, slot):
        buffer = turn % 2
        rows = pl.ds(pl.multiple_of(slot * self.rows, self.rows), self.rows)
        moves = [self.place.keep(self.left.at[rows, :], self.lhs.at[buffer])]
        if self.lead:
            lead = pl.ds(pl.multiple_of(slot * self.lead, self.lead), self.lead)
            moves.append(self.place.keep(self.varied.at[lead, :], self.rhs.at[buffer, pl.ds(0, self.lead), :]))
        self.waits[turn] = moves

    def ready(self, turn):
        for move in self.setup:
            move.wait()
        self.setup = []
        for move in self.waits.pop(turn):
            move.wait()

    def make(self, turn, core, target):
        buffer = turn % 2
        right = self.rhs.at[buffer if self.lead else 0]
        wide = min(self.columns, 512)

        def body(at, carry):
            source = pl.ds(pl.multiple_of(core * self.columns + at * wide, wide), wide)
            into = pl.ds(pl.multiple_of(at * wide, wide), wide)
            target[:, into] = jnp.dot(
                self.lhs[buffer], right[:, source], preferred_element_type=f32
            ).astype(bf16)
            return carry

        lax.fori_loop(0, self.columns // wide, body, 0)


def scatter(place, members, source, room, view, shape, halves):
    block = Block(place, members)
    deep, e, t = block.deep, place.e, place.t
    rows, columns = shape
    order = 1 - lax.rem(t, 2)
    cores = place.cores if halves else 1
    mine, outgoing, land0, land1, land2, land3, final = room
    s0, r0 = place.take(4 * deep * cores), place.take(4 * deep * cores)
    s1, r1 = place.take(2 * deep), place.take(2 * deep)
    s2, r2 = place.take(deep), place.take(deep)
    s3, r3 = place.take(deep), place.take(deep)
    s4, r4 = place.take(cores), place.take(cores)
    walk = list(range(1, deep)) + [0]
    one, two = block.flips(order)
    sent, loads = [], {}
    quads = [(1, 1), (1, 0), (0, 1), (0, 0)]
    turns = [(k, i, j) for k in walk for i, j in quads]
    ring = outgoing.shape[0]
    leaving = []

    def slot_of(k, i, j):
        return block.slot(k, i, j, order)

    def produce(number):
        k, i, j = turns[number]
        if isinstance(source, Product):
            if number == 0:
                source.fetch(0, slot_of(*turns[0]))
            source.ready(number)
            if number + 1 < len(turns):
                source.fetch(number + 1, slot_of(*turns[number + 1]))
            if number >= ring:
                for move in leaving[number - ring]:
                    move.wait_send()
            moves = []
            for d in range(1, cores):
                target = place.ring(d)
                buffer = outgoing.at[number % ring, d - 1]
                source.make(number, target, buffer)
                at = (d - 1) * deep * 4 + k * 4 + (j * 2 + i if d % 2 else i * 2 + j)
                moves.append(place.send(buffer, land0.at[at], s0 + at, r0 + at, e, target))
            leaving.append(moves)
            source.make(number, t, mine.at[slot_of(k, i, j)])
        else:
            loads[k, i, j] = place.keep(source(slot_of(k, i, j)), mine.at[slot_of(k, i, j)])

    def terms_of(k, i, j):
        at = k * 4 + i * 2 + j
        if (k, i, j) in loads:
            loads[k, i, j].wait()
        terms = [mine.at[slot_of(k, i, j)]]
        for d in range(1, cores):
            place_at = (d - 1) * deep * 4 + at
            place.arrived(land0.at[place_at], r0 + place_at)
            terms.append(land0.at[place_at])
        if i == 0:
            place.arrived(land1.at[2 * k + j], r1 + 2 * k + j)
            terms.append(land1.at[2 * k + j])
            if j == 0:
                place.arrived(land2.at[k], r2 + k)
                terms.append(land2.at[k])
        return terms

    def first_flip(k, j):
        terms, ref = terms_of(k, 1, j), mine.at[slot_of(k, 1, j)]
        if len(terms) > 1:
            add_up(ref, terms, rows, columns)
        sent.append(place.send(ref, land1.at[2 * k + j], s1 + 2 * k + j, r1 + 2 * k + j, e + one, t))

    def second_flip(k):
        ref = mine.at[slot_of(k, 0, 1)]
        add_up(ref, terms_of(k, 0, 1), rows, columns)
        sent.append(place.send(ref, land2.at[k], s2 + k, r2 + k, e + two, t))

    def line(k):
        terms, ref = terms_of(k, 0, 0), mine.at[slot_of(k, 0, 0)]
        if k > 0:
            add_up(ref, terms, rows, columns)
            peer = block.device(lax.rem(block.rank + k, deep) * 4 + place.quad)
            sent.append(place.send(ref, land3.at[k], s3 + k, r3 + k, peer, t))
            return
        for far in range(1, deep):
            place.arrived(land3.at[far], r3 + far)
            terms.append(land3.at[far])
        add_up(final, terms, rows, columns)

    for step in range(deep + 3):
        if step < deep:
            for number in range(4 * step, 4 * step + 4):
                produce(number)
                yield
        if 0 <= step - 1 < deep:
            first_flip(walk[step - 1], 1)
            yield
            first_flip(walk[step - 1], 0)
            yield
        if 0 <= step - 2 < deep:
            second_flip(walk[step - 2])
            yield
        if 0 <= step - 3 < deep:
            line(walk[step - 3])
            yield
    kept = place.keep(final, view(t))
    for d in range(1, cores):
        sent.append(place.send(final, view(t), s4 + d, r4 + d, e, place.ring(d)))
    yield
    for d in range(1, cores):
        place.arrived(view(place.ring(cores - d)), r4 + d)
    for moves in leaving[-ring:]:
        for move in moves:
            move.wait_send()
    for move in sent:
        move.wait_send()
    kept.wait()


def scatter_scratch(members, cores, rows, columns, depth=0, lead=0):
    deep = members // 4
    held = pltpu.VMEM((max(1, (cores - 1) * members), rows if cores > 1 else 16, columns), bf16)
    ring = pltpu.VMEM((min(8, members), max(1, cores - 1), rows if cores > 1 else 16, columns), bf16)
    rooms = [
        pltpu.VMEM((members, rows, columns), bf16),
        ring,
        held,
        pltpu.VMEM((2 * deep, rows, columns), bf16),
        pltpu.VMEM((deep, rows, columns), bf16),
        pltpu.VMEM((deep, rows, columns), bf16),
        pltpu.VMEM((rows, columns), bf16),
    ]
    if depth:
        rooms.append(pltpu.VMEM((2, rows, depth), bf16))
        rooms.append(pltpu.VMEM((2 if lead else 1, depth, columns * cores), bf16))
    return rooms


def exchange(place, members, source, landing):
    e, t = place.e, place.t
    own = lax.rem(e, members)
    base = e - own
    sends, arrivals = place.take(members), place.take(members)
    sent = []
    for d in range(1, members):
        target = lax.rem(own + d, members)
        sent.append(place.send(source(target), landing(own), sends + d, arrivals + d, base + target, t))
    kept = place.keep(source(own), landing(own))
    yield
    for d in range(1, members):
        place.arrived(landing(lax.rem(own + members - d, members)), arrivals + d)
    for move in sent:
        move.wait_send()
    kept.wait()


def both(place, members, source, landing, part):
    yield from exchange(place, members, source, lambda slot: landing(place.t, slot))
    sends, arrivals = place.take(place.cores), place.take(place.cores)
    sent = []
    for d in range(1, place.cores):
        mine = part(place.t)
        sent.append(place.send(mine, mine, sends + d, arrivals + d, place.e, place.ring(d)))
    yield
    for d in range(1, place.cores):
        place.arrived(part(place.ring(place.cores - d)), arrivals + d)
    for move in sent:
        move.wait_send()


def run(tasks):
    tasks = list(tasks)
    while tasks:
        left = []
        for task in tasks:
            try:
                next(task)
                left.append(task)
            except StopIteration:
                pass
        tasks = left


def transfer(name, number, mesh, body, ins, outs, scratch=(), semaphores=400, vmem=None):
    count, cores = mesh.shape["expert"], mesh.shape["tensor"]
    semaphores = semaphores * max(1, count * cores // 32)

    def kernel(*refs):
        given = refs[: len(ins)]
        made = refs[len(ins) : len(ins) + len(outs)]
        room = refs[len(ins) + len(outs) : -1]
        place = Place(refs[-1], count, cores)
        place.meet()
        run(body(place, given, made, room))
        assert place.used <= semaphores, place.used

    size = sum(x.size * x.dtype.itemsize for x in list(ins) + list(outs))
    return pl.pallas_call(
        kernel,
        name=name,
        out_shape=[jax.ShapeDtypeStruct(shape, dtype) for shape, dtype in outs_of(outs)],
        in_specs=[ANY] * len(ins),
        out_specs=[ANY] * len(outs),
        scratch_shapes=list(scratch) + [pltpu.SemaphoreType.DMA((semaphores,))],
        cost_estimate=pl.CostEstimate(flops=0, bytes_accessed=size, transcendentals=0),
        compiler_params=pltpu.CompilerParams(
            collective_id=number, has_side_effects=True, vmem_limit_bytes=vmem
        ),
    )(*ins)


def outs_of(outs):
    return [(x.shape, x.dtype) for x in outs]


def like(shape, dtype=bf16):
    return jax.ShapeDtypeStruct(shape, dtype)


def part_view(ref, rows, columns, pieces=1):
    height = rows // pieces

    def view(slot, core, piece=0):
        at = 0 if isinstance(slot, int) else pl.multiple_of(slot * rows, rows)
        return ref.at[
            pl.ds(at + piece * height, height), pl.ds(pl.multiple_of(core * columns, columns), columns)
        ]

    return view


PIECES = 2


def lanes(at, columns):
    return pl.ds(pl.multiple_of(at * columns, columns), columns)


class Strips:
    def __init__(self, count, columns):
        self.count, self.columns = count, columns
        self.direct = columns % 128 == 0

    def shape(self, rows):
        return (rows, self.count * self.columns) if self.direct else (self.count, rows, self.columns)

    def at(self, ref, slot):
        return ref.at[:, lanes(slot, self.columns)] if self.direct else ref.at[slot]

    def cut(self, array):
        rows = array.shape[0]
        return array if self.direct else array.reshape(rows, self.count, self.columns).transpose(1, 0, 2)

    def join(self, array):
        rows = array.shape[0 if self.direct else 1]
        return array if self.direct else array.transpose(1, 0, 2).reshape(rows, self.count * self.columns)


def row_gather(place, members, source, landing, rows, part):
    def mine(piece):
        height = rows // PIECES
        return source.at[pl.ds(piece * height, height), lanes(place.t, part)]

    whole = (source, lambda slot: landing.at[pl.ds(pl.multiple_of(slot * rows, rows), rows), :])
    return gather(place, members, mine, whole, part_view(landing, rows, part, PIECES), True, PIECES)


def rotary(values, cosine, sine):
    half = values.shape[-1] // 2
    first = values[..., :half]
    second = values[..., half:]
    return jnp.concatenate([first * cosine - second * sine, second * cosine + first * sine], axis=-1)


def rotary_back(grads, cosine, sine):
    half = grads.shape[-1] // 2
    first = grads[..., :half]
    second = grads[..., half:]
    return jnp.concatenate([first * cosine + second * sine, second * cosine - first * sine], axis=-1)


def sequence_tables(lengths_rows, tok_rows):
    ends = jnp.cumsum(lengths_rows, axis=1)
    starts = ends - lengths_rows
    places = jnp.arange(tok_rows, dtype=jnp.int32)
    segment = jnp.sum((places[None, :, None] >= ends[:, None, :]).astype(jnp.int32), axis=2)
    member = segment[:, :, None] == jnp.arange(lengths_rows.shape[1], dtype=jnp.int32)[None, None, :]
    first = jnp.sum(jnp.where(member, starts[:, None, :], 0), axis=2)
    return segment, places[None, :] - first


def silu_parts(values):
    sigmoid_value = jax.nn.sigmoid(values)
    return values * sigmoid_value, sigmoid_value * (1.0 + values * (1.0 - sigmoid_value))


def mm(form, left, right):
    return jnp.einsum(form, left, right, preferred_element_type=f32)


def up_to(value, step):
    return -(-value // step) * step


def local(
    mesh,
    tokens,
    lengths,
    routes,
    gain_attn,
    w_query,
    w_key,
    w_value,
    w_out,
    gain_ffn,
    w_router,
    routed_gate_weight,
    routed_up_weight,
    w_down,
    w_shared_gate,
    w_shared_up,
    w_shared_down,
    out_grad,
):
    count, cores = mesh.shape["expert"], mesh.shape["tensor"]
    rows, width = tokens.shape
    part = width // cores
    deep = w_query.shape[0]
    experts = w_router.shape[1]
    heads = w_query.shape[1] // HEAD_DIM
    capacity = min(rows, rows * TOP * 4 // (3 * count))
    hidden_units = w_shared_gate.shape[1] // count
    scale = HEAD_DIM ** (-0.5)
    e = lax.axis_index("expert")
    t = lax.axis_index("tensor")
    chunk = heads * rows
    strips = Strips(count, deep)

    expert_ids = jnp.arange(experts, dtype=jnp.int32)
    choose = jnp.any(routes[:, :, None] == expert_ids[None, None, :], axis=1)
    mask_t = choose.T.astype(bf16)
    vectors = jnp.concatenate(
        [
            w_router.T,
            gain_attn[None],
            gain_ffn[None],
            jnp.pad(lengths.astype(bf16), ((0, 0), (0, deep - lengths.shape[1]))),
        ],
        axis=0,
    )
    head_rows = up_to(vectors.shape[0], 16)
    vectors = jnp.pad(vectors, ((0, head_rows - vectors.shape[0]), (0, 0)))
    pieces = rows // deep
    mask_rows = mask_t.reshape(experts * pieces, deep)
    small = jnp.concatenate([vectors, mask_rows], axis=0)
    small_rows = up_to(small.shape[0], 16)
    small = jnp.pad(small, ((0, small_rows - small.shape[0]), (0, 0)))

    def by_head(weight):
        return weight.reshape(deep, heads, HEAD_DIM).transpose(1, 0, 2)

    w_heads = jnp.concatenate([by_head(w_query), by_head(w_key), by_head(w_value)], axis=2)

    def first_body(place, given, made, room):
        tok, wh, sm = given
        tok_all, wh_all, sm_all = made
        yield exchange(place, count, lambda s: sm, lambda s: sm_all.at[s])
        yield row_gather(place, heads, tok, tok_all, rows, part)
        yield exchange(place, count, lambda s: wh.at[lax.rem(s, heads)], lambda s: wh_all.at[s])

    tok_chunk, w_qkv, small_all = transfer(
        "gather_tokens",
        0,
        mesh,
        first_body,
        (tokens, w_heads, small),
        (like((chunk, width)), like((count, deep, 3 * HEAD_DIM)), like((count, small_rows, deep))),
    )
    w_qkv = w_qkv.reshape(width, 3 * HEAD_DIM)

    router_full = small_all[:, :experts].transpose(1, 0, 2).reshape(experts, width)
    attn_gain = small_all[:, experts].reshape(width).astype(f32)
    ffn_gain = small_all[:, experts + 1].reshape(width).astype(f32)
    lengths_all = small_all[:, experts + 2, : lengths.shape[1]].astype(f32).astype(jnp.int32)
    masks = small_all[:, head_rows : head_rows + experts * pieces].reshape(count, experts, rows)

    member = e % heads
    lengths_chunk = lax.dynamic_slice_in_dim(lengths_all, e - member, heads, axis=0)
    segment, positions = sequence_tables(lengths_chunk, rows)
    half = HEAD_DIM // 2
    inverse = 10000.0 ** (-2.0 * jnp.arange(half, dtype=f32) / HEAD_DIM)
    angles = positions.astype(f32)[:, :, None] * inverse[None, None, :]
    cosine, sine = jnp.cos(angles), jnp.sin(angles)

    tok32 = tok_chunk.astype(f32)
    rstd_chunk = lax.rsqrt(jnp.mean(tok32 * tok32, axis=-1, keepdims=True) + eps)
    xn_chunk = (tok32 * rstd_chunk * attn_gain).astype(bf16)
    qkv = jnp.dot(xn_chunk, w_qkv, preferred_element_type=f32).reshape(heads, rows, 3 * HEAD_DIM)
    query = rotary(qkv[..., :HEAD_DIM], cosine, sine).astype(bf16)
    keyed = rotary(qkv[..., HEAD_DIM : 2 * HEAD_DIM], cosine, sine).astype(bf16)
    valued = qkv[..., 2 * HEAD_DIM :].astype(bf16)
    places = jnp.arange(rows, dtype=jnp.int32)
    allowed = (segment[:, :, None] == segment[:, None, :]) & (places[None, :] <= places[:, None])[None]
    scores = jnp.where(allowed, mm("gqd,gkd->gqk", query, keyed) * scale, floor_score)
    top_score = jnp.max(scores, axis=-1, keepdims=True)
    raised = jnp.exp(scores - top_score)
    probs = raised / jnp.sum(raised, axis=-1, keepdims=True)
    probs_low = probs.astype(bf16)
    head_out = mm("gqk,gkd->gqd", probs_low, valued).astype(bf16)

    shared_pack = jnp.concatenate(
        [
            w_shared_gate.T.reshape(count, hidden_units, deep),
            w_shared_up.T.reshape(count, hidden_units, deep),
            w_shared_down.reshape(count, hidden_units, deep),
        ],
        axis=1,
    )
    pack_rows = up_to(3 * hidden_units, 16)
    shared_pack = jnp.pad(shared_pack, ((0, 0), (0, pack_rows - 3 * hidden_units), (0, 0)))
    out_rows = w_out.shape[0]

    def second_body(place, given, made, room):
        ho, og, wo, sp = given
        ho_all, og_all, wo_all, sp_all = made
        yield exchange(place, heads, lambda s: ho.at[s], lambda s: ho_all.at[:, lanes(s, HEAD_DIM)])
        yield row_gather(place, count, og, og_all, rows, part)

        def wo_view(slot, core=0, piece=0):
            return strips.at(wo_all, slot)

        yield gather(place, count, lambda p: wo, (wo, wo_view), wo_view, False)
        yield exchange(place, count, lambda s: sp.at[s], lambda s: strips.at(sp_all, s))

    heads_out, grad_all, out_full, shared_all = transfer(
        "gather_inputs",
        1,
        mesh,
        second_body,
        (head_out, out_grad, w_out, shared_pack),
        (
            like((rows, heads * HEAD_DIM)),
            like((count * rows, width)),
            like(strips.shape(out_rows)),
            like(strips.shape(pack_rows)),
        ),
        semaphores=640,
    )
    out_full, shared_all = strips.join(out_full), strips.join(shared_all)
    sh_in = shared_all[: 2 * hidden_units]
    sh_down = shared_all[2 * hidden_units : 3 * hidden_units]
    attention_part = jnp.dot(heads_out, out_full, preferred_element_type=f32).astype(bf16)

    def third_body(place, given, made, room):
        ap, tok, gn, rt, mk = given
        hid_out, xn_all, gt_all = made
        parts, tok_v, gn_v, rt_v, mk_v, hid, xn, gt = room
        t = place.t
        sends, arrivals = place.take(cores), place.take(cores)
        sent = [place.send(ap, parts.at[t], sends + d, arrivals + d, place.e, place.ring(d)) for d in range(1, cores)]
        kept = [place.keep(ap, parts.at[t])]
        kept += [place.keep(a, b) for a, b in ((tok, tok_v), (gn, gn_v), (rt, rt_v), (mk, mk_v))]
        for move in kept:
            move.wait()
        for d in range(1, cores):
            place.arrived(parts.at[place.ring(cores - d)], arrivals + d)

        def body(at, carry):
            piece = pl.ds(pl.multiple_of(at * 16, 16), 16)
            total = parts[0, piece, :].astype(f32)
            for core in range(1, cores):
                total = total + parts[core, piece, :].astype(f32)
            values = tok_v[piece, :].astype(f32) + total
            hid[piece, :] = values
            rstd = lax.rsqrt(jnp.mean(values * values, axis=1, keepdims=True) + eps)
            xn[piece, :] = (values * rstd * gn_v[...]).astype(bf16)
            return carry

        lax.fori_loop(0, rows // 16, body, 0)
        saved = place.keep(hid, hid_out)
        yield row_gather(place, count, xn, xn_all, rows, part)
        logits = lax.dot_general(rt_v[...], xn[...], (((1,), (1,)), ((), ())), preferred_element_type=f32)
        picked = mk_v[...] > 0.5
        top_logit = jnp.max(jnp.where(picked, logits, floor_score), axis=0, keepdims=True)
        lifted = jnp.where(picked, jnp.exp(jnp.where(picked, logits - top_logit, 0.0)), 0.0)
        gt[...] = lifted / jnp.sum(lifted, axis=0, keepdims=True)
        yield exchange(place, count, lambda s: gt, lambda s: gt_all.at[s])
        for move in sent:
            move.wait_send()
        saved.wait()

    hidden, xn_all, gates_all = transfer(
        "gather_rows",
        2,
        mesh,
        third_body,
        (attention_part, tokens, ffn_gain[None], router_full, mask_t.astype(f32)),
        (like((rows, width), f32), like((count * rows, width)), like((count, experts, rows), f32)),
        [
            pltpu.VMEM((cores, rows, width), bf16),
            pltpu.VMEM((rows, width), bf16),
            pltpu.VMEM((1, width), f32),
            pltpu.VMEM((experts, width), bf16),
            pltpu.VMEM((experts, rows), f32),
            pltpu.VMEM((rows, width), f32),
            pltpu.VMEM((rows, width), bf16),
            pltpu.VMEM((experts, rows), f32),
        ],
        semaphores=400,
        vmem=40 * 2**20,
    )
    inputs = tokens.astype(f32)
    rstd_two = lax.rsqrt(jnp.mean(hidden * hidden, axis=-1, keepdims=True) + eps)
    gates = lax.dynamic_index_in_dim(gates_all, e, axis=0, keepdims=False).T

    own_mask = lax.dynamic_index_in_dim(masks, e, axis=1, keepdims=False).astype(f32)
    own_gate = lax.dynamic_index_in_dim(gates_all, e, axis=1, keepdims=False)
    position = (jnp.cumsum(own_mask, axis=1) - own_mask).astype(jnp.int32)
    slots = jnp.arange(capacity, dtype=jnp.int32)
    chosen = (position[:, None, :] == slots[None, :, None]) & (own_mask[:, None, :] > 0.5)
    onehot = chosen.astype(bf16)
    slot_gate = jnp.sum(jnp.where(chosen, own_gate[:, None, :], 0.0), axis=2)
    gate_column = slot_gate.reshape(count * capacity, 1)
    gate_weight, up_weight, down_weight = routed_gate_weight[0], routed_up_weight[0], w_down[0]

    received = mm("gst,gtd->gsd", onehot, xn_all.reshape(count, rows, width)).astype(bf16)
    received = received.reshape(count * capacity, width)
    grad_rows = mm("gst,gtd->gsd", onehot, grad_all.reshape(count, rows, width))
    grad_rows = grad_rows.reshape(count * capacity, width)
    gated_grad = (gate_column * grad_rows).astype(bf16)

    exp_gate = jnp.dot(received, gate_weight, preferred_element_type=f32)
    exp_up = jnp.dot(received, up_weight, preferred_element_type=f32)
    exp_silu, exp_slope = silu_parts(exp_gate)
    exp_act = (exp_silu * exp_up).astype(bf16)
    exp_out = jnp.dot(exp_act, down_weight, preferred_element_type=f32)
    slot_dots = jnp.sum(grad_rows * exp_out, axis=1).reshape(count, capacity)
    token_dots = jnp.sum(jnp.where(chosen, slot_dots[:, :, None], 0.0), axis=1)
    exp_low = (gate_column * exp_out).astype(bf16)

    sh_both = mm("td,hd->th", xn_all, sh_in)
    sh_gate, sh_up = sh_both[:, :hidden_units], sh_both[:, hidden_units:]
    sh_silu, sh_slope = silu_parts(sh_gate)
    sh_act = (sh_silu * sh_up).astype(bf16)
    back_onehot = onehot.transpose(0, 2, 1).reshape(count * rows, capacity)

    def widen(columns, fixed):
        extra = up_to(columns.shape[1], 128) - columns.shape[1]
        left = jnp.concatenate([back_onehot, jnp.pad(columns, ((0, 0), (0, extra)))], axis=1)
        return left, jnp.pad(fixed, ((0, extra), (0, 0)))

    left_forward, fixed_forward = widen(sh_act, sh_down)

    def fourth_body(place, given, made, room):
        lf, el, ff, td = given
        mixed, dots = made
        mixed_view = part_view(mixed, rows, part)
        made_here = Product(place, lf, el, ff, room[7:], count, rows, part)
        yield scatter(place, count, made_here, room[:7], lambda c: mixed_view(0, c), (rows, part), True)
        yield both(place, count, lambda s: td.at[s], lambda c, s: dots.at[c, s], lambda c: dots.at[c])

    dots_sent = jnp.pad(token_dots[:, None, :], ((0, 0), (0, 7), (0, 0)))
    mixture, dots_all = transfer(
        "scatter_output",
        3,
        mesh,
        fourth_body,
        (left_forward, exp_low, fixed_forward, dots_sent),
        (like((rows, width)), like((cores, count, 8, rows), f32)),
        scatter_scratch(count, cores, rows, part, left_forward.shape[1], capacity),
        vmem=56 * 2**20,
    )
    output = (hidden + mixture.astype(f32)).astype(bf16)

    gate_total = jnp.sum(dots_all[:, :, 0, :], axis=0).T
    weighted_dots = jnp.sum(gates * gate_total, axis=1, keepdims=True)
    grad_logits = gates * (gate_total - weighted_dots)

    act_grad = mm("rd,fd->rf", gated_grad, down_weight)
    gate_back = (act_grad * exp_up * exp_slope).astype(bf16)
    up_back = (act_grad * exp_silu).astype(bf16)
    back_rows = (mm("rf,df->rd", gate_back, gate_weight) + mm("rf,df->rd", up_back, up_weight)).astype(bf16)
    grad_shact = mm("td,fd->tf", grad_all, sh_down)
    back_shared = jnp.concatenate(
        [(grad_shact * sh_up * sh_slope).astype(bf16), (grad_shact * sh_silu).astype(bf16)], axis=1
    )
    left_backward, fixed_backward = widen(back_shared, sh_in)

    def fifth_body(place, given, made, room):
        lb, br, fb, gl = given
        summed, logit_all = made
        summed_view = part_view(summed, rows, part)
        made_here = Product(place, lb, br, fb, room[7:], count, rows, part)
        yield scatter(place, count, made_here, room[:7], lambda c: summed_view(0, c), (rows, part), True)
        yield exchange(place, count, lambda s: gl, lambda s: logit_all.at[s])

    summed_back, logits_all = transfer(
        "scatter_back",
        4,
        mesh,
        fifth_body,
        (left_backward, back_rows, fixed_backward, grad_logits.T),
        (like((rows, width)), like((count, experts, rows), f32)),
        scatter_scratch(count, cores, rows, part, left_backward.shape[1], capacity),
        vmem=56 * 2**20,
    )

    down_grad = mm("rf,rd->fd", exp_act, gated_grad)
    gate_grad = mm("rd,rf->df", received, gate_back)
    up_grad = mm("rd,rf->df", received, up_back)
    shared_grads = jnp.concatenate(
        [mm("tf,td->fd", back_shared, xn_all).astype(bf16), mm("tf,td->fd", sh_act, grad_all).astype(bf16)],
        axis=0,
    )
    shared_grads = jnp.pad(shared_grads, ((0, pack_rows - 3 * hidden_units), (0, 0)))
    xn_columns = lax.dynamic_slice_in_dim(xn_all, e * deep, deep, axis=1).astype(f32).reshape(count, rows, deep)
    router_grad = jnp.einsum("gtd,get->de", xn_columns, logits_all, precision=highest)

    cotangent = out_grad.astype(f32)
    grad_two = summed_back.astype(f32) + jnp.einsum(
        "te,ed->td", grad_logits, router_full.astype(f32), precision=highest
    )
    scaled = grad_two * ffn_gain
    inner = jnp.mean(scaled * hidden, axis=-1, keepdims=True)
    grad_hidden = cotangent + rstd_two * scaled - hidden * (rstd_two * rstd_two * rstd_two) * inner
    ffn_gain_part = jnp.sum(grad_two * hidden * rstd_two, axis=0)
    grad_branch = grad_hidden.astype(bf16)
    grad_heads = mm("td,cd->tc", grad_branch, out_full).astype(bf16)
    out_proj_part = mm("tc,td->cd", heads_out, grad_branch).astype(bf16)

    def sixth_body(place, given, made, room):
        yield exchange(place, heads, lambda s: given[0].at[:, lanes(s, HEAD_DIM)], lambda s: made[0].at[s])

    (grad_head,) = transfer(
        "exchange_heads",
        5,
        mesh,
        sixth_body,
        (grad_heads,),
        (like((heads, rows, HEAD_DIM)),),
    )

    grad_value = mm("gqk,gqd->gkd", probs_low, grad_head)
    grad_probs = mm("gqd,gkd->gqk", grad_head, valued)
    weighted = jnp.sum(probs * grad_probs, axis=-1, keepdims=True)
    grad_scores = (probs * (grad_probs - weighted)).astype(bf16)
    grad_query = mm("gqk,gkd->gqd", grad_scores, keyed) * scale
    grad_key = mm("gqk,gqd->gkd", grad_scores, query) * scale
    grad_qkv = jnp.concatenate(
        [
            rotary_back(grad_query, cosine, sine).astype(bf16),
            rotary_back(grad_key, cosine, sine).astype(bf16),
            grad_value.astype(bf16),
        ],
        axis=2,
    ).reshape(chunk, 3 * HEAD_DIM)
    qkv_grad = mm("td,tc->dc", xn_chunk, grad_qkv)
    attn_gain_part = jnp.sum(qkv_grad * w_qkv.astype(f32), axis=1) / attn_gain
    qkv_grad = qkv_grad.astype(bf16).reshape(count, deep, 3 * HEAD_DIM)

    def spread(vector):
        return jnp.pad(vector.reshape(count, 1, deep), ((0, 0), (0, 7), (0, 0)))

    def seventh_body(place, given, made, room):
        gq, wq, qg, op, sg, ag, fg = given
        one, qg_all, op_sum, sg_all, ag_all, fg_all = made
        one_view = part_view(one, rows, part)
        made_here = Product(place, gq, None, wq, room[7:9], heads, rows, part)
        yield scatter(place, heads, made_here, room[:7], lambda c: one_view(0, c), (rows, part), True)
        yield scatter(
            place, count, lambda s: strips.at(op, s), room[9:], lambda c: op_sum, (out_rows, deep), False
        )
        yield both(place, count, lambda s: ag.at[s], lambda c, s: ag_all.at[c, s], lambda c: ag_all.at[c])
        yield exchange(place, count, lambda s: fg.at[s], lambda s: fg_all.at[s])
        yield exchange(place, count, lambda s: qg.at[s], lambda s: qg_all.at[s])
        yield exchange(place, count, lambda s: strips.at(sg, s), lambda s: sg_all.at[s])

    grad_one, qkv_all, out_proj_sum, shared_back, attn_gains, ffn_gains = transfer(
        "scatter_grads",
        6,
        mesh,
        seventh_body,
        (
            grad_qkv,
            w_qkv.T,
            qkv_grad,
            strips.cut(out_proj_part),
            strips.cut(shared_grads),
            spread(attn_gain_part),
            spread(ffn_gain_part),
        ),
        (
            like((rows, width)),
            like((count, deep, 3 * HEAD_DIM)),
            like((out_rows, deep)),
            like((count, pack_rows, deep)),
            like((cores, count, 8, deep), f32),
            like((count, 8, deep), f32),
        ),
        scatter_scratch(heads, cores, rows, part, 3 * HEAD_DIM) + scatter_scratch(count, 1, out_rows, deep),
        semaphores=600,
        vmem=56 * 2**20,
    )

    grad_one = grad_one.astype(f32)
    rstd_one = lax.rsqrt(jnp.mean(inputs * inputs, axis=-1, keepdims=True) + eps)
    scaled_one = grad_one * attn_gain
    inner_one = jnp.mean(scaled_one * inputs, axis=-1, keepdims=True)
    input_grad = (
        grad_hidden + rstd_one * scaled_one - inputs * (rstd_one * rstd_one * rstd_one) * inner_one
    ).astype(bf16)
    qkv_sum = jnp.sum(qkv_all.reshape(count // heads, heads, deep, 3 * HEAD_DIM).astype(f32), axis=0)
    qkv_sum = qkv_sum.transpose(1, 0, 2)

    def of_heads(which):
        return qkv_sum[:, :, which * HEAD_DIM : (which + 1) * HEAD_DIM].reshape(deep, heads * HEAD_DIM)

    def of_shared(which):
        return shared_back[:, which * hidden_units : (which + 1) * hidden_units].reshape(-1, deep).astype(f32)

    return (
        output,
        input_grad,
        jnp.sum(attn_gains[:, :, 0, :], axis=(0, 1)),
        of_heads(0),
        of_heads(1),
        of_heads(2),
        out_proj_sum.astype(f32),
        jnp.sum(ffn_gains[:, 0, :], axis=0),
        router_grad,
        gate_grad[None],
        up_grad[None],
        down_grad[None],
        of_shared(0).T,
        of_shared(1).T,
        of_shared(2),
    )


def solution(mesh):
    in_specs = (
        P("expert", None),
        P("expert", None),
        P("expert", None),
        P("expert"),
        P("expert", "tensor"),
        P("expert", "tensor"),
        P("expert", "tensor"),
        P("tensor", "expert"),
        P("expert"),
        P("expert", None),
        P("expert", None, "tensor"),
        P("expert", None, "tensor"),
        P("expert", "tensor", None),
        P("expert", "tensor"),
        P("expert", "tensor"),
        P("tensor", "expert"),
        P("expert", None),
    )
    out_specs = (
        P("expert", None),
        P("expert", None),
        P("expert"),
        P("expert", "tensor"),
        P("expert", "tensor"),
        P("expert", "tensor"),
        P("tensor", "expert"),
        P("expert"),
        P("expert", None),
        P("expert", None, "tensor"),
        P("expert", None, "tensor"),
        P("expert", "tensor", None),
        P("expert", "tensor"),
        P("expert", "tensor"),
        P("tensor", "expert"),
    )
    return jax.shard_map(
        functools.partial(local, mesh), mesh=mesh, in_specs=in_specs, out_specs=out_specs, check_vma=False
    )
```

```python
import functools

import jax
import jax.numpy as jnp
from jax import lax
from jax.experimental import pallas as pl
from jax.experimental.pallas import tpu as pltpu
from jax.sharding import PartitionSpec as P

HEAD_DIM = 128
TOP = 6
MESH = pl.DeviceIdType.MESH
ANY = pl.BlockSpec(memory_space=pl.ANY)

bf16 = jnp.bfloat16
f32 = jnp.float32
eps = 1e-06
highest = lax.Precision.HIGHEST
floor_score = -1e30


class Place:
    def __init__(self, sems, count, cores):
        self.sems, self.used = sems, 0
        self.count, self.cores = count, cores
        self.e = lax.axis_index("expert")
        self.t = lax.axis_index("tensor")
        self.quad = lax.rem(self.e, 4)
        self.far = lax.div(self.e, 4)

    def take(self, number):
        first = self.used
        self.used = first + number
        return first

    def ring(self, distance):
        return lax.rem(self.t + distance, self.cores)

    def copy(self, src, dst, out_sem, in_sem, e, t):
        return pltpu.make_async_remote_copy(
            src_ref=src,
            dst_ref=dst,
            send_sem=self.sems.at[out_sem],
            recv_sem=self.sems.at[in_sem],
            device_id={"expert": e, "tensor": t},
            device_id_type=MESH,
        )

    def send(self, src, dst, out_sem, in_sem, e, t):
        move = self.copy(src, dst, out_sem, in_sem, e, t)
        move.start()
        return move

    def arrived(self, landing, in_sem):
        self.copy(landing, landing, in_sem, in_sem, self.e, self.t).wait_recv()

    def keep(self, src, dst):
        move = pltpu.make_async_copy(src, dst, self.sems.at[self.take(1)])
        move.start()
        return move

    def meet(self):
        barrier = pltpu.get_barrier_semaphore()
        for step in range(1, self.count):
            pl.semaphore_signal(
                barrier,
                inc=1,
                device_id={"expert": lax.rem(self.e + step, self.count), "tensor": self.t},
                device_id_type=MESH,
            )
        for step in range(1, self.cores):
            pl.semaphore_signal(
                barrier,
                inc=1,
                device_id={"expert": self.e, "tensor": self.ring(step)},
                device_id_type=MESH,
            )
        pl.semaphore_wait(barrier, self.count + self.cores - 2)


class Block:
    def __init__(self, place, members):
        self.place, self.deep = place, members // 4
        self.rank = lax.rem(place.far, self.deep)
        self.start = place.far - self.rank

    def flips(self, order):
        high, low = lax.div(self.place.quad, 2), lax.rem(self.place.quad, 2)
        one = high + (low - high) * order
        two = low + (high - low) * order
        return (2 - order) * (1 - 2 * one), (1 + order) * (1 - 2 * two)

    def slot(self, k, i, j, order):
        one, two = self.flips(order)
        return lax.rem(self.rank + k, self.deep) * 4 + self.place.quad + i * one + j * two

    def own(self):
        return self.rank * 4 + self.place.quad

    def device(self, slot):
        return self.start * 4 + slot


def when(condition, action):
    if condition is None:
        action()
    else:
        pl.when(condition)(action)


def gather(place, members, mine, whole, view, halves, pieces=1):
    block = Block(place, members)
    deep, e, t, rank = block.deep, place.e, place.t, block.rank
    order = lax.rem(t, 2)
    cores = place.cores if halves else 1
    spots = 2 * deep - 1

    def lots(number):
        return place.take(number * pieces)

    zs, zr = lots(spots + 1), lots(spots)
    s2, r2 = lots(spots), lots(spots)
    s3, r3 = lots(2 * spots), lots(2 * spots)
    s4, r4 = lots(4 * spots * (cores - 1)), lots(4 * spots * (cores - 1))
    one, two = block.flips(order)
    own = block.own()
    sent, kept = [], place.keep(whole[0], whole[1](own))
    line = [(0, 0)] + [(d, way) for d in range(1, deep) for way in (1, -1)]

    def index(d, way):
        return 0 if d == 0 else 2 * d - (1 if way > 0 else 0)

    def valid(d, way):
        return None if d == 0 else (rank >= d if way > 0 else rank < deep - d)

    def slot_of(d, way, i, j, order=order):
        one, two = block.flips(order)
        return (rank - way * d) * 4 + place.quad + i * one + j * two

    ends = {1: (rank < deep - 1, 4), -1: (rank >= 1, -4)}

    def onward(d, way, p):
        condition, step = ends[way]
        if d > 0:
            condition = jnp.logical_and(condition, valid(d, way))
        v = index(d, way)
        out = 1 + v if d > 0 else (0 if way > 0 else 1)
        source = view(slot_of(d, way, 0, 0), t, p) if d > 0 else mine(p)
        landing = view(slot_of(d, way, 0, 0), t, p)
        move = place.copy(source, landing, zs + out * pieces + p, zr + index(d + 1, way) * pieces + p, e + step, t)
        sent.append((condition, move))
        when(condition, move.start)

    def pass_on(source, landing, condition, out, into, number, p, target):
        move = place.copy(source, landing, out + number * pieces + p, into + number * pieces + p, target, t)
        sent.append((condition, move))
        return move

    def share(d, way, i, j, p):
        moves = []
        ref = view(slot_of(d, way, i, j), t, p)
        for far in range(1, cores):
            at = (((far - 1) * spots + index(d, way)) * 4 + i * 2 + j) * pieces + p
            move = place.copy(ref, ref, s4 + at, r4 + at, e, place.ring(far))
            sent.append((valid(d, way), move))
            moves.append(move)
        return moves

    def start(moves):
        for move in moves:
            move.start()

    for p in range(pieces):
        if deep > 1:
            onward(0, 1, p)
            onward(0, -1, p)
        pass_on(mine(p), view(own, t, p), None, s2, r2, 0, p, e + one).start()
        pass_on(mine(p), view(own, t, p), None, s3, r3, 0, p, e + two).start()
        yield

    def from_line(d, way, p):
        ref = view(slot_of(d, way, 0, 0), t, p)
        v, condition = index(d, way), valid(d, way)
        when(condition, lambda: place.arrived(ref, zr + v * pieces + p))
        if d < deep - 1:
            onward(d, way, p)
        moves = [
            pass_on(ref, ref, condition, s2, r2, v, p, e + one),
            pass_on(ref, ref, condition, s3, r3, 2 * v, p, e + two),
        ] + share(d, way, 0, 0, p)
        when(condition, lambda: start(moves))

    def from_one(d, way, p):
        ref = view(slot_of(d, way, 1, 0), t, p)
        v, condition = index(d, way), valid(d, way)
        moves = [pass_on(ref, ref, condition, s3, r3, 2 * v + 1, p, e + two)] + share(d, way, 1, 0, p)

        def act():
            place.arrived(ref, r2 + v * pieces + p)
            start(moves)

        when(condition, act)

    def from_two(d, way, i, p):
        ref = view(slot_of(d, way, i, 1), t, p)
        v, condition = index(d, way), valid(d, way)
        moves = share(d, way, i, 1, p)

        def act():
            place.arrived(ref, r3 + (2 * v + i) * pieces + p)
            start(moves)

        when(condition, act)

    for d in range(1, deep + 1):
        for p in range(pieces):
            for way in (1, -1) if d > 1 else (1,):
                from_one(d - 1, way if d > 1 else 0, p)
            if d < deep:
                for way in (1, -1):
                    from_line(d, way, p)
            yield
    for d, way in line:
        for i in range(2):
            for p in range(pieces):
                from_two(d, way, i, p)
        yield
    for far in range(1, cores):
        source = place.ring(cores - far)
        for d, way in line:
            for i in range(2):
                for j in range(2):
                    if d + i + j > 0:
                        for p in range(pieces):
                            at = (((far - 1) * spots + index(d, way)) * 4 + i * 2 + j) * pieces + p
                            ref = view(slot_of(d, way, i, j, lax.rem(source, 2)), source, p)
                            when(valid(d, way), functools.partial(place.arrived, ref, r4 + at))
    for condition, move in sent:
        when(condition, move.wait_send)
    kept.wait()


def add_up(target, sources, rows, columns):
    step = max(16, min(rows, 16384 // columns // 16 * 16))

    def body(at, carry):
        piece = pl.ds(pl.multiple_of(at * step, step), step)
        total = sources[0][piece, :].astype(f32)
        for other in sources[1:]:
            total = total + other[piece, :].astype(f32)
        target[piece, :] = total.astype(target.dtype)
        return carry

    lax.fori_loop(0, rows // step, body, 0)


class Product:
    def __init__(self, place, left, varied, fixed, rooms, members, rows, columns):
        self.place, self.left, self.varied = place, left, varied
        self.lhs, self.rhs = rooms
        self.rows, self.columns = rows, columns
        self.lead = 0 if varied is None else varied.shape[0] // members
        self.waits, self.turn = {}, 0
        self.setup = []
        for buffer in range(self.rhs.shape[0]):
            self.setup.append(place.keep(fixed, self.rhs.at[buffer, pl.ds(self.lead, fixed.shape[0]), :]))

    def fetch(self, turn, slot):
        buffer = turn % 2
        rows = pl.ds(pl.multiple_of(slot * self.rows, self.rows), self.rows)
        moves = [self.place.keep(self.left.at[rows, :], self.lhs.at[buffer])]
        if self.lead:
            lead = pl.ds(pl.multiple_of(slot * self.lead, self.lead), self.lead)
            moves.append(self.place.keep(self.varied.at[lead, :], self.rhs.at[buffer, pl.ds(0, self.lead), :]))
        self.waits[turn] = moves

    def ready(self, turn):
        for move in self.setup:
            move.wait()
        self.setup = []
        for move in self.waits.pop(turn):
            move.wait()

    def make(self, turn, core, target):
        buffer = turn % 2
        right = self.rhs.at[buffer if self.lead else 0]
        wide = min(self.columns, 512)

        def body(at, carry):
            source = pl.ds(pl.multiple_of(core * self.columns + at * wide, wide), wide)
            into = pl.ds(pl.multiple_of(at * wide, wide), wide)
            target[:, into] = jnp.dot(
                self.lhs[buffer], right[:, source], preferred_element_type=f32
            ).astype(bf16)
            return carry

        lax.fori_loop(0, self.columns // wide, body, 0)


def scatter(place, members, source, room, view, shape, halves):
    block = Block(place, members)
    deep, e, t = block.deep, place.e, place.t
    rows, columns = shape
    order = 1 - lax.rem(t, 2)
    cores = place.cores if halves else 1
    mine, outgoing, land0, land1, land2, land3, final = room
    s0, r0 = place.take(4 * deep * cores), place.take(4 * deep * cores)
    s1, r1 = place.take(2 * deep), place.take(2 * deep)
    s2, r2 = place.take(deep), place.take(deep)
    s3, r3 = place.take(deep), place.take(deep)
    s4, r4 = place.take(cores), place.take(cores)
    walk = list(range(1, deep)) + [0]
    one, two = block.flips(order)
    sent, loads = [], {}
    quads = [(1, 1), (1, 0), (0, 1), (0, 0)]
    turns = [(k, i, j) for k in walk for i, j in quads]
    ring = outgoing.shape[0]
    leaving = []

    def slot_of(k, i, j):
        return block.slot(k, i, j, order)

    def produce(number):
        k, i, j = turns[number]
        if isinstance(source, Product):
            if number == 0:
                source.fetch(0, slot_of(*turns[0]))
            source.ready(number)
            if number + 1 < len(turns):
                source.fetch(number + 1, slot_of(*turns[number + 1]))
            if number >= ring:
                for move in leaving[number - ring]:
                    move.wait_send()
            moves = []
            for d in range(1, cores):
                target = place.ring(d)
                buffer = outgoing.at[number % ring, d - 1]
                source.make(number, target, buffer)
                at = (d - 1) * deep * 4 + k * 4 + (j * 2 + i if d % 2 else i * 2 + j)
                moves.append(place.send(buffer, land0.at[at], s0 + at, r0 + at, e, target))
            leaving.append(moves)
            source.make(number, t, mine.at[slot_of(k, i, j)])
        else:
            loads[k, i, j] = place.keep(source(slot_of(k, i, j)), mine.at[slot_of(k, i, j)])

    def terms_of(k, i, j):
        at = k * 4 + i * 2 + j
        if (k, i, j) in loads:
            loads[k, i, j].wait()
        terms = [mine.at[slot_of(k, i, j)]]
        for d in range(1, cores):
            place_at = (d - 1) * deep * 4 + at
            place.arrived(land0.at[place_at], r0 + place_at)
            terms.append(land0.at[place_at])
        if i == 0:
            place.arrived(land1.at[2 * k + j], r1 + 2 * k + j)
            terms.append(land1.at[2 * k + j])
            if j == 0:
                place.arrived(land2.at[k], r2 + k)
                terms.append(land2.at[k])
        return terms

    def first_flip(k, j):
        terms, ref = terms_of(k, 1, j), mine.at[slot_of(k, 1, j)]
        if len(terms) > 1:
            add_up(ref, terms, rows, columns)
        sent.append(place.send(ref, land1.at[2 * k + j], s1 + 2 * k + j, r1 + 2 * k + j, e + one, t))

    def second_flip(k):
        ref = mine.at[slot_of(k, 0, 1)]
        add_up(ref, terms_of(k, 0, 1), rows, columns)
        sent.append(place.send(ref, land2.at[k], s2 + k, r2 + k, e + two, t))

    def line(k):
        terms, ref = terms_of(k, 0, 0), mine.at[slot_of(k, 0, 0)]
        if k > 0:
            add_up(ref, terms, rows, columns)
            peer = block.device(lax.rem(block.rank + k, deep) * 4 + place.quad)
            sent.append(place.send(ref, land3.at[k], s3 + k, r3 + k, peer, t))
            return
        for far in range(1, deep):
            place.arrived(land3.at[far], r3 + far)
            terms.append(land3.at[far])
        add_up(final, terms, rows, columns)

    for step in range(deep + 2):
        fresh = step < deep
        if fresh:
            produce(4 * step)
            yield
            produce(4 * step + 1)
            yield
            first_flip(walk[step], 1)
            yield
            produce(4 * step + 2)
            yield
        if 0 <= step - 1 < deep:
            second_flip(walk[step - 1])
            yield
        if fresh:
            produce(4 * step + 3)
            yield
            first_flip(walk[step], 0)
            yield
        if 0 <= step - 2 < deep:
            line(walk[step - 2])
            yield
    kept = place.keep(final, view(t))
    for d in range(1, cores):
        sent.append(place.send(final, view(t), s4 + d, r4 + d, e, place.ring(d)))
    yield
    for d in range(1, cores):
        place.arrived(view(place.ring(cores - d)), r4 + d)
    for moves in leaving[-ring:]:
        for move in moves:
            move.wait_send()
    for move in sent:
        move.wait_send()
    kept.wait()


def scatter_scratch(members, cores, rows, columns, depth=0, lead=0):
    deep = members // 4
    held = pltpu.VMEM((max(1, (cores - 1) * members), rows if cores > 1 else 16, columns), bf16)
    ring = pltpu.VMEM((min(8, members), max(1, cores - 1), rows if cores > 1 else 16, columns), bf16)
    rooms = [
        pltpu.VMEM((members, rows, columns), bf16),
        ring,
        held,
        pltpu.VMEM((2 * deep, rows, columns), bf16),
        pltpu.VMEM((deep, rows, columns), bf16),
        pltpu.VMEM((deep, rows, columns), bf16),
        pltpu.VMEM((rows, columns), bf16),
    ]
    if depth:
        rooms.append(pltpu.VMEM((2, rows, depth), bf16))
        rooms.append(pltpu.VMEM((2 if lead else 1, depth, columns * cores), bf16))
    return rooms


def exchange(place, members, source, landing):
    e, t = place.e, place.t
    own = lax.rem(e, members)
    base = e - own
    sends, arrivals = place.take(members), place.take(members)
    sent = []
    for d in range(1, members):
        target = lax.rem(own + d, members)
        sent.append(place.send(source(target), landing(own), sends + d, arrivals + d, base + target, t))
    kept = place.keep(source(own), landing(own))
    yield
    for d in range(1, members):
        place.arrived(landing(lax.rem(own + members - d, members)), arrivals + d)
    for move in sent:
        move.wait_send()
    kept.wait()


def both(place, members, source, landing, part):
    yield from exchange(place, members, source, lambda slot: landing(place.t, slot))
    sends, arrivals = place.take(place.cores), place.take(place.cores)
    sent = []
    for d in range(1, place.cores):
        mine = part(place.t)
        sent.append(place.send(mine, mine, sends + d, arrivals + d, place.e, place.ring(d)))
    yield
    for d in range(1, place.cores):
        place.arrived(part(place.ring(place.cores - d)), arrivals + d)
    for move in sent:
        move.wait_send()


def later(task, rounds):
    for _ in range(rounds):
        yield
    yield from task


def run(tasks):
    tasks = list(tasks)
    while tasks:
        left = []
        for task in tasks:
            try:
                next(task)
                left.append(task)
            except StopIteration:
                pass
        tasks = left


def transfer(name, number, mesh, body, ins, outs, scratch=(), semaphores=400, vmem=None):
    count, cores = mesh.shape["expert"], mesh.shape["tensor"]
    semaphores = semaphores * max(1, count * cores // 32)

    def kernel(*refs):
        given = refs[: len(ins)]
        made = refs[len(ins) : len(ins) + len(outs)]
        room = refs[len(ins) + len(outs) : -1]
        place = Place(refs[-1], count, cores)
        place.meet()
        run(body(place, given, made, room))
        assert place.used <= semaphores, place.used

    size = sum(x.size * x.dtype.itemsize for x in list(ins) + list(outs))
    return pl.pallas_call(
        kernel,
        name=name,
        out_shape=[jax.ShapeDtypeStruct(shape, dtype) for shape, dtype in outs_of(outs)],
        in_specs=[ANY] * len(ins),
        out_specs=[ANY] * len(outs),
        scratch_shapes=list(scratch) + [pltpu.SemaphoreType.DMA((semaphores,))],
        cost_estimate=pl.CostEstimate(flops=0, bytes_accessed=size, transcendentals=0),
        compiler_params=pltpu.CompilerParams(
            collective_id=number, has_side_effects=True, vmem_limit_bytes=vmem
        ),
    )(*ins)


def outs_of(outs):
    return [(x.shape, x.dtype) for x in outs]


def like(shape, dtype=bf16):
    return jax.ShapeDtypeStruct(shape, dtype)


def part_view(ref, rows, columns, pieces=1):
    height = rows // pieces

    def view(slot, core, piece=0):
        at = 0 if isinstance(slot, int) else pl.multiple_of(slot * rows, rows)
        return ref.at[
            pl.ds(at + piece * height, height), pl.ds(pl.multiple_of(core * columns, columns), columns)
        ]

    return view


PIECES = 2


def lanes(at, columns):
    return pl.ds(pl.multiple_of(at * columns, columns), columns)


class Strips:
    def __init__(self, count, columns):
        self.count, self.columns = count, columns
        self.direct = columns % 128 == 0

    def shape(self, rows):
        return (rows, self.count * self.columns) if self.direct else (self.count, rows, self.columns)

    def at(self, ref, slot):
        return ref.at[:, lanes(slot, self.columns)] if self.direct else ref.at[slot]

    def cut(self, array):
        rows = array.shape[0]
        return array if self.direct else array.reshape(rows, self.count, self.columns).transpose(1, 0, 2)

    def join(self, array):
        rows = array.shape[0 if self.direct else 1]
        return array if self.direct else array.transpose(1, 0, 2).reshape(rows, self.count * self.columns)


def row_gather(place, members, source, landing, rows, part):
    def mine(piece):
        height = rows // PIECES
        return source.at[pl.ds(piece * height, height), lanes(place.t, part)]

    whole = (source, lambda slot: landing.at[pl.ds(pl.multiple_of(slot * rows, rows), rows), :])
    return gather(place, members, mine, whole, part_view(landing, rows, part, PIECES), True, PIECES)


def rotary(values, cosine, sine):
    half = values.shape[-1] // 2
    first = values[..., :half]
    second = values[..., half:]
    return jnp.concatenate([first * cosine - second * sine, second * cosine + first * sine], axis=-1)


def rotary_back(grads, cosine, sine):
    half = grads.shape[-1] // 2
    first = grads[..., :half]
    second = grads[..., half:]
    return jnp.concatenate([first * cosine + second * sine, second * cosine - first * sine], axis=-1)


def sequence_tables(lengths_rows, tok_rows):
    ends = jnp.cumsum(lengths_rows, axis=1)
    starts = ends - lengths_rows
    places = jnp.arange(tok_rows, dtype=jnp.int32)
    segment = jnp.sum((places[None, :, None] >= ends[:, None, :]).astype(jnp.int32), axis=2)
    member = segment[:, :, None] == jnp.arange(lengths_rows.shape[1], dtype=jnp.int32)[None, None, :]
    first = jnp.sum(jnp.where(member, starts[:, None, :], 0), axis=2)
    return segment, places[None, :] - first


def silu_parts(values):
    sigmoid_value = jax.nn.sigmoid(values)
    return values * sigmoid_value, sigmoid_value * (1.0 + values * (1.0 - sigmoid_value))


def mm(form, left, right):
    return jnp.einsum(form, left, right, preferred_element_type=f32)


def up_to(value, step):
    return -(-value // step) * step


def experts_kernel(
    groups,
    capacity,
    rows,
    xn_ref,
    grad_ref,
    position_ref,
    gate_ref,
    wg_ref,
    wu_ref,
    wd_ref,
    sh_in_ref,
    sh_down_ref,
    received_ref,
    gated_ref,
    low_ref,
    back_ref,
    act_ref,
    gate_back_ref,
    up_back_ref,
    dots_ref,
    left_forward_ref,
    left_backward_ref,
):
    def dot(left, right, sides=((1,), (0,))):
        return lax.dot_general(left, right, (sides, ((), ())), preferred_element_type=f32)

    places = lax.broadcasted_iota(jnp.int32, (capacity, rows), 0).astype(f32)
    gates, grads, onehots = [], [], []
    for g in range(groups):
        token = pl.ds(g * rows, rows)
        slot = pl.ds(g * capacity, capacity)
        chosen = (position_ref[g] == places).astype(f32)
        onehot = chosen.astype(bf16)
        onehots.append(chosen)
        received_ref[slot, :] = dot(onehot, xn_ref[token, :]).astype(bf16)
        gate = jnp.sum(chosen * gate_ref[g], axis=1, keepdims=True)
        row_grads = dot(onehot, grad_ref[token, :])
        gated_ref[slot, :] = (gate * row_grads).astype(bf16)
        low_ref[slot, :] = row_grads.astype(bf16)
        gates.append(gate)
        turned = chosen.T.astype(bf16)
        left_forward_ref[token, :capacity] = turned
        left_backward_ref[token, :capacity] = turned
    gate = jnp.concatenate(gates, axis=0)
    received = received_ref[...]
    exp_gate = dot(received, wg_ref[...])
    exp_up = dot(received, wu_ref[...])
    silu, slope = silu_parts(exp_gate)
    act = (silu * exp_up).astype(bf16)
    act_ref[...] = act
    out = dot(act, wd_ref[...])
    dots = jnp.sum(low_ref[...].astype(f32) * out, axis=1, keepdims=True)
    low_ref[...] = (gate * out).astype(bf16)
    for g in range(groups):
        column = dots[g * capacity : (g + 1) * capacity]
        token_dots = jnp.sum(onehots[g] * column, axis=0, keepdims=True)
        dots_ref[g] = jnp.broadcast_to(token_dots, (8, rows))
    act_grad = dot(gated_ref[...], wd_ref[...], ((1,), (1,)))
    gate_back = (act_grad * exp_up * slope).astype(bf16)
    up_back = (act_grad * silu).astype(bf16)
    gate_back_ref[...] = gate_back
    up_back_ref[...] = up_back
    back_ref[...] = (
        dot(gate_back, wg_ref[...], ((1,), (1,))) + dot(up_back, wu_ref[...], ((1,), (1,)))
    ).astype(bf16)
    wide = sh_down_ref.shape[0]
    both = dot(xn_ref[...], sh_in_ref[...], ((1,), (1,)))
    sh_gate, sh_up = both[:, :wide], both[:, wide:]
    sh_silu, sh_slope = silu_parts(sh_gate)
    left_forward_ref[:, capacity:] = (sh_silu * sh_up).astype(bf16)
    sh_grad = dot(grad_ref[...], sh_down_ref[...], ((1,), (1,)))
    left_backward_ref[:, capacity : capacity + wide] = (sh_grad * sh_up * sh_slope).astype(bf16)
    left_backward_ref[:, capacity + wide :] = (sh_grad * sh_silu).astype(bf16)


def experts_pass(count, capacity, rows, xn_all, grad_all, position, gate, wg, wu, wd, sh_in, sh_down):
    groups = 2
    width, units = wg.shape
    wide = sh_down.shape[0]

    def along(*shape):
        return pl.BlockSpec(shape, lambda i: (i,) + (0,) * (len(shape) - 1))

    def whole(array):
        return pl.BlockSpec(array.shape, lambda i: (0,) * array.ndim, pipeline_mode=pl.Buffered(1))

    slots = groups * capacity
    tokens = groups * rows
    flops = 2 * count * capacity * width * units * 6
    return pl.pallas_call(
        functools.partial(experts_kernel, groups, capacity, rows),
        name="experts_pass",
        grid=(count // groups,),
        in_specs=[
            along(tokens, width),
            along(tokens, width),
            along(groups, 1, rows),
            along(groups, 1, rows),
            whole(wg),
            whole(wu),
            whole(wd),
            whole(sh_in),
            whole(sh_down),
        ],
        out_specs=[
            along(slots, width),
            along(slots, width),
            along(slots, width),
            along(slots, width),
            along(slots, units),
            along(slots, units),
            along(slots, units),
            along(groups, 8, rows),
            along(tokens, capacity + wide),
            along(tokens, capacity + 2 * wide),
        ],
        out_shape=[like((count * capacity, width))] * 4
        + [like((count * capacity, units))] * 3
        + [
            like((count, 8, rows), f32),
            like((count * rows, capacity + wide)),
            like((count * rows, capacity + 2 * wide)),
        ],
        cost_estimate=pl.CostEstimate(
            flops=flops, bytes_accessed=4 * count * (rows + 2 * capacity) * width, transcendentals=0
        ),
        compiler_params=pltpu.CompilerParams(vmem_limit_bytes=58 * 2**20),
    )(xn_all, grad_all, position, gate, wg, wu, wd, sh_in, sh_down)


def local(
    mesh,
    tokens,
    lengths,
    routes,
    gain_attn,
    w_query,
    w_key,
    w_value,
    w_out,
    gain_ffn,
    w_router,
    routed_gate_weight,
    routed_up_weight,
    w_down,
    w_shared_gate,
    w_shared_up,
    w_shared_down,
    out_grad,
):
    count, cores = mesh.shape["expert"], mesh.shape["tensor"]
    rows, width = tokens.shape
    part = width // cores
    deep = w_query.shape[0]
    experts = w_router.shape[1]
    heads = w_query.shape[1] // HEAD_DIM
    capacity = up_to(min(rows, rows * TOP * 4 // (3 * count)), 128)
    hidden_units = w_shared_gate.shape[1] // count
    scale = HEAD_DIM ** (-0.5)
    e = lax.axis_index("expert")
    t = lax.axis_index("tensor")
    chunk = heads * rows
    strips = Strips(count, deep)

    expert_ids = jnp.arange(experts, dtype=jnp.int32)
    choose = jnp.any(routes[:, :, None] == expert_ids[None, None, :], axis=1)
    mask_t = choose.T.astype(bf16)
    vectors = jnp.concatenate(
        [
            w_router.T,
            gain_attn[None],
            gain_ffn[None],
            jnp.pad(lengths.astype(bf16), ((0, 0), (0, deep - lengths.shape[1]))),
        ],
        axis=0,
    )
    head_rows = up_to(vectors.shape[0], 16)
    vectors = jnp.pad(vectors, ((0, head_rows - vectors.shape[0]), (0, 0)))
    pieces = rows // deep
    mask_rows = mask_t.reshape(experts * pieces, deep)
    small = jnp.concatenate([vectors, mask_rows], axis=0)
    small_rows = up_to(small.shape[0], 16)
    small = jnp.pad(small, ((0, small_rows - small.shape[0]), (0, 0)))

    def by_head(weight):
        return weight.reshape(deep, heads, HEAD_DIM).transpose(1, 0, 2)

    w_heads = jnp.concatenate([by_head(w_query), by_head(w_key), by_head(w_value)], axis=2)

    def first_body(place, given, made, room):
        tok, wh, sm = given
        tok_all, wh_all, sm_all = made
        yield exchange(place, count, lambda s: sm, lambda s: sm_all.at[s])
        yield row_gather(place, heads, tok, tok_all, rows, part)
        yield exchange(place, count, lambda s: wh.at[lax.rem(s, heads)], lambda s: wh_all.at[s])

    tok_chunk, w_qkv, small_all = transfer(
        "gather_tokens",
        0,
        mesh,
        first_body,
        (tokens, w_heads, small),
        (like((chunk, width)), like((count, deep, 3 * HEAD_DIM)), like((count, small_rows, deep))),
    )
    w_qkv = w_qkv.reshape(width, 3 * HEAD_DIM)

    router_full = small_all[:, :experts].transpose(1, 0, 2).reshape(experts, width)
    attn_gain = small_all[:, experts].reshape(width).astype(f32)
    ffn_gain = small_all[:, experts + 1].reshape(width).astype(f32)
    lengths_all = small_all[:, experts + 2, : lengths.shape[1]].astype(f32).astype(jnp.int32)
    masks = small_all[:, head_rows : head_rows + experts * pieces].reshape(count, experts, rows)

    member = e % heads
    lengths_chunk = lax.dynamic_slice_in_dim(lengths_all, e - member, heads, axis=0)
    segment, positions = sequence_tables(lengths_chunk, rows)
    half = HEAD_DIM // 2
    inverse = 10000.0 ** (-2.0 * jnp.arange(half, dtype=f32) / HEAD_DIM)
    angles = positions.astype(f32)[:, :, None] * inverse[None, None, :]
    cosine, sine = jnp.cos(angles), jnp.sin(angles)

    tok32 = tok_chunk.astype(f32)
    rstd_chunk = lax.rsqrt(jnp.mean(tok32 * tok32, axis=-1, keepdims=True) + eps)
    xn_chunk = (tok32 * rstd_chunk * attn_gain).astype(bf16)
    qkv = jnp.dot(xn_chunk, w_qkv, preferred_element_type=f32).reshape(heads, rows, 3 * HEAD_DIM)
    query = rotary(qkv[..., :HEAD_DIM], cosine, sine).astype(bf16)
    keyed = rotary(qkv[..., HEAD_DIM : 2 * HEAD_DIM], cosine, sine).astype(bf16)
    valued = qkv[..., 2 * HEAD_DIM :].astype(bf16)
    places = jnp.arange(rows, dtype=jnp.int32)
    allowed = (segment[:, :, None] == segment[:, None, :]) & (places[None, :] <= places[:, None])[None]
    scores = jnp.where(allowed, mm("gqd,gkd->gqk", query, keyed) * scale, floor_score)
    top_score = jnp.max(scores, axis=-1, keepdims=True)
    raised = jnp.exp(scores - top_score)
    probs = raised / jnp.sum(raised, axis=-1, keepdims=True)
    probs_low = probs.astype(bf16)
    head_out = mm("gqk,gkd->gqd", probs_low, valued).astype(bf16)

    shared_pack = jnp.concatenate(
        [
            w_shared_gate.T.reshape(count, hidden_units, deep),
            w_shared_up.T.reshape(count, hidden_units, deep),
            w_shared_down.reshape(count, hidden_units, deep),
        ],
        axis=1,
    )
    pack_rows = up_to(3 * hidden_units, 16)
    shared_pack = jnp.pad(shared_pack, ((0, 0), (0, pack_rows - 3 * hidden_units), (0, 0)))
    out_rows = w_out.shape[0]

    def second_body(place, given, made, room):
        ho, og, wo, sp = given
        ho_all, og_all, wo_all, sp_all = made
        yield exchange(place, heads, lambda s: ho.at[s], lambda s: ho_all.at[:, lanes(s, HEAD_DIM)])
        yield row_gather(place, count, og, og_all, rows, part)

        def wo_view(slot, core=0, piece=0):
            return strips.at(wo_all, slot)

        yield gather(place, count, lambda p: wo, (wo, wo_view), wo_view, False)
        yield exchange(place, count, lambda s: sp.at[s], lambda s: strips.at(sp_all, s))

    heads_out, grad_all, out_full, shared_all = transfer(
        "gather_inputs",
        1,
        mesh,
        second_body,
        (head_out, out_grad, w_out, shared_pack),
        (
            like((rows, heads * HEAD_DIM)),
            like((count * rows, width)),
            like(strips.shape(out_rows)),
            like(strips.shape(pack_rows)),
        ),
        semaphores=640,
    )
    out_full, shared_all = strips.join(out_full), strips.join(shared_all)
    attention_part = jnp.dot(heads_out, out_full, preferred_element_type=f32).astype(bf16)

    def third_body(place, given, made, room):
        ap, tok, gn, rt, mk = given
        hid_out, xn_all, gt_all = made
        parts, tok_v, gn_v, rt_v, mk_v, hid, xn, gt = room
        t = place.t
        sends, arrivals = place.take(cores), place.take(cores)
        sent = [place.send(ap, parts.at[t], sends + d, arrivals + d, place.e, place.ring(d)) for d in range(1, cores)]
        kept = [place.keep(ap, parts.at[t])]
        kept += [place.keep(a, b) for a, b in ((tok, tok_v), (gn, gn_v), (rt, rt_v), (mk, mk_v))]
        for move in kept:
            move.wait()
        for d in range(1, cores):
            place.arrived(parts.at[place.ring(cores - d)], arrivals + d)

        def body(at, carry):
            piece = pl.ds(pl.multiple_of(at * 16, 16), 16)
            total = parts[0, piece, :].astype(f32)
            for core in range(1, cores):
                total = total + parts[core, piece, :].astype(f32)
            values = tok_v[piece, :].astype(f32) + total
            hid[piece, :] = values
            rstd = lax.rsqrt(jnp.mean(values * values, axis=1, keepdims=True) + eps)
            xn[piece, :] = (values * rstd * gn_v[...]).astype(bf16)
            return carry

        lax.fori_loop(0, rows // 16, body, 0)
        saved = place.keep(hid, hid_out)
        yield row_gather(place, count, xn, xn_all, rows, part)
        logits = lax.dot_general(rt_v[...], xn[...], (((1,), (1,)), ((), ())), preferred_element_type=f32)
        picked = mk_v[...] > 0.5
        top_logit = jnp.max(jnp.where(picked, logits, floor_score), axis=0, keepdims=True)
        lifted = jnp.where(picked, jnp.exp(jnp.where(picked, logits - top_logit, 0.0)), 0.0)
        gt[...] = lifted / jnp.sum(lifted, axis=0, keepdims=True)
        yield exchange(place, count, lambda s: gt, lambda s: gt_all.at[s])
        for move in sent:
            move.wait_send()
        saved.wait()

    hidden, xn_all, gates_all = transfer(
        "gather_rows",
        2,
        mesh,
        third_body,
        (attention_part, tokens, ffn_gain[None], router_full, mask_t.astype(f32)),
        (like((rows, width), f32), like((count * rows, width)), like((count, experts, rows), f32)),
        [
            pltpu.VMEM((cores, rows, width), bf16),
            pltpu.VMEM((rows, width), bf16),
            pltpu.VMEM((1, width), f32),
            pltpu.VMEM((experts, width), bf16),
            pltpu.VMEM((experts, rows), f32),
            pltpu.VMEM((rows, width), f32),
            pltpu.VMEM((rows, width), bf16),
            pltpu.VMEM((experts, rows), f32),
        ],
        semaphores=400,
        vmem=40 * 2**20,
    )
    inputs = tokens.astype(f32)
    rstd_two = lax.rsqrt(jnp.mean(hidden * hidden, axis=-1, keepdims=True) + eps)
    gates = lax.dynamic_index_in_dim(gates_all, e, axis=0, keepdims=False).T

    own_mask = lax.dynamic_index_in_dim(masks, e, axis=1, keepdims=False).astype(f32)
    own_gate = lax.dynamic_index_in_dim(gates_all, e, axis=1, keepdims=False)
    position = jnp.where(own_mask > 0.5, jnp.cumsum(own_mask, axis=1) - own_mask, -1.0)
    gate_weight, up_weight, down_weight = routed_gate_weight[0], routed_up_weight[0], w_down[0]
    sh_wide = up_to(hidden_units, 128)

    def widened(which):
        piece = shared_all[which * hidden_units : (which + 1) * hidden_units]
        return jnp.pad(piece, ((0, sh_wide - hidden_units), (0, 0)))

    fixed_backward = jnp.concatenate([widened(0), widened(1)], axis=0)
    fixed_forward = widened(2)
    (
        received,
        gated_grad,
        exp_low,
        back_rows,
        exp_act,
        gate_back,
        up_back,
        token_dots,
        left_forward,
        left_backward,
    ) = experts_pass(
        count,
        capacity,
        rows,
        xn_all,
        grad_all,
        position[:, None],
        own_gate[:, None],
        gate_weight,
        up_weight,
        down_weight,
        fixed_backward,
        fixed_forward,
    )

    def fourth_body(place, given, made, room):
        lf, el, ff, td = given
        mixed, dots = made
        mixed_view = part_view(mixed, rows, part)
        made_here = Product(place, lf, el, ff, room[7:], count, rows, part)
        yield scatter(place, count, made_here, room[:7], lambda c: mixed_view(0, c), (rows, part), True)
        yield both(place, count, lambda s: td.at[s], lambda c, s: dots.at[c, s], lambda c: dots.at[c])

    dots_sent = token_dots
    mixture, dots_all = transfer(
        "scatter_output",
        3,
        mesh,
        fourth_body,
        (left_forward, exp_low, fixed_forward, dots_sent),
        (like((rows, width)), like((cores, count, 8, rows), f32)),
        scatter_scratch(count, cores, rows, part, left_forward.shape[1], capacity),
        vmem=56 * 2**20,
    )
    output = (hidden + mixture.astype(f32)).astype(bf16)

    gate_total = jnp.sum(dots_all[:, :, 0, :], axis=0).T
    weighted_dots = jnp.sum(gates * gate_total, axis=1, keepdims=True)
    grad_logits = gates * (gate_total - weighted_dots)

    sh_grads = mm("tf,td->fd", left_backward[:, capacity:], xn_all).astype(bf16)
    shared_grads = jnp.concatenate(
        [
            sh_grads[:hidden_units],
            sh_grads[sh_wide : sh_wide + hidden_units],
            mm("tf,td->fd", left_forward[:, capacity:], grad_all).astype(bf16)[:hidden_units],
        ],
        axis=0,
    )
    shared_grads = jnp.pad(shared_grads, ((0, pack_rows - 3 * hidden_units), (0, 0)))

    def fifth_body(place, given, made, room):
        lb, br, fb, gl, sg = given
        summed, logit_all, sg_all = made
        summed_view = part_view(summed, rows, part)
        made_here = Product(place, lb, br, fb, room[7:], count, rows, part)
        yield scatter(place, count, made_here, room[:7], lambda c: summed_view(0, c), (rows, part), True)
        yield exchange(place, count, lambda s: gl, lambda s: logit_all.at[s])
        yield later(exchange(place, count, lambda s: strips.at(sg, s), lambda s: sg_all.at[s]), 8)

    summed_back, logits_all, shared_back = transfer(
        "scatter_back",
        4,
        mesh,
        fifth_body,
        (left_backward, back_rows, fixed_backward, grad_logits.T, strips.cut(shared_grads)),
        (like((rows, width)), like((count, experts, rows), f32), like((count, pack_rows, deep))),
        scatter_scratch(count, cores, rows, part, left_backward.shape[1], capacity),
        vmem=56 * 2**20,
    )

    down_grad = mm("rf,rd->fd", exp_act, gated_grad)
    gate_grad = mm("rd,rf->df", received, gate_back)
    up_grad = mm("rd,rf->df", received, up_back)
    xn_columns = lax.dynamic_slice_in_dim(xn_all, e * deep, deep, axis=1).astype(f32).reshape(count, rows, deep)
    router_grad = jnp.einsum("gtd,get->de", xn_columns, logits_all, precision=highest)

    cotangent = out_grad.astype(f32)
    grad_two = summed_back.astype(f32) + jnp.einsum(
        "te,ed->td", grad_logits, router_full.astype(f32), precision=highest
    )
    scaled = grad_two * ffn_gain
    inner = jnp.mean(scaled * hidden, axis=-1, keepdims=True)
    grad_hidden = cotangent + rstd_two * scaled - hidden * (rstd_two * rstd_two * rstd_two) * inner
    ffn_gain_part = jnp.sum(grad_two * hidden * rstd_two, axis=0)
    grad_branch = grad_hidden.astype(bf16)
    grad_heads = mm("td,cd->tc", grad_branch, out_full).astype(bf16)
    out_proj_part = mm("tc,td->cd", heads_out, grad_branch).astype(bf16)

    def sixth_body(place, given, made, room):
        yield exchange(place, heads, lambda s: given[0].at[:, lanes(s, HEAD_DIM)], lambda s: made[0].at[s])

    (grad_head,) = transfer(
        "exchange_heads",
        5,
        mesh,
        sixth_body,
        (grad_heads,),
        (like((heads, rows, HEAD_DIM)),),
    )

    grad_value = mm("gqk,gqd->gkd", probs_low, grad_head)
    grad_probs = mm("gqd,gkd->gqk", grad_head, valued)
    weighted = jnp.sum(probs * grad_probs, axis=-1, keepdims=True)
    grad_scores = (probs * (grad_probs - weighted)).astype(bf16)
    grad_query = mm("gqk,gkd->gqd", grad_scores, keyed) * scale
    grad_key = mm("gqk,gqd->gkd", grad_scores, query) * scale
    grad_qkv = jnp.concatenate(
        [
            rotary_back(grad_query, cosine, sine).astype(bf16),
            rotary_back(grad_key, cosine, sine).astype(bf16),
            grad_value.astype(bf16),
        ],
        axis=2,
    ).reshape(chunk, 3 * HEAD_DIM)
    qkv_grad = mm("td,tc->dc", xn_chunk, grad_qkv)
    attn_gain_part = jnp.sum(qkv_grad * w_qkv.astype(f32), axis=1) / attn_gain
    qkv_grad = qkv_grad.astype(bf16).reshape(count, deep, 3 * HEAD_DIM)

    def spread(vector):
        return jnp.pad(vector.reshape(count, 1, deep), ((0, 0), (0, 7), (0, 0)))

    def seventh_body(place, given, made, room):
        gq, wq, qg, op, ag, fg = given
        one, qg_all, op_sum, ag_all, fg_all = made
        one_view = part_view(one, rows, part)
        made_here = Product(place, gq, None, wq, room[7:9], heads, rows, part)
        yield scatter(place, heads, made_here, room[:7], lambda c: one_view(0, c), (rows, part), True)
        yield scatter(
            place, count, lambda s: strips.at(op, s), room[9:], lambda c: op_sum, (out_rows, deep), False
        )
        yield both(place, count, lambda s: ag.at[s], lambda c, s: ag_all.at[c, s], lambda c: ag_all.at[c])
        yield exchange(place, count, lambda s: fg.at[s], lambda s: fg_all.at[s])
        yield later(exchange(place, count, lambda s: qg.at[s], lambda s: qg_all.at[s]), 6)

    grad_one, qkv_all, out_proj_sum, attn_gains, ffn_gains = transfer(
        "scatter_grads",
        6,
        mesh,
        seventh_body,
        (
            grad_qkv,
            w_qkv.T,
            qkv_grad,
            strips.cut(out_proj_part),
            spread(attn_gain_part),
            spread(ffn_gain_part),
        ),
        (
            like((rows, width)),
            like((count, deep, 3 * HEAD_DIM)),
            like((out_rows, deep)),
            like((cores, count, 8, deep), f32),
            like((count, 8, deep), f32),
        ),
        scatter_scratch(heads, cores, rows, part, 3 * HEAD_DIM) + scatter_scratch(count, 1, out_rows, deep),
        semaphores=600,
        vmem=56 * 2**20,
    )

    grad_one = grad_one.astype(f32)
    rstd_one = lax.rsqrt(jnp.mean(inputs * inputs, axis=-1, keepdims=True) + eps)
    scaled_one = grad_one * attn_gain
    inner_one = jnp.mean(scaled_one * inputs, axis=-1, keepdims=True)
    input_grad = (
        grad_hidden + rstd_one * scaled_one - inputs * (rstd_one * rstd_one * rstd_one) * inner_one
    ).astype(bf16)
    qkv_sum = jnp.sum(qkv_all.reshape(count // heads, heads, deep, 3 * HEAD_DIM).astype(f32), axis=0)
    qkv_sum = qkv_sum.transpose(1, 0, 2)

    def of_heads(which):
        return qkv_sum[:, :, which * HEAD_DIM : (which + 1) * HEAD_DIM].reshape(deep, heads * HEAD_DIM)

    def of_shared(which):
        return shared_back[:, which * hidden_units : (which + 1) * hidden_units].reshape(-1, deep).astype(f32)

    return (
        output,
        input_grad,
        jnp.sum(attn_gains[:, :, 0, :], axis=(0, 1)),
        of_heads(0),
        of_heads(1),
        of_heads(2),
        out_proj_sum.astype(f32),
        jnp.sum(ffn_gains[:, 0, :], axis=0),
        router_grad,
        gate_grad[None],
        up_grad[None],
        down_grad[None],
        of_shared(0).T,
        of_shared(1).T,
        of_shared(2),
    )


def solution(mesh):
    in_specs = (
        P("expert", None),
        P("expert", None),
        P("expert", None),
        P("expert"),
        P("expert", "tensor"),
        P("expert", "tensor"),
        P("expert", "tensor"),
        P("tensor", "expert"),
        P("expert"),
        P("expert", None),
        P("expert", None, "tensor"),
        P("expert", None, "tensor"),
        P("expert", "tensor", None),
        P("expert", "tensor"),
        P("expert", "tensor"),
        P("tensor", "expert"),
        P("expert", None),
    )
    out_specs = (
        P("expert", None),
        P("expert", None),
        P("expert"),
        P("expert", "tensor"),
        P("expert", "tensor"),
        P("expert", "tensor"),
        P("tensor", "expert"),
        P("expert"),
        P("expert", None),
        P("expert", None, "tensor"),
        P("expert", None, "tensor"),
        P("expert", "tensor", None),
        P("expert", "tensor"),
        P("expert", "tensor"),
        P("tensor", "expert"),
    )
    return jax.shard_map(
        functools.partial(local, mesh), mesh=mesh, in_specs=in_specs, out_specs=out_specs, check_vma=False
    )
```

```python
import functools

import jax
import jax.numpy as jnp
from jax import lax
from jax.experimental import pallas as pl
from jax.experimental.pallas import tpu as pltpu
from jax.sharding import PartitionSpec as P

HEAD_DIM = 128
TOP = 6
MESH = pl.DeviceIdType.MESH
ANY = pl.BlockSpec(memory_space=pl.ANY)

bf16 = jnp.bfloat16
f32 = jnp.float32
eps = 1e-06
highest = lax.Precision.HIGHEST
floor_score = -1e30


class Place:
    def __init__(self, sems, count, cores):
        self.sems, self.used = sems, 0
        self.count, self.cores = count, cores
        self.e = lax.axis_index("expert")
        self.t = lax.axis_index("tensor")
        self.quad = lax.rem(self.e, 4)
        self.far = lax.div(self.e, 4)

    def take(self, number):
        first = self.used
        self.used = first + number
        return first

    def ring(self, distance):
        return lax.rem(self.t + distance, self.cores)

    def copy(self, src, dst, out_sem, in_sem, e, t):
        return pltpu.make_async_remote_copy(
            src_ref=src,
            dst_ref=dst,
            send_sem=self.sems.at[out_sem],
            recv_sem=self.sems.at[in_sem],
            device_id={"expert": e, "tensor": t},
            device_id_type=MESH,
        )

    def send(self, src, dst, out_sem, in_sem, e, t):
        move = self.copy(src, dst, out_sem, in_sem, e, t)
        move.start()
        return move

    def arrived(self, landing, in_sem):
        self.copy(landing, landing, in_sem, in_sem, self.e, self.t).wait_recv()

    def keep(self, src, dst):
        move = pltpu.make_async_copy(src, dst, self.sems.at[self.take(1)])
        move.start()
        return move

    def meet(self):
        barrier = pltpu.get_barrier_semaphore()
        for step in range(1, self.count):
            pl.semaphore_signal(
                barrier,
                inc=1,
                device_id={"expert": lax.rem(self.e + step, self.count), "tensor": self.t},
                device_id_type=MESH,
            )
        for step in range(1, self.cores):
            pl.semaphore_signal(
                barrier,
                inc=1,
                device_id={"expert": self.e, "tensor": self.ring(step)},
                device_id_type=MESH,
            )
        pl.semaphore_wait(barrier, self.count + self.cores - 2)


class Block:
    def __init__(self, place, members):
        self.place, self.deep = place, members // 4
        self.rank = lax.rem(place.far, self.deep)
        self.start = place.far - self.rank

    def flips(self, order):
        high, low = lax.div(self.place.quad, 2), lax.rem(self.place.quad, 2)
        one = high + (low - high) * order
        two = low + (high - low) * order
        return (2 - order) * (1 - 2 * one), (1 + order) * (1 - 2 * two)

    def slot(self, k, i, j, order):
        one, two = self.flips(order)
        return lax.rem(self.rank + k, self.deep) * 4 + self.place.quad + i * one + j * two

    def own(self):
        return self.rank * 4 + self.place.quad

    def device(self, slot):
        return self.start * 4 + slot


def when(condition, action):
    if condition is None:
        action()
    else:
        pl.when(condition)(action)


def gather(place, members, mine, whole, view, halves, pieces=1):
    block = Block(place, members)
    deep, e, t, rank = block.deep, place.e, place.t, block.rank
    order = lax.rem(t, 2)
    cores = place.cores if halves else 1
    spots = 2 * deep - 1

    def lots(number):
        return place.take(number * pieces)

    zs, zr = lots(spots + 1), lots(spots)
    s2, r2 = lots(spots), lots(spots)
    s3, r3 = lots(2 * spots), lots(2 * spots)
    s4, r4 = lots(4 * spots * (cores - 1)), lots(4 * spots * (cores - 1))
    one, two = block.flips(order)
    own = block.own()
    sent, kept = [], place.keep(whole[0], whole[1](own))
    line = [(0, 0)] + [(d, way) for d in range(1, deep) for way in (1, -1)]

    def index(d, way):
        return 0 if d == 0 else 2 * d - (1 if way > 0 else 0)

    def valid(d, way):
        return None if d == 0 else (rank >= d if way > 0 else rank < deep - d)

    def slot_of(d, way, i, j, order=order):
        one, two = block.flips(order)
        return (rank - way * d) * 4 + place.quad + i * one + j * two

    ends = {1: (rank < deep - 1, 4), -1: (rank >= 1, -4)}

    def onward(d, way, p):
        condition, step = ends[way]
        if d > 0:
            condition = jnp.logical_and(condition, valid(d, way))
        v = index(d, way)
        out = 1 + v if d > 0 else (0 if way > 0 else 1)
        source = view(slot_of(d, way, 0, 0), t, p) if d > 0 else mine(p)
        landing = view(slot_of(d, way, 0, 0), t, p)
        move = place.copy(source, landing, zs + out * pieces + p, zr + index(d + 1, way) * pieces + p, e + step, t)
        sent.append((condition, move))
        when(condition, move.start)

    def pass_on(source, landing, condition, out, into, number, p, target):
        move = place.copy(source, landing, out + number * pieces + p, into + number * pieces + p, target, t)
        sent.append((condition, move))
        return move

    def share(d, way, i, j, p):
        moves = []
        ref = view(slot_of(d, way, i, j), t, p)
        for far in range(1, cores):
            at = (((far - 1) * spots + index(d, way)) * 4 + i * 2 + j) * pieces + p
            move = place.copy(ref, ref, s4 + at, r4 + at, e, place.ring(far))
            sent.append((valid(d, way), move))
            moves.append(move)
        return moves

    def start(moves):
        for move in moves:
            move.start()

    for p in range(pieces):
        if deep > 1:
            onward(0, 1, p)
            onward(0, -1, p)
        pass_on(mine(p), view(own, t, p), None, s2, r2, 0, p, e + one).start()
        pass_on(mine(p), view(own, t, p), None, s3, r3, 0, p, e + two).start()
        yield

    def from_line(d, way, p):
        ref = view(slot_of(d, way, 0, 0), t, p)
        v, condition = index(d, way), valid(d, way)
        when(condition, lambda: place.arrived(ref, zr + v * pieces + p))
        if d < deep - 1:
            onward(d, way, p)
        moves = [
            pass_on(ref, ref, condition, s2, r2, v, p, e + one),
            pass_on(ref, ref, condition, s3, r3, 2 * v, p, e + two),
        ] + share(d, way, 0, 0, p)
        when(condition, lambda: start(moves))

    def from_one(d, way, p):
        ref = view(slot_of(d, way, 1, 0), t, p)
        v, condition = index(d, way), valid(d, way)
        moves = [pass_on(ref, ref, condition, s3, r3, 2 * v + 1, p, e + two)] + share(d, way, 1, 0, p)

        def act():
            place.arrived(ref, r2 + v * pieces + p)
            start(moves)

        when(condition, act)

    def from_two(d, way, i, p):
        ref = view(slot_of(d, way, i, 1), t, p)
        v, condition = index(d, way), valid(d, way)
        moves = share(d, way, i, 1, p)

        def act():
            place.arrived(ref, r3 + (2 * v + i) * pieces + p)
            start(moves)

        when(condition, act)

    for d in range(1, deep + 1):
        for p in range(pieces):
            for way in (1, -1) if d > 1 else (1,):
                from_one(d - 1, way if d > 1 else 0, p)
            if d < deep:
                for way in (1, -1):
                    from_line(d, way, p)
            yield
    for d, way in line:
        for i in range(2):
            for p in range(pieces):
                from_two(d, way, i, p)
        yield
    for far in range(1, cores):
        source = place.ring(cores - far)
        for d, way in line:
            for i in range(2):
                for j in range(2):
                    if d + i + j > 0:
                        for p in range(pieces):
                            at = (((far - 1) * spots + index(d, way)) * 4 + i * 2 + j) * pieces + p
                            ref = view(slot_of(d, way, i, j, lax.rem(source, 2)), source, p)
                            when(valid(d, way), functools.partial(place.arrived, ref, r4 + at))
    for condition, move in sent:
        when(condition, move.wait_send)
    kept.wait()


def add_up(target, sources, rows, columns):
    step = max(16, min(rows, 16384 // columns // 16 * 16))

    def body(at, carry):
        piece = pl.ds(pl.multiple_of(at * step, step), step)
        total = sources[0][piece, :].astype(f32)
        for other in sources[1:]:
            total = total + other[piece, :].astype(f32)
        target[piece, :] = total.astype(target.dtype)
        return carry

    lax.fori_loop(0, rows // step, body, 0)


class Product:
    def __init__(self, place, left, varied, fixed, rooms, members, rows, columns):
        self.place, self.left, self.varied = place, left, varied
        self.lhs, self.rhs = rooms
        self.rows, self.columns = rows, columns
        self.lead = 0 if varied is None else varied.shape[0] // members
        self.waits, self.turn = {}, 0
        self.setup = []
        for buffer in range(self.rhs.shape[0]):
            self.setup.append(place.keep(fixed, self.rhs.at[buffer, pl.ds(self.lead, fixed.shape[0]), :]))

    def fetch(self, turn, slot):
        buffer = turn % 2
        rows = pl.ds(pl.multiple_of(slot * self.rows, self.rows), self.rows)
        moves = [self.place.keep(self.left.at[rows, :], self.lhs.at[buffer])]
        if self.lead:
            lead = pl.ds(pl.multiple_of(slot * self.lead, self.lead), self.lead)
            moves.append(self.place.keep(self.varied.at[lead, :], self.rhs.at[buffer, pl.ds(0, self.lead), :]))
        self.waits[turn] = moves

    def ready(self, turn):
        for move in self.setup:
            move.wait()
        self.setup = []
        for move in self.waits.pop(turn):
            move.wait()

    def make(self, turn, core, target):
        buffer = turn % 2
        right = self.rhs.at[buffer if self.lead else 0]
        wide = min(self.columns, 512)

        def body(at, carry):
            source = pl.ds(pl.multiple_of(core * self.columns + at * wide, wide), wide)
            into = pl.ds(pl.multiple_of(at * wide, wide), wide)
            target[:, into] = jnp.dot(
                self.lhs[buffer], right[:, source], preferred_element_type=f32
            ).astype(bf16)
            return carry

        lax.fori_loop(0, self.columns // wide, body, 0)


def scatter(place, members, sources, room, views, shape, halves, credit=None):
    block = Block(place, members)
    deep, e, t = block.deep, place.e, place.t
    rows, columns = shape
    order = 1 - lax.rem(t, 2)
    cores = place.cores if halves else 1
    count = len(sources)
    mine, outgoing, land0, land1s, land2s, land3s, finals = room
    s0, r0 = place.take(4 * deep * cores * count), place.take(4 * deep * cores * count)
    s1, r1 = place.take(2 * deep * count), place.take(2 * deep * count)
    s2, r2 = place.take(deep * count), place.take(deep * count)
    s3, r3 = place.take(deep * count), place.take(deep * count)
    s4, r4 = place.take(cores * count), place.take(cores * count)
    walk = [(f, k) for f in range(count) for k in list(range(1, deep)) + [0]]
    one, two = block.flips(order)
    sent, loads, last, kept = [], {}, {}, []
    quads = [(1, 1), (1, 0), (0, 1), (0, 0)]
    turns = [(f, k, i, j) for f, k in walk for i, j in quads]
    ring = outgoing.shape[0]
    leaving = []

    def slot_of(k, i, j):
        return block.slot(k, i, j, order)

    def land_index(d, k, i, j):
        return (d - 1) * deep * 4 + k * 4 + i * 2 + j

    def produce(number):
        f, k, i, j = turns[number]
        source = sources[f]
        if (k, i, j) in last:
            last.pop((k, i, j)).wait_send()
        if not isinstance(source, Product):
            loads[f, k, i, j] = place.keep(source(slot_of(k, i, j)), mine.at[slot_of(k, i, j)])
            return
        local_number = number - f * 4 * deep
        if local_number == 0:
            source.fetch(0, slot_of(k, i, j))
        source.ready(local_number)
        if local_number + 1 < 4 * deep:
            source.fetch(local_number + 1, slot_of(*turns[number + 1][1:]))
        if number >= ring:
            for move in leaving[number - ring]:
                move.wait_send()
        moves = []
        for d in range(1, cores):
            target = place.ring(d)
            buffer = outgoing.at[number % ring, d - 1]
            source.make(local_number, target, buffer)
            at = land_index(d, k, *((j, i) if d % 2 else (i, j)))
            if f > 0:
                pl.semaphore_wait(credit.at[at], 1)
            sem = f * 4 * deep * cores + at
            moves.append(place.send(buffer, land0.at[at], s0 + sem, r0 + sem, e, target))
        leaving.append(moves)
        source.make(local_number, t, mine.at[slot_of(k, i, j)])

    def terms_of(f, k, i, j):
        if (f, k, i, j) in loads:
            loads[f, k, i, j].wait()
        terms = [mine.at[slot_of(k, i, j)]]
        for d in range(1, cores):
            at = land_index(d, k, i, j)
            place.arrived(land0.at[at], r0 + f * 4 * deep * cores + at)
            terms.append(land0.at[at])
        if i == 0:
            at = (f * deep + k) * 2 + j
            place.arrived(land1s.at[at], r1 + at)
            terms.append(land1s.at[at])
            if j == 0:
                at = f * deep + k
                place.arrived(land2s.at[at], r2 + at)
                terms.append(land2s.at[at])
        return terms

    def give_back(f, k, i, j):
        if f + 1 < count:
            for d in range(1, cores):
                pl.semaphore_signal(
                    credit.at[land_index(d, k, i, j)],
                    inc=1,
                    device_id={"expert": e, "tensor": place.ring(cores - d)},
                    device_id_type=MESH,
                )

    def leave(f, k, i, j, landing, out, into, at, target):
        move = place.send(mine.at[slot_of(k, i, j)], landing.at[at], out + at, into + at, target, t)
        last[k, i, j] = move

    def first_flip(f, k, j):
        terms, ref = terms_of(f, k, 1, j), mine.at[slot_of(k, 1, j)]
        if len(terms) > 1:
            add_up(ref, terms, rows, columns)
        give_back(f, k, 1, j)
        leave(f, k, 1, j, land1s, s1, r1, (f * deep + k) * 2 + j, e + one)

    def second_flip(f, k):
        add_up(mine.at[slot_of(k, 0, 1)], terms_of(f, k, 0, 1), rows, columns)
        give_back(f, k, 0, 1)
        leave(f, k, 0, 1, land2s, s2, r2, f * deep + k, e + two)

    def line(f, k):
        terms, ref = terms_of(f, k, 0, 0), mine.at[slot_of(k, 0, 0)]
        if k > 0:
            add_up(ref, terms, rows, columns)
            give_back(f, k, 0, 0)
            peer = block.device(lax.rem(block.rank + k, deep) * 4 + place.quad)
            leave(f, k, 0, 0, land3s, s3, r3, f * deep + k, peer)
            return
        for far in range(1, deep):
            place.arrived(land3s.at[f * deep + far], r3 + f * deep + far)
            terms.append(land3s.at[f * deep + far])
        final = finals.at[f]
        add_up(final, terms, rows, columns)
        give_back(f, k, 0, 0)
        kept.append(place.keep(final, views[f](t)))
        for d in range(1, cores):
            at = f * cores + d
            sent.append(place.send(final, views[f](t), s4 + at, r4 + at, e, place.ring(d)))

    for step in range(len(walk) + 2):
        fresh = step < len(walk)
        if fresh:
            produce(4 * step)
            yield
            produce(4 * step + 1)
            yield
            first_flip(*walk[step], 1)
            yield
            produce(4 * step + 2)
            yield
        if 0 <= step - 1 < len(walk):
            second_flip(*walk[step - 1])
            yield
        if fresh:
            produce(4 * step + 3)
            yield
            first_flip(*walk[step], 0)
            yield
        if 0 <= step - 2 < len(walk):
            line(*walk[step - 2])
            yield
    for f in range(count):
        for d in range(1, cores):
            place.arrived(views[f](place.ring(cores - d)), r4 + f * cores + d)
    for moves in leaving[-ring:]:
        for move in moves:
            move.wait_send()
    for move in list(last.values()) + sent:
        move.wait_send()
    for move in kept:
        move.wait()


def scatter_scratch(members, cores, rows, columns, products=(), ring=4):
    deep = members // 4
    count = max(1, len(products))
    short = rows if cores > 1 else 16
    rooms = [
        pltpu.VMEM((members, rows, columns), bf16),
        pltpu.VMEM((ring, max(1, cores - 1), short, columns), bf16),
        pltpu.VMEM((max(1, (cores - 1) * members), short, columns), bf16),
        pltpu.VMEM((2 * deep * count, rows, columns), bf16),
        pltpu.VMEM((deep * count, rows, columns), bf16),
        pltpu.VMEM((deep * count, rows, columns), bf16),
        pltpu.VMEM((count, rows, columns), bf16),
    ]
    for depth, varied in products:
        rooms.append(pltpu.VMEM((2, rows, depth), bf16))
        rooms.append(pltpu.VMEM((2 if varied else 1, depth, columns * cores), bf16))
    return rooms


def exchange(place, members, source, landing):
    e, t = place.e, place.t
    own = lax.rem(e, members)
    base = e - own
    sends, arrivals = place.take(members), place.take(members)
    sent = []
    for d in range(1, members):
        target = lax.rem(own + d, members)
        sent.append(place.send(source(target), landing(own), sends + d, arrivals + d, base + target, t))
    kept = place.keep(source(own), landing(own))
    yield
    for d in range(1, members):
        place.arrived(landing(lax.rem(own + members - d, members)), arrivals + d)
    for move in sent:
        move.wait_send()
    kept.wait()


def both(place, members, source, landing, part):
    yield from exchange(place, members, source, lambda slot: landing(place.t, slot))
    sends, arrivals = place.take(place.cores), place.take(place.cores)
    sent = []
    for d in range(1, place.cores):
        mine = part(place.t)
        sent.append(place.send(mine, mine, sends + d, arrivals + d, place.e, place.ring(d)))
    yield
    for d in range(1, place.cores):
        place.arrived(part(place.ring(place.cores - d)), arrivals + d)
    for move in sent:
        move.wait_send()


def later(task, rounds):
    for _ in range(rounds):
        yield
    yield from task


def run(tasks):
    tasks = list(tasks)
    while tasks:
        left = []
        for task in tasks:
            try:
                next(task)
                left.append(task)
            except StopIteration:
                pass
        tasks = left


def transfer(name, number, mesh, body, ins, outs, scratch=(), semaphores=400, vmem=None):
    count, cores = mesh.shape["expert"], mesh.shape["tensor"]
    semaphores = semaphores * max(1, count * cores // 32)

    def kernel(*refs):
        given = refs[: len(ins)]
        made = refs[len(ins) : len(ins) + len(outs)]
        room = refs[len(ins) + len(outs) : -1]
        place = Place(refs[-1], count, cores)
        place.meet()
        run(body(place, given, made, room))
        assert place.used <= semaphores, place.used

    size = sum(x.size * x.dtype.itemsize for x in list(ins) + list(outs))
    return pl.pallas_call(
        kernel,
        name=name,
        out_shape=[jax.ShapeDtypeStruct(shape, dtype) for shape, dtype in outs_of(outs)],
        in_specs=[ANY] * len(ins),
        out_specs=[ANY] * len(outs),
        scratch_shapes=list(scratch) + [pltpu.SemaphoreType.DMA((semaphores,))],
        cost_estimate=pl.CostEstimate(flops=0, bytes_accessed=size, transcendentals=0),
        compiler_params=pltpu.CompilerParams(
            collective_id=number, has_side_effects=True, vmem_limit_bytes=vmem
        ),
    )(*ins)


def outs_of(outs):
    return [(x.shape, x.dtype) for x in outs]


def like(shape, dtype=bf16):
    return jax.ShapeDtypeStruct(shape, dtype)


def part_view(ref, rows, columns, pieces=1):
    height = rows // pieces

    def view(slot, core, piece=0):
        at = 0 if isinstance(slot, int) else pl.multiple_of(slot * rows, rows)
        return ref.at[
            pl.ds(at + piece * height, height), pl.ds(pl.multiple_of(core * columns, columns), columns)
        ]

    return view


PIECES = 2


def lanes(at, columns):
    return pl.ds(pl.multiple_of(at * columns, columns), columns)


class Strips:
    def __init__(self, count, columns):
        self.count, self.columns = count, columns
        self.direct = columns % 128 == 0

    def shape(self, rows):
        return (rows, self.count * self.columns) if self.direct else (self.count, rows, self.columns)

    def at(self, ref, slot):
        return ref.at[:, lanes(slot, self.columns)] if self.direct else ref.at[slot]

    def cut(self, array):
        rows = array.shape[0]
        return array if self.direct else array.reshape(rows, self.count, self.columns).transpose(1, 0, 2)

    def join(self, array):
        rows = array.shape[0 if self.direct else 1]
        return array if self.direct else array.transpose(1, 0, 2).reshape(rows, self.count * self.columns)


def row_gather(place, members, source, landing, rows, part):
    def mine(piece):
        height = rows // PIECES
        return source.at[pl.ds(piece * height, height), lanes(place.t, part)]

    whole = (source, lambda slot: landing.at[pl.ds(pl.multiple_of(slot * rows, rows), rows), :])
    return gather(place, members, mine, whole, part_view(landing, rows, part, PIECES), True, PIECES)


def rotary(values, cosine, sine):
    half = values.shape[-1] // 2
    first = values[..., :half]
    second = values[..., half:]
    return jnp.concatenate([first * cosine - second * sine, second * cosine + first * sine], axis=-1)


def rotary_back(grads, cosine, sine):
    half = grads.shape[-1] // 2
    first = grads[..., :half]
    second = grads[..., half:]
    return jnp.concatenate([first * cosine + second * sine, second * cosine - first * sine], axis=-1)


def sequence_tables(lengths_rows, tok_rows):
    ends = jnp.cumsum(lengths_rows, axis=1)
    starts = ends - lengths_rows
    places = jnp.arange(tok_rows, dtype=jnp.int32)
    segment = jnp.sum((places[None, :, None] >= ends[:, None, :]).astype(jnp.int32), axis=2)
    member = segment[:, :, None] == jnp.arange(lengths_rows.shape[1], dtype=jnp.int32)[None, None, :]
    first = jnp.sum(jnp.where(member, starts[:, None, :], 0), axis=2)
    return segment, places[None, :] - first


def silu_parts(values):
    sigmoid_value = jax.nn.sigmoid(values)
    return values * sigmoid_value, sigmoid_value * (1.0 + values * (1.0 - sigmoid_value))


def mm(form, left, right):
    return jnp.einsum(form, left, right, preferred_element_type=f32)


def up_to(value, step):
    return -(-value // step) * step


def experts_kernel(
    groups,
    capacity,
    rows,
    xn_ref,
    grad_ref,
    position_ref,
    gate_ref,
    wg_ref,
    wu_ref,
    wd_ref,
    sh_in_ref,
    sh_down_ref,
    received_ref,
    gated_ref,
    low_ref,
    back_ref,
    act_ref,
    gate_back_ref,
    up_back_ref,
    dots_ref,
    left_forward_ref,
    left_backward_ref,
):
    def dot(left, right, sides=((1,), (0,))):
        return lax.dot_general(left, right, (sides, ((), ())), preferred_element_type=f32)

    places = lax.broadcasted_iota(jnp.int32, (capacity, rows), 0).astype(f32)
    gates, grads, onehots = [], [], []
    for g in range(groups):
        token = pl.ds(g * rows, rows)
        slot = pl.ds(g * capacity, capacity)
        chosen = (position_ref[g] == places).astype(f32)
        onehot = chosen.astype(bf16)
        onehots.append(chosen)
        received_ref[slot, :] = dot(onehot, xn_ref[token, :]).astype(bf16)
        gate = jnp.sum(chosen * gate_ref[g], axis=1, keepdims=True)
        row_grads = dot(onehot, grad_ref[token, :])
        gated_ref[slot, :] = (gate * row_grads).astype(bf16)
        low_ref[slot, :] = row_grads.astype(bf16)
        gates.append(gate)
        turned = chosen.T.astype(bf16)
        left_forward_ref[token, :capacity] = turned
        left_backward_ref[token, :capacity] = turned
    gate = jnp.concatenate(gates, axis=0)
    received = received_ref[...]
    exp_gate = dot(received, wg_ref[...], ((1,), (1,)))
    exp_up = dot(received, wu_ref[...], ((1,), (1,)))
    silu, slope = silu_parts(exp_gate)
    act = (silu * exp_up).astype(bf16)
    act_ref[...] = act
    out = dot(act, wd_ref[...])
    dots = jnp.sum(low_ref[...].astype(f32) * out, axis=1, keepdims=True)
    low_ref[...] = (gate * out).astype(bf16)
    for g in range(groups):
        column = dots[g * capacity : (g + 1) * capacity]
        token_dots = jnp.sum(onehots[g] * column, axis=0, keepdims=True)
        dots_ref[g] = jnp.broadcast_to(token_dots, (8, rows))
    act_grad = dot(gated_ref[...], wd_ref[...], ((1,), (1,)))
    gate_back = (act_grad * exp_up * slope).astype(bf16)
    up_back = (act_grad * silu).astype(bf16)
    gate_back_ref[...] = gate_back
    up_back_ref[...] = up_back
    back_ref[...] = (
        dot(gate_back, wg_ref[...]) + dot(up_back, wu_ref[...])
    ).astype(bf16)
    wide = sh_down_ref.shape[0]
    both = dot(xn_ref[...], sh_in_ref[...], ((1,), (1,)))
    sh_gate, sh_up = both[:, :wide], both[:, wide:]
    sh_silu, sh_slope = silu_parts(sh_gate)
    left_forward_ref[:, capacity:] = (sh_silu * sh_up).astype(bf16)
    sh_grad = dot(grad_ref[...], sh_down_ref[...], ((1,), (1,)))
    left_backward_ref[:, capacity : capacity + wide] = (sh_grad * sh_up * sh_slope).astype(bf16)
    left_backward_ref[:, capacity + wide :] = (sh_grad * sh_silu).astype(bf16)


def experts_pass(count, capacity, rows, xn_all, grad_all, position, gate, wg, wu, wd, sh_in, sh_down):
    groups = 2
    units, width = wg.shape
    wide = sh_down.shape[0]

    def along(*shape):
        return pl.BlockSpec(shape, lambda i: (i,) + (0,) * (len(shape) - 1))

    def whole(array):
        return pl.BlockSpec(array.shape, lambda i: (0,) * array.ndim, pipeline_mode=pl.Buffered(1))

    slots = groups * capacity
    tokens = groups * rows
    flops = 2 * count * capacity * width * units * 6
    return pl.pallas_call(
        functools.partial(experts_kernel, groups, capacity, rows),
        name="experts_pass",
        grid=(count // groups,),
        in_specs=[
            along(tokens, width),
            along(tokens, width),
            along(groups, 1, rows),
            along(groups, 1, rows),
            whole(wg),
            whole(wu),
            whole(wd),
            whole(sh_in),
            whole(sh_down),
        ],
        out_specs=[
            along(slots, width),
            along(slots, width),
            along(slots, width),
            along(slots, width),
            along(slots, units),
            along(slots, units),
            along(slots, units),
            along(groups, 8, rows),
            along(tokens, capacity + wide),
            along(tokens, capacity + 2 * wide),
        ],
        out_shape=[like((count * capacity, width))] * 4
        + [like((count * capacity, units))] * 3
        + [
            like((count, 8, rows), f32),
            like((count * rows, capacity + wide)),
            like((count * rows, capacity + 2 * wide)),
        ],
        cost_estimate=pl.CostEstimate(
            flops=flops, bytes_accessed=4 * count * (rows + 2 * capacity) * width, transcendentals=0
        ),
        compiler_params=pltpu.CompilerParams(vmem_limit_bytes=58 * 2**20),
    )(xn_all, grad_all, position, gate, wg, wu, wd, sh_in, sh_down)


def local(
    mesh,
    tokens,
    lengths,
    routes,
    gain_attn,
    w_query,
    w_key,
    w_value,
    w_out,
    gain_ffn,
    w_router,
    routed_gate_weight,
    routed_up_weight,
    w_down,
    w_shared_gate,
    w_shared_up,
    w_shared_down,
    out_grad,
):
    count, cores = mesh.shape["expert"], mesh.shape["tensor"]
    rows, width = tokens.shape
    part = width // cores
    deep = w_query.shape[0]
    experts = w_router.shape[1]
    heads = w_query.shape[1] // HEAD_DIM
    capacity = up_to(min(rows, rows * TOP * 4 // (3 * count)), 128)
    hidden_units = w_shared_gate.shape[1] // count
    scale = HEAD_DIM ** (-0.5)
    e = lax.axis_index("expert")
    t = lax.axis_index("tensor")
    chunk = heads * rows
    strips = Strips(count, deep)

    expert_ids = jnp.arange(experts, dtype=jnp.int32)
    choose = jnp.any(routes[:, :, None] == expert_ids[None, None, :], axis=1)
    mask_t = choose.T.astype(bf16)
    vectors = jnp.concatenate(
        [
            w_router.T,
            gain_attn[None],
            gain_ffn[None],
            jnp.pad(lengths.astype(bf16), ((0, 0), (0, deep - lengths.shape[1]))),
        ],
        axis=0,
    )
    head_rows = up_to(vectors.shape[0], 16)
    vectors = jnp.pad(vectors, ((0, head_rows - vectors.shape[0]), (0, 0)))
    pieces = rows // deep
    mask_rows = mask_t.reshape(experts * pieces, deep)
    small = jnp.concatenate([vectors, mask_rows], axis=0)
    small_rows = up_to(small.shape[0], 16)
    small = jnp.pad(small, ((0, small_rows - small.shape[0]), (0, 0)))

    def first_body(place, given, made, room):
        tok, sm, *weights = given
        tok_all, sm_all, w_all = made
        yield exchange(place, count, lambda s: sm, lambda s: sm_all.at[s])
        yield row_gather(place, heads, tok, tok_all, rows, part)
        for which, weight in enumerate(weights):

            def landing(slot, which=which):
                at = pl.ds(pl.multiple_of(slot * deep, deep), deep)
                return w_all.at[at, pl.ds(which * HEAD_DIM, HEAD_DIM)]

            yield exchange(
                place, count, lambda s, w=weight: w.at[:, lanes(lax.rem(s, heads), HEAD_DIM)], landing
            )

    tok_chunk, small_all, w_qkv = transfer(
        "gather_tokens",
        0,
        mesh,
        first_body,
        (tokens, small, w_query, w_key, w_value),
        (like((chunk, width)), like((count, small_rows, deep)), like((width, 3 * HEAD_DIM))),
    )

    router_full = small_all[:, :experts].transpose(1, 0, 2).reshape(experts, width)
    attn_gain = small_all[:, experts].reshape(width).astype(f32)
    ffn_gain = small_all[:, experts + 1].reshape(width).astype(f32)
    lengths_all = small_all[:, experts + 2, : lengths.shape[1]].astype(f32).astype(jnp.int32)
    masks = small_all[:, head_rows : head_rows + experts * pieces].reshape(count, experts, rows)

    member = e % heads
    lengths_chunk = lax.dynamic_slice_in_dim(lengths_all, e - member, heads, axis=0)
    segment, positions = sequence_tables(lengths_chunk, rows)
    half = HEAD_DIM // 2
    inverse = 10000.0 ** (-2.0 * jnp.arange(half, dtype=f32) / HEAD_DIM)
    angles = positions.astype(f32)[:, :, None] * inverse[None, None, :]
    cosine, sine = jnp.cos(angles), jnp.sin(angles)

    tok32 = tok_chunk.astype(f32)
    rstd_chunk = lax.rsqrt(jnp.mean(tok32 * tok32, axis=-1, keepdims=True) + eps)
    xn_chunk = (tok32 * rstd_chunk * attn_gain).astype(bf16)
    qkv = jnp.dot(xn_chunk, w_qkv, preferred_element_type=f32).reshape(heads, rows, 3 * HEAD_DIM)
    query = rotary(qkv[..., :HEAD_DIM], cosine, sine).astype(bf16)
    keyed = rotary(qkv[..., HEAD_DIM : 2 * HEAD_DIM], cosine, sine).astype(bf16)
    valued = qkv[..., 2 * HEAD_DIM :].astype(bf16)
    places = jnp.arange(rows, dtype=jnp.int32)
    allowed = (segment[:, :, None] == segment[:, None, :]) & (places[None, :] <= places[:, None])[None]
    scores = jnp.where(allowed, mm("gqd,gkd->gqk", query, keyed) * scale, floor_score)
    top_score = jnp.max(scores, axis=-1, keepdims=True)
    raised = jnp.exp(scores - top_score)
    probs = raised / jnp.sum(raised, axis=-1, keepdims=True)
    probs_low = probs.astype(bf16)
    head_out = mm("gqk,gkd->gqd", probs_low, valued).astype(bf16)

    shared_pack = jnp.concatenate(
        [
            w_shared_gate.T.reshape(count, hidden_units, deep),
            w_shared_up.T.reshape(count, hidden_units, deep),
            w_shared_down.reshape(count, hidden_units, deep),
        ],
        axis=1,
    )
    pack_rows = up_to(3 * hidden_units, 16)
    shared_pack = jnp.pad(shared_pack, ((0, 0), (0, pack_rows - 3 * hidden_units), (0, 0)))
    out_rows = w_out.shape[0]

    def second_body(place, given, made, room):
        ho, og, wo, sp = given
        ho_all, og_all, wo_all, sp_all = made
        yield exchange(place, heads, lambda s: ho.at[s], lambda s: ho_all.at[:, lanes(s, HEAD_DIM)])
        yield row_gather(place, count, og, og_all, rows, part)

        def wo_view(slot, core=0, piece=0):
            return strips.at(wo_all, slot)

        yield gather(place, count, lambda p: wo, (wo, wo_view), wo_view, False)
        yield exchange(place, count, lambda s: sp.at[s], lambda s: strips.at(sp_all, s))

    heads_out, grad_all, out_full, shared_all = transfer(
        "gather_inputs",
        1,
        mesh,
        second_body,
        (head_out, out_grad, w_out, shared_pack),
        (
            like((rows, heads * HEAD_DIM)),
            like((count * rows, width)),
            like(strips.shape(out_rows)),
            like(strips.shape(pack_rows)),
        ),
        semaphores=640,
    )
    out_full, shared_all = strips.join(out_full), strips.join(shared_all)
    attention_part = jnp.dot(heads_out, out_full, preferred_element_type=f32).astype(bf16)

    def third_body(place, given, made, room):
        ap, tok, gn, rt, mk = given
        hid_out, xn_all, gt_all = made
        parts, tok_v, gn_v, rt_v, mk_v, hid, xn, gt = room
        t = place.t
        sends, arrivals = place.take(cores), place.take(cores)
        sent = [place.send(ap, parts.at[t], sends + d, arrivals + d, place.e, place.ring(d)) for d in range(1, cores)]
        kept = [place.keep(ap, parts.at[t])]
        kept += [place.keep(a, b) for a, b in ((tok, tok_v), (gn, gn_v), (rt, rt_v), (mk, mk_v))]
        for move in kept:
            move.wait()
        for d in range(1, cores):
            place.arrived(parts.at[place.ring(cores - d)], arrivals + d)

        def body(at, carry):
            piece = pl.ds(pl.multiple_of(at * 16, 16), 16)
            total = parts[0, piece, :].astype(f32)
            for core in range(1, cores):
                total = total + parts[core, piece, :].astype(f32)
            values = tok_v[piece, :].astype(f32) + total
            hid[piece, :] = values
            rstd = lax.rsqrt(jnp.mean(values * values, axis=1, keepdims=True) + eps)
            xn[piece, :] = (values * rstd * gn_v[...]).astype(bf16)
            return carry

        lax.fori_loop(0, rows // 16, body, 0)
        saved = place.keep(hid, hid_out)
        yield row_gather(place, count, xn, xn_all, rows, part)
        logits = lax.dot_general(rt_v[...], xn[...], (((1,), (1,)), ((), ())), preferred_element_type=f32)
        picked = mk_v[...] > 0.5
        top_logit = jnp.max(jnp.where(picked, logits, floor_score), axis=0, keepdims=True)
        lifted = jnp.where(picked, jnp.exp(jnp.where(picked, logits - top_logit, 0.0)), 0.0)
        gt[...] = lifted / jnp.sum(lifted, axis=0, keepdims=True)
        yield exchange(place, count, lambda s: gt, lambda s: gt_all.at[s])
        for move in sent:
            move.wait_send()
        saved.wait()

    hidden, xn_all, gates_all = transfer(
        "gather_rows",
        2,
        mesh,
        third_body,
        (attention_part, tokens, ffn_gain[None], router_full, mask_t.astype(f32)),
        (like((rows, width), f32), like((count * rows, width)), like((count, experts, rows), f32)),
        [
            pltpu.VMEM((cores, rows, width), bf16),
            pltpu.VMEM((rows, width), bf16),
            pltpu.VMEM((1, width), f32),
            pltpu.VMEM((experts, width), bf16),
            pltpu.VMEM((experts, rows), f32),
            pltpu.VMEM((rows, width), f32),
            pltpu.VMEM((rows, width), bf16),
            pltpu.VMEM((experts, rows), f32),
        ],
        semaphores=400,
        vmem=40 * 2**20,
    )
    inputs = tokens.astype(f32)
    rstd_two = lax.rsqrt(jnp.mean(hidden * hidden, axis=-1, keepdims=True) + eps)
    gates = lax.dynamic_index_in_dim(gates_all, e, axis=0, keepdims=False).T

    own_mask = lax.dynamic_index_in_dim(masks, e, axis=1, keepdims=False).astype(f32)
    own_gate = lax.dynamic_index_in_dim(gates_all, e, axis=1, keepdims=False)
    at_row = jnp.arange(rows, dtype=jnp.int32)
    earlier = (at_row[:, None] < at_row[None, :]).astype(bf16)
    position = jnp.where(own_mask > 0.5, jnp.dot(own_mask.astype(bf16), earlier, preferred_element_type=f32), -1.0)
    gate_weight, up_weight, down_weight = routed_gate_weight[0].T, routed_up_weight[0].T, w_down[0]
    sh_wide = up_to(hidden_units, 128)

    def widened(which):
        piece = shared_all[which * hidden_units : (which + 1) * hidden_units]
        return jnp.pad(piece, ((0, sh_wide - hidden_units), (0, 0)))

    fixed_backward = jnp.concatenate([widened(0), widened(1)], axis=0)
    fixed_forward = widened(2)
    (
        received,
        gated_grad,
        exp_low,
        back_rows,
        exp_act,
        gate_back,
        up_back,
        token_dots,
        left_forward,
        left_backward,
    ) = experts_pass(
        count,
        capacity,
        rows,
        xn_all,
        grad_all,
        position[:, None],
        own_gate[:, None],
        gate_weight,
        up_weight,
        down_weight,
        fixed_backward,
        fixed_forward,
    )

    sh_grads = mm("tf,td->fd", left_backward[:, capacity:], xn_all).astype(bf16)
    shared_grads = jnp.concatenate(
        [
            sh_grads[:hidden_units],
            sh_grads[sh_wide : sh_wide + hidden_units],
            mm("tf,td->fd", left_forward[:, capacity:], grad_all).astype(bf16)[:hidden_units],
        ],
        axis=0,
    )
    shared_grads = jnp.pad(shared_grads, ((0, pack_rows - 3 * hidden_units), (0, 0)))

    def fourth_body(place, given, made, room):
        lf, el, ff, lb, br, fb, td, sg = given
        mixed, summed, dots, sg_all = made
        mixed_view, summed_view = part_view(mixed, rows, part), part_view(summed, rows, part)
        forward = Product(place, lf, el, ff, room[7:9], count, rows, part)
        backward = Product(place, lb, br, fb, room[9:11], count, rows, part)
        yield scatter(
            place,
            count,
            [forward, backward],
            room[:7],
            [lambda c: mixed_view(0, c), lambda c: summed_view(0, c)],
            (rows, part),
            True,
            room[11],
        )
        yield both(place, count, lambda s: td.at[s], lambda c, s: dots.at[c, s], lambda c: dots.at[c])
        yield later(exchange(place, count, lambda s: strips.at(sg, s), lambda s: sg_all.at[s]), 8)

    mixture, summed_back, dots_all, shared_back = transfer(
        "scatter_both",
        3,
        mesh,
        fourth_body,
        (
            left_forward,
            exp_low,
            fixed_forward,
            left_backward,
            back_rows,
            fixed_backward,
            token_dots,
            strips.cut(shared_grads),
        ),
        (
            like((rows, width)),
            like((rows, width)),
            like((cores, count, 8, rows), f32),
            like((count, pack_rows, deep)),
        ),
        scatter_scratch(
            count,
            cores,
            rows,
            part,
            [(left_forward.shape[1], True), (left_backward.shape[1], True)],
        )
        + [pltpu.SemaphoreType.REGULAR((count * (cores - 1),))],
        vmem=60 * 2**20,
    )
    output = (hidden + mixture.astype(f32)).astype(bf16)

    gate_total = jnp.sum(dots_all[:, :, 0, :], axis=0).T
    weighted_dots = jnp.sum(gates * gate_total, axis=1, keepdims=True)
    grad_logits = gates * (gate_total - weighted_dots)

    down_grad = mm("rf,rd->fd", exp_act, gated_grad)
    gate_grad = mm("rd,rf->df", received, gate_back)
    up_grad = mm("rd,rf->df", received, up_back)
    cotangent = out_grad.astype(f32)
    grad_two = summed_back.astype(f32) + jnp.einsum(
        "te,ed->td", grad_logits, router_full.astype(f32), precision=highest
    )
    scaled = grad_two * ffn_gain
    inner = jnp.mean(scaled * hidden, axis=-1, keepdims=True)
    grad_hidden = cotangent + rstd_two * scaled - hidden * (rstd_two * rstd_two * rstd_two) * inner
    ffn_gain_part = jnp.sum(grad_two * hidden * rstd_two, axis=0)
    grad_branch = grad_hidden.astype(bf16)
    grad_heads = mm("td,cd->tc", grad_branch, out_full).astype(bf16)
    out_proj_part = mm("tc,td->cd", heads_out, grad_branch).astype(bf16)

    def fifth_body(place, given, made, room):
        gl, logit_all = given[1], made[1]
        yield exchange(place, count, lambda s: gl, lambda s: logit_all.at[s])
        yield exchange(place, heads, lambda s: given[0].at[:, lanes(s, HEAD_DIM)], lambda s: made[0].at[s])

    grad_head, logits_all = transfer(
        "exchange_heads",
        4,
        mesh,
        fifth_body,
        (grad_heads, grad_logits.T),
        (like((heads, rows, HEAD_DIM)), like((count, experts, rows), f32)),
    )
    xn_columns = lax.dynamic_slice_in_dim(xn_all, e * deep, deep, axis=1).astype(f32).reshape(count, rows, deep)
    router_grad = jnp.einsum("gtd,get->de", xn_columns, logits_all, precision=highest)

    grad_value = mm("gqk,gqd->gkd", probs_low, grad_head)
    grad_probs = mm("gqd,gkd->gqk", grad_head, valued)
    weighted = jnp.sum(probs * grad_probs, axis=-1, keepdims=True)
    grad_scores = (probs * (grad_probs - weighted)).astype(bf16)
    grad_query = mm("gqk,gkd->gqd", grad_scores, keyed) * scale
    grad_key = mm("gqk,gqd->gkd", grad_scores, query) * scale
    grad_qkv = jnp.concatenate(
        [
            rotary_back(grad_query, cosine, sine).astype(bf16),
            rotary_back(grad_key, cosine, sine).astype(bf16),
            grad_value.astype(bf16),
        ],
        axis=2,
    ).reshape(chunk, 3 * HEAD_DIM)
    qkv_grad = mm("td,tc->dc", xn_chunk, grad_qkv)
    attn_gain_part = jnp.sum(qkv_grad * w_qkv.astype(f32), axis=1) / attn_gain
    qkv_grad = qkv_grad.astype(bf16)

    def spread(vector):
        return jnp.pad(vector.reshape(count, 1, deep), ((0, 0), (0, 7), (0, 0)))

    turns = count // heads

    def sixth_body(place, given, made, room):
        gq, wq, qg, op, ag, fg = given
        one, qg_all, op_sum, ag_all, fg_all = made
        one_view = part_view(one, rows, part)
        made_here = Product(place, gq, None, wq, room[7:9], heads, rows, part)
        yield scatter(place, heads, [made_here], room[:7], [lambda c: one_view(0, c)], (rows, part), True)
        yield scatter(
            place, count, [lambda s: strips.at(op, s)], room[9:], [lambda c: op_sum], (out_rows, deep), False
        )
        yield both(place, count, lambda s: ag.at[s], lambda c, s: ag_all.at[c, s], lambda c: ag_all.at[c])
        yield exchange(place, count, lambda s: fg.at[s], lambda s: fg_all.at[s])
        for which in range(3):

            def source(slot, which=which):
                at = pl.ds(pl.multiple_of(slot * deep, deep), deep)
                return qg.at[at, pl.ds(which * HEAD_DIM, HEAD_DIM)]

            def landing(slot, which=which):
                return qg_all.at[which, lax.div(slot, heads), :, lanes(lax.rem(slot, heads), HEAD_DIM)]

            yield later(exchange(place, count, source, landing), 6)

    grad_one, qkv_all, out_proj_sum, attn_gains, ffn_gains = transfer(
        "scatter_grads",
        5,
        mesh,
        sixth_body,
        (
            grad_qkv,
            w_qkv.T,
            qkv_grad,
            strips.cut(out_proj_part),
            spread(attn_gain_part),
            spread(ffn_gain_part),
        ),
        (
            like((rows, width)),
            like((3, turns, deep, heads * HEAD_DIM)),
            like((out_rows, deep)),
            like((cores, count, 8, deep), f32),
            like((count, 8, deep), f32),
        ),
        scatter_scratch(heads, cores, rows, part, [(3 * HEAD_DIM, False)])
        + scatter_scratch(count, 1, out_rows, deep),
        semaphores=600,
        vmem=56 * 2**20,
    )

    grad_one = grad_one.astype(f32)
    rstd_one = lax.rsqrt(jnp.mean(inputs * inputs, axis=-1, keepdims=True) + eps)
    scaled_one = grad_one * attn_gain
    inner_one = jnp.mean(scaled_one * inputs, axis=-1, keepdims=True)
    input_grad = (
        grad_hidden + rstd_one * scaled_one - inputs * (rstd_one * rstd_one * rstd_one) * inner_one
    ).astype(bf16)

    def of_heads(which):
        return jnp.sum(qkv_all[which].astype(f32), axis=0)

    def of_shared(which):
        return shared_back[:, which * hidden_units : (which + 1) * hidden_units].reshape(-1, deep).astype(f32)

    return (
        output,
        input_grad,
        jnp.sum(attn_gains[:, :, 0, :], axis=(0, 1)),
        of_heads(0),
        of_heads(1),
        of_heads(2),
        out_proj_sum.astype(f32),
        jnp.sum(ffn_gains[:, 0, :], axis=0),
        router_grad,
        gate_grad[None],
        up_grad[None],
        down_grad[None],
        of_shared(0).T,
        of_shared(1).T,
        of_shared(2),
    )


def solution(mesh):
    in_specs = (
        P("expert", None),
        P("expert", None),
        P("expert", None),
        P("expert"),
        P("expert", "tensor"),
        P("expert", "tensor"),
        P("expert", "tensor"),
        P("tensor", "expert"),
        P("expert"),
        P("expert", None),
        P("expert", None, "tensor"),
        P("expert", None, "tensor"),
        P("expert", "tensor", None),
        P("expert", "tensor"),
        P("expert", "tensor"),
        P("tensor", "expert"),
        P("expert", None),
    )
    out_specs = (
        P("expert", None),
        P("expert", None),
        P("expert"),
        P("expert", "tensor"),
        P("expert", "tensor"),
        P("expert", "tensor"),
        P("tensor", "expert"),
        P("expert"),
        P("expert", None),
        P("expert", None, "tensor"),
        P("expert", None, "tensor"),
        P("expert", "tensor", None),
        P("expert", "tensor"),
        P("expert", "tensor"),
        P("tensor", "expert"),
    )
    return jax.shard_map(
        functools.partial(local, mesh), mesh=mesh, in_specs=in_specs, out_specs=out_specs, check_vma=False
    )
```

```python
import functools

import jax
import jax.numpy as jnp
from jax import lax
from jax.experimental import pallas as pl
from jax.experimental.pallas import tpu as pltpu
from jax.sharding import PartitionSpec as P

HEAD_DIM = 128
TOP = 6
MESH = pl.DeviceIdType.MESH
ANY = pl.BlockSpec(memory_space=pl.ANY)

bf16 = jnp.bfloat16
f32 = jnp.float32
eps = 1e-06
highest = lax.Precision.HIGHEST
floor_score = -1e30


class Place:
    def __init__(self, sems, count, cores):
        self.sems, self.used = sems, 0
        self.count, self.cores = count, cores
        self.e = lax.axis_index("expert")
        self.t = lax.axis_index("tensor")
        self.quad = lax.rem(self.e, 4)
        self.far = lax.div(self.e, 4)

    def take(self, number):
        first = self.used
        self.used = first + number
        return first

    def ring(self, distance):
        return lax.rem(self.t + distance, self.cores)

    def copy(self, src, dst, out_sem, in_sem, e, t):
        return pltpu.make_async_remote_copy(
            src_ref=src,
            dst_ref=dst,
            send_sem=self.sems.at[out_sem],
            recv_sem=self.sems.at[in_sem],
            device_id={"expert": e, "tensor": t},
            device_id_type=MESH,
        )

    def send(self, src, dst, out_sem, in_sem, e, t):
        move = self.copy(src, dst, out_sem, in_sem, e, t)
        move.start()
        return move

    def arrived(self, landing, in_sem):
        self.copy(landing, landing, in_sem, in_sem, self.e, self.t).wait_recv()

    def keep(self, src, dst):
        move = pltpu.make_async_copy(src, dst, self.sems.at[self.take(1)])
        move.start()
        return move

    def meet(self):
        barrier = pltpu.get_barrier_semaphore()
        for step in range(1, self.count):
            pl.semaphore_signal(
                barrier,
                inc=1,
                device_id={"expert": lax.rem(self.e + step, self.count), "tensor": self.t},
                device_id_type=MESH,
            )
        for step in range(1, self.cores):
            pl.semaphore_signal(
                barrier,
                inc=1,
                device_id={"expert": self.e, "tensor": self.ring(step)},
                device_id_type=MESH,
            )
        pl.semaphore_wait(barrier, self.count + self.cores - 2)


class Block:
    def __init__(self, place, members):
        self.place, self.deep = place, members // 4
        self.rank = lax.rem(place.far, self.deep)
        self.start = place.far - self.rank

    def flips(self, order):
        high, low = lax.div(self.place.quad, 2), lax.rem(self.place.quad, 2)
        one = high + (low - high) * order
        two = low + (high - low) * order
        return (2 - order) * (1 - 2 * one), (1 + order) * (1 - 2 * two)

    def slot(self, k, i, j, order):
        one, two = self.flips(order)
        return lax.rem(self.rank + k, self.deep) * 4 + self.place.quad + i * one + j * two

    def own(self):
        return self.rank * 4 + self.place.quad

    def device(self, slot):
        return self.start * 4 + slot


def when(condition, action):
    if condition is None:
        action()
    else:
        pl.when(condition)(action)


def gather(place, members, mine, whole, view, halves, pieces=1):
    block = Block(place, members)
    deep, e, t, rank = block.deep, place.e, place.t, block.rank
    order = lax.rem(t, 2)
    cores = place.cores if halves else 1
    spots = 2 * deep - 1

    def lots(number):
        return place.take(number * pieces)

    zs, zr = lots(spots + 1), lots(spots)
    s2, r2 = lots(spots), lots(spots)
    s3, r3 = lots(2 * spots), lots(2 * spots)
    s4, r4 = lots(4 * spots * (cores - 1)), lots(4 * spots * (cores - 1))
    one, two = block.flips(order)
    own = block.own()
    sent, kept = [], place.keep(whole[0], whole[1](own))
    line = [(0, 0)] + [(d, way) for d in range(1, deep) for way in (1, -1)]

    def index(d, way):
        return 0 if d == 0 else 2 * d - (1 if way > 0 else 0)

    def valid(d, way):
        return None if d == 0 else (rank >= d if way > 0 else rank < deep - d)

    def slot_of(d, way, i, j, order=order):
        one, two = block.flips(order)
        return (rank - way * d) * 4 + place.quad + i * one + j * two

    ends = {1: (rank < deep - 1, 4), -1: (rank >= 1, -4)}

    def onward(d, way, p):
        condition, step = ends[way]
        if d > 0:
            condition = jnp.logical_and(condition, valid(d, way))
        v = index(d, way)
        out = 1 + v if d > 0 else (0 if way > 0 else 1)
        source = view(slot_of(d, way, 0, 0), t, p) if d > 0 else mine(p)
        landing = view(slot_of(d, way, 0, 0), t, p)
        move = place.copy(source, landing, zs + out * pieces + p, zr + index(d + 1, way) * pieces + p, e + step, t)
        sent.append((condition, move))
        when(condition, move.start)

    def pass_on(source, landing, condition, out, into, number, p, target):
        move = place.copy(source, landing, out + number * pieces + p, into + number * pieces + p, target, t)
        sent.append((condition, move))
        return move

    def share(d, way, i, j, p):
        moves = []
        ref = view(slot_of(d, way, i, j), t, p)
        for far in range(1, cores):
            at = (((far - 1) * spots + index(d, way)) * 4 + i * 2 + j) * pieces + p
            move = place.copy(ref, ref, s4 + at, r4 + at, e, place.ring(far))
            sent.append((valid(d, way), move))
            moves.append(move)
        return moves

    def start(moves):
        for move in moves:
            move.start()

    for p in range(pieces):
        if deep > 1:
            onward(0, 1, p)
            onward(0, -1, p)
        pass_on(mine(p), view(own, t, p), None, s2, r2, 0, p, e + one).start()
        pass_on(mine(p), view(own, t, p), None, s3, r3, 0, p, e + two).start()
        yield

    def from_line(d, way, p):
        ref = view(slot_of(d, way, 0, 0), t, p)
        v, condition = index(d, way), valid(d, way)
        when(condition, lambda: place.arrived(ref, zr + v * pieces + p))
        if d < deep - 1:
            onward(d, way, p)
        moves = [
            pass_on(ref, ref, condition, s2, r2, v, p, e + one),
            pass_on(ref, ref, condition, s3, r3, 2 * v, p, e + two),
        ] + share(d, way, 0, 0, p)
        when(condition, lambda: start(moves))

    def from_one(d, way, p):
        ref = view(slot_of(d, way, 1, 0), t, p)
        v, condition = index(d, way), valid(d, way)
        moves = [pass_on(ref, ref, condition, s3, r3, 2 * v + 1, p, e + two)] + share(d, way, 1, 0, p)

        def act():
            place.arrived(ref, r2 + v * pieces + p)
            start(moves)

        when(condition, act)

    def from_two(d, way, i, p):
        ref = view(slot_of(d, way, i, 1), t, p)
        v, condition = index(d, way), valid(d, way)
        moves = share(d, way, i, 1, p)

        def act():
            place.arrived(ref, r3 + (2 * v + i) * pieces + p)
            start(moves)

        when(condition, act)

    for d in range(1, deep + 1):
        for p in range(pieces):
            for way in (1, -1) if d > 1 else (1,):
                from_one(d - 1, way if d > 1 else 0, p)
            if d < deep:
                for way in (1, -1):
                    from_line(d, way, p)
            yield
    for d, way in line:
        for i in range(2):
            for p in range(pieces):
                from_two(d, way, i, p)
        yield
    for far in range(1, cores):
        source = place.ring(cores - far)
        for d, way in line:
            for i in range(2):
                for j in range(2):
                    if d + i + j > 0:
                        for p in range(pieces):
                            at = (((far - 1) * spots + index(d, way)) * 4 + i * 2 + j) * pieces + p
                            ref = view(slot_of(d, way, i, j, lax.rem(source, 2)), source, p)
                            when(valid(d, way), functools.partial(place.arrived, ref, r4 + at))
    for condition, move in sent:
        when(condition, move.wait_send)
    kept.wait()


class Attention:
    def __init__(self, place, rows, arrival, given, rooms, lhs, right, moves):
        self.place, self.rows, self.arrival = place, rows, arrival
        self.normed = given
        self.qkv, self.probs, self.cosine, self.sine, self.heads, self.held, self.sums = rooms
        self.lhs, self.right, self.setup = lhs, right, moves
        self.columns = None
        self.waits = {}

    def fetch(self, turn, slot):
        rows = pl.ds(pl.multiple_of(slot * self.rows, self.rows), self.rows)
        self.waits[turn] = (self.place.keep(self.normed.at[rows, :], self.held.at[turn % 2]), slot, rows)

    def ready(self, turn):
        for move in self.setup:
            move.wait()
        self.setup = []
        move, slot, rows = self.waits.pop(turn)
        self.arrival(slot)
        at = turn % 2

        def dot(left, right, sides=((1,), (0,))):
            return lax.dot_general(left, right, (sides, ((), ())), preferred_element_type=f32)

        query = self.qkv[rows, :HEAD_DIM]
        keyed = self.qkv[rows, HEAD_DIM : 2 * HEAD_DIM]
        valued = self.qkv[rows, 2 * HEAD_DIM :]
        cosine, sine = self.cosine[rows, :], self.sine[rows, :]
        probs, grad = self.probs[rows, :], self.heads[slot]
        scale = HEAD_DIM ** (-0.5)

        def turn_back(values):
            return (values * cosine - pltpu.roll(values, HEAD_DIM // 2, 1) * sine).astype(bf16)

        self.lhs[at, :, 2 * HEAD_DIM :] = dot(probs.astype(bf16), grad, ((0,), (0,))).astype(bf16)
        grad_probs = dot(grad, valued, ((1,), (1,)))
        weighted = jnp.sum(probs * grad_probs, axis=1, keepdims=True)
        grad_scores = (probs * (grad_probs - weighted)).astype(bf16)
        self.lhs[at, :, :HEAD_DIM] = turn_back(dot(grad_scores, keyed) * scale)
        self.lhs[at, :, HEAD_DIM : 2 * HEAD_DIM] = turn_back(dot(grad_scores, query, ((0,), (0,))) * scale)
        move.wait()
        wide = 512

        def body(tile, carry):
            into = pl.ds(pl.multiple_of(tile * wide, wide), wide)
            product = dot(self.lhs[at], self.held[at, :, into], ((0,), (0,)))
            self.sums[:, into] = product if turn == 0 else self.sums[:, into] + product
            return carry

        lax.fori_loop(0, self.sums.shape[1] // wide, body, 0)

    def make(self, turn, core, target):
        wide, columns = 512, target.shape[1]

        def body(tile, carry):
            source = pl.ds(pl.multiple_of(core * columns + tile * wide, wide), wide)
            into = pl.ds(pl.multiple_of(tile * wide, wide), wide)
            target[:, into] = jnp.dot(
                self.lhs[turn % 2], self.right[:, source], preferred_element_type=f32
            ).astype(bf16)
            return carry

        lax.fori_loop(0, columns // wide, body, 0)


def add_up(target, sources, rows, columns):
    step = max(16, min(rows, 16384 // columns // 16 * 16))

    def body(at, carry):
        piece = pl.ds(pl.multiple_of(at * step, step), step)
        total = sources[0][piece, :].astype(f32)
        for other in sources[1:]:
            total = total + other[piece, :].astype(f32)
        target[piece, :] = total.astype(target.dtype)
        return carry

    lax.fori_loop(0, rows // step, body, 0)


class Product:
    def __init__(self, place, left, varied, fixed, rooms, members, rows, columns):
        self.place, self.left, self.varied = place, left, varied
        self.lhs, self.rhs = rooms
        self.rows, self.columns = rows, columns
        self.lead = 0 if varied is None else varied.shape[0] // members
        self.waits, self.turn = {}, 0
        self.setup = []
        for buffer in range(self.rhs.shape[0]):
            self.setup.append(place.keep(fixed, self.rhs.at[buffer, pl.ds(self.lead, fixed.shape[0]), :]))

    def fetch(self, turn, slot):
        buffer = turn % 2
        rows = pl.ds(pl.multiple_of(slot * self.rows, self.rows), self.rows)
        moves = [self.place.keep(self.left.at[rows, :], self.lhs.at[buffer])]
        if self.lead:
            lead = pl.ds(pl.multiple_of(slot * self.lead, self.lead), self.lead)
            moves.append(self.place.keep(self.varied.at[lead, :], self.rhs.at[buffer, pl.ds(0, self.lead), :]))
        self.waits[turn] = moves

    def ready(self, turn):
        for move in self.setup:
            move.wait()
        self.setup = []
        for move in self.waits.pop(turn):
            move.wait()

    def make(self, turn, core, target):
        buffer = turn % 2
        right = self.rhs.at[buffer if self.lead else 0]
        wide = min(self.columns, 512)

        def body(at, carry):
            source = pl.ds(pl.multiple_of(core * self.columns + at * wide, wide), wide)
            into = pl.ds(pl.multiple_of(at * wide, wide), wide)
            target[:, into] = jnp.dot(
                self.lhs[buffer], right[:, source], preferred_element_type=f32
            ).astype(bf16)
            return carry

        lax.fori_loop(0, self.columns // wide, body, 0)


def scatter(place, members, sources, room, views, shape, halves, credit=None, done=None):
    block = Block(place, members)
    deep, e, t = block.deep, place.e, place.t
    rows, columns = shape
    order = 1 - lax.rem(t, 2)
    cores = place.cores if halves else 1
    count = len(sources)
    mine, outgoing, land0, land1s, land2s, land3s, finals = room
    s0, r0 = place.take(4 * deep * cores * count), place.take(4 * deep * cores * count)
    s1, r1 = place.take(2 * deep * count), place.take(2 * deep * count)
    s2, r2 = place.take(deep * count), place.take(deep * count)
    s3, r3 = place.take(deep * count), place.take(deep * count)
    s4, r4 = place.take(cores * count), place.take(cores * count)
    walk = [(f, k) for f in range(count) for k in list(range(1, deep)) + [0]]
    one, two = block.flips(order)
    sent, loads, last, kept = [], {}, {}, []
    quads = [(1, 1), (1, 0), (0, 1), (0, 0)]
    turns = [(f, k, i, j) for f, k in walk for i, j in quads]
    ring = outgoing.shape[0]
    leaving = []

    def slot_of(k, i, j):
        return block.slot(k, i, j, order)

    def land_index(d, k, i, j):
        return (d - 1) * deep * 4 + k * 4 + i * 2 + j

    def produce(number):
        f, k, i, j = turns[number]
        source = sources[f]
        if (k, i, j) in last:
            last.pop((k, i, j)).wait_send()
        if not isinstance(source, (Product, Attention)):
            loads[f, k, i, j] = place.keep(source(slot_of(k, i, j)), mine.at[slot_of(k, i, j)])
            return
        local_number = number - f * 4 * deep
        if local_number == 0:
            source.fetch(0, slot_of(k, i, j))
        source.ready(local_number)
        if local_number + 1 < 4 * deep:
            source.fetch(local_number + 1, slot_of(*turns[number + 1][1:]))
        if number >= ring:
            for move in leaving[number - ring]:
                move.wait_send()
        moves = []
        for d in range(1, cores):
            target = place.ring(d)
            buffer = outgoing.at[number % ring, d - 1]
            source.make(local_number, target, buffer)
            at = land_index(d, k, *((j, i) if d % 2 else (i, j)))
            if f > 0:
                pl.semaphore_wait(credit.at[at], 1)
            sem = f * 4 * deep * cores + at
            moves.append(place.send(buffer, land0.at[at], s0 + sem, r0 + sem, e, target))
        leaving.append(moves)
        source.make(local_number, t, mine.at[slot_of(k, i, j)])

    def terms_of(f, k, i, j):
        if (f, k, i, j) in loads:
            loads[f, k, i, j].wait()
        terms = [mine.at[slot_of(k, i, j)]]
        for d in range(1, cores):
            at = land_index(d, k, i, j)
            place.arrived(land0.at[at], r0 + f * 4 * deep * cores + at)
            terms.append(land0.at[at])
        if i == 0:
            at = (f * deep + k) * 2 + j
            place.arrived(land1s.at[at], r1 + at)
            terms.append(land1s.at[at])
            if j == 0:
                at = f * deep + k
                place.arrived(land2s.at[at], r2 + at)
                terms.append(land2s.at[at])
        return terms

    def give_back(f, k, i, j):
        if f + 1 < count:
            for d in range(1, cores):
                pl.semaphore_signal(
                    credit.at[land_index(d, k, i, j)],
                    inc=1,
                    device_id={"expert": e, "tensor": place.ring(cores - d)},
                    device_id_type=MESH,
                )

    def leave(f, k, i, j, landing, out, into, at, target):
        move = place.send(mine.at[slot_of(k, i, j)], landing.at[at], out + at, into + at, target, t)
        last[k, i, j] = move

    def first_flip(f, k, j):
        terms, ref = terms_of(f, k, 1, j), mine.at[slot_of(k, 1, j)]
        if len(terms) > 1:
            add_up(ref, terms, rows, columns)
        give_back(f, k, 1, j)
        leave(f, k, 1, j, land1s, s1, r1, (f * deep + k) * 2 + j, e + one)

    def second_flip(f, k):
        add_up(mine.at[slot_of(k, 0, 1)], terms_of(f, k, 0, 1), rows, columns)
        give_back(f, k, 0, 1)
        leave(f, k, 0, 1, land2s, s2, r2, f * deep + k, e + two)

    def line(f, k):
        terms, ref = terms_of(f, k, 0, 0), mine.at[slot_of(k, 0, 0)]
        if k > 0:
            add_up(ref, terms, rows, columns)
            give_back(f, k, 0, 0)
            peer = block.device(lax.rem(block.rank + k, deep) * 4 + place.quad)
            leave(f, k, 0, 0, land3s, s3, r3, f * deep + k, peer)
            return
        for far in range(1, deep):
            place.arrived(land3s.at[f * deep + far], r3 + f * deep + far)
            terms.append(land3s.at[f * deep + far])
        final = finals.at[f]
        add_up(final, terms, rows, columns)
        give_back(f, k, 0, 0)
        kept.append(place.keep(final, views[f](t)))
        for d in range(1, cores):
            at = f * cores + d
            sent.append(place.send(final, views[f](t), s4 + at, r4 + at, e, place.ring(d)))

    for step in range(len(walk) + 2):
        fresh = step < len(walk)
        if fresh:
            produce(4 * step)
            yield
            produce(4 * step + 1)
            yield
            first_flip(*walk[step], 1)
            yield
            produce(4 * step + 2)
            yield
        if 0 <= step - 1 < len(walk):
            second_flip(*walk[step - 1])
            yield
        if fresh:
            produce(4 * step + 3)
            if done is not None and step + 1 == len(walk):
                done()
            yield
            first_flip(*walk[step], 0)
            yield
        if 0 <= step - 2 < len(walk):
            line(*walk[step - 2])
            yield
    for f in range(count):
        for d in range(1, cores):
            place.arrived(views[f](place.ring(cores - d)), r4 + f * cores + d)
    for moves in leaving[-ring:]:
        for move in moves:
            move.wait_send()
    for move in list(last.values()) + sent:
        move.wait_send()
    for move in kept:
        move.wait()


def scatter_scratch(members, cores, rows, columns, products=(), ring=4):
    deep = members // 4
    count = max(1, len(products))
    short = rows if cores > 1 else 16
    rooms = [
        pltpu.VMEM((members, rows, columns), bf16),
        pltpu.VMEM((ring, max(1, cores - 1), short, columns), bf16),
        pltpu.VMEM((max(1, (cores - 1) * members), short, columns), bf16),
        pltpu.VMEM((2 * deep * count, rows, columns), bf16),
        pltpu.VMEM((deep * count, rows, columns), bf16),
        pltpu.VMEM((deep * count, rows, columns), bf16),
        pltpu.VMEM((count, rows, columns), bf16),
    ]
    for depth, varied in products:
        rooms.append(pltpu.VMEM((2, rows, depth), bf16))
        rooms.append(pltpu.VMEM((2 if varied else 1, depth, columns * cores), bf16))
    return rooms


def exchange(place, members, source, landing):
    e, t = place.e, place.t
    own = lax.rem(e, members)
    base = e - own
    sends, arrivals = place.take(members), place.take(members)
    sent = []
    for d in range(1, members):
        target = lax.rem(own + d, members)
        sent.append(place.send(source(target), landing(own), sends + d, arrivals + d, base + target, t))
    kept = place.keep(source(own), landing(own))
    yield
    for d in range(1, members):
        place.arrived(landing(lax.rem(own + members - d, members)), arrivals + d)
    for move in sent:
        move.wait_send()
    kept.wait()


def start_exchange(place, members, source, landing):
    e, t = place.e, place.t
    own = lax.rem(e, members)
    base = e - own
    sends, arrivals = place.take(members), place.take(members)
    sent = []
    for d in range(1, members):
        target = lax.rem(own + d, members)
        sent.append(place.send(source(target), landing(own), sends + target, arrivals + own, base + target, t))
    place.keep(source(own), landing(own)).wait()

    def arrived(slot):
        pl.when(slot != own)(lambda: place.arrived(landing(slot), arrivals + slot))

    def finish():
        for move in sent:
            move.wait_send()

    return arrived, finish


def both(place, members, source, landing, part):
    yield from exchange(place, members, source, lambda slot: landing(place.t, slot))
    sends, arrivals = place.take(place.cores), place.take(place.cores)
    sent = []
    for d in range(1, place.cores):
        mine = part(place.t)
        sent.append(place.send(mine, mine, sends + d, arrivals + d, place.e, place.ring(d)))
    yield
    for d in range(1, place.cores):
        place.arrived(part(place.ring(place.cores - d)), arrivals + d)
    for move in sent:
        move.wait_send()


def later(task, rounds):
    for _ in range(rounds):
        yield
    yield from task


def run(tasks):
    while tasks:
        for task in list(tasks):
            try:
                next(task)
            except StopIteration:
                tasks.remove(task)


def transfer(name, number, mesh, body, ins, outs, scratch=(), semaphores=400, vmem=None):
    count, cores = mesh.shape["expert"], mesh.shape["tensor"]
    semaphores = semaphores * max(1, count * cores // 32)

    def kernel(*refs):
        given = refs[: len(ins)]
        made = refs[len(ins) : len(ins) + len(outs)]
        room = refs[len(ins) + len(outs) : -1]
        place = Place(refs[-1], count, cores)
        place.meet()
        tasks = []
        for task in body(place, given, made, room):
            if isinstance(task, list):
                run(task)
            else:
                tasks.append(task)
        run(tasks)
        assert place.used <= semaphores, place.used

    size = sum(x.size * x.dtype.itemsize for x in list(ins) + list(outs))
    return pl.pallas_call(
        kernel,
        name=name,
        out_shape=[jax.ShapeDtypeStruct(shape, dtype) for shape, dtype in outs_of(outs)],
        in_specs=[ANY] * len(ins),
        out_specs=[ANY] * len(outs),
        scratch_shapes=list(scratch) + [pltpu.SemaphoreType.DMA((semaphores,))],
        cost_estimate=pl.CostEstimate(flops=0, bytes_accessed=size, transcendentals=0),
        compiler_params=pltpu.CompilerParams(
            collective_id=number, has_side_effects=True, vmem_limit_bytes=vmem
        ),
    )(*ins)


def outs_of(outs):
    return [(x.shape, x.dtype) for x in outs]


def like(shape, dtype=bf16):
    return jax.ShapeDtypeStruct(shape, dtype)


def part_view(ref, rows, columns, pieces=1):
    height = rows // pieces

    def view(slot, core, piece=0):
        at = 0 if isinstance(slot, int) else pl.multiple_of(slot * rows, rows)
        return ref.at[
            pl.ds(at + piece * height, height), pl.ds(pl.multiple_of(core * columns, columns), columns)
        ]

    return view


PIECES = 2


def lanes(at, columns):
    return pl.ds(pl.multiple_of(at * columns, columns), columns)


class Strips:
    def __init__(self, count, columns):
        self.count, self.columns = count, columns
        self.direct = columns % 128 == 0

    def shape(self, rows):
        return (rows, self.count * self.columns) if self.direct else (self.count, rows, self.columns)

    def at(self, ref, slot):
        return ref.at[:, lanes(slot, self.columns)] if self.direct else ref.at[slot]

    def cut(self, array):
        rows = array.shape[0]
        return array if self.direct else array.reshape(rows, self.count, self.columns).transpose(1, 0, 2)

    def join(self, array):
        rows = array.shape[0 if self.direct else 1]
        return array if self.direct else array.transpose(1, 0, 2).reshape(rows, self.count * self.columns)


def row_gather(place, members, source, landing, rows, part):
    def mine(piece):
        height = rows // PIECES
        return source.at[pl.ds(piece * height, height), lanes(place.t, part)]

    whole = (source, lambda slot: landing.at[pl.ds(pl.multiple_of(slot * rows, rows), rows), :])
    return gather(place, members, mine, whole, part_view(landing, rows, part, PIECES), True, PIECES)


def rotary(values, cosine, sine):
    half = values.shape[-1] // 2
    first = values[..., :half]
    second = values[..., half:]
    return jnp.concatenate([first * cosine - second * sine, second * cosine + first * sine], axis=-1)


def rotary_back(grads, cosine, sine):
    half = grads.shape[-1] // 2
    first = grads[..., :half]
    second = grads[..., half:]
    return jnp.concatenate([first * cosine + second * sine, second * cosine - first * sine], axis=-1)


def sequence_tables(lengths_rows, tok_rows):
    ends = jnp.cumsum(lengths_rows, axis=1)
    starts = ends - lengths_rows
    places = jnp.arange(tok_rows, dtype=jnp.int32)
    segment = jnp.sum((places[None, :, None] >= ends[:, None, :]).astype(jnp.int32), axis=2)
    member = segment[:, :, None] == jnp.arange(lengths_rows.shape[1], dtype=jnp.int32)[None, None, :]
    first = jnp.sum(jnp.where(member, starts[:, None, :], 0), axis=2)
    return segment, places[None, :] - first


def silu_parts(values):
    sigmoid_value = jax.nn.sigmoid(values)
    return values * sigmoid_value, sigmoid_value * (1.0 + values * (1.0 - sigmoid_value))


def mm(form, left, right):
    return jnp.einsum(form, left, right, preferred_element_type=f32)


def up_to(value, step):
    return -(-value // step) * step


def experts_kernel(
    groups,
    capacity,
    rows,
    xn_ref,
    grad_ref,
    position_ref,
    gate_ref,
    wg_ref,
    wu_ref,
    wd_ref,
    sh_in_ref,
    sh_down_ref,
    received_ref,
    gated_ref,
    low_ref,
    back_ref,
    act_ref,
    gate_back_ref,
    up_back_ref,
    dots_ref,
    left_forward_ref,
    left_backward_ref,
):
    def dot(left, right, sides=((1,), (0,))):
        return lax.dot_general(left, right, (sides, ((), ())), preferred_element_type=f32)

    places = lax.broadcasted_iota(jnp.int32, (capacity, rows), 0).astype(f32)
    gates, grads, onehots = [], [], []
    for g in range(groups):
        token = pl.ds(g * rows, rows)
        slot = pl.ds(g * capacity, capacity)
        chosen = (position_ref[g] == places).astype(f32)
        onehot = chosen.astype(bf16)
        onehots.append(chosen)
        received_ref[slot, :] = dot(onehot, xn_ref[token, :]).astype(bf16)
        gate = jnp.sum(chosen * gate_ref[g], axis=1, keepdims=True)
        row_grads = dot(onehot, grad_ref[token, :])
        gated_ref[slot, :] = (gate * row_grads).astype(bf16)
        low_ref[slot, :] = row_grads.astype(bf16)
        gates.append(gate)
        turned = chosen.T.astype(bf16)
        left_forward_ref[token, :capacity] = turned
        left_backward_ref[token, :capacity] = turned
    gate = jnp.concatenate(gates, axis=0)
    received = received_ref[...]
    exp_gate = dot(received, wg_ref[...], ((1,), (1,)))
    exp_up = dot(received, wu_ref[...], ((1,), (1,)))
    silu, slope = silu_parts(exp_gate)
    act = (silu * exp_up).astype(bf16)
    act_ref[...] = act
    out = dot(act, wd_ref[...])
    dots = jnp.sum(low_ref[...].astype(f32) * out, axis=1, keepdims=True)
    low_ref[...] = (gate * out).astype(bf16)
    for g in range(groups):
        column = dots[g * capacity : (g + 1) * capacity]
        token_dots = jnp.sum(onehots[g] * column, axis=0, keepdims=True)
        dots_ref[g] = jnp.broadcast_to(token_dots, (8, rows))
    act_grad = dot(gated_ref[...], wd_ref[...], ((1,), (1,)))
    gate_back = (act_grad * exp_up * slope).astype(bf16)
    up_back = (act_grad * silu).astype(bf16)
    gate_back_ref[...] = gate_back
    up_back_ref[...] = up_back
    back_ref[...] = (
        dot(gate_back, wg_ref[...]) + dot(up_back, wu_ref[...])
    ).astype(bf16)
    wide = sh_down_ref.shape[0]
    both = dot(xn_ref[...], sh_in_ref[...], ((1,), (1,)))
    sh_gate, sh_up = both[:, :wide], both[:, wide:]
    sh_silu, sh_slope = silu_parts(sh_gate)
    left_forward_ref[:, capacity:] = (sh_silu * sh_up).astype(bf16)
    sh_grad = dot(grad_ref[...], sh_down_ref[...], ((1,), (1,)))
    left_backward_ref[:, capacity : capacity + wide] = (sh_grad * sh_up * sh_slope).astype(bf16)
    left_backward_ref[:, capacity + wide :] = (sh_grad * sh_silu).astype(bf16)


def experts_pass(count, capacity, rows, xn_all, grad_all, position, gate, wg, wu, wd, sh_in, sh_down):
    groups = 2
    units, width = wg.shape
    wide = sh_down.shape[0]

    def along(*shape):
        return pl.BlockSpec(shape, lambda i: (i,) + (0,) * (len(shape) - 1))

    def whole(array):
        return pl.BlockSpec(array.shape, lambda i: (0,) * array.ndim, pipeline_mode=pl.Buffered(1))

    slots = groups * capacity
    tokens = groups * rows
    flops = 2 * count * capacity * width * units * 6
    return pl.pallas_call(
        functools.partial(experts_kernel, groups, capacity, rows),
        name="experts_pass",
        grid=(count // groups,),
        in_specs=[
            along(tokens, width),
            along(tokens, width),
            along(groups, 1, rows),
            along(groups, 1, rows),
            whole(wg),
            whole(wu),
            whole(wd),
            whole(sh_in),
            whole(sh_down),
        ],
        out_specs=[
            along(slots, width),
            along(slots, width),
            along(slots, width),
            along(slots, width),
            along(slots, units),
            along(slots, units),
            along(slots, units),
            along(groups, 8, rows),
            along(tokens, capacity + wide),
            along(tokens, capacity + 2 * wide),
        ],
        out_shape=[like((count * capacity, width))] * 4
        + [like((count * capacity, units))] * 3
        + [
            like((count, 8, rows), f32),
            like((count * rows, capacity + wide)),
            like((count * rows, capacity + 2 * wide)),
        ],
        cost_estimate=pl.CostEstimate(
            flops=flops, bytes_accessed=4 * count * (rows + 2 * capacity) * width, transcendentals=0
        ),
        compiler_params=pltpu.CompilerParams(vmem_limit_bytes=58 * 2**20),
    )(xn_all, grad_all, position, gate, wg, wu, wd, sh_in, sh_down)


def local(
    mesh,
    tokens,
    lengths,
    routes,
    gain_attn,
    w_query,
    w_key,
    w_value,
    w_out,
    gain_ffn,
    w_router,
    routed_gate_weight,
    routed_up_weight,
    w_down,
    w_shared_gate,
    w_shared_up,
    w_shared_down,
    out_grad,
):
    count, cores = mesh.shape["expert"], mesh.shape["tensor"]
    rows, width = tokens.shape
    part = width // cores
    deep = w_query.shape[0]
    experts = w_router.shape[1]
    heads = w_query.shape[1] // HEAD_DIM
    capacity = up_to(min(rows, rows * TOP * 4 // (3 * count)), 128)
    hidden_units = w_shared_gate.shape[1] // count
    scale = HEAD_DIM ** (-0.5)
    e = lax.axis_index("expert")
    t = lax.axis_index("tensor")
    chunk = heads * rows
    strips = Strips(count, deep)

    expert_ids = jnp.arange(experts, dtype=jnp.int32)
    choose = jnp.any(routes[:, :, None] == expert_ids[None, None, :], axis=1)
    mask_t = choose.T.astype(bf16)
    vectors = jnp.concatenate(
        [
            w_router.T,
            gain_attn[None],
            gain_ffn[None],
            jnp.pad(lengths.astype(bf16), ((0, 0), (0, deep - lengths.shape[1]))),
        ],
        axis=0,
    )
    head_rows = up_to(vectors.shape[0], 16)
    vectors = jnp.pad(vectors, ((0, head_rows - vectors.shape[0]), (0, 0)))
    pieces = rows // deep
    mask_rows = mask_t.reshape(experts * pieces, deep)
    small = jnp.concatenate([vectors, mask_rows], axis=0)
    small_rows = up_to(small.shape[0], 16)
    small = jnp.pad(small, ((0, small_rows - small.shape[0]), (0, 0)))

    def first_body(place, given, made, room):
        tok, sm, *weights = given
        tok_all, sm_all, w_all = made
        yield exchange(place, count, lambda s: sm, lambda s: sm_all.at[s])
        yield row_gather(place, heads, tok, tok_all, rows, part)
        for which, weight in enumerate(weights):

            def landing(slot, which=which):
                at = pl.ds(pl.multiple_of(slot * deep, deep), deep)
                return w_all.at[at, pl.ds(which * HEAD_DIM, HEAD_DIM)]

            yield exchange(
                place, count, lambda s, w=weight: w.at[:, lanes(lax.rem(s, heads), HEAD_DIM)], landing
            )

    tok_chunk, small_all, w_qkv = transfer(
        "gather_tokens",
        0,
        mesh,
        first_body,
        (tokens, small, w_query, w_key, w_value),
        (like((chunk, width)), like((count, small_rows, deep)), like((width, 3 * HEAD_DIM))),
    )

    router_full = small_all[:, :experts].transpose(1, 0, 2).reshape(experts, width)
    attn_gain = small_all[:, experts].reshape(width).astype(f32)
    ffn_gain = small_all[:, experts + 1].reshape(width).astype(f32)
    lengths_all = small_all[:, experts + 2, : lengths.shape[1]].astype(f32).astype(jnp.int32)
    masks = small_all[:, head_rows : head_rows + experts * pieces].reshape(count, experts, rows)

    member = e % heads
    lengths_chunk = lax.dynamic_slice_in_dim(lengths_all, e - member, heads, axis=0)
    segment, positions = sequence_tables(lengths_chunk, rows)
    half = HEAD_DIM // 2
    inverse = 10000.0 ** (-2.0 * jnp.arange(half, dtype=f32) / HEAD_DIM)
    angles = positions.astype(f32)[:, :, None] * inverse[None, None, :]
    cosine, sine = jnp.cos(angles), jnp.sin(angles)

    tok32 = tok_chunk.astype(f32)
    rstd_chunk = lax.rsqrt(jnp.mean(tok32 * tok32, axis=-1, keepdims=True) + eps)
    xn_chunk = (tok32 * rstd_chunk * attn_gain).astype(bf16)
    qkv = jnp.dot(xn_chunk, w_qkv, preferred_element_type=f32).reshape(heads, rows, 3 * HEAD_DIM)
    query = rotary(qkv[..., :HEAD_DIM], cosine, sine).astype(bf16)
    keyed = rotary(qkv[..., HEAD_DIM : 2 * HEAD_DIM], cosine, sine).astype(bf16)
    valued = qkv[..., 2 * HEAD_DIM :].astype(bf16)
    places = jnp.arange(rows, dtype=jnp.int32)
    allowed = (segment[:, :, None] == segment[:, None, :]) & (places[None, :] <= places[:, None])[None]
    scores = jnp.where(allowed, mm("gqd,gkd->gqk", query, keyed) * scale, floor_score)
    top_score = jnp.max(scores, axis=-1, keepdims=True)
    raised = jnp.exp(scores - top_score)
    probs = raised / jnp.sum(raised, axis=-1, keepdims=True)
    probs_low = probs.astype(bf16)
    head_out = mm("gqk,gkd->gqd", probs_low, valued).astype(bf16)

    shared_pack = jnp.concatenate(
        [
            w_shared_gate.T.reshape(count, hidden_units, deep),
            w_shared_up.T.reshape(count, hidden_units, deep),
            w_shared_down.reshape(count, hidden_units, deep),
        ],
        axis=1,
    )
    pack_rows = up_to(3 * hidden_units, 16)
    shared_pack = jnp.pad(shared_pack, ((0, 0), (0, pack_rows - 3 * hidden_units), (0, 0)))
    out_rows = w_out.shape[0]

    def second_body(place, given, made, room):
        ho, og, wo, sp = given
        ho_all, og_all, wo_all, sp_all = made
        yield exchange(place, heads, lambda s: ho.at[s], lambda s: ho_all.at[:, lanes(s, HEAD_DIM)])
        yield row_gather(place, count, og, og_all, rows, part)

        def wo_view(slot, core=0, piece=0):
            return strips.at(wo_all, slot)

        yield gather(place, count, lambda p: wo, (wo, wo_view), wo_view, False)
        yield exchange(place, count, lambda s: sp.at[s], lambda s: strips.at(sp_all, s))

    heads_out, grad_all, out_full, shared_all = transfer(
        "gather_inputs",
        1,
        mesh,
        second_body,
        (head_out, out_grad, w_out, shared_pack),
        (
            like((rows, heads * HEAD_DIM)),
            like((count * rows, width)),
            like(strips.shape(out_rows)),
            like(strips.shape(pack_rows)),
        ),
        semaphores=640,
    )
    out_full, shared_all = strips.join(out_full), strips.join(shared_all)
    attention_part = jnp.dot(heads_out, out_full, preferred_element_type=f32).astype(bf16)

    def third_body(place, given, made, room):
        ap, tok, gn, rt, mk = given
        hid_out, xn_all, gt_all = made
        parts, tok_v, gn_v, rt_v, mk_v, hid, xn, gt = room
        t = place.t
        sends, arrivals = place.take(cores), place.take(cores)
        sent = [place.send(ap, parts.at[t], sends + d, arrivals + d, place.e, place.ring(d)) for d in range(1, cores)]
        kept = [place.keep(ap, parts.at[t])]
        kept += [place.keep(a, b) for a, b in ((tok, tok_v), (gn, gn_v), (rt, rt_v), (mk, mk_v))]
        for move in kept:
            move.wait()
        for d in range(1, cores):
            place.arrived(parts.at[place.ring(cores - d)], arrivals + d)

        def body(at, carry):
            piece = pl.ds(pl.multiple_of(at * 16, 16), 16)
            total = parts[0, piece, :].astype(f32)
            for core in range(1, cores):
                total = total + parts[core, piece, :].astype(f32)
            values = tok_v[piece, :].astype(f32) + total
            hid[piece, :] = values
            rstd = lax.rsqrt(jnp.mean(values * values, axis=1, keepdims=True) + eps)
            xn[piece, :] = (values * rstd * gn_v[...]).astype(bf16)
            return carry

        lax.fori_loop(0, rows // 16, body, 0)
        saved = place.keep(hid, hid_out)
        yield row_gather(place, count, xn, xn_all, rows, part)
        logits = lax.dot_general(rt_v[...], xn[...], (((1,), (1,)), ((), ())), preferred_element_type=f32)
        picked = mk_v[...] > 0.5
        top_logit = jnp.max(jnp.where(picked, logits, floor_score), axis=0, keepdims=True)
        lifted = jnp.where(picked, jnp.exp(jnp.where(picked, logits - top_logit, 0.0)), 0.0)
        gt[...] = lifted / jnp.sum(lifted, axis=0, keepdims=True)
        yield exchange(place, count, lambda s: gt, lambda s: gt_all.at[s])
        for move in sent:
            move.wait_send()
        saved.wait()

    hidden, xn_all, gates_all = transfer(
        "gather_rows",
        2,
        mesh,
        third_body,
        (attention_part, tokens, ffn_gain[None], router_full, mask_t.astype(f32)),
        (like((rows, width), f32), like((count * rows, width)), like((count, experts, rows), f32)),
        [
            pltpu.VMEM((cores, rows, width), bf16),
            pltpu.VMEM((rows, width), bf16),
            pltpu.VMEM((1, width), f32),
            pltpu.VMEM((experts, width), bf16),
            pltpu.VMEM((experts, rows), f32),
            pltpu.VMEM((rows, width), f32),
            pltpu.VMEM((rows, width), bf16),
            pltpu.VMEM((experts, rows), f32),
        ],
        semaphores=400,
        vmem=40 * 2**20,
    )
    inputs = tokens.astype(f32)
    rstd_two = lax.rsqrt(jnp.mean(hidden * hidden, axis=-1, keepdims=True) + eps)
    gates = lax.dynamic_index_in_dim(gates_all, e, axis=0, keepdims=False).T

    own_mask = lax.dynamic_index_in_dim(masks, e, axis=1, keepdims=False).astype(f32)
    own_gate = lax.dynamic_index_in_dim(gates_all, e, axis=1, keepdims=False)
    at_row = jnp.arange(rows, dtype=jnp.int32)
    earlier = (at_row[:, None] < at_row[None, :]).astype(bf16)
    position = jnp.where(own_mask > 0.5, jnp.dot(own_mask.astype(bf16), earlier, preferred_element_type=f32), -1.0)
    gate_weight, up_weight, down_weight = routed_gate_weight[0].T, routed_up_weight[0].T, w_down[0]
    sh_wide = up_to(hidden_units, 128)

    def widened(which):
        piece = shared_all[which * hidden_units : (which + 1) * hidden_units]
        return jnp.pad(piece, ((0, sh_wide - hidden_units), (0, 0)))

    fixed_backward = jnp.concatenate([widened(0), widened(1)], axis=0)
    fixed_forward = widened(2)
    (
        received,
        gated_grad,
        exp_low,
        back_rows,
        exp_act,
        gate_back,
        up_back,
        token_dots,
        left_forward,
        left_backward,
    ) = experts_pass(
        count,
        capacity,
        rows,
        xn_all,
        grad_all,
        position[:, None],
        own_gate[:, None],
        gate_weight,
        up_weight,
        down_weight,
        fixed_backward,
        fixed_forward,
    )

    sh_grads = mm("tf,td->fd", left_backward[:, capacity:], xn_all).astype(bf16)
    shared_grads = jnp.concatenate(
        [
            sh_grads[:hidden_units],
            sh_grads[sh_wide : sh_wide + hidden_units],
            mm("tf,td->fd", left_forward[:, capacity:], grad_all).astype(bf16)[:hidden_units],
        ],
        axis=0,
    )
    shared_grads = jnp.pad(shared_grads, ((0, pack_rows - 3 * hidden_units), (0, 0)))

    def fourth_body(place, given, made, room):
        lf, el, ff, lb, br, fb, td, sg = given
        mixed, summed, dots, sg_all = made
        mixed_view, summed_view = part_view(mixed, rows, part), part_view(summed, rows, part)
        forward = Product(place, lf, el, ff, room[7:9], count, rows, part)
        backward = Product(place, lb, br, fb, room[9:11], count, rows, part)
        yield scatter(
            place,
            count,
            [forward, backward],
            room[:7],
            [lambda c: mixed_view(0, c), lambda c: summed_view(0, c)],
            (rows, part),
            True,
            room[11],
        )
        yield both(place, count, lambda s: td.at[s], lambda c, s: dots.at[c, s], lambda c: dots.at[c])
        yield later(exchange(place, count, lambda s: strips.at(sg, s), lambda s: sg_all.at[s]), 8)

    mixture, summed_back, dots_all, shared_back = transfer(
        "scatter_both",
        3,
        mesh,
        fourth_body,
        (
            left_forward,
            exp_low,
            fixed_forward,
            left_backward,
            back_rows,
            fixed_backward,
            token_dots,
            strips.cut(shared_grads),
        ),
        (
            like((rows, width)),
            like((rows, width)),
            like((cores, count, 8, rows), f32),
            like((count, pack_rows, deep)),
        ),
        scatter_scratch(
            count,
            cores,
            rows,
            part,
            [(left_forward.shape[1], True), (left_backward.shape[1], True)],
        )
        + [pltpu.SemaphoreType.REGULAR((count * (cores - 1),))],
        vmem=60 * 2**20,
    )
    output = (hidden + mixture.astype(f32)).astype(bf16)

    gate_total = jnp.sum(dots_all[:, :, 0, :], axis=0).T
    weighted_dots = jnp.sum(gates * gate_total, axis=1, keepdims=True)
    grad_logits = gates * (gate_total - weighted_dots)

    down_grad = mm("rf,rd->fd", exp_act, gated_grad)
    gate_grad = mm("rd,rf->df", received, gate_back)
    up_grad = mm("rd,rf->df", received, up_back)
    cotangent = out_grad.astype(f32)
    grad_two = summed_back.astype(f32) + jnp.einsum(
        "te,ed->td", grad_logits, router_full.astype(f32), precision=highest
    )
    scaled = grad_two * ffn_gain
    inner = jnp.mean(scaled * hidden, axis=-1, keepdims=True)
    grad_hidden = cotangent + rstd_two * scaled - hidden * (rstd_two * rstd_two * rstd_two) * inner
    ffn_gain_part = jnp.sum(grad_two * hidden * rstd_two, axis=0)
    grad_branch = grad_hidden.astype(bf16)
    grad_heads = mm("td,cd->tc", grad_branch, out_full).astype(bf16)
    out_proj_part = mm("tc,td->cd", heads_out, grad_branch).astype(bf16)

    turns = count // heads

    def spread(vector):
        return jnp.pad(vector.reshape(count, 1, deep), ((0, 0), (0, 7), (0, 0)))

    if strips.direct:

        def back_body(place, given, made, room):
            gh, gl, op, fg, qkv_s, pr, ct, st, xn, wt = given
            one, qg_all, op_sum, ag_all, fg_all, logit_all = made
            qkv_v, pr_v, ct_v, st_v, gh_v, held, sums, lhs, right, gains, blocks = room[14:]
            moves = [place.keep(x, y) for x, y in ((qkv_s, qkv_v), (pr, pr_v), (ct, ct_v), (st, st_v), (wt, right))]
            arrived, finish = start_exchange(
                place, heads, lambda s: gh.at[:, lanes(s, HEAD_DIM)], lambda s: gh_v.at[s]
            )
            one_view = part_view(one, rows, part)
            source = Attention(
                place, rows, arrived, xn, (qkv_v, pr_v, ct_v, st_v, gh_v, held, sums), lhs, right, moves
            )

            def main():
                yield from scatter(
                    place, heads, [source], room[:7], [lambda c: one_view(0, c)], (rows, part), True, None, tail
                )

            def tail():
                gains[...] = jnp.broadcast_to(
                    jnp.sum(sums[...] * right[...].astype(f32), axis=0, keepdims=True), gains.shape
                )
                tasks.append(
                    both(
                        place,
                        count,
                        lambda s: gains.at[:, lanes(s, deep)],
                        lambda c, s: ag_all.at[c, s],
                        lambda c: ag_all.at[c],
                    )
                )

                def body(at, carry):
                    blocks[at] = sums[:, pl.ds(pl.multiple_of(at * deep, deep), deep)].T.astype(bf16)
                    return carry

                lax.fori_loop(0, count, body, 0)
                for which in range(3):

                    def landing(slot, which=which):
                        return qg_all.at[which, lax.div(slot, heads), :, lanes(lax.rem(slot, heads), HEAD_DIM)]

                    def block(slot, which=which):
                        return blocks.at[slot, :, pl.ds(which * HEAD_DIM, HEAD_DIM)]

                    tasks.append(exchange(place, count, block, landing))

            tasks = [
                main(),
                scatter(
                    place, count, [lambda s: strips.at(op, s)], room[7:14], [lambda c: op_sum], (out_rows, deep), False
                ),
                exchange(place, count, lambda s: gl, lambda s: logit_all.at[s]),
                exchange(place, count, lambda s: fg.at[s], lambda s: fg_all.at[s]),
            ]
            yield tasks
            finish()

        qkv_saved = jnp.concatenate([query, keyed, valued], axis=2).reshape(chunk, 3 * HEAD_DIM)
        cosine_wide = jnp.concatenate([cosine, cosine], axis=2).reshape(chunk, HEAD_DIM)
        sine_wide = jnp.concatenate([-sine, sine], axis=2).reshape(chunk, HEAD_DIM)
        grad_one, qkv_all, out_proj_sum, attn_gains, ffn_gains, logits_all = transfer(
            "attention_back",
            4,
            mesh,
            back_body,
            (
                grad_heads,
                grad_logits.T,
                out_proj_part,
                spread(ffn_gain_part),
                qkv_saved,
                probs.reshape(chunk, rows),
                cosine_wide,
                sine_wide,
                xn_chunk,
                w_qkv.T,
            ),
            (
                like((rows, width)),
                like((3, turns, deep, heads * HEAD_DIM)),
                like((out_rows, deep)),
                like((cores, count, 8, deep), f32),
                like((count, 8, deep), f32),
                like((count, experts, rows), f32),
            ),
            scatter_scratch(heads, cores, rows, part)
            + scatter_scratch(count, 1, out_rows, deep)
            + [
                pltpu.VMEM((chunk, 3 * HEAD_DIM), bf16),
                pltpu.VMEM((chunk, rows), f32),
                pltpu.VMEM((chunk, HEAD_DIM), f32),
                pltpu.VMEM((chunk, HEAD_DIM), f32),
                pltpu.VMEM((heads, rows, HEAD_DIM), bf16),
                pltpu.VMEM((2, rows, width), bf16),
                pltpu.VMEM((3 * HEAD_DIM, width), f32),
                pltpu.VMEM((2, rows, 3 * HEAD_DIM), bf16),
                pltpu.VMEM((3 * HEAD_DIM, width), bf16),
                pltpu.VMEM((8, width), f32),
                pltpu.VMEM((count, deep, 3 * HEAD_DIM), bf16),
            ],
            semaphores=640,
            vmem=56 * 2**20,
        )
    else:
        def fifth_body(place, given, made, room):
            gl, logit_all = given[1], made[1]
            yield exchange(place, count, lambda s: gl, lambda s: logit_all.at[s])
            yield exchange(place, heads, lambda s: given[0].at[:, lanes(s, HEAD_DIM)], lambda s: made[0].at[s])

        grad_head, logits_all = transfer(
            "exchange_heads",
            4,
            mesh,
            fifth_body,
            (grad_heads, grad_logits.T),
            (like((heads, rows, HEAD_DIM)), like((count, experts, rows), f32)),
        )
        grad_value = mm("gqk,gqd->gkd", probs_low, grad_head)
        grad_probs = mm("gqd,gkd->gqk", grad_head, valued)
        weighted = jnp.sum(probs * grad_probs, axis=-1, keepdims=True)
        grad_scores = (probs * (grad_probs - weighted)).astype(bf16)
        grad_query = mm("gqk,gkd->gqd", grad_scores, keyed) * scale
        grad_key = mm("gqk,gqd->gkd", grad_scores, query) * scale
        grad_qkv = jnp.concatenate(
            [
                rotary_back(grad_query, cosine, sine).astype(bf16),
                rotary_back(grad_key, cosine, sine).astype(bf16),
                grad_value.astype(bf16),
            ],
            axis=2,
        ).reshape(chunk, 3 * HEAD_DIM)
        qkv_grad = mm("td,tc->dc", xn_chunk, grad_qkv)
        attn_gain_part = jnp.sum(qkv_grad * w_qkv.astype(f32), axis=1)
        qkv_grad = qkv_grad.astype(bf16)

        def sixth_body(place, given, made, room):
            gq, wq, qg, op, ag, fg = given
            one, qg_all, op_sum, ag_all, fg_all = made
            one_view = part_view(one, rows, part)
            made_here = Product(place, gq, None, wq, room[7:9], heads, rows, part)
            yield scatter(place, heads, [made_here], room[:7], [lambda c: one_view(0, c)], (rows, part), True)
            yield scatter(
                place, count, [lambda s: strips.at(op, s)], room[9:], [lambda c: op_sum], (out_rows, deep), False
            )
            yield both(place, count, lambda s: ag.at[s], lambda c, s: ag_all.at[c, s], lambda c: ag_all.at[c])
            yield exchange(place, count, lambda s: fg.at[s], lambda s: fg_all.at[s])
            for which in range(3):

                def source(slot, which=which):
                    at = pl.ds(pl.multiple_of(slot * deep, deep), deep)
                    return qg.at[at, pl.ds(which * HEAD_DIM, HEAD_DIM)]

                def landing(slot, which=which):
                    return qg_all.at[which, lax.div(slot, heads), :, lanes(lax.rem(slot, heads), HEAD_DIM)]

                yield later(exchange(place, count, source, landing), 6)

        grad_one, qkv_all, out_proj_sum, attn_gains, ffn_gains = transfer(
            "scatter_grads",
            5,
            mesh,
            sixth_body,
            (
                grad_qkv,
                w_qkv.T,
                qkv_grad,
                strips.cut(out_proj_part),
                spread(attn_gain_part),
                spread(ffn_gain_part),
            ),
            (
                like((rows, width)),
                like((3, turns, deep, heads * HEAD_DIM)),
                like((out_rows, deep)),
                like((cores, count, 8, deep), f32),
                like((count, 8, deep), f32),
            ),
            scatter_scratch(heads, cores, rows, part, [(3 * HEAD_DIM, False)])
            + scatter_scratch(count, 1, out_rows, deep),
            semaphores=600,
            vmem=56 * 2**20,
        )

    xn_columns = lax.dynamic_slice_in_dim(xn_all, e * deep, deep, axis=1).astype(f32).reshape(count, rows, deep)
    router_grad = jnp.einsum("gtd,get->de", xn_columns, logits_all, precision=highest)
    grad_one = grad_one.astype(f32)
    rstd_one = lax.rsqrt(jnp.mean(inputs * inputs, axis=-1, keepdims=True) + eps)
    scaled_one = grad_one * attn_gain
    inner_one = jnp.mean(scaled_one * inputs, axis=-1, keepdims=True)
    input_grad = (
        grad_hidden + rstd_one * scaled_one - inputs * (rstd_one * rstd_one * rstd_one) * inner_one
    ).astype(bf16)

    def of_heads(which):
        return jnp.sum(qkv_all[which].astype(f32), axis=0)

    def of_shared(which):
        return shared_back[:, which * hidden_units : (which + 1) * hidden_units].reshape(-1, deep).astype(f32)

    return (
        output,
        input_grad,
        jnp.sum(attn_gains[:, :, 0, :], axis=(0, 1)) / gain_attn.astype(f32),
        of_heads(0),
        of_heads(1),
        of_heads(2),
        out_proj_sum.astype(f32),
        jnp.sum(ffn_gains[:, 0, :], axis=0),
        router_grad,
        gate_grad[None],
        up_grad[None],
        down_grad[None],
        of_shared(0).T,
        of_shared(1).T,
        of_shared(2),
    )


def solution(mesh):
    in_specs = (
        P("expert", None),
        P("expert", None),
        P("expert", None),
        P("expert"),
        P("expert", "tensor"),
        P("expert", "tensor"),
        P("expert", "tensor"),
        P("tensor", "expert"),
        P("expert"),
        P("expert", None),
        P("expert", None, "tensor"),
        P("expert", None, "tensor"),
        P("expert", "tensor", None),
        P("expert", "tensor"),
        P("expert", "tensor"),
        P("tensor", "expert"),
        P("expert", None),
    )
    out_specs = (
        P("expert", None),
        P("expert", None),
        P("expert"),
        P("expert", "tensor"),
        P("expert", "tensor"),
        P("expert", "tensor"),
        P("tensor", "expert"),
        P("expert"),
        P("expert", None),
        P("expert", None, "tensor"),
        P("expert", None, "tensor"),
        P("expert", "tensor", None),
        P("expert", "tensor"),
        P("expert", "tensor"),
        P("tensor", "expert"),
    )
    return jax.shard_map(
        functools.partial(local, mesh), mesh=mesh, in_specs=in_specs, out_specs=out_specs, check_vma=False
    )
```

```python
import functools

import jax
import jax.numpy as jnp
from jax import lax
from jax.experimental import pallas as pl
from jax.experimental.pallas import tpu as pltpu
from jax.sharding import PartitionSpec as P

HEAD_DIM = 128
TOP = 6
MESH = pl.DeviceIdType.MESH
ANY = pl.BlockSpec(memory_space=pl.ANY)

bf16 = jnp.bfloat16
f32 = jnp.float32
eps = 1e-06
highest = lax.Precision.HIGHEST
floor_score = -1e30


class Place:
    def __init__(self, sems, count, cores):
        self.sems, self.used = sems, 0
        self.count, self.cores = count, cores
        self.e = lax.axis_index("expert")
        self.t = lax.axis_index("tensor")
        self.quad = lax.rem(self.e, 4)
        self.far = lax.div(self.e, 4)

    def take(self, number):
        first = self.used
        self.used = first + number
        return first

    def ring(self, distance):
        return lax.rem(self.t + distance, self.cores)

    def copy(self, src, dst, out_sem, in_sem, e, t):
        return pltpu.make_async_remote_copy(
            src_ref=src,
            dst_ref=dst,
            send_sem=self.sems.at[out_sem],
            recv_sem=self.sems.at[in_sem],
            device_id={"expert": e, "tensor": t},
            device_id_type=MESH,
        )

    def send(self, src, dst, out_sem, in_sem, e, t):
        move = self.copy(src, dst, out_sem, in_sem, e, t)
        move.start()
        return move

    def arrived(self, landing, in_sem):
        self.copy(landing, landing, in_sem, in_sem, self.e, self.t).wait_recv()

    def keep(self, src, dst):
        move = pltpu.make_async_copy(src, dst, self.sems.at[self.take(1)])
        move.start()
        return move

    def meet(self):
        barrier = pltpu.get_barrier_semaphore()
        for step in range(1, self.count):
            pl.semaphore_signal(
                barrier,
                inc=1,
                device_id={"expert": lax.rem(self.e + step, self.count), "tensor": self.t},
                device_id_type=MESH,
            )
        for step in range(1, self.cores):
            pl.semaphore_signal(
                barrier,
                inc=1,
                device_id={"expert": self.e, "tensor": self.ring(step)},
                device_id_type=MESH,
            )
        pl.semaphore_wait(barrier, self.count + self.cores - 2)


class Block:
    def __init__(self, place, members):
        self.place, self.deep = place, members // 4
        self.rank = lax.rem(place.far, self.deep)
        self.start = place.far - self.rank

    def flips(self, order):
        high, low = lax.div(self.place.quad, 2), lax.rem(self.place.quad, 2)
        one = high + (low - high) * order
        two = low + (high - low) * order
        return (2 - order) * (1 - 2 * one), (1 + order) * (1 - 2 * two)

    def slot(self, k, i, j, order):
        one, two = self.flips(order)
        return lax.rem(self.rank + k, self.deep) * 4 + self.place.quad + i * one + j * two

    def own(self):
        return self.rank * 4 + self.place.quad

    def device(self, slot):
        return self.start * 4 + slot


class Gather:
    def __init__(self, place, members, mine, whole, view, halves, pieces=1):
        self.place, self.block = place, Block(place, members)
        self.mine, self.whole, self.view, self.pieces = mine, whole, view, pieces
        self.deep, self.order = self.block.deep, lax.rem(place.t, 2)
        self.cores = place.cores if halves else 1
        self.zs, self.zr = self.lots(2), self.lots(1)
        self.s2, self.r2 = self.lots(1), self.lots(1)
        self.s3, self.r3 = self.lots(2), self.lots(2)
        self.s4, self.r4 = self.lots(4 * (self.cores - 1)), self.lots(4 * (self.cores - 1))
        self.sent = []

    def lots(self, number):
        return self.place.take(number * self.deep * self.pieces)

    def near(self, n):
        rank, deep = self.block.rank, self.deep
        if n == 0:
            return rank
        low = jnp.minimum(rank, deep - 1 - rank)
        paired = rank - (n + 1) // 2 if n % 2 else rank + n // 2
        single = jnp.where(rank < deep - 1 - rank, rank + (n - low), rank - (n - low))
        return jnp.where(n <= 2 * low, paired, single)

    def slot(self, n, i, j, order=None):
        one, two = self.block.flips(self.order if order is None else order)
        return self.near(n) * 4 + self.place.quad + i * one + j * two

    def index(self, n, kind, kinds, p):
        return (self.near(n) * kinds + kind) * self.pieces + p

    def pass_on(self, source, landing, out, into, at, e, t, condition=None):
        move = self.place.copy(source, landing, out + at[0], into + at[1], e, t)
        self.sent.append((condition, move))
        when(condition, move.start)

    def along(self, n, p, source, landing):
        rank, e = self.block.rank, self.place.e
        near = self.near(n)
        for way in (1, -1):
            fits = rank < self.deep - 1 if way > 0 else rank >= 1
            if n > 0:
                fits = jnp.logical_and(fits, near < rank if way > 0 else near > rank)
            out = self.index(n, 0 if way > 0 else 1, 2, p)
            into = self.index(n, 0, 1, p)
            self.pass_on(source, landing, self.zs, self.zr, (out, into), e + 4 * way, self.place.t, fits)

    def across(self, n, i, p, source, landing):
        one, two = self.block.flips(self.order)
        e, t = self.place.e, self.place.t
        if i == 0:
            at = self.index(n, 0, 1, p)
            self.pass_on(source, landing, self.s2, self.r2, (at, at), e + one, t)
        at = self.index(n, i, 2, p)
        self.pass_on(source, landing, self.s3, self.r3, (at, at), e + two, t)

    def share(self, n, i, j, p):
        ref = self.view(self.slot(n, i, j), self.place.t, p)
        for far in range(1, self.cores):
            kind = (far - 1) * 4 + i * 2 + j
            at = self.index(n, kind, 4 * (self.cores - 1), p)
            self.pass_on(ref, ref, self.s4, self.r4, (at, at), self.place.e, self.place.ring(far))

    def start(self, p):
        if p == 0:
            self.kept = self.place.keep(self.whole[0], self.whole[1](self.block.own()))
        source, landing = self.mine(p), self.view(self.block.own(), self.place.t, p)
        if self.deep > 1:
            self.along(0, p, source, landing)
        self.across(0, 0, p, source, landing)

    def from_line(self, n, p):
        ref = self.view(self.slot(n, 0, 0), self.place.t, p)
        self.place.arrived(ref, self.zr + self.index(n, 0, 1, p))
        if self.deep > 2:
            self.along(n, p, ref, ref)
        self.across(n, 0, p, ref, ref)
        self.share(n, 0, 0, p)

    def from_one(self, n, p):
        ref = self.view(self.slot(n, 1, 0), self.place.t, p)
        self.place.arrived(ref, self.r2 + self.index(n, 0, 1, p))
        self.across(n, 1, p, ref, ref)
        self.share(n, 1, 0, p)

    def from_two(self, n, i, p):
        ref = self.view(self.slot(n, i, 1), self.place.t, p)
        self.place.arrived(ref, self.r3 + self.index(n, i, 2, p))
        self.share(n, i, 1, p)

    def from_cores(self, n, i, j):
        if n + i + j == 0:
            return
        for far in range(1, self.cores):
            source = self.place.ring(self.cores - far)
            first, second = (j, i) if far % 2 else (i, j)
            kind = (far - 1) * 4 + first * 2 + second
            for p in range(self.pieces):
                ref = self.view(self.slot(n, i, j), source, p)
                self.place.arrived(ref, self.r4 + self.index(n, kind, 4 * (self.cores - 1), p))

    def finish(self):
        for condition, move in self.sent:
            when(condition, move.wait_send)

    def links(self):
        for p in range(self.pieces):
            self.start(p)
            yield
        for n in range(1, self.deep + 1):
            for p in range(self.pieces):
                self.from_one(n - 1, p)
                yield
                if n < self.deep:
                    self.from_line(n, p)
                    yield

    def last(self, n):
        for i in range(2):
            for p in range(self.pieces):
                self.from_two(n, i, p)

    def all(self):
        yield from self.links()
        for n in range(self.deep):
            self.last(n)
            yield
        for n in range(self.deep):
            for i in range(2):
                for j in range(2):
                    self.from_cores(n, i, j)
        self.finish()
        self.kept.wait()


def when(condition, action):
    if condition is None:
        action()
    else:
        pl.when(condition)(action)


def gather(place, members, mine, whole, view, halves, pieces=1):
    return Gather(place, members, mine, whole, view, halves, pieces).all()


class Kept:
    def __init__(self, left, right, rows):
        self.left, self.right, self.rows, self.slots = left, right, rows, {}

    def fetch(self, turn, slot):
        self.slots[turn] = pl.ds(pl.multiple_of(slot * self.rows, self.rows), self.rows)

    def ready(self, turn):
        pass

    def make(self, turn, core, target):
        columns = target.shape[1]
        wide = min(columns, 512)

        def body(tile, carry):
            source = pl.ds(pl.multiple_of(core * columns + tile * wide, wide), wide)
            into = pl.ds(pl.multiple_of(tile * wide, wide), wide)
            target[:, into] = dot(self.left[self.slots[turn], :], self.right[source, :], ((1,), (1,))).astype(bf16)
            return carry

        lax.fori_loop(0, columns // wide, body, 0)


def dot(left, right, sides=((1,), (0,)), precision=None):
    return lax.dot_general(left, right, (sides, ((), ())), precision=precision, preferred_element_type=f32)


def attend(tokens, gain, weights, first, position_rows, rooms, at, slot, rows):
    normed, qkv, probs, cosines, sines, out, inverse = rooms
    own = pl.ds(pl.multiple_of(slot * rows, rows), rows)

    def norm(piece_at, carry):
        source = pl.ds(pl.multiple_of(slot * rows + piece_at * 16, 16), 16)
        values = tokens[source, :].astype(f32)
        rstd = lax.rsqrt(jnp.mean(values * values, axis=1, keepdims=True) + eps)
        normed[at, pl.ds(pl.multiple_of(piece_at * 16, 16), 16), :] = (values * rstd * gain).astype(bf16)
        return carry

    lax.fori_loop(0, rows // 16, norm, 0)
    half = HEAD_DIM // 2
    angles = (position_rows - first) * inverse[...]
    lane = lax.broadcasted_iota(jnp.int32, (rows, HEAD_DIM), 1)
    cosine, sine = jnp.cos(angles), jnp.sin(angles)
    sine = jnp.where(lane < half, -sine, sine)
    cosines[own, :] = cosine
    sines[own, :] = sine
    lin = dot(normed[at], weights[...])

    def turn(values):
        return (values * cosine + pltpu.roll(values, half, 1) * sine).astype(bf16)

    query, keyed = turn(lin[:, :HEAD_DIM]), turn(lin[:, HEAD_DIM : 2 * HEAD_DIM])
    valued = lin[:, 2 * HEAD_DIM :].astype(bf16)
    qkv[own, :HEAD_DIM] = query
    qkv[own, HEAD_DIM : 2 * HEAD_DIM] = keyed
    qkv[own, 2 * HEAD_DIM :] = valued
    key_at = lax.broadcasted_iota(jnp.int32, (rows, rows), 1).astype(f32)
    query_at = lax.broadcasted_iota(jnp.int32, (rows, rows), 0).astype(f32)
    allowed = (key_at <= query_at) & (key_at >= first[:, :1])
    scores = jnp.where(allowed, dot(query, keyed, ((1,), (1,))) * (HEAD_DIM ** (-0.5)), floor_score)
    raised = jnp.exp(scores - jnp.max(scores, axis=1, keepdims=True))
    chances = raised / jnp.sum(raised, axis=1, keepdims=True)
    probs[own, :] = chances
    out[slot] = dot(chances.astype(bf16), valued).astype(bf16)


def attend_back(normed, rooms, slot, rows, start):
    qkv, probs, cosines, sines, grads, grad_qkv, sums = rooms
    own = pl.ds(pl.multiple_of(slot * rows, rows), rows)
    query = qkv[own, :HEAD_DIM]
    keyed = qkv[own, HEAD_DIM : 2 * HEAD_DIM]
    valued = qkv[own, 2 * HEAD_DIM :]
    cosine, sine = cosines[own, :], sines[own, :]
    chances, grad = probs[own, :], grads[slot]
    scale = HEAD_DIM ** (-0.5)

    def turn_back(values):
        return (values * cosine - pltpu.roll(values, HEAD_DIM // 2, 1) * sine).astype(bf16)

    grad_qkv[own, 2 * HEAD_DIM :] = dot(chances.astype(bf16), grad, ((0,), (0,))).astype(bf16)
    grad_chances = dot(grad, valued, ((1,), (1,)))
    weighted = jnp.sum(chances * grad_chances, axis=1, keepdims=True)
    grad_scores = (chances * (grad_chances - weighted)).astype(bf16)
    grad_qkv[own, :HEAD_DIM] = turn_back(dot(grad_scores, keyed) * scale)
    grad_qkv[own, HEAD_DIM : 2 * HEAD_DIM] = turn_back(dot(grad_scores, query, ((0,), (0,))) * scale)
    wide = 512

    def body(tile, carry):
        into = pl.ds(pl.multiple_of(tile * wide, wide), wide)
        product = dot(grad_qkv[own, :], normed[:, into], ((0,), (0,)))
        sums[:, into] = product if start else sums[:, into] + product
        return carry

    lax.fori_loop(0, sums.shape[1] // wide, body, 0)


def add_up(target, sources, rows, columns):
    step = max(16, min(rows, 16384 // columns // 16 * 16))

    def body(at, carry):
        piece = pl.ds(pl.multiple_of(at * step, step), step)
        total = sources[0][piece, :].astype(f32)
        for other in sources[1:]:
            total = total + other[piece, :].astype(f32)
        target[piece, :] = total.astype(target.dtype)
        return carry

    lax.fori_loop(0, rows // step, body, 0)


class Product:
    def __init__(self, place, left, varied, fixed, rooms, members, rows, columns):
        self.place, self.left, self.varied = place, left, varied
        self.lhs, self.rhs = rooms
        self.rows, self.columns = rows, columns
        self.lead = 0 if varied is None else varied.shape[0] // members
        self.waits, self.turn = {}, 0
        self.setup = []
        for buffer in range(self.rhs.shape[0]):
            self.setup.append(place.keep(fixed, self.rhs.at[buffer, pl.ds(self.lead, fixed.shape[0]), :]))

    def fetch(self, turn, slot):
        buffer = turn % 2
        rows = pl.ds(pl.multiple_of(slot * self.rows, self.rows), self.rows)
        moves = [self.place.keep(self.left.at[rows, :], self.lhs.at[buffer])]
        if self.lead:
            lead = pl.ds(pl.multiple_of(slot * self.lead, self.lead), self.lead)
            moves.append(self.place.keep(self.varied.at[lead, :], self.rhs.at[buffer, pl.ds(0, self.lead), :]))
        self.waits[turn] = moves

    def ready(self, turn):
        for move in self.setup:
            move.wait()
        self.setup = []
        for move in self.waits.pop(turn):
            move.wait()

    def make(self, turn, core, target):
        buffer = turn % 2
        right = self.rhs.at[buffer if self.lead else 0]
        wide = min(self.columns, 512)

        def body(at, carry):
            source = pl.ds(pl.multiple_of(core * self.columns + at * wide, wide), wide)
            into = pl.ds(pl.multiple_of(at * wide, wide), wide)
            target[:, into] = jnp.dot(
                self.lhs[buffer], right[:, source], preferred_element_type=f32
            ).astype(bf16)
            return carry

        lax.fori_loop(0, self.columns // wide, body, 0)


def scatter(place, members, sources, room, views, shape, halves, credit=None):
    block = Block(place, members)
    deep, e, t = block.deep, place.e, place.t
    rows, columns = shape
    order = 1 - lax.rem(t, 2)
    cores = place.cores if halves else 1
    count = len(sources)
    mine, outgoing, land0, land1s, land2s, land3s, finals = room
    s0, r0 = place.take(4 * deep * cores * count), place.take(4 * deep * cores * count)
    s1, r1 = place.take(2 * deep * count), place.take(2 * deep * count)
    s2, r2 = place.take(deep * count), place.take(deep * count)
    s3, r3 = place.take(deep * count), place.take(deep * count)
    s4, r4 = place.take(cores * count), place.take(cores * count)
    walk = [(f, k) for f in range(count) for k in list(range(1, deep)) + [0]]
    one, two = block.flips(order)
    sent, loads, last, kept = [], {}, {}, []
    quads = [(1, 1), (1, 0), (0, 1), (0, 0)]
    turns = [(f, k, i, j) for f, k in walk for i, j in quads]
    ring = outgoing.shape[0]
    leaving = []

    def slot_of(k, i, j):
        return block.slot(k, i, j, order)

    def land_index(d, k, i, j):
        return (d - 1) * deep * 4 + k * 4 + i * 2 + j

    def produce(number):
        f, k, i, j = turns[number]
        source = sources[f]
        if (k, i, j) in last:
            last.pop((k, i, j)).wait_send()
        if not isinstance(source, (Product, Kept)):
            loads[f, k, i, j] = place.keep(source(slot_of(k, i, j)), mine.at[slot_of(k, i, j)])
            return
        local_number = number - f * 4 * deep
        if local_number == 0:
            source.fetch(0, slot_of(k, i, j))
        source.ready(local_number)
        if local_number + 1 < 4 * deep:
            source.fetch(local_number + 1, slot_of(*turns[number + 1][1:]))
        if number >= ring:
            for move in leaving[number - ring]:
                move.wait_send()
        moves = []
        for d in range(1, cores):
            target = place.ring(d)
            buffer = outgoing.at[number % ring, d - 1]
            source.make(local_number, target, buffer)
            at = land_index(d, k, *((j, i) if d % 2 else (i, j)))
            if f > 0:
                pl.semaphore_wait(credit.at[at], 1)
            sem = f * 4 * deep * cores + at
            moves.append(place.send(buffer, land0.at[at], s0 + sem, r0 + sem, e, target))
        leaving.append(moves)
        source.make(local_number, t, mine.at[slot_of(k, i, j)])

    def terms_of(f, k, i, j):
        if (f, k, i, j) in loads:
            loads[f, k, i, j].wait()
        terms = [mine.at[slot_of(k, i, j)]]
        for d in range(1, cores):
            at = land_index(d, k, i, j)
            place.arrived(land0.at[at], r0 + f * 4 * deep * cores + at)
            terms.append(land0.at[at])
        if i == 0:
            at = (f * deep + k) * 2 + j
            place.arrived(land1s.at[at], r1 + at)
            terms.append(land1s.at[at])
            if j == 0:
                at = f * deep + k
                place.arrived(land2s.at[at], r2 + at)
                terms.append(land2s.at[at])
        return terms

    def give_back(f, k, i, j):
        if f + 1 < count:
            for d in range(1, cores):
                pl.semaphore_signal(
                    credit.at[land_index(d, k, i, j)],
                    inc=1,
                    device_id={"expert": e, "tensor": place.ring(cores - d)},
                    device_id_type=MESH,
                )

    def leave(f, k, i, j, landing, out, into, at, target):
        move = place.send(mine.at[slot_of(k, i, j)], landing.at[at], out + at, into + at, target, t)
        last[k, i, j] = move

    def first_flip(f, k, j):
        terms, ref = terms_of(f, k, 1, j), mine.at[slot_of(k, 1, j)]
        if len(terms) > 1:
            add_up(ref, terms, rows, columns)
        give_back(f, k, 1, j)
        leave(f, k, 1, j, land1s, s1, r1, (f * deep + k) * 2 + j, e + one)

    def second_flip(f, k):
        add_up(mine.at[slot_of(k, 0, 1)], terms_of(f, k, 0, 1), rows, columns)
        give_back(f, k, 0, 1)
        leave(f, k, 0, 1, land2s, s2, r2, f * deep + k, e + two)

    def line(f, k):
        terms, ref = terms_of(f, k, 0, 0), mine.at[slot_of(k, 0, 0)]
        if k > 0:
            add_up(ref, terms, rows, columns)
            give_back(f, k, 0, 0)
            peer = block.device(lax.rem(block.rank + k, deep) * 4 + place.quad)
            leave(f, k, 0, 0, land3s, s3, r3, f * deep + k, peer)
            return
        for far in range(1, deep):
            place.arrived(land3s.at[f * deep + far], r3 + f * deep + far)
            terms.append(land3s.at[f * deep + far])
        final = finals.at[f]
        add_up(final, terms, rows, columns)
        give_back(f, k, 0, 0)
        kept.append(place.keep(final, views[f](t)))
        for d in range(1, cores):
            at = f * cores + d
            sent.append(place.send(final, views[f](t), s4 + at, r4 + at, e, place.ring(d)))

    for step in range(len(walk) + 2):
        fresh = step < len(walk)
        if fresh:
            produce(4 * step)
            yield
            produce(4 * step + 1)
            yield
            first_flip(*walk[step], 1)
            yield
            produce(4 * step + 2)
            yield
        if 0 <= step - 1 < len(walk):
            second_flip(*walk[step - 1])
            yield
        if fresh:
            produce(4 * step + 3)
            yield
            first_flip(*walk[step], 0)
            yield
        if 0 <= step - 2 < len(walk):
            line(*walk[step - 2])
            yield
    for f in range(count):
        for d in range(1, cores):
            place.arrived(views[f](place.ring(cores - d)), r4 + f * cores + d)
    for moves in leaving[-ring:]:
        for move in moves:
            move.wait_send()
    for move in list(last.values()) + sent:
        move.wait_send()
    for move in kept:
        move.wait()


def scatter_scratch(members, cores, rows, columns, products=(), ring=4):
    deep = members // 4
    count = max(1, len(products))
    short = rows if cores > 1 else 16
    rooms = [
        pltpu.VMEM((members, rows, columns), bf16),
        pltpu.VMEM((ring, max(1, cores - 1), short, columns), bf16),
        pltpu.VMEM((max(1, (cores - 1) * members), short, columns), bf16),
        pltpu.VMEM((2 * deep * count, rows, columns), bf16),
        pltpu.VMEM((deep * count, rows, columns), bf16),
        pltpu.VMEM((deep * count, rows, columns), bf16),
        pltpu.VMEM((count, rows, columns), bf16),
    ]
    for depth, varied in products:
        rooms.append(pltpu.VMEM((2, rows, depth), bf16))
        rooms.append(pltpu.VMEM((2 if varied else 1, depth, columns * cores), bf16))
    return rooms


def exchange(place, members, source, landing):
    e, t = place.e, place.t
    own = lax.rem(e, members)
    base = e - own
    sends, arrivals = place.take(members), place.take(members)
    sent = []
    for d in range(1, members):
        target = lax.rem(own + d, members)
        sent.append(place.send(source(target), landing(own), sends + d, arrivals + d, base + target, t))
    kept = place.keep(source(own), landing(own))
    yield
    for d in range(1, members):
        place.arrived(landing(lax.rem(own + members - d, members)), arrivals + d)
    for move in sent:
        move.wait_send()
    kept.wait()


def start_exchange(place, members, source, landing):
    e, t = place.e, place.t
    own = lax.rem(e, members)
    base = e - own
    sends, arrivals = place.take(members), place.take(members)
    sent = []
    for d in range(1, members):
        target = lax.rem(own + d, members)
        sent.append(place.send(source(target), landing(own), sends + target, arrivals + own, base + target, t))
    place.keep(source(own), landing(own)).wait()

    def arrived(slot):
        pl.when(slot != own)(lambda: place.arrived(landing(slot), arrivals + slot))

    def finish():
        for move in sent:
            move.wait_send()

    return arrived, finish


def both(place, members, source, landing, part):
    yield from exchange(place, members, source, lambda slot: landing(place.t, slot))
    sends, arrivals = place.take(place.cores), place.take(place.cores)
    sent = []
    for d in range(1, place.cores):
        mine = part(place.t)
        sent.append(place.send(mine, mine, sends + d, arrivals + d, place.e, place.ring(d)))
    yield
    for d in range(1, place.cores):
        place.arrived(part(place.ring(place.cores - d)), arrivals + d)
    for move in sent:
        move.wait_send()


def twice(task):
    for _ in task:
        next(task, None)
        yield


def later(task, rounds):
    for _ in range(rounds):
        yield
    yield from task


def run(tasks):
    while tasks:
        for task in list(tasks):
            try:
                next(task)
            except StopIteration:
                tasks.remove(task)


def transfer(name, number, mesh, body, ins, outs, scratch=(), semaphores=400, vmem=None):
    count, cores = mesh.shape["expert"], mesh.shape["tensor"]
    semaphores = semaphores * max(1, count * cores // 32)

    def kernel(*refs):
        given = refs[: len(ins)]
        made = refs[len(ins) : len(ins) + len(outs)]
        room = refs[len(ins) + len(outs) : -1]
        place = Place(refs[-1], count, cores)
        place.meet()
        tasks = []
        for task in body(place, given, made, room):
            if isinstance(task, list):
                run(task)
            else:
                tasks.append(task)
        run(tasks)
        assert place.used <= semaphores, place.used

    size = sum(x.size * x.dtype.itemsize for x in list(ins) + list(outs))
    return pl.pallas_call(
        kernel,
        name=name,
        out_shape=[jax.ShapeDtypeStruct(shape, dtype) for shape, dtype in outs_of(outs)],
        in_specs=[ANY] * len(ins),
        out_specs=[ANY] * len(outs),
        scratch_shapes=list(scratch) + [pltpu.SemaphoreType.DMA((semaphores,))],
        cost_estimate=pl.CostEstimate(flops=0, bytes_accessed=size, transcendentals=0),
        compiler_params=pltpu.CompilerParams(
            collective_id=number, has_side_effects=True, vmem_limit_bytes=vmem
        ),
    )(*ins)


def outs_of(outs):
    return [(x.shape, x.dtype) for x in outs]


def like(shape, dtype=bf16):
    return jax.ShapeDtypeStruct(shape, dtype)


def part_view(ref, rows, columns, pieces=1):
    height = rows // pieces

    def view(slot, core, piece=0):
        at = 0 if isinstance(slot, int) else pl.multiple_of(slot * rows, rows)
        return ref.at[
            pl.ds(at + piece * height, height), pl.ds(pl.multiple_of(core * columns, columns), columns)
        ]

    return view


PIECES = 2


def lanes(at, columns):
    return pl.ds(pl.multiple_of(at * columns, columns), columns)


class Strips:
    def __init__(self, count, columns):
        self.count, self.columns = count, columns
        self.direct = columns % 128 == 0

    def shape(self, rows):
        return (rows, self.count * self.columns) if self.direct else (self.count, rows, self.columns)

    def at(self, ref, slot):
        return ref.at[:, lanes(slot, self.columns)] if self.direct else ref.at[slot]

    def cut(self, array):
        rows = array.shape[0]
        return array if self.direct else array.reshape(rows, self.count, self.columns).transpose(1, 0, 2)

    def join(self, array):
        rows = array.shape[0 if self.direct else 1]
        return array if self.direct else array.transpose(1, 0, 2).reshape(rows, self.count * self.columns)


def row_gather(place, members, source, landing, rows, part):
    def mine(piece):
        height = rows // PIECES
        return source.at[pl.ds(piece * height, height), lanes(place.t, part)]

    whole = (source, lambda slot: landing.at[pl.ds(pl.multiple_of(slot * rows, rows), rows), :])
    return Gather(place, members, mine, whole, part_view(landing, rows, part, PIECES), True, PIECES)


def rotary(values, cosine, sine):
    half = values.shape[-1] // 2
    first = values[..., :half]
    second = values[..., half:]
    return jnp.concatenate([first * cosine - second * sine, second * cosine + first * sine], axis=-1)


def rotary_back(grads, cosine, sine):
    half = grads.shape[-1] // 2
    first = grads[..., :half]
    second = grads[..., half:]
    return jnp.concatenate([first * cosine + second * sine, second * cosine - first * sine], axis=-1)


def sequence_tables(lengths_rows, tok_rows):
    ends = jnp.cumsum(lengths_rows, axis=1)
    starts = ends - lengths_rows
    places = jnp.arange(tok_rows, dtype=jnp.int32)
    segment = jnp.sum((places[None, :, None] >= ends[:, None, :]).astype(jnp.int32), axis=2)
    member = segment[:, :, None] == jnp.arange(lengths_rows.shape[1], dtype=jnp.int32)[None, None, :]
    first = jnp.sum(jnp.where(member, starts[:, None, :], 0), axis=2)
    return segment, places[None, :] - first


def silu_parts(values):
    sigmoid_value = jax.nn.sigmoid(values)
    return values * sigmoid_value, sigmoid_value * (1.0 + values * (1.0 - sigmoid_value))


def mm(form, left, right):
    return jnp.einsum(form, left, right, preferred_element_type=f32)


def up_to(value, step):
    return -(-value // step) * step


def experts_kernel(
    groups,
    capacity,
    rows,
    xn_ref,
    grad_ref,
    position_ref,
    gate_ref,
    wg_ref,
    wu_ref,
    wd_ref,
    sh_in_ref,
    sh_down_ref,
    received_ref,
    gated_ref,
    low_ref,
    back_ref,
    act_ref,
    gate_back_ref,
    up_back_ref,
    dots_ref,
    left_forward_ref,
    left_backward_ref,
):
    places = lax.broadcasted_iota(jnp.int32, (capacity, rows), 0).astype(f32)
    gates, grads, onehots = [], [], []
    for g in range(groups):
        token = pl.ds(g * rows, rows)
        slot = pl.ds(g * capacity, capacity)
        chosen = (position_ref[g] == places).astype(f32)
        onehot = chosen.astype(bf16)
        onehots.append(chosen)
        received_ref[slot, :] = dot(onehot, xn_ref[token, :]).astype(bf16)
        gate = jnp.sum(chosen * gate_ref[g], axis=1, keepdims=True)
        row_grads = dot(onehot, grad_ref[token, :])
        gated_ref[slot, :] = (gate * row_grads).astype(bf16)
        low_ref[slot, :] = row_grads.astype(bf16)
        gates.append(gate)
        turned = chosen.T.astype(bf16)
        left_forward_ref[token, :capacity] = turned
        left_backward_ref[token, :capacity] = turned
    gate = jnp.concatenate(gates, axis=0)
    received = received_ref[...]
    exp_gate = dot(received, wg_ref[...], ((1,), (1,)))
    exp_up = dot(received, wu_ref[...], ((1,), (1,)))
    silu, slope = silu_parts(exp_gate)
    act = (silu * exp_up).astype(bf16)
    act_ref[...] = act
    out = dot(act, wd_ref[...])
    dots = jnp.sum(low_ref[...].astype(f32) * out, axis=1, keepdims=True)
    low_ref[...] = (gate * out).astype(bf16)
    for g in range(groups):
        column = dots[g * capacity : (g + 1) * capacity]
        token_dots = jnp.sum(onehots[g] * column, axis=0, keepdims=True)
        dots_ref[g] = jnp.broadcast_to(token_dots, (8, rows))
    act_grad = dot(gated_ref[...], wd_ref[...], ((1,), (1,)))
    gate_back = (act_grad * exp_up * slope).astype(bf16)
    up_back = (act_grad * silu).astype(bf16)
    gate_back_ref[...] = gate_back
    up_back_ref[...] = up_back
    back_ref[...] = (
        dot(gate_back, wg_ref[...]) + dot(up_back, wu_ref[...])
    ).astype(bf16)
    wide = sh_down_ref.shape[0]
    both = dot(xn_ref[...], sh_in_ref[...], ((1,), (1,)))
    sh_gate, sh_up = both[:, :wide], both[:, wide:]
    sh_silu, sh_slope = silu_parts(sh_gate)
    left_forward_ref[:, capacity:] = (sh_silu * sh_up).astype(bf16)
    sh_grad = dot(grad_ref[...], sh_down_ref[...], ((1,), (1,)))
    left_backward_ref[:, capacity : capacity + wide] = (sh_grad * sh_up * sh_slope).astype(bf16)
    left_backward_ref[:, capacity + wide :] = (sh_grad * sh_silu).astype(bf16)


def experts_pass(count, capacity, rows, xn_all, grad_all, position, gate, wg, wu, wd, sh_in, sh_down):
    groups = 2
    units, width = wg.shape
    wide = sh_down.shape[0]

    def along(*shape):
        return pl.BlockSpec(shape, lambda i: (i,) + (0,) * (len(shape) - 1))

    def whole(array):
        return pl.BlockSpec(array.shape, lambda i: (0,) * array.ndim, pipeline_mode=pl.Buffered(1))

    slots = groups * capacity
    tokens = groups * rows
    flops = 2 * count * capacity * width * units * 6
    return pl.pallas_call(
        functools.partial(experts_kernel, groups, capacity, rows),
        name="experts_pass",
        grid=(count // groups,),
        in_specs=[
            along(tokens, width),
            along(tokens, width),
            along(groups, 1, rows),
            along(groups, 1, rows),
            whole(wg),
            whole(wu),
            whole(wd),
            whole(sh_in),
            whole(sh_down),
        ],
        out_specs=[
            along(slots, width),
            along(slots, width),
            along(slots, width),
            along(slots, width),
            along(slots, units),
            along(slots, units),
            along(slots, units),
            along(groups, 8, rows),
            along(tokens, capacity + wide),
            along(tokens, capacity + 2 * wide),
        ],
        out_shape=[like((count * capacity, width))] * 4
        + [like((count * capacity, units))] * 3
        + [
            like((count, 8, rows), f32),
            like((count * rows, capacity + wide)),
            like((count * rows, capacity + 2 * wide)),
        ],
        cost_estimate=pl.CostEstimate(
            flops=flops, bytes_accessed=4 * count * (rows + 2 * capacity) * width, transcendentals=0
        ),
        compiler_params=pltpu.CompilerParams(vmem_limit_bytes=58 * 2**20),
    )(xn_all, grad_all, position, gate, wg, wu, wd, sh_in, sh_down)


def local(
    mesh,
    tokens,
    lengths,
    routes,
    gain_attn,
    w_query,
    w_key,
    w_value,
    w_out,
    gain_ffn,
    w_router,
    routed_gate_weight,
    routed_up_weight,
    w_down,
    w_shared_gate,
    w_shared_up,
    w_shared_down,
    out_grad,
):
    count, cores = mesh.shape["expert"], mesh.shape["tensor"]
    rows, width = tokens.shape
    part = width // cores
    deep = w_query.shape[0]
    experts = w_router.shape[1]
    heads = w_query.shape[1] // HEAD_DIM
    capacity = up_to(min(rows, rows * TOP * 4 // (3 * count)), 128)
    hidden_units = w_shared_gate.shape[1] // count
    scale = HEAD_DIM ** (-0.5)
    e = lax.axis_index("expert")
    t = lax.axis_index("tensor")
    chunk = heads * rows
    strips = Strips(count, deep)

    expert_ids = jnp.arange(experts, dtype=jnp.int32)
    choose = jnp.any(routes[:, :, None] == expert_ids[None, None, :], axis=1)
    mask_t = choose.T.astype(bf16)
    vectors = jnp.concatenate(
        [
            w_router.T,
            gain_attn[None],
            gain_ffn[None],
            jnp.pad(lengths.astype(bf16), ((0, 0), (0, deep - lengths.shape[1]))),
        ],
        axis=0,
    )
    head_rows = up_to(vectors.shape[0], 16)
    vectors = jnp.pad(vectors, ((0, head_rows - vectors.shape[0]), (0, 0)))
    pieces = rows // deep
    mask_rows = mask_t.reshape(experts * pieces, deep)
    small = jnp.concatenate([vectors, mask_rows], axis=0)
    small_rows = up_to(small.shape[0], 16)
    small = jnp.pad(small, ((0, small_rows - small.shape[0]), (0, 0)))

    def unpack(gathered):
        router = gathered[:experts]
        attn_gain, ffn_gain = gathered[experts].astype(f32), gathered[experts + 1].astype(f32)
        rows_of = gathered[experts + 2].reshape(count, deep)[:, : lengths.shape[1]].astype(f32).astype(jnp.int32)
        masks = gathered[head_rows : head_rows + experts * pieces].reshape(experts, pieces, count, deep)
        return router, attn_gain, ffn_gain, rows_of, masks.transpose(2, 0, 1, 3).reshape(count, experts, rows)

    shared_pack = jnp.concatenate(
        [
            w_shared_gate.T.reshape(count, hidden_units, deep),
            w_shared_up.T.reshape(count, hidden_units, deep),
            w_shared_down.reshape(count, hidden_units, deep),
        ],
        axis=1,
    )
    pack_rows = up_to(3 * hidden_units, 16)
    shared_pack = jnp.pad(shared_pack, ((0, 0), (0, pack_rows - 3 * hidden_units), (0, 0)))
    out_rows = w_out.shape[0]

    if strips.direct:

        def front_body(place, given, made, room):
            tok, sm, wq, wk, wv, og, wo, sp, inv = given
            sm_all, w_all, xn_all, qkv_all, pr_all, ct_all, st_all, ho_all, og_all, wo_all, sp_all = made
            sm_v, tok_v, w_v, normed, qkv, probs, cosines, sines, out, inverse = room
            own = lax.rem(place.e, heads)
            base = place.e - own
            ready = place.keep(inv, inverse)
            small_in, small_out = start_exchange(place, count, lambda s: sm, lambda s: sm_v.at[:, lanes(s, deep)])
            tokens_in = row_gather(place, heads, tok, tok_v, rows, part)
            sends, arrivals = place.take(heads), place.take(heads)

            def wo_view(slot, core=0, piece=0):
                return strips.at(wo_all, slot)

            def attention():
                links = tokens_in.links()
                for _ in range(PIECES):
                    next(links)
                pulls = []
                for which, weight in enumerate((wq, wk, wv)):

                    def landing(slot, which=which):
                        at = pl.ds(pl.multiple_of(slot * deep, deep), deep)
                        return w_v.at[at, pl.ds(which * HEAD_DIM, HEAD_DIM)]

                    pulls.append(
                        start_exchange(
                            place, count, lambda s, w=weight: w.at[:, lanes(lax.rem(s, heads), HEAD_DIM)], landing
                        )
                    )
                yield
                yield from links
                for d in range(1, count):
                    slot = lax.rem(place.e + d, count)
                    for arrived in [small_in] + [pull[0] for pull in pulls]:
                        arrived(slot)
                ready.wait()
                saved = [place.keep(sm_v, sm_all), place.keep(w_v, w_all)]
                head = experts - experts % 16
                vectors = sm_v[pl.ds(head, 16), :].astype(f32)
                gain = vectors[experts - head : experts - head + 1, :]
                position = lax.broadcasted_iota(jnp.int32, (rows, HEAD_DIM), 0).astype(f32)
                gave, stored = [], []

                def group(n, i, j):
                    tokens_in.from_cores(n, i, j)
                    slot = tokens_in.slot(n, i, j)
                    at = len(stored) % 2
                    if len(stored) >= 2:
                        stored[-2].wait()
                    row = sm_v[pl.ds(head, 16), lanes(tokens_in.block.device(slot), deep)].astype(f32)
                    row = row[experts + 2 - head : experts + 3 - head, :]
                    end, first = jnp.zeros((1, 1), f32), jnp.zeros((rows, HEAD_DIM), f32)
                    for place_in in range(lengths.shape[1]):
                        end = end + row[:, place_in : place_in + 1]
                        first = jnp.where(position >= end, end, first)
                    attend(
                        tok_v,
                        gain,
                        w_v,
                        first,
                        position,
                        (normed, qkv, probs, cosines, sines, out, inverse),
                        at,
                        slot,
                        rows,
                    )
                    stored.append(
                        place.keep(
                            normed.at[at], xn_all.at[pl.ds(pl.multiple_of(slot * rows, rows), rows), :]
                        )
                    )
                    landing = ho_all.at[:, lanes(own, HEAD_DIM)]
                    if n + i + j == 0:
                        saved.append(place.keep(out.at[slot], landing))
                    else:
                        gave.append(
                            place.send(out.at[slot], landing, sends + slot, arrivals + own, base + slot, place.t)
                        )

                for n in range(tokens_in.deep):
                    if n == 0:
                        tokens_in.kept.wait()
                    group(n, 0, 0)
                    yield
                for n in range(tokens_in.deep):
                    tokens_in.last(n)
                    for i, j in ((1, 0), (0, 1), (1, 1)):
                        group(n, i, j)
                        yield
                for source, target in ((qkv, qkv_all), (probs, pr_all), (cosines, ct_all), (sines, st_all)):
                    saved.append(place.keep(source, target))
                yield
                for d in range(1, heads):
                    slot = lax.rem(own + d, heads)
                    place.arrived(ho_all.at[:, lanes(slot, HEAD_DIM)], arrivals + slot)
                for move in gave:
                    move.wait_send()
                for move in stored[-2:] + saved:
                    move.wait()
                for pull in pulls:
                    pull[1]()
                small_out()
                tokens_in.finish()

            yield attention()
            yield later(row_gather(place, count, og, og_all, rows, part).all(), 3)
            yield later(gather(place, count, lambda p: wo, (wo, wo_view), wo_view, False), 3)
            yield later(exchange(place, count, lambda s: sp.at[s], lambda s: strips.at(sp_all, s)), 6)

        half = HEAD_DIM // 2
        inverse = 10000.0 ** (-2.0 * jnp.arange(half, dtype=f32) / HEAD_DIM)
        (
            small_all,
            w_qkv,
            xn_chunk,
            qkv_saved,
            probs_saved,
            cosine_wide,
            sine_wide,
            heads_out,
            grad_all,
            out_full,
            shared_all,
        ) = transfer(
            "attention_front",
            0,
            mesh,
            front_body,
            (
                tokens,
                small,
                w_query,
                w_key,
                w_value,
                out_grad,
                w_out,
                shared_pack,
                jnp.concatenate([inverse, inverse])[None],
            ),
            (
                like((small_rows, width)),
                like((width, 3 * HEAD_DIM)),
                like((chunk, width)),
                like((chunk, 3 * HEAD_DIM)),
                like((chunk, rows), f32),
                like((chunk, HEAD_DIM), f32),
                like((chunk, HEAD_DIM), f32),
                like((rows, heads * HEAD_DIM)),
                like((count * rows, width)),
                like((out_rows, width)),
                like((pack_rows, width)),
            ),
            [
                pltpu.VMEM((small_rows, width), bf16),
                pltpu.VMEM((chunk, width), bf16),
                pltpu.VMEM((width, 3 * HEAD_DIM), bf16),
                pltpu.VMEM((2, rows, width), bf16),
                pltpu.VMEM((chunk, 3 * HEAD_DIM), bf16),
                pltpu.VMEM((chunk, rows), f32),
                pltpu.VMEM((chunk, HEAD_DIM), f32),
                pltpu.VMEM((chunk, HEAD_DIM), f32),
                pltpu.VMEM((heads, rows, HEAD_DIM), bf16),
                pltpu.VMEM((1, HEAD_DIM), f32),
            ],
            semaphores=640,
            vmem=56 * 2**20,
        )
        router_full, attn_gain, ffn_gain, _, masks = unpack(small_all)
    else:
        def first_body(place, given, made, room):
            tok, sm, *weights = given
            tok_all, sm_all, w_all = made
            yield exchange(place, count, lambda s: sm, lambda s: sm_all.at[s])
            yield row_gather(place, heads, tok, tok_all, rows, part).all()
            for which, weight in enumerate(weights):

                def landing(slot, which=which):
                    at = pl.ds(pl.multiple_of(slot * deep, deep), deep)
                    return w_all.at[at, pl.ds(which * HEAD_DIM, HEAD_DIM)]

                yield exchange(
                    place, count, lambda s, w=weight: w.at[:, lanes(lax.rem(s, heads), HEAD_DIM)], landing
                )

        tok_chunk, small_all, w_qkv = transfer(
            "gather_tokens",
            0,
            mesh,
            first_body,
            (tokens, small, w_query, w_key, w_value),
            (like((chunk, width)), like((count, small_rows, deep)), like((width, 3 * HEAD_DIM))),
        )

        router_full, attn_gain, ffn_gain, lengths_all, masks = unpack(strips.join(small_all))

        member = e % heads
        lengths_chunk = lax.dynamic_slice_in_dim(lengths_all, e - member, heads, axis=0)
        segment, positions = sequence_tables(lengths_chunk, rows)
        half = HEAD_DIM // 2
        inverse = 10000.0 ** (-2.0 * jnp.arange(half, dtype=f32) / HEAD_DIM)
        angles = positions.astype(f32)[:, :, None] * inverse[None, None, :]
        cosine, sine = jnp.cos(angles), jnp.sin(angles)

        tok32 = tok_chunk.astype(f32)
        rstd_chunk = lax.rsqrt(jnp.mean(tok32 * tok32, axis=-1, keepdims=True) + eps)
        xn_chunk = (tok32 * rstd_chunk * attn_gain).astype(bf16)
        qkv = jnp.dot(xn_chunk, w_qkv, preferred_element_type=f32).reshape(heads, rows, 3 * HEAD_DIM)
        query = rotary(qkv[..., :HEAD_DIM], cosine, sine).astype(bf16)
        keyed = rotary(qkv[..., HEAD_DIM : 2 * HEAD_DIM], cosine, sine).astype(bf16)
        valued = qkv[..., 2 * HEAD_DIM :].astype(bf16)
        places = jnp.arange(rows, dtype=jnp.int32)
        allowed = (segment[:, :, None] == segment[:, None, :]) & (places[None, :] <= places[:, None])[None]
        scores = jnp.where(allowed, mm("gqd,gkd->gqk", query, keyed) * scale, floor_score)
        top_score = jnp.max(scores, axis=-1, keepdims=True)
        raised = jnp.exp(scores - top_score)
        probs = raised / jnp.sum(raised, axis=-1, keepdims=True)
        probs_low = probs.astype(bf16)
        head_out = mm("gqk,gkd->gqd", probs_low, valued).astype(bf16)

        def second_body(place, given, made, room):
            ho, og, wo, sp = given
            ho_all, og_all, wo_all, sp_all = made
            yield exchange(place, heads, lambda s: ho.at[s], lambda s: ho_all.at[:, lanes(s, HEAD_DIM)])
            yield row_gather(place, count, og, og_all, rows, part).all()

            def wo_view(slot, core=0, piece=0):
                return strips.at(wo_all, slot)

            yield gather(place, count, lambda p: wo, (wo, wo_view), wo_view, False)
            yield exchange(place, count, lambda s: sp.at[s], lambda s: strips.at(sp_all, s))

        heads_out, grad_all, out_full, shared_all = transfer(
            "gather_inputs",
            1,
            mesh,
            second_body,
            (head_out, out_grad, w_out, shared_pack),
            (
                like((rows, heads * HEAD_DIM)),
                like((count * rows, width)),
                like(strips.shape(out_rows)),
                like(strips.shape(pack_rows)),
            ),
            semaphores=640,
        )
        out_full, shared_all = strips.join(out_full), strips.join(shared_all)
    attention_part = jnp.dot(heads_out, out_full, preferred_element_type=f32).astype(bf16)

    def third_body(place, given, made, room):
        ap, tok, gn, rt, mk = given
        hid_out, xn_all, gt_all = made
        parts, tok_v, gn_v, rt_v, mk_v, hid, xn, gt = room
        t = place.t
        sends, arrivals = place.take(cores), place.take(cores)
        sent = [place.send(ap, parts.at[t], sends + d, arrivals + d, place.e, place.ring(d)) for d in range(1, cores)]
        kept = [place.keep(ap, parts.at[t])]
        kept += [place.keep(a, b) for a, b in ((tok, tok_v), (gn, gn_v), (rt, rt_v), (mk, mk_v))]
        for move in kept:
            move.wait()
        for d in range(1, cores):
            place.arrived(parts.at[place.ring(cores - d)], arrivals + d)

        def body(at, carry):
            piece = pl.ds(pl.multiple_of(at * 16, 16), 16)
            total = parts[0, piece, :].astype(f32)
            for core in range(1, cores):
                total = total + parts[core, piece, :].astype(f32)
            values = tok_v[piece, :].astype(f32) + total
            hid[piece, :] = values
            rstd = lax.rsqrt(jnp.mean(values * values, axis=1, keepdims=True) + eps)
            xn[piece, :] = (values * rstd * gn_v[...]).astype(bf16)
            return carry

        lax.fori_loop(0, rows // 16, body, 0)
        saved = place.keep(hid, hid_out)
        yield row_gather(place, count, xn, xn_all, rows, part).all()
        logits = lax.dot_general(rt_v[...], xn[...], (((1,), (1,)), ((), ())), preferred_element_type=f32)
        picked = mk_v[...] > 0.5
        top_logit = jnp.max(jnp.where(picked, logits, floor_score), axis=0, keepdims=True)
        lifted = jnp.where(picked, jnp.exp(jnp.where(picked, logits - top_logit, 0.0)), 0.0)
        gt[...] = lifted / jnp.sum(lifted, axis=0, keepdims=True)
        yield exchange(place, count, lambda s: gt, lambda s: gt_all.at[s])
        for move in sent:
            move.wait_send()
        saved.wait()

    hidden, xn_all, gates_all = transfer(
        "gather_rows",
        2,
        mesh,
        third_body,
        (attention_part, tokens, ffn_gain[None], router_full, mask_t.astype(f32)),
        (like((rows, width), f32), like((count * rows, width)), like((count, experts, rows), f32)),
        [
            pltpu.VMEM((cores, rows, width), bf16),
            pltpu.VMEM((rows, width), bf16),
            pltpu.VMEM((1, width), f32),
            pltpu.VMEM((experts, width), bf16),
            pltpu.VMEM((experts, rows), f32),
            pltpu.VMEM((rows, width), f32),
            pltpu.VMEM((rows, width), bf16),
            pltpu.VMEM((experts, rows), f32),
        ],
        semaphores=400,
        vmem=40 * 2**20,
    )
    inputs = tokens.astype(f32)
    rstd_two = lax.rsqrt(jnp.mean(hidden * hidden, axis=-1, keepdims=True) + eps)
    gates = lax.dynamic_index_in_dim(gates_all, e, axis=0, keepdims=False).T

    own_mask = lax.dynamic_index_in_dim(masks, e, axis=1, keepdims=False).astype(f32)
    own_gate = lax.dynamic_index_in_dim(gates_all, e, axis=1, keepdims=False)
    at_row = jnp.arange(rows, dtype=jnp.int32)
    earlier = (at_row[:, None] < at_row[None, :]).astype(bf16)
    position = jnp.where(own_mask > 0.5, jnp.dot(own_mask.astype(bf16), earlier, preferred_element_type=f32), -1.0)
    gate_weight, up_weight, down_weight = routed_gate_weight[0].T, routed_up_weight[0].T, w_down[0]
    sh_wide = up_to(hidden_units, 128)

    def widened(which):
        piece = shared_all[which * hidden_units : (which + 1) * hidden_units]
        return jnp.pad(piece, ((0, sh_wide - hidden_units), (0, 0)))

    fixed_backward = jnp.concatenate([widened(0), widened(1)], axis=0)
    fixed_forward = widened(2)
    (
        received,
        gated_grad,
        exp_low,
        back_rows,
        exp_act,
        gate_back,
        up_back,
        token_dots,
        left_forward,
        left_backward,
    ) = experts_pass(
        count,
        capacity,
        rows,
        xn_all,
        grad_all,
        position[:, None],
        own_gate[:, None],
        gate_weight,
        up_weight,
        down_weight,
        fixed_backward,
        fixed_forward,
    )

    sh_grads = mm("tf,td->fd", left_backward[:, capacity:], xn_all).astype(bf16)
    shared_grads = jnp.concatenate(
        [
            sh_grads[:hidden_units],
            sh_grads[sh_wide : sh_wide + hidden_units],
            mm("tf,td->fd", left_forward[:, capacity:], grad_all).astype(bf16)[:hidden_units],
        ],
        axis=0,
    )
    shared_grads = jnp.pad(shared_grads, ((0, pack_rows - 3 * hidden_units), (0, 0)))

    def fourth_body(place, given, made, room):
        lf, el, ff, lb, br, fb, td, sg = given
        mixed, summed, dots, sg_all = made
        mixed_view, summed_view = part_view(mixed, rows, part), part_view(summed, rows, part)
        forward = Product(place, lf, el, ff, room[7:9], count, rows, part)
        backward = Product(place, lb, br, fb, room[9:11], count, rows, part)
        yield scatter(
            place,
            count,
            [forward, backward],
            room[:7],
            [lambda c: mixed_view(0, c), lambda c: summed_view(0, c)],
            (rows, part),
            True,
            room[11],
        )
        yield both(place, count, lambda s: td.at[s], lambda c, s: dots.at[c, s], lambda c: dots.at[c])
        yield later(exchange(place, count, lambda s: strips.at(sg, s), lambda s: sg_all.at[s]), 8)

    mixture, summed_back, dots_all, shared_back = transfer(
        "scatter_both",
        3,
        mesh,
        fourth_body,
        (
            left_forward,
            exp_low,
            fixed_forward,
            left_backward,
            back_rows,
            fixed_backward,
            token_dots,
            strips.cut(shared_grads),
        ),
        (
            like((rows, width)),
            like((rows, width)),
            like((cores, count, 8, rows), f32),
            like((count, pack_rows, deep)),
        ),
        scatter_scratch(
            count,
            cores,
            rows,
            part,
            [(left_forward.shape[1], True), (left_backward.shape[1], True)],
        )
        + [pltpu.SemaphoreType.REGULAR((count * (cores - 1),))],
        vmem=60 * 2**20,
    )
    output = (hidden + mixture.astype(f32)).astype(bf16)

    gate_total = jnp.sum(dots_all[:, :, 0, :], axis=0).T
    weighted_dots = jnp.sum(gates * gate_total, axis=1, keepdims=True)
    grad_logits = gates * (gate_total - weighted_dots)

    down_grad = mm("rf,rd->fd", exp_act, gated_grad)
    gate_grad = mm("rd,rf->df", received, gate_back)
    up_grad = mm("rd,rf->df", received, up_back)
    cotangent = out_grad.astype(f32)
    grad_two = summed_back.astype(f32) + jnp.einsum(
        "te,ed->td", grad_logits, router_full.astype(f32), precision=highest
    )
    scaled = grad_two * ffn_gain
    inner = jnp.mean(scaled * hidden, axis=-1, keepdims=True)
    grad_hidden = cotangent + rstd_two * scaled - hidden * (rstd_two * rstd_two * rstd_two) * inner
    ffn_gain_part = jnp.sum(grad_two * hidden * rstd_two, axis=0)
    grad_branch = grad_hidden.astype(bf16)
    grad_heads = mm("td,cd->tc", grad_branch, out_full).astype(bf16)
    out_proj_part = mm("tc,td->cd", heads_out, grad_branch).astype(bf16)

    turns = count // heads

    def spread(vector):
        return jnp.pad(vector.reshape(count, 1, deep), ((0, 0), (0, 7), (0, 0)))

    if strips.direct:

        def back_body(place, given, made, room):
            gh, gl, op, fg, qkv_s, pr, ct, st, xn, wt = given
            one, qg_all, op_sum, ag_all, fg_all, logit_all = made
            qkv_v, pr_v, ct_v, st_v, gh_v, held, sums, grad_qkv, right, gains, blocks = room[14:]
            own = lax.rem(place.e, heads)
            moves = [place.keep(x, y) for x, y in ((qkv_s, qkv_v), (pr, pr_v), (ct, ct_v), (st, st_v), (wt, right))]
            arrived, finish = start_exchange(
                place, heads, lambda s: gh.at[:, lanes(s, HEAD_DIM)], lambda s: gh_v.at[s]
            )
            one_view = part_view(one, rows, part)

            def fetch(d):
                slot = lax.rem(own + d, heads)
                source = xn.at[pl.ds(pl.multiple_of(slot * rows, rows), rows), :]
                return place.keep(source, held.at[d % 2])

            def main():
                coming = fetch(0)
                for move in moves:
                    move.wait()
                for d in range(heads):
                    now, slot = coming, lax.rem(own + d, heads)
                    if d + 1 < heads:
                        coming = fetch(d + 1)
                    if d > 0:
                        arrived(slot)
                    now.wait()
                    attend_back(
                        held.at[d % 2], (qkv_v, pr_v, ct_v, st_v, gh_v, grad_qkv, sums), slot, rows, d == 0
                    )
                    yield
                tail()
                yield
                kept = Kept(grad_qkv, right, rows)
                yield from scatter(place, heads, [kept], room[:7], [lambda c: one_view(0, c)], (rows, part), True)

            def tail():
                ones = jnp.ones((8, 3 * HEAD_DIM), f32)

                def body(at, carry):
                    block = sums[:, lanes(at, deep)].T
                    blocks[at] = block.astype(bf16)
                    weights = right[pl.ds(pl.multiple_of(at * deep, deep), deep), :].astype(f32)
                    gains[:, lanes(at, deep)] = dot(ones, block * weights, ((1,), (1,)), highest)
                    return carry

                lax.fori_loop(0, count, body, 0)
                for which in range(3):

                    def landing(slot, which=which):
                        return qg_all.at[which, lax.div(slot, heads), :, lanes(lax.rem(slot, heads), HEAD_DIM)]

                    def block(slot, which=which):
                        return blocks.at[slot, :, pl.ds(which * HEAD_DIM, HEAD_DIM)]

                    tasks.append(exchange(place, count, block, landing))
                tasks.append(
                    both(
                        place,
                        count,
                        lambda s: gains.at[:, lanes(s, deep)],
                        lambda c, s: ag_all.at[c, s],
                        lambda c: ag_all.at[c],
                    )
                )

            projection = scatter(
                place, count, [lambda s: strips.at(op, s)], room[7:14], [lambda c: op_sum], (out_rows, deep), False
            )
            tasks = [
                main(),
                twice(projection),
                exchange(place, count, lambda s: gl, lambda s: logit_all.at[s]),
                exchange(place, count, lambda s: fg.at[s], lambda s: fg_all.at[s]),
            ]
            yield tasks
            finish()

        grad_one, qkv_all, out_proj_sum, attn_gains, ffn_gains, logits_all = transfer(
            "attention_back",
            4,
            mesh,
            back_body,
            (
                grad_heads,
                grad_logits.T,
                out_proj_part,
                spread(ffn_gain_part),
                qkv_saved,
                probs_saved,
                cosine_wide,
                sine_wide,
                xn_chunk,
                w_qkv,
            ),
            (
                like((rows, width)),
                like((3, turns, deep, heads * HEAD_DIM)),
                like((out_rows, deep)),
                like((cores, count, 8, deep), f32),
                like((count, 8, deep), f32),
                like((count, experts, rows), f32),
            ),
            scatter_scratch(heads, cores, rows, part)
            + scatter_scratch(count, 1, out_rows, deep)
            + [
                pltpu.VMEM((chunk, 3 * HEAD_DIM), bf16),
                pltpu.VMEM((chunk, rows), f32),
                pltpu.VMEM((chunk, HEAD_DIM), f32),
                pltpu.VMEM((chunk, HEAD_DIM), f32),
                pltpu.VMEM((heads, rows, HEAD_DIM), bf16),
                pltpu.VMEM((2, rows, width), bf16),
                pltpu.VMEM((3 * HEAD_DIM, width), f32),
                pltpu.VMEM((chunk, 3 * HEAD_DIM), bf16),
                pltpu.VMEM((width, 3 * HEAD_DIM), bf16),
                pltpu.VMEM((8, width), f32),
                pltpu.VMEM((count, deep, 3 * HEAD_DIM), bf16),
            ],
            semaphores=640,
            vmem=56 * 2**20,
        )
    else:
        def fifth_body(place, given, made, room):
            gl, logit_all = given[1], made[1]
            yield exchange(place, count, lambda s: gl, lambda s: logit_all.at[s])
            yield exchange(place, heads, lambda s: given[0].at[:, lanes(s, HEAD_DIM)], lambda s: made[0].at[s])

        grad_head, logits_all = transfer(
            "exchange_heads",
            4,
            mesh,
            fifth_body,
            (grad_heads, grad_logits.T),
            (like((heads, rows, HEAD_DIM)), like((count, experts, rows), f32)),
        )
        grad_value = mm("gqk,gqd->gkd", probs_low, grad_head)
        grad_probs = mm("gqd,gkd->gqk", grad_head, valued)
        weighted = jnp.sum(probs * grad_probs, axis=-1, keepdims=True)
        grad_scores = (probs * (grad_probs - weighted)).astype(bf16)
        grad_query = mm("gqk,gkd->gqd", grad_scores, keyed) * scale
        grad_key = mm("gqk,gqd->gkd", grad_scores, query) * scale
        grad_qkv = jnp.concatenate(
            [
                rotary_back(grad_query, cosine, sine).astype(bf16),
                rotary_back(grad_key, cosine, sine).astype(bf16),
                grad_value.astype(bf16),
            ],
            axis=2,
        ).reshape(chunk, 3 * HEAD_DIM)
        qkv_grad = mm("td,tc->dc", xn_chunk, grad_qkv)
        attn_gain_part = jnp.sum(qkv_grad * w_qkv.astype(f32), axis=1)
        qkv_grad = qkv_grad.astype(bf16)

        def sixth_body(place, given, made, room):
            gq, wq, qg, op, ag, fg = given
            one, qg_all, op_sum, ag_all, fg_all = made
            one_view = part_view(one, rows, part)
            made_here = Product(place, gq, None, wq, room[7:9], heads, rows, part)
            yield scatter(place, heads, [made_here], room[:7], [lambda c: one_view(0, c)], (rows, part), True)
            yield scatter(
                place, count, [lambda s: strips.at(op, s)], room[9:], [lambda c: op_sum], (out_rows, deep), False
            )
            yield both(place, count, lambda s: ag.at[s], lambda c, s: ag_all.at[c, s], lambda c: ag_all.at[c])
            yield exchange(place, count, lambda s: fg.at[s], lambda s: fg_all.at[s])
            for which in range(3):

                def source(slot, which=which):
                    at = pl.ds(pl.multiple_of(slot * deep, deep), deep)
                    return qg.at[at, pl.ds(which * HEAD_DIM, HEAD_DIM)]

                def landing(slot, which=which):
                    return qg_all.at[which, lax.div(slot, heads), :, lanes(lax.rem(slot, heads), HEAD_DIM)]

                yield later(exchange(place, count, source, landing), 6)

        grad_one, qkv_all, out_proj_sum, attn_gains, ffn_gains = transfer(
            "scatter_grads",
            5,
            mesh,
            sixth_body,
            (
                grad_qkv,
                w_qkv.T,
                qkv_grad,
                strips.cut(out_proj_part),
                spread(attn_gain_part),
                spread(ffn_gain_part),
            ),
            (
                like((rows, width)),
                like((3, turns, deep, heads * HEAD_DIM)),
                like((out_rows, deep)),
                like((cores, count, 8, deep), f32),
                like((count, 8, deep), f32),
            ),
            scatter_scratch(heads, cores, rows, part, [(3 * HEAD_DIM, False)])
            + scatter_scratch(count, 1, out_rows, deep),
            semaphores=600,
            vmem=56 * 2**20,
        )

    xn_columns = lax.dynamic_slice_in_dim(xn_all, e * deep, deep, axis=1).astype(f32).reshape(count, rows, deep)
    router_grad = jnp.einsum("gtd,get->de", xn_columns, logits_all, precision=highest)
    grad_one = grad_one.astype(f32)
    rstd_one = lax.rsqrt(jnp.mean(inputs * inputs, axis=-1, keepdims=True) + eps)
    scaled_one = grad_one * attn_gain
    inner_one = jnp.mean(scaled_one * inputs, axis=-1, keepdims=True)
    input_grad = (
        grad_hidden + rstd_one * scaled_one - inputs * (rstd_one * rstd_one * rstd_one) * inner_one
    ).astype(bf16)

    def of_heads(which):
        return jnp.sum(qkv_all[which].astype(f32), axis=0)

    def of_shared(which):
        return shared_back[:, which * hidden_units : (which + 1) * hidden_units].reshape(-1, deep).astype(f32)

    return (
        output,
        input_grad,
        jnp.sum(attn_gains[:, :, 0, :], axis=(0, 1)) / gain_attn.astype(f32),
        of_heads(0),
        of_heads(1),
        of_heads(2),
        out_proj_sum.astype(f32),
        jnp.sum(ffn_gains[:, 0, :], axis=0),
        router_grad,
        gate_grad[None],
        up_grad[None],
        down_grad[None],
        of_shared(0).T,
        of_shared(1).T,
        of_shared(2),
    )


def solution(mesh):
    in_specs = (
        P("expert", None),
        P("expert", None),
        P("expert", None),
        P("expert"),
        P("expert", "tensor"),
        P("expert", "tensor"),
        P("expert", "tensor"),
        P("tensor", "expert"),
        P("expert"),
        P("expert", None),
        P("expert", None, "tensor"),
        P("expert", None, "tensor"),
        P("expert", "tensor", None),
        P("expert", "tensor"),
        P("expert", "tensor"),
        P("tensor", "expert"),
        P("expert", None),
    )
    out_specs = (
        P("expert", None),
        P("expert", None),
        P("expert"),
        P("expert", "tensor"),
        P("expert", "tensor"),
        P("expert", "tensor"),
        P("tensor", "expert"),
        P("expert"),
        P("expert", None),
        P("expert", None, "tensor"),
        P("expert", None, "tensor"),
        P("expert", "tensor", None),
        P("expert", "tensor"),
        P("expert", "tensor"),
        P("tensor", "expert"),
    )
    return jax.shard_map(
        functools.partial(local, mesh), mesh=mesh, in_specs=in_specs, out_specs=out_specs, check_vma=False
    )
```

```python
import functools

import jax
import jax.numpy as jnp
from jax import lax
from jax.experimental import pallas as pl
from jax.experimental.pallas import tpu as pltpu
from jax.sharding import PartitionSpec as P

HEAD_DIM = 128
TOP = 6
MESH = pl.DeviceIdType.MESH
ANY = pl.BlockSpec(memory_space=pl.ANY)

bf16 = jnp.bfloat16
f32 = jnp.float32
eps = 1e-06
highest = lax.Precision.HIGHEST
floor_score = -1e30


class Place:
    def __init__(self, sems, count, cores):
        self.sems, self.used = sems, 0
        self.count, self.cores = count, cores
        self.e = lax.axis_index("expert")
        self.t = lax.axis_index("tensor")
        self.quad = lax.rem(self.e, 4)
        self.far = lax.div(self.e, 4)

    def take(self, number):
        first = self.used
        self.used = first + number
        return first

    def ring(self, distance):
        return lax.rem(self.t + distance, self.cores)

    def copy(self, src, dst, out_sem, in_sem, e, t):
        return pltpu.make_async_remote_copy(
            src_ref=src,
            dst_ref=dst,
            send_sem=self.sems.at[out_sem],
            recv_sem=self.sems.at[in_sem],
            device_id={"expert": e, "tensor": t},
            device_id_type=MESH,
        )

    def send(self, src, dst, out_sem, in_sem, e, t):
        move = self.copy(src, dst, out_sem, in_sem, e, t)
        move.start()
        return move

    def arrived(self, landing, in_sem):
        self.copy(landing, landing, in_sem, in_sem, self.e, self.t).wait_recv()

    def keep(self, src, dst):
        move = pltpu.make_async_copy(src, dst, self.sems.at[self.take(1)])
        move.start()
        return move

    def local(self, src, dst, sem):
        return pltpu.make_async_copy(src, dst, self.sems.at[sem])

    def meet(self):
        barrier = pltpu.get_barrier_semaphore()
        for step in range(1, self.count):
            pl.semaphore_signal(
                barrier,
                inc=1,
                device_id={"expert": lax.rem(self.e + step, self.count), "tensor": self.t},
                device_id_type=MESH,
            )
        for step in range(1, self.cores):
            pl.semaphore_signal(
                barrier,
                inc=1,
                device_id={"expert": self.e, "tensor": self.ring(step)},
                device_id_type=MESH,
            )
        pl.semaphore_wait(barrier, self.count + self.cores - 2)


class Block:
    def __init__(self, place, members):
        self.place, self.deep = place, members // 4
        self.rank = lax.rem(place.far, self.deep)
        self.start = place.far - self.rank

    def flips(self, order):
        high, low = lax.div(self.place.quad, 2), lax.rem(self.place.quad, 2)
        one = high + (low - high) * order
        two = low + (high - low) * order
        return (2 - order) * (1 - 2 * one), (1 + order) * (1 - 2 * two)

    def slot(self, k, i, j, order):
        one, two = self.flips(order)
        return lax.rem(self.rank + k, self.deep) * 4 + self.place.quad + i * one + j * two

    def own(self):
        return self.rank * 4 + self.place.quad

    def device(self, slot):
        return self.start * 4 + slot


class Gather:
    def __init__(self, place, members, mine, whole, view, halves, pieces=1):
        self.place, self.block = place, Block(place, members)
        self.mine, self.whole, self.view, self.pieces = mine, whole, view, pieces
        self.deep, self.order = self.block.deep, lax.rem(place.t, 2)
        self.cores = place.cores if halves else 1
        self.zs, self.zr = self.lots(2), self.lots(1)
        self.s2, self.r2 = self.lots(1), self.lots(1)
        self.s3, self.r3 = self.lots(2), self.lots(2)
        self.s4, self.r4 = self.lots(4 * (self.cores - 1)), self.lots(4 * (self.cores - 1))
        self.sent, self.closing = [], False

    def lots(self, number):
        return self.place.take(number * self.deep * self.pieces)

    def near(self, n):
        rank, deep = self.block.rank, self.deep
        if isinstance(n, int) and n == 0:
            return rank
        low = jnp.minimum(rank, deep - 1 - rank)
        if isinstance(n, int):
            paired = rank - (n + 1) // 2 if n % 2 else rank + n // 2
        else:
            paired = rank + jnp.where(lax.rem(n, 2) == 1, -lax.div(n + 1, 2), lax.div(n, 2))
        single = jnp.where(rank < deep - 1 - rank, rank + (n - low), rank - (n - low))
        return jnp.where(n <= 2 * low, paired, single)

    def slot(self, n, i, j, order=None):
        one, two = self.block.flips(self.order if order is None else order)
        return self.near(n) * 4 + self.place.quad + i * one + j * two

    def index(self, n, kind, kinds, p):
        return (self.near(n) * kinds + kind) * self.pieces + p

    def pass_on(self, source, landing, out, into, at, e, t, condition=None):
        move = self.place.copy(source, landing, out + at[0], into + at[1], e, t)
        if self.closing:
            when(condition, move.wait_send)
            return
        self.sent.append((condition, move))
        when(condition, move.start)

    def along(self, n, p, source, landing):
        rank, e = self.block.rank, self.place.e
        near = self.near(n)
        for way in (1, -1):
            fits = rank < self.deep - 1 if way > 0 else rank >= 1
            if not isinstance(n, int) or n > 0:
                fits = jnp.logical_and(fits, near < rank if way > 0 else near > rank)
            out = self.index(n, 0 if way > 0 else 1, 2, p)
            into = self.index(n, 0, 1, p)
            self.pass_on(source, landing, self.zs, self.zr, (out, into), e + 4 * way, self.place.t, fits)

    def across(self, n, i, p, source, landing):
        one, two = self.block.flips(self.order)
        e, t = self.place.e, self.place.t
        if i == 0:
            at = self.index(n, 0, 1, p)
            self.pass_on(source, landing, self.s2, self.r2, (at, at), e + one, t)
        at = self.index(n, i, 2, p)
        self.pass_on(source, landing, self.s3, self.r3, (at, at), e + two, t)

    def share(self, n, i, j, p):
        ref = self.view(self.slot(n, i, j), self.place.t, p)
        for far in range(1, self.cores):
            kind = (far - 1) * 4 + i * 2 + j
            at = self.index(n, kind, 4 * (self.cores - 1), p)
            self.pass_on(ref, ref, self.s4, self.r4, (at, at), self.place.e, self.place.ring(far))

    def start(self, p):
        if p == 0:
            self.kept = self.place.keep(self.whole[0], self.whole[1](self.block.own()))
        source, landing = self.mine(p), self.view(self.block.own(), self.place.t, p)
        if self.deep > 1:
            self.along(0, p, source, landing)
        self.across(0, 0, p, source, landing)

    def from_line(self, n, p):
        ref = self.view(self.slot(n, 0, 0), self.place.t, p)
        self.place.arrived(ref, self.zr + self.index(n, 0, 1, p))
        if self.deep > 2:
            self.along(n, p, ref, ref)
        self.across(n, 0, p, ref, ref)
        self.share(n, 0, 0, p)

    def from_one(self, n, p):
        ref = self.view(self.slot(n, 1, 0), self.place.t, p)
        self.place.arrived(ref, self.r2 + self.index(n, 0, 1, p))
        self.across(n, 1, p, ref, ref)
        self.share(n, 1, 0, p)

    def from_two(self, n, i, p):
        ref = self.view(self.slot(n, i, 1), self.place.t, p)
        self.place.arrived(ref, self.r3 + self.index(n, i, 2, p))
        self.share(n, i, 1, p)

    def from_cores(self, n, i, j):
        if i + j == 0 and isinstance(n, int) and n == 0:
            return
        if i + j == 0 and not isinstance(n, int):
            pl.when(n > 0)(lambda: self.of_cores(n, i, j))
        else:
            self.of_cores(n, i, j)

    def of_cores(self, n, i, j):
        for far in range(1, self.cores):
            source = self.place.ring(self.cores - far)
            first, second = (j, i) if far % 2 else (i, j)
            kind = (far - 1) * 4 + first * 2 + second
            for p in range(self.pieces):
                ref = self.view(self.slot(n, i, j), source, p)
                self.place.arrived(ref, self.r4 + self.index(n, kind, 4 * (self.cores - 1), p))

    def finish(self):
        for condition, move in self.sent:
            when(condition, move.wait_send)

    def close(self):
        self.closing = True
        for p in range(self.pieces):
            source, landing = self.mine(p), self.view(self.block.own(), self.place.t, p)
            self.along(0, p, source, landing)
            self.across(0, 0, p, source, landing)
            for n in range(self.deep):
                if n > 0:
                    ref = self.view(self.slot(n, 0, 0), self.place.t, p)
                    self.along(n, p, ref, ref)
                    self.across(n, 0, p, ref, ref)
                    self.share(n, 0, 0, p)
                ref = self.view(self.slot(n, 1, 0), self.place.t, p)
                self.across(n, 1, p, ref, ref)
                self.share(n, 1, 0, p)
                self.share(n, 0, 1, p)
                self.share(n, 1, 1, p)

    def links(self):
        for p in range(self.pieces):
            self.start(p)
            yield
        for n in range(1, self.deep + 1):
            for p in range(self.pieces):
                self.from_one(n - 1, p)
                yield
                if n < self.deep:
                    self.from_line(n, p)
                    yield

    def last(self, n):
        for i in range(2):
            for p in range(self.pieces):
                self.from_two(n, i, p)

    def all(self):
        yield from self.links()
        for n in range(self.deep):
            self.last(n)
            yield
        for n in range(self.deep):
            for i in range(2):
                for j in range(2):
                    self.from_cores(n, i, j)
        self.finish()
        self.kept.wait()


def when(condition, action):
    if condition is None:
        action()
    else:
        pl.when(condition)(action)


def gather(place, members, mine, whole, view, halves, pieces=1):
    return Gather(place, members, mine, whole, view, halves, pieces).all()


class Kept:
    def __init__(self, left, right, rows):
        self.left, self.right, self.rows, self.slots = left, right, rows, {}

    def fetch(self, turn, slot):
        self.slots[turn] = pl.ds(pl.multiple_of(slot * self.rows, self.rows), self.rows)

    def ready(self, turn):
        pass

    def make(self, turn, core, target):
        columns = target.shape[1]
        wide = min(columns, 512)

        def body(tile, carry):
            source = pl.ds(pl.multiple_of(core * columns + tile * wide, wide), wide)
            into = pl.ds(pl.multiple_of(tile * wide, wide), wide)
            target[:, into] = dot(self.left[self.slots[turn], :], self.right[source, :], ((1,), (1,))).astype(bf16)
            return carry

        lax.fori_loop(0, columns // wide, body, 0)


def dot(left, right, sides=((1,), (0,)), precision=None):
    return lax.dot_general(left, right, (sides, ((), ())), precision=precision, preferred_element_type=f32)


def attend(tokens, gain, weights, first, position_rows, rooms, at, slot, rows):
    normed, qkv, probs, cosines, sines, out, inverse = rooms
    own = pl.ds(pl.multiple_of(slot * rows, rows), rows)

    def norm(piece_at, carry):
        source = pl.ds(pl.multiple_of(slot * rows + piece_at * 16, 16), 16)
        values = tokens[source, :].astype(f32)
        rstd = lax.rsqrt(jnp.mean(values * values, axis=1, keepdims=True) + eps)
        normed[at, pl.ds(pl.multiple_of(piece_at * 16, 16), 16), :] = (values * rstd * gain).astype(bf16)
        return carry

    lax.fori_loop(0, rows // 16, norm, 0)
    half = HEAD_DIM // 2
    angles = (position_rows - first) * inverse[...]
    lane = lax.broadcasted_iota(jnp.int32, (rows, HEAD_DIM), 1)
    cosine, sine = jnp.cos(angles), jnp.sin(angles)
    sine = jnp.where(lane < half, -sine, sine)
    cosines[own, :] = cosine
    sines[own, :] = sine
    lin = dot(normed[at], weights[...])

    def turn(values):
        return (values * cosine + pltpu.roll(values, half, 1) * sine).astype(bf16)

    query, keyed = turn(lin[:, :HEAD_DIM]), turn(lin[:, HEAD_DIM : 2 * HEAD_DIM])
    valued = lin[:, 2 * HEAD_DIM :].astype(bf16)
    qkv[own, :HEAD_DIM] = query
    qkv[own, HEAD_DIM : 2 * HEAD_DIM] = keyed
    qkv[own, 2 * HEAD_DIM :] = valued
    key_at = lax.broadcasted_iota(jnp.int32, (rows, rows), 1).astype(f32)
    query_at = lax.broadcasted_iota(jnp.int32, (rows, rows), 0).astype(f32)
    allowed = (key_at <= query_at) & (key_at >= first[:, :1])
    scores = jnp.where(allowed, dot(query, keyed, ((1,), (1,))) * (HEAD_DIM ** (-0.5)), floor_score)
    raised = jnp.exp(scores - jnp.max(scores, axis=1, keepdims=True))
    chances = raised / jnp.sum(raised, axis=1, keepdims=True)
    probs[own, :] = chances
    out[slot] = dot(chances.astype(bf16), valued).astype(bf16)


def attend_back(normed, rooms, slot, rows, start):
    qkv, probs, cosines, sines, grads, grad_qkv, sums = rooms
    own = pl.ds(pl.multiple_of(slot * rows, rows), rows)
    query = qkv[own, :HEAD_DIM]
    keyed = qkv[own, HEAD_DIM : 2 * HEAD_DIM]
    valued = qkv[own, 2 * HEAD_DIM :]
    cosine, sine = cosines[own, :], sines[own, :]
    chances, grad = probs[own, :], grads[slot]
    scale = HEAD_DIM ** (-0.5)

    def turn_back(values):
        return (values * cosine - pltpu.roll(values, HEAD_DIM // 2, 1) * sine).astype(bf16)

    grad_qkv[own, 2 * HEAD_DIM :] = dot(chances.astype(bf16), grad, ((0,), (0,))).astype(bf16)
    grad_chances = dot(grad, valued, ((1,), (1,)))
    weighted = jnp.sum(chances * grad_chances, axis=1, keepdims=True)
    grad_scores = (chances * (grad_chances - weighted)).astype(bf16)
    grad_qkv[own, :HEAD_DIM] = turn_back(dot(grad_scores, keyed) * scale)
    grad_qkv[own, HEAD_DIM : 2 * HEAD_DIM] = turn_back(dot(grad_scores, query, ((0,), (0,))) * scale)
    wide = 512

    def body(tile, carry):
        into = pl.ds(pl.multiple_of(tile * wide, wide), wide)
        product = dot(grad_qkv[own, :], normed[:, into], ((0,), (0,)))
        sums[:, into] = product if start else sums[:, into] + product
        return carry

    lax.fori_loop(0, sums.shape[1] // wide, body, 0)


def add_up(target, sources, rows, columns):
    step = max(16, min(rows, 16384 // columns // 16 * 16))

    def body(at, carry):
        piece = pl.ds(pl.multiple_of(at * step, step), step)
        total = sources[0][piece, :].astype(f32)
        for other in sources[1:]:
            total = total + other[piece, :].astype(f32)
        target[piece, :] = total.astype(target.dtype)
        return carry

    lax.fori_loop(0, rows // step, body, 0)


class Product:
    def __init__(self, place, left, varied, fixed, rooms, members, rows, columns):
        self.place, self.left, self.varied = place, left, varied
        self.lhs, self.rhs = rooms
        self.rows, self.columns = rows, columns
        self.lead = 0 if varied is None else varied.shape[0] // members
        self.waits, self.turn = {}, 0
        self.setup = []
        for buffer in range(self.rhs.shape[0]):
            self.setup.append(place.keep(fixed, self.rhs.at[buffer, pl.ds(self.lead, fixed.shape[0]), :]))

    def fetch(self, turn, slot):
        buffer = turn % 2
        rows = pl.ds(pl.multiple_of(slot * self.rows, self.rows), self.rows)
        moves = [self.place.keep(self.left.at[rows, :], self.lhs.at[buffer])]
        if self.lead:
            lead = pl.ds(pl.multiple_of(slot * self.lead, self.lead), self.lead)
            moves.append(self.place.keep(self.varied.at[lead, :], self.rhs.at[buffer, pl.ds(0, self.lead), :]))
        self.waits[turn] = moves

    def ready(self, turn):
        for move in self.setup:
            move.wait()
        self.setup = []
        for move in self.waits.pop(turn):
            move.wait()

    def make(self, turn, core, target):
        buffer = turn % 2
        right = self.rhs.at[buffer if self.lead else 0]
        wide = min(self.columns, 512)

        def body(at, carry):
            source = pl.ds(pl.multiple_of(core * self.columns + at * wide, wide), wide)
            into = pl.ds(pl.multiple_of(at * wide, wide), wide)
            target[:, into] = jnp.dot(
                self.lhs[buffer], right[:, source], preferred_element_type=f32
            ).astype(bf16)
            return carry

        lax.fori_loop(0, self.columns // wide, body, 0)


def scatter(place, members, sources, room, views, shape, halves, credit=None):
    block = Block(place, members)
    deep, e, t = block.deep, place.e, place.t
    rows, columns = shape
    order = 1 - lax.rem(t, 2)
    cores = place.cores if halves else 1
    count = len(sources)
    mine, outgoing, land0, land1s, land2s, land3s, finals = room
    s0, r0 = place.take(4 * deep * cores * count), place.take(4 * deep * cores * count)
    s1, r1 = place.take(2 * deep * count), place.take(2 * deep * count)
    s2, r2 = place.take(deep * count), place.take(deep * count)
    s3, r3 = place.take(deep * count), place.take(deep * count)
    s4, r4 = place.take(cores * count), place.take(cores * count)
    walk = [(f, k) for f in range(count) for k in list(range(1, deep)) + [0]]
    one, two = block.flips(order)
    sent, loads, last, kept = [], {}, {}, []
    quads = [(1, 1), (1, 0), (0, 1), (0, 0)]
    turns = [(f, k, i, j) for f, k in walk for i, j in quads]
    ring = outgoing.shape[0]
    leaving = []

    def slot_of(k, i, j):
        return block.slot(k, i, j, order)

    def land_index(d, k, i, j):
        return (d - 1) * deep * 4 + k * 4 + i * 2 + j

    def produce(number):
        f, k, i, j = turns[number]
        source = sources[f]
        if (k, i, j) in last:
            last.pop((k, i, j)).wait_send()
        if not isinstance(source, (Product, Kept)):
            loads[f, k, i, j] = place.keep(source(slot_of(k, i, j)), mine.at[slot_of(k, i, j)])
            return
        local_number = number - f * 4 * deep
        if local_number == 0:
            source.fetch(0, slot_of(k, i, j))
        source.ready(local_number)
        if local_number + 1 < 4 * deep:
            source.fetch(local_number + 1, slot_of(*turns[number + 1][1:]))
        if number >= ring:
            for move in leaving[number - ring]:
                move.wait_send()
        moves = []
        for d in range(1, cores):
            target = place.ring(d)
            buffer = outgoing.at[number % ring, d - 1]
            source.make(local_number, target, buffer)
            at = land_index(d, k, *((j, i) if d % 2 else (i, j)))
            if f > 0:
                pl.semaphore_wait(credit.at[at], 1)
            sem = f * 4 * deep * cores + at
            moves.append(place.send(buffer, land0.at[at], s0 + sem, r0 + sem, e, target))
        leaving.append(moves)
        source.make(local_number, t, mine.at[slot_of(k, i, j)])

    def terms_of(f, k, i, j):
        if (f, k, i, j) in loads:
            loads[f, k, i, j].wait()
        terms = [mine.at[slot_of(k, i, j)]]
        for d in range(1, cores):
            at = land_index(d, k, i, j)
            place.arrived(land0.at[at], r0 + f * 4 * deep * cores + at)
            terms.append(land0.at[at])
        if i == 0:
            at = (f * deep + k) * 2 + j
            place.arrived(land1s.at[at], r1 + at)
            terms.append(land1s.at[at])
            if j == 0:
                at = f * deep + k
                place.arrived(land2s.at[at], r2 + at)
                terms.append(land2s.at[at])
        return terms

    def give_back(f, k, i, j):
        if f + 1 < count:
            for d in range(1, cores):
                pl.semaphore_signal(
                    credit.at[land_index(d, k, i, j)],
                    inc=1,
                    device_id={"expert": e, "tensor": place.ring(cores - d)},
                    device_id_type=MESH,
                )

    def leave(f, k, i, j, landing, out, into, at, target):
        move = place.send(mine.at[slot_of(k, i, j)], landing.at[at], out + at, into + at, target, t)
        last[k, i, j] = move

    def first_flip(f, k, j):
        terms, ref = terms_of(f, k, 1, j), mine.at[slot_of(k, 1, j)]
        if len(terms) > 1:
            add_up(ref, terms, rows, columns)
        give_back(f, k, 1, j)
        leave(f, k, 1, j, land1s, s1, r1, (f * deep + k) * 2 + j, e + one)

    def second_flip(f, k):
        add_up(mine.at[slot_of(k, 0, 1)], terms_of(f, k, 0, 1), rows, columns)
        give_back(f, k, 0, 1)
        leave(f, k, 0, 1, land2s, s2, r2, f * deep + k, e + two)

    def line(f, k):
        terms, ref = terms_of(f, k, 0, 0), mine.at[slot_of(k, 0, 0)]
        if k > 0:
            add_up(ref, terms, rows, columns)
            give_back(f, k, 0, 0)
            peer = block.device(lax.rem(block.rank + k, deep) * 4 + place.quad)
            leave(f, k, 0, 0, land3s, s3, r3, f * deep + k, peer)
            return
        for far in range(1, deep):
            place.arrived(land3s.at[f * deep + far], r3 + f * deep + far)
            terms.append(land3s.at[f * deep + far])
        final = finals.at[f]
        add_up(final, terms, rows, columns)
        give_back(f, k, 0, 0)
        kept.append(place.keep(final, views[f](t)))
        for d in range(1, cores):
            at = f * cores + d
            sent.append(place.send(final, views[f](t), s4 + at, r4 + at, e, place.ring(d)))

    for step in range(len(walk) + 2):
        fresh = step < len(walk)
        if fresh:
            produce(4 * step)
            yield
            produce(4 * step + 1)
            yield
            first_flip(*walk[step], 1)
            yield
            produce(4 * step + 2)
            yield
        if 0 <= step - 1 < len(walk):
            second_flip(*walk[step - 1])
            yield
        if fresh:
            produce(4 * step + 3)
            yield
            first_flip(*walk[step], 0)
            yield
        if 0 <= step - 2 < len(walk):
            line(*walk[step - 2])
            yield
    for f in range(count):
        for d in range(1, cores):
            place.arrived(views[f](place.ring(cores - d)), r4 + f * cores + d)
    for moves in leaving[-ring:]:
        for move in moves:
            move.wait_send()
    for move in list(last.values()) + sent:
        move.wait_send()
    for move in kept:
        move.wait()


def scatter_scratch(members, cores, rows, columns, products=(), ring=4):
    deep = members // 4
    count = max(1, len(products))
    short = rows if cores > 1 else 16
    rooms = [
        pltpu.VMEM((members, rows, columns), bf16),
        pltpu.VMEM((ring, max(1, cores - 1), short, columns), bf16),
        pltpu.VMEM((max(1, (cores - 1) * members), short, columns), bf16),
        pltpu.VMEM((2 * deep * count, rows, columns), bf16),
        pltpu.VMEM((deep * count, rows, columns), bf16),
        pltpu.VMEM((deep * count, rows, columns), bf16),
        pltpu.VMEM((count, rows, columns), bf16),
    ]
    for depth, varied in products:
        rooms.append(pltpu.VMEM((2, rows, depth), bf16))
        rooms.append(pltpu.VMEM((2 if varied else 1, depth, columns * cores), bf16))
    return rooms


def exchange(place, members, source, landing):
    e, t = place.e, place.t
    own = lax.rem(e, members)
    base = e - own
    sends, arrivals = place.take(members), place.take(members)
    sent = []
    for d in range(1, members):
        target = lax.rem(own + d, members)
        sent.append(place.send(source(target), landing(own), sends + d, arrivals + d, base + target, t))
    kept = place.keep(source(own), landing(own))
    yield
    for d in range(1, members):
        place.arrived(landing(lax.rem(own + members - d, members)), arrivals + d)
    for move in sent:
        move.wait_send()
    kept.wait()


def start_exchange(place, members, source, landing):
    e, t = place.e, place.t
    own = lax.rem(e, members)
    base = e - own
    sends, arrivals = place.take(members), place.take(members)
    sent = []
    for d in range(1, members):
        target = lax.rem(own + d, members)
        sent.append(place.send(source(target), landing(own), sends + target, arrivals + own, base + target, t))
    place.keep(source(own), landing(own)).wait()

    def arrived(slot):
        pl.when(slot != own)(lambda: place.arrived(landing(slot), arrivals + slot))

    def finish():
        for move in sent:
            move.wait_send()

    return arrived, finish


def both(place, members, source, landing, part):
    yield from exchange(place, members, source, lambda slot: landing(place.t, slot))
    sends, arrivals = place.take(place.cores), place.take(place.cores)
    sent = []
    for d in range(1, place.cores):
        mine = part(place.t)
        sent.append(place.send(mine, mine, sends + d, arrivals + d, place.e, place.ring(d)))
    yield
    for d in range(1, place.cores):
        place.arrived(part(place.ring(place.cores - d)), arrivals + d)
    for move in sent:
        move.wait_send()


def twice(task):
    for _ in task:
        next(task, None)
        yield


def later(task, rounds):
    for _ in range(rounds):
        yield
    yield from task


def run(tasks):
    while tasks:
        for task in list(tasks):
            try:
                next(task)
            except StopIteration:
                tasks.remove(task)


def transfer(name, number, mesh, body, ins, outs, scratch=(), semaphores=400, vmem=None):
    count, cores = mesh.shape["expert"], mesh.shape["tensor"]
    semaphores = semaphores * max(1, count * cores // 32)

    def kernel(*refs):
        given = refs[: len(ins)]
        made = refs[len(ins) : len(ins) + len(outs)]
        room = refs[len(ins) + len(outs) : -1]
        place = Place(refs[-1], count, cores)
        place.meet()
        tasks = []
        for task in body(place, given, made, room):
            if isinstance(task, list):
                run(task)
            else:
                tasks.append(task)
        run(tasks)
        assert place.used <= semaphores, place.used

    size = sum(x.size * x.dtype.itemsize for x in list(ins) + list(outs))
    return pl.pallas_call(
        kernel,
        name=name,
        out_shape=[jax.ShapeDtypeStruct(shape, dtype) for shape, dtype in outs_of(outs)],
        in_specs=[ANY] * len(ins),
        out_specs=[ANY] * len(outs),
        scratch_shapes=list(scratch) + [pltpu.SemaphoreType.DMA((semaphores,))],
        cost_estimate=pl.CostEstimate(flops=0, bytes_accessed=size, transcendentals=0),
        compiler_params=pltpu.CompilerParams(
            collective_id=number, has_side_effects=True, vmem_limit_bytes=vmem
        ),
    )(*ins)


def outs_of(outs):
    return [(x.shape, x.dtype) for x in outs]


def like(shape, dtype=bf16):
    return jax.ShapeDtypeStruct(shape, dtype)


def part_view(ref, rows, columns, pieces=1):
    height = rows // pieces

    def view(slot, core, piece=0):
        at = 0 if isinstance(slot, int) else pl.multiple_of(slot * rows, rows)
        return ref.at[
            pl.ds(at + piece * height, height), pl.ds(pl.multiple_of(core * columns, columns), columns)
        ]

    return view


PIECES = 2


def lanes(at, columns):
    return pl.ds(pl.multiple_of(at * columns, columns), columns)


class Strips:
    def __init__(self, count, columns):
        self.count, self.columns = count, columns
        self.direct = columns % 128 == 0

    def shape(self, rows):
        return (rows, self.count * self.columns) if self.direct else (self.count, rows, self.columns)

    def at(self, ref, slot):
        return ref.at[:, lanes(slot, self.columns)] if self.direct else ref.at[slot]

    def cut(self, array):
        rows = array.shape[0]
        return array if self.direct else array.reshape(rows, self.count, self.columns).transpose(1, 0, 2)

    def join(self, array):
        rows = array.shape[0 if self.direct else 1]
        return array if self.direct else array.transpose(1, 0, 2).reshape(rows, self.count * self.columns)


def row_gather(place, members, source, landing, rows, part):
    def mine(piece):
        height = rows // PIECES
        return source.at[pl.ds(piece * height, height), lanes(place.t, part)]

    whole = (source, lambda slot: landing.at[pl.ds(pl.multiple_of(slot * rows, rows), rows), :])
    return Gather(place, members, mine, whole, part_view(landing, rows, part, PIECES), True, PIECES)


def rotary(values, cosine, sine):
    half = values.shape[-1] // 2
    first = values[..., :half]
    second = values[..., half:]
    return jnp.concatenate([first * cosine - second * sine, second * cosine + first * sine], axis=-1)


def rotary_back(grads, cosine, sine):
    half = grads.shape[-1] // 2
    first = grads[..., :half]
    second = grads[..., half:]
    return jnp.concatenate([first * cosine + second * sine, second * cosine - first * sine], axis=-1)


def sequence_tables(lengths_rows, tok_rows):
    ends = jnp.cumsum(lengths_rows, axis=1)
    starts = ends - lengths_rows
    places = jnp.arange(tok_rows, dtype=jnp.int32)
    segment = jnp.sum((places[None, :, None] >= ends[:, None, :]).astype(jnp.int32), axis=2)
    member = segment[:, :, None] == jnp.arange(lengths_rows.shape[1], dtype=jnp.int32)[None, None, :]
    first = jnp.sum(jnp.where(member, starts[:, None, :], 0), axis=2)
    return segment, places[None, :] - first


def silu_parts(values):
    sigmoid_value = jax.nn.sigmoid(values)
    return values * sigmoid_value, sigmoid_value * (1.0 + values * (1.0 - sigmoid_value))


def mm(form, left, right):
    return jnp.einsum(form, left, right, preferred_element_type=f32)


def up_to(value, step):
    return -(-value // step) * step


def second_norm(place, cores, rows, given, hid_out, room):
    ap, tok, gn, rt, mk = given
    parts, tok_v, gn_v, rt_v, mk_v, hid, xn, _ = room
    t = place.t
    sends, arrivals = place.take(cores), place.take(cores)
    sent = [place.send(ap, parts.at[t], sends + d, arrivals + d, place.e, place.ring(d)) for d in range(1, cores)]
    kept = [place.keep(ap, parts.at[t])]
    kept += [place.keep(a, b) for a, b in ((tok, tok_v), (gn, gn_v), (rt, rt_v), (mk, mk_v))]
    for move in kept:
        move.wait()
    for d in range(1, cores):
        place.arrived(parts.at[place.ring(cores - d)], arrivals + d)

    def body(at, carry):
        piece = pl.ds(pl.multiple_of(at * 16, 16), 16)
        total = parts[0, piece, :].astype(f32)
        for core in range(1, cores):
            total = total + parts[core, piece, :].astype(f32)
        values = tok_v[piece, :].astype(f32) + total
        hid[piece, :] = values
        rstd = lax.rsqrt(jnp.mean(values * values, axis=1, keepdims=True) + eps)
        xn[piece, :] = (values * rstd * gn_v[...]).astype(bf16)
        return carry

    lax.fori_loop(0, rows // 16, body, 0)
    saved = place.keep(hid, hid_out)
    return sent, saved


def route(room):
    _, _, _, rt_v, mk_v, _, xn, gt = room
    logits = lax.dot_general(rt_v[...], xn[...], (((1,), (1,)), ((), ())), preferred_element_type=f32)
    picked = mk_v[...] > 0.5
    top_logit = jnp.max(jnp.where(picked, logits, floor_score), axis=0, keepdims=True)
    lifted = jnp.where(picked, jnp.exp(jnp.where(picked, logits - top_logit, 0.0)), 0.0)
    gt[...] = lifted / jnp.sum(lifted, axis=0, keepdims=True)


class Out:
    def __init__(self, place, buffer, array, unit):
        self.place, self.buffer, self.array, self.unit = place, buffer, array, unit
        self.sem = place.take(2)

    def moves(self, slots):
        for at, slot in enumerate(slots):
            if self.unit is None:
                yield self.place.local(self.buffer.at[at], self.array.at[slot], self.sem + at)
            else:
                into = pl.ds(pl.multiple_of(slot * self.unit, self.unit), self.unit)
                source = self.buffer.at[pl.ds(at * self.unit, self.unit), :]
                yield self.place.local(source, self.array.at[into, :], self.sem + at)

    def go(self, slots):
        for move in self.moves(slots):
            move.start()

    def free(self, condition=None):
        for move in self.moves((jnp.int32(0), jnp.int32(0))):
            when(condition, move.wait)


def experts_pair(slots, used, capacity, rows, rows_in, grads_in, position, gate_of, weights, outs):
    wg, wu, wd, sh_in, sh_down = weights
    received, gated, low, back, acts, gate_backs, up_backs, dots_out, left_forward, left_backward = outs
    wide = sh_down.shape[0]
    places = lax.broadcasted_iota(jnp.int32, (capacity, rows), 0).astype(f32)
    gates, onehots = [], []
    for out in (received, gated, low, left_forward, left_backward):
        out.free(used)
    for at, slot in enumerate(slots):
        token, own = pl.ds(pl.multiple_of(slot * rows, rows), rows), pl.ds(at * capacity, capacity)
        mine = pl.ds(at * rows, rows)
        chosen = (position[slot] == places).astype(f32)
        onehot = chosen.astype(bf16)
        onehots.append(chosen)
        received.buffer[own, :] = dot(onehot, rows_in[token, :]).astype(bf16)
        gate = jnp.sum(chosen * gate_of(slot), axis=1, keepdims=True)
        row_grads = dot(onehot, grads_in[mine, :])
        gated.buffer[own, :] = (gate * row_grads).astype(bf16)
        low.buffer[own, :] = row_grads.astype(bf16)
        gates.append(gate)
        turned = chosen.T.astype(bf16)
        left_forward.buffer[mine, :capacity] = turned
        left_backward.buffer[mine, :capacity] = turned
    received.go(slots)
    gated.go(slots)
    gate = jnp.concatenate(gates, axis=0)
    rows_now = received.buffer[...]
    exp_gate = dot(rows_now, wg[...], ((1,), (1,)))
    exp_up = dot(rows_now, wu[...], ((1,), (1,)))
    silu, slope = silu_parts(exp_gate)
    act = (silu * exp_up).astype(bf16)
    acts.free(used)
    acts.buffer[...] = act
    acts.go(slots)
    out = dot(act, wd[...])
    dots = jnp.sum(low.buffer[...].astype(f32) * out, axis=1, keepdims=True)
    low.buffer[...] = (gate * out).astype(bf16)
    low.go(slots)
    dots_out.free(used)
    for at in range(2):
        column = dots[at * capacity : (at + 1) * capacity]
        token_dots = jnp.sum(onehots[at] * column, axis=0, keepdims=True)
        dots_out.buffer[at] = jnp.broadcast_to(token_dots, (8, rows))
    dots_out.go(slots)
    act_grad = dot(gated.buffer[...], wd[...], ((1,), (1,)))
    gate_back = (act_grad * exp_up * slope).astype(bf16)
    up_back = (act_grad * silu).astype(bf16)
    gate_backs.free(used)
    up_backs.free(used)
    gate_backs.buffer[...] = gate_back
    up_backs.buffer[...] = up_back
    gate_backs.go(slots)
    up_backs.go(slots)
    back.free(used)
    back.buffer[...] = (dot(gate_back, wg[...]) + dot(up_back, wu[...])).astype(bf16)
    back.go(slots)
    for at, slot in enumerate(slots):
        token, mine = pl.ds(pl.multiple_of(slot * rows, rows), rows), pl.ds(at * rows, rows)
        both_sides = dot(rows_in[token, :], sh_in[...], ((1,), (1,)))
        sh_gate, sh_up = both_sides[:, :wide], both_sides[:, wide:]
        sh_silu, sh_slope = silu_parts(sh_gate)
        left_forward.buffer[mine, capacity:] = (sh_silu * sh_up).astype(bf16)
        sh_grad = dot(grads_in[mine, :], sh_down[...], ((1,), (1,)))
        left_backward.buffer[mine, capacity : capacity + wide] = (sh_grad * sh_up * sh_slope).astype(bf16)
        left_backward.buffer[mine, capacity + wide :] = (sh_grad * sh_silu).astype(bf16)
    left_forward.go(slots)
    left_backward.go(slots)


def experts_kernel(
    groups,
    capacity,
    rows,
    xn_ref,
    grad_ref,
    position_ref,
    gate_ref,
    wg_ref,
    wu_ref,
    wd_ref,
    sh_in_ref,
    sh_down_ref,
    received_ref,
    gated_ref,
    low_ref,
    back_ref,
    act_ref,
    gate_back_ref,
    up_back_ref,
    dots_ref,
    left_forward_ref,
    left_backward_ref,
):
    places = lax.broadcasted_iota(jnp.int32, (capacity, rows), 0).astype(f32)
    gates, grads, onehots = [], [], []
    for g in range(groups):
        token = pl.ds(g * rows, rows)
        slot = pl.ds(g * capacity, capacity)
        chosen = (position_ref[g] == places).astype(f32)
        onehot = chosen.astype(bf16)
        onehots.append(chosen)
        received_ref[slot, :] = dot(onehot, xn_ref[token, :]).astype(bf16)
        gate = jnp.sum(chosen * gate_ref[g], axis=1, keepdims=True)
        row_grads = dot(onehot, grad_ref[token, :])
        gated_ref[slot, :] = (gate * row_grads).astype(bf16)
        low_ref[slot, :] = row_grads.astype(bf16)
        gates.append(gate)
        turned = chosen.T.astype(bf16)
        left_forward_ref[token, :capacity] = turned
        left_backward_ref[token, :capacity] = turned
    gate = jnp.concatenate(gates, axis=0)
    received = received_ref[...]
    exp_gate = dot(received, wg_ref[...], ((1,), (1,)))
    exp_up = dot(received, wu_ref[...], ((1,), (1,)))
    silu, slope = silu_parts(exp_gate)
    act = (silu * exp_up).astype(bf16)
    act_ref[...] = act
    out = dot(act, wd_ref[...])
    dots = jnp.sum(low_ref[...].astype(f32) * out, axis=1, keepdims=True)
    low_ref[...] = (gate * out).astype(bf16)
    for g in range(groups):
        column = dots[g * capacity : (g + 1) * capacity]
        token_dots = jnp.sum(onehots[g] * column, axis=0, keepdims=True)
        dots_ref[g] = jnp.broadcast_to(token_dots, (8, rows))
    act_grad = dot(gated_ref[...], wd_ref[...], ((1,), (1,)))
    gate_back = (act_grad * exp_up * slope).astype(bf16)
    up_back = (act_grad * silu).astype(bf16)
    gate_back_ref[...] = gate_back
    up_back_ref[...] = up_back
    back_ref[...] = (
        dot(gate_back, wg_ref[...]) + dot(up_back, wu_ref[...])
    ).astype(bf16)
    wide = sh_down_ref.shape[0]
    both = dot(xn_ref[...], sh_in_ref[...], ((1,), (1,)))
    sh_gate, sh_up = both[:, :wide], both[:, wide:]
    sh_silu, sh_slope = silu_parts(sh_gate)
    left_forward_ref[:, capacity:] = (sh_silu * sh_up).astype(bf16)
    sh_grad = dot(grad_ref[...], sh_down_ref[...], ((1,), (1,)))
    left_backward_ref[:, capacity : capacity + wide] = (sh_grad * sh_up * sh_slope).astype(bf16)
    left_backward_ref[:, capacity + wide :] = (sh_grad * sh_silu).astype(bf16)


def experts_pass(count, capacity, rows, xn_all, grad_all, position, gate, wg, wu, wd, sh_in, sh_down):
    groups = 2
    units, width = wg.shape
    wide = sh_down.shape[0]

    def along(*shape):
        return pl.BlockSpec(shape, lambda i: (i,) + (0,) * (len(shape) - 1))

    def whole(array):
        return pl.BlockSpec(array.shape, lambda i: (0,) * array.ndim, pipeline_mode=pl.Buffered(1))

    slots = groups * capacity
    tokens = groups * rows
    flops = 2 * count * capacity * width * units * 6
    return pl.pallas_call(
        functools.partial(experts_kernel, groups, capacity, rows),
        name="experts_pass",
        grid=(count // groups,),
        in_specs=[
            along(tokens, width),
            along(tokens, width),
            along(groups, 1, rows),
            along(groups, 1, rows),
            whole(wg),
            whole(wu),
            whole(wd),
            whole(sh_in),
            whole(sh_down),
        ],
        out_specs=[
            along(slots, width),
            along(slots, width),
            along(slots, width),
            along(slots, width),
            along(slots, units),
            along(slots, units),
            along(slots, units),
            along(groups, 8, rows),
            along(tokens, capacity + wide),
            along(tokens, capacity + 2 * wide),
        ],
        out_shape=[like((count * capacity, width))] * 4
        + [like((count * capacity, units))] * 3
        + [
            like((count, 8, rows), f32),
            like((count * rows, capacity + wide)),
            like((count * rows, capacity + 2 * wide)),
        ],
        cost_estimate=pl.CostEstimate(
            flops=flops, bytes_accessed=4 * count * (rows + 2 * capacity) * width, transcendentals=0
        ),
        compiler_params=pltpu.CompilerParams(vmem_limit_bytes=58 * 2**20),
    )(xn_all, grad_all, position, gate, wg, wu, wd, sh_in, sh_down)


def local(
    mesh,
    tokens,
    lengths,
    routes,
    gain_attn,
    w_query,
    w_key,
    w_value,
    w_out,
    gain_ffn,
    w_router,
    routed_gate_weight,
    routed_up_weight,
    w_down,
    w_shared_gate,
    w_shared_up,
    w_shared_down,
    out_grad,
):
    count, cores = mesh.shape["expert"], mesh.shape["tensor"]
    rows, width = tokens.shape
    part = width // cores
    deep = w_query.shape[0]
    experts = w_router.shape[1]
    heads = w_query.shape[1] // HEAD_DIM
    capacity = up_to(min(rows, rows * TOP * 4 // (3 * count)), 128)
    hidden_units = w_shared_gate.shape[1] // count
    scale = HEAD_DIM ** (-0.5)
    e = lax.axis_index("expert")
    t = lax.axis_index("tensor")
    chunk = heads * rows
    strips = Strips(count, deep)

    expert_ids = jnp.arange(experts, dtype=jnp.int32)
    choose = jnp.any(routes[:, :, None] == expert_ids[None, None, :], axis=1)
    mask_t = choose.T.astype(bf16)
    vectors = jnp.concatenate(
        [
            w_router.T,
            gain_attn[None],
            gain_ffn[None],
            jnp.pad(lengths.astype(bf16), ((0, 0), (0, deep - lengths.shape[1]))),
        ],
        axis=0,
    )
    head_rows = up_to(vectors.shape[0], 16)
    vectors = jnp.pad(vectors, ((0, head_rows - vectors.shape[0]), (0, 0)))
    pieces = rows // deep
    mask_rows = mask_t.reshape(experts * pieces, deep)
    small = jnp.concatenate([vectors, mask_rows], axis=0)
    small_rows = up_to(small.shape[0], 16)
    small = jnp.pad(small, ((0, small_rows - small.shape[0]), (0, 0)))

    def unpack(gathered):
        router = gathered[:experts]
        attn_gain, ffn_gain = gathered[experts].astype(f32), gathered[experts + 1].astype(f32)
        rows_of = gathered[experts + 2].reshape(count, deep)[:, : lengths.shape[1]].astype(f32).astype(jnp.int32)
        masks = gathered[head_rows : head_rows + experts * pieces].reshape(experts, pieces, count, deep)
        return router, attn_gain, ffn_gain, rows_of, masks.transpose(2, 0, 1, 3).reshape(count, experts, rows)

    shared_pack = jnp.concatenate(
        [
            w_shared_gate.T.reshape(count, hidden_units, deep),
            w_shared_up.T.reshape(count, hidden_units, deep),
            w_shared_down.reshape(count, hidden_units, deep),
        ],
        axis=1,
    )
    pack_rows = up_to(3 * hidden_units, 16)
    shared_pack = jnp.pad(shared_pack, ((0, 0), (0, pack_rows - 3 * hidden_units), (0, 0)))
    out_rows = w_out.shape[0]

    if strips.direct:

        def front_body(place, given, made, room):
            tok, sm, wq, wk, wv, og, wo, sp, inv = given
            sm_all, w_all, xn_all, qkv_all, pr_all, ct_all, st_all, ho_all, og_all, wo_all, sp_all = made
            sm_v, tok_v, w_v, normed, qkv, probs, cosines, sines, out, inverse = room
            own = lax.rem(place.e, heads)
            base = place.e - own
            ready = place.keep(inv, inverse)
            small_in, small_out = start_exchange(place, count, lambda s: sm, lambda s: sm_v.at[:, lanes(s, deep)])
            tokens_in = row_gather(place, heads, tok, tok_v, rows, part)
            sends, arrivals = place.take(heads), place.take(heads)

            def wo_view(slot, core=0, piece=0):
                return strips.at(wo_all, slot)

            def attention():
                links = tokens_in.links()
                for _ in range(PIECES):
                    next(links)
                pulls = []
                for which, weight in enumerate((wq, wk, wv)):

                    def landing(slot, which=which):
                        at = pl.ds(pl.multiple_of(slot * deep, deep), deep)
                        return w_v.at[at, pl.ds(which * HEAD_DIM, HEAD_DIM)]

                    pulls.append(
                        start_exchange(
                            place, count, lambda s, w=weight: w.at[:, lanes(lax.rem(s, heads), HEAD_DIM)], landing
                        )
                    )
                yield
                yield from links
                for d in range(1, count):
                    slot = lax.rem(place.e + d, count)
                    for arrived in [small_in] + [pull[0] for pull in pulls]:
                        arrived(slot)
                ready.wait()
                saved = [place.keep(sm_v, sm_all), place.keep(w_v, w_all)]
                head = experts - experts % 16
                vectors = sm_v[pl.ds(head, 16), :].astype(f32)
                gain = vectors[experts - head : experts - head + 1, :]
                position = lax.broadcasted_iota(jnp.int32, (rows, HEAD_DIM), 0).astype(f32)
                gave, stored = [], []

                def group(n, i, j):
                    tokens_in.from_cores(n, i, j)
                    slot = tokens_in.slot(n, i, j)
                    at = len(stored) % 2
                    if len(stored) >= 2:
                        stored[-2].wait()
                    row = sm_v[pl.ds(head, 16), lanes(tokens_in.block.device(slot), deep)].astype(f32)
                    row = row[experts + 2 - head : experts + 3 - head, :]
                    end, first = jnp.zeros((1, 1), f32), jnp.zeros((rows, HEAD_DIM), f32)
                    for place_in in range(lengths.shape[1]):
                        end = end + row[:, place_in : place_in + 1]
                        first = jnp.where(position >= end, end, first)
                    attend(
                        tok_v,
                        gain,
                        w_v,
                        first,
                        position,
                        (normed, qkv, probs, cosines, sines, out, inverse),
                        at,
                        slot,
                        rows,
                    )
                    stored.append(
                        place.keep(
                            normed.at[at], xn_all.at[pl.ds(pl.multiple_of(slot * rows, rows), rows), :]
                        )
                    )
                    landing = ho_all.at[:, lanes(own, HEAD_DIM)]
                    if n + i + j == 0:
                        saved.append(place.keep(out.at[slot], landing))
                    else:
                        gave.append(
                            place.send(out.at[slot], landing, sends + slot, arrivals + own, base + slot, place.t)
                        )

                for n in range(tokens_in.deep):
                    if n == 0:
                        tokens_in.kept.wait()
                    group(n, 0, 0)
                    yield
                for n in range(tokens_in.deep):
                    tokens_in.last(n)
                    for i, j in ((1, 0), (0, 1), (1, 1)):
                        group(n, i, j)
                        yield
                for source, target in ((qkv, qkv_all), (probs, pr_all), (cosines, ct_all), (sines, st_all)):
                    saved.append(place.keep(source, target))
                yield
                for d in range(1, heads):
                    slot = lax.rem(own + d, heads)
                    place.arrived(ho_all.at[:, lanes(slot, HEAD_DIM)], arrivals + slot)
                for move in gave:
                    move.wait_send()
                for move in stored[-2:] + saved:
                    move.wait()
                for pull in pulls:
                    pull[1]()
                small_out()
                tokens_in.finish()

            yield attention()
            yield later(row_gather(place, count, og, og_all, rows, part).all(), 3)
            yield later(gather(place, count, lambda p: wo, (wo, wo_view), wo_view, False), 3)
            yield later(exchange(place, count, lambda s: sp.at[s], lambda s: strips.at(sp_all, s)), 6)

        half = HEAD_DIM // 2
        inverse = 10000.0 ** (-2.0 * jnp.arange(half, dtype=f32) / HEAD_DIM)
        (
            small_all,
            w_qkv,
            xn_chunk,
            qkv_saved,
            probs_saved,
            cosine_wide,
            sine_wide,
            heads_out,
            grad_all,
            out_full,
            shared_all,
        ) = transfer(
            "attention_front",
            0,
            mesh,
            front_body,
            (
                tokens,
                small,
                w_query,
                w_key,
                w_value,
                out_grad,
                w_out,
                shared_pack,
                jnp.concatenate([inverse, inverse])[None],
            ),
            (
                like((small_rows, width)),
                like((width, 3 * HEAD_DIM)),
                like((chunk, width)),
                like((chunk, 3 * HEAD_DIM)),
                like((chunk, rows), f32),
                like((chunk, HEAD_DIM), f32),
                like((chunk, HEAD_DIM), f32),
                like((rows, heads * HEAD_DIM)),
                like((count * rows, width)),
                like((out_rows, width)),
                like((pack_rows, width)),
            ),
            [
                pltpu.VMEM((small_rows, width), bf16),
                pltpu.VMEM((chunk, width), bf16),
                pltpu.VMEM((width, 3 * HEAD_DIM), bf16),
                pltpu.VMEM((2, rows, width), bf16),
                pltpu.VMEM((chunk, 3 * HEAD_DIM), bf16),
                pltpu.VMEM((chunk, rows), f32),
                pltpu.VMEM((chunk, HEAD_DIM), f32),
                pltpu.VMEM((chunk, HEAD_DIM), f32),
                pltpu.VMEM((heads, rows, HEAD_DIM), bf16),
                pltpu.VMEM((1, HEAD_DIM), f32),
            ],
            semaphores=640,
            vmem=56 * 2**20,
        )
        router_full, attn_gain, ffn_gain, _, masks = unpack(small_all)
    else:
        def first_body(place, given, made, room):
            tok, sm, *weights = given
            tok_all, sm_all, w_all = made
            yield exchange(place, count, lambda s: sm, lambda s: sm_all.at[s])
            yield row_gather(place, heads, tok, tok_all, rows, part).all()
            for which, weight in enumerate(weights):

                def landing(slot, which=which):
                    at = pl.ds(pl.multiple_of(slot * deep, deep), deep)
                    return w_all.at[at, pl.ds(which * HEAD_DIM, HEAD_DIM)]

                yield exchange(
                    place, count, lambda s, w=weight: w.at[:, lanes(lax.rem(s, heads), HEAD_DIM)], landing
                )

        tok_chunk, small_all, w_qkv = transfer(
            "gather_tokens",
            0,
            mesh,
            first_body,
            (tokens, small, w_query, w_key, w_value),
            (like((chunk, width)), like((count, small_rows, deep)), like((width, 3 * HEAD_DIM))),
        )

        router_full, attn_gain, ffn_gain, lengths_all, masks = unpack(strips.join(small_all))

        member = e % heads
        lengths_chunk = lax.dynamic_slice_in_dim(lengths_all, e - member, heads, axis=0)
        segment, positions = sequence_tables(lengths_chunk, rows)
        half = HEAD_DIM // 2
        inverse = 10000.0 ** (-2.0 * jnp.arange(half, dtype=f32) / HEAD_DIM)
        angles = positions.astype(f32)[:, :, None] * inverse[None, None, :]
        cosine, sine = jnp.cos(angles), jnp.sin(angles)

        tok32 = tok_chunk.astype(f32)
        rstd_chunk = lax.rsqrt(jnp.mean(tok32 * tok32, axis=-1, keepdims=True) + eps)
        xn_chunk = (tok32 * rstd_chunk * attn_gain).astype(bf16)
        qkv = jnp.dot(xn_chunk, w_qkv, preferred_element_type=f32).reshape(heads, rows, 3 * HEAD_DIM)
        query = rotary(qkv[..., :HEAD_DIM], cosine, sine).astype(bf16)
        keyed = rotary(qkv[..., HEAD_DIM : 2 * HEAD_DIM], cosine, sine).astype(bf16)
        valued = qkv[..., 2 * HEAD_DIM :].astype(bf16)
        places = jnp.arange(rows, dtype=jnp.int32)
        allowed = (segment[:, :, None] == segment[:, None, :]) & (places[None, :] <= places[:, None])[None]
        scores = jnp.where(allowed, mm("gqd,gkd->gqk", query, keyed) * scale, floor_score)
        top_score = jnp.max(scores, axis=-1, keepdims=True)
        raised = jnp.exp(scores - top_score)
        probs = raised / jnp.sum(raised, axis=-1, keepdims=True)
        probs_low = probs.astype(bf16)
        head_out = mm("gqk,gkd->gqd", probs_low, valued).astype(bf16)

        def second_body(place, given, made, room):
            ho, og, wo, sp = given
            ho_all, og_all, wo_all, sp_all = made
            yield exchange(place, heads, lambda s: ho.at[s], lambda s: ho_all.at[:, lanes(s, HEAD_DIM)])
            yield row_gather(place, count, og, og_all, rows, part).all()

            def wo_view(slot, core=0, piece=0):
                return strips.at(wo_all, slot)

            yield gather(place, count, lambda p: wo, (wo, wo_view), wo_view, False)
            yield exchange(place, count, lambda s: sp.at[s], lambda s: strips.at(sp_all, s))

        heads_out, grad_all, out_full, shared_all = transfer(
            "gather_inputs",
            1,
            mesh,
            second_body,
            (head_out, out_grad, w_out, shared_pack),
            (
                like((rows, heads * HEAD_DIM)),
                like((count * rows, width)),
                like(strips.shape(out_rows)),
                like(strips.shape(pack_rows)),
            ),
            semaphores=640,
        )
        out_full, shared_all = strips.join(out_full), strips.join(shared_all)
    attention_part = jnp.dot(heads_out, out_full, preferred_element_type=f32).astype(bf16)

    own_mask = lax.dynamic_index_in_dim(masks, e, axis=1, keepdims=False).astype(f32)
    at_row = jnp.arange(rows, dtype=jnp.int32)
    earlier = (at_row[:, None] < at_row[None, :]).astype(bf16)
    position = jnp.where(own_mask > 0.5, jnp.dot(own_mask.astype(bf16), earlier, preferred_element_type=f32), -1.0)
    gate_weight, up_weight, down_weight = routed_gate_weight[0].T, routed_up_weight[0].T, w_down[0]
    sh_wide = up_to(hidden_units, 128)

    def widened(which):
        piece = shared_all[which * hidden_units : (which + 1) * hidden_units]
        return jnp.pad(piece, ((0, sh_wide - hidden_units), (0, 0)))

    fixed_backward = jnp.concatenate([widened(0), widened(1)], axis=0)
    fixed_forward = widened(2)
    units = gate_weight.shape[0]
    norm_rooms = [
        pltpu.VMEM((cores, rows, width), bf16),
        pltpu.VMEM((rows, width), bf16),
        pltpu.VMEM((1, width), f32),
        pltpu.VMEM((experts, width), bf16),
        pltpu.VMEM((experts, rows), f32),
        pltpu.VMEM((rows, width), f32),
        pltpu.VMEM((rows, width), bf16),
        pltpu.VMEM((experts, rows), f32),
    ]
    if strips.direct:

        def rows_body(place, given, made, room):
            og, pos, *weights = given[5:]
            hid_out, xn_all, gt_out, *arrays = made
            xn, gt = room[6:8]
            gates_v, xn_v, og_v, pos_v = room[8:12]
            weights_v, buffers = room[12:17], room[17:]
            loads = [place.keep(pos, pos_v)] + [place.keep(x, y) for x, y in zip(weights, weights_v)]
            sent, saved = second_norm(place, cores, rows, given[:5], hid_out, room[:8])
            moving = row_gather(place, count, xn, xn_v, rows, part)
            for p in range(PIECES):
                moving.start(p)
            route(room[:8])
            saved_gates = place.keep(gt, gt_out)
            gate_in, gate_out = start_exchange(place, count, lambda s: gt, lambda s: gates_v.at[s])
            sizes = [capacity] * 7 + [None] + [rows] * 2
            outs = [Out(place, buffer, array, unit) for buffer, array, unit in zip(buffers, arrays, sizes)]
            grad_sems, row_sems = place.take(4), place.take(4)
            quads = (((0, 0), (1, 0)), ((0, 1), (1, 1)))
            expert = lax.broadcasted_iota(jnp.int32, (experts, rows), 0)

            def gate_of(slot):
                return jnp.sum(jnp.where(expert == place.e, gates_v[slot], 0.0), axis=0, keepdims=True)

            def of_rows(slot):
                return pl.ds(pl.multiple_of(slot * rows, rows), rows)

            def grads(m, pair):
                for at, (i, j) in enumerate(quads[pair]):
                    source = og.at[of_rows(moving.slot(m, i, j)), :]
                    yield place.local(
                        source, og_v.at[pair, pl.ds(at * rows, rows), :], grad_sems + 2 * pair + at
                    )

            def keep_rows(m):
                for at, (i, j) in enumerate(quads[0] + quads[1]):
                    own = of_rows(moving.slot(m, i, j))
                    yield place.local(xn_v.at[own, :], xn_all.at[own, :], row_sems + at)

            def link(n):
                for p in range(PIECES):
                    moving.from_one(n, p)
                    pl.when(n + 1 < moving.deep)(lambda: moving.from_line(n + 1, p))

            def work(m):
                moving.last(m)
                for pair in quads:
                    for i, j in pair:
                        moving.from_cores(m, i, j)
                        gate_in(moving.slot(m, i, j))
                for move in keep_rows(m):
                    when(m > 0, move.wait)
                    move.start()
                for pair in range(2):
                    if pair == 0:
                        for move in grads(m, 1):
                            move.start()
                    else:
                        for move in grads(m + 1, 0):
                            when(m + 1 < moving.deep, move.start)
                    for move in grads(m, pair):
                        move.wait()
                    slots = [moving.slot(m, i, j) for i, j in quads[pair]]
                    experts_pair(
                        slots,
                        m > 0 if pair == 0 else None,
                        capacity,
                        rows,
                        xn_v,
                        og_v.at[pair],
                        pos_v,
                        gate_of,
                        weights_v,
                        outs,
                    )

            for move in grads(0, 0):
                move.start()
            for move in loads:
                move.wait()
            moving.kept.wait()

            def stage(n, carry):
                pl.when(n < moving.deep)(lambda: link(n))
                pl.when(n >= 1)(lambda: work(n - 1))
                return carry

            lax.fori_loop(0, moving.deep + 1, stage, 0)
            for out in outs:
                out.free()
            for move in keep_rows(0):
                move.wait()
            gate_out()
            moving.close()
            for move in sent:
                move.wait_send()
            saved.wait()
            saved_gates.wait()
            yield from ()

        shapes = [(count * capacity, width)] * 4 + [(count * capacity, units)] * 3
        shapes += [(count, 8, rows), (count * rows, capacity + sh_wide), (count * rows, capacity + 2 * sh_wide)]
        pair_shapes = [(2 * capacity, width)] * 4 + [(2 * capacity, units)] * 3
        pair_shapes += [(2, 8, rows), (2 * rows, capacity + sh_wide), (2 * rows, capacity + 2 * sh_wide)]
        kinds = [bf16] * 7 + [f32] + [bf16] * 2
        (
            hidden,
            xn_all,
            gates_t,
            received,
            gated_grad,
            exp_low,
            back_rows,
            exp_act,
            gate_back,
            up_back,
            token_dots,
            left_forward,
            left_backward,
        ) = transfer(
            "rows_and_experts",
            2,
            mesh,
            rows_body,
            (
                attention_part,
                tokens,
                ffn_gain[None],
                router_full,
                mask_t.astype(f32),
                grad_all,
                position[:, None],
                gate_weight,
                up_weight,
                down_weight,
                fixed_backward,
                fixed_forward,
            ),
            (like((rows, width), f32), like((count * rows, width)), like((experts, rows), f32))
            + tuple(like(shape, kind) for shape, kind in zip(shapes, kinds)),
            norm_rooms
            + [
                pltpu.VMEM((count, experts, rows), f32),
                pltpu.VMEM((count * rows, width), bf16),
                pltpu.VMEM((2, 2 * rows, width), bf16),
                pltpu.VMEM((count, 1, rows), f32),
                pltpu.VMEM((units, width), bf16),
                pltpu.VMEM((units, width), bf16),
                pltpu.VMEM((units, width), bf16),
                pltpu.VMEM((2 * sh_wide, width), bf16),
                pltpu.VMEM((sh_wide, width), bf16),
            ]
            + [pltpu.VMEM(shape, kind) for shape, kind in zip(pair_shapes, kinds)],
            semaphores=400,
            vmem=62 * 2**20,
        )
        gates = gates_t.T
    else:
        def third_body(place, given, made, room):
            ap, tok, gn, rt, mk = given
            hid_out, xn_all, gt_all = made
            xn, gt = room[6:]
            sent, saved = second_norm(place, cores, rows, given, hid_out, room)
            yield row_gather(place, count, xn, xn_all, rows, part).all()
            route(room)
            yield exchange(place, count, lambda s: gt, lambda s: gt_all.at[s])
            for move in sent:
                move.wait_send()
            saved.wait()

        hidden, xn_all, gates_all = transfer(
            "gather_rows",
            2,
            mesh,
            third_body,
            (attention_part, tokens, ffn_gain[None], router_full, mask_t.astype(f32)),
            (like((rows, width), f32), like((count * rows, width)), like((count, experts, rows), f32)),
            norm_rooms,
            semaphores=400,
            vmem=40 * 2**20,
        )
        gates = lax.dynamic_index_in_dim(gates_all, e, axis=0, keepdims=False).T
        own_gate = lax.dynamic_index_in_dim(gates_all, e, axis=1, keepdims=False)
        (
            received,
            gated_grad,
            exp_low,
            back_rows,
            exp_act,
            gate_back,
            up_back,
            token_dots,
            left_forward,
            left_backward,
        ) = experts_pass(
            count,
            capacity,
            rows,
            xn_all,
            grad_all,
            position[:, None],
            own_gate[:, None],
            gate_weight,
            up_weight,
            down_weight,
            fixed_backward,
            fixed_forward,
        )

    inputs = tokens.astype(f32)
    rstd_two = lax.rsqrt(jnp.mean(hidden * hidden, axis=-1, keepdims=True) + eps)

    sh_grads = mm("tf,td->fd", left_backward[:, capacity:], xn_all).astype(bf16)
    shared_grads = jnp.concatenate(
        [
            sh_grads[:hidden_units],
            sh_grads[sh_wide : sh_wide + hidden_units],
            mm("tf,td->fd", left_forward[:, capacity:], grad_all).astype(bf16)[:hidden_units],
        ],
        axis=0,
    )
    shared_grads = jnp.pad(shared_grads, ((0, pack_rows - 3 * hidden_units), (0, 0)))

    def fourth_body(place, given, made, room):
        lf, el, ff, lb, br, fb, td, sg = given
        mixed, summed, dots, sg_all = made
        mixed_view, summed_view = part_view(mixed, rows, part), part_view(summed, rows, part)
        forward = Product(place, lf, el, ff, room[7:9], count, rows, part)
        backward = Product(place, lb, br, fb, room[9:11], count, rows, part)
        yield scatter(
            place,
            count,
            [forward, backward],
            room[:7],
            [lambda c: mixed_view(0, c), lambda c: summed_view(0, c)],
            (rows, part),
            True,
            room[11],
        )
        yield both(place, count, lambda s: td.at[s], lambda c, s: dots.at[c, s], lambda c: dots.at[c])
        yield later(exchange(place, count, lambda s: strips.at(sg, s), lambda s: sg_all.at[s]), 8)

    mixture, summed_back, dots_all, shared_back = transfer(
        "scatter_both",
        3,
        mesh,
        fourth_body,
        (
            left_forward,
            exp_low,
            fixed_forward,
            left_backward,
            back_rows,
            fixed_backward,
            token_dots,
            strips.cut(shared_grads),
        ),
        (
            like((rows, width)),
            like((rows, width)),
            like((cores, count, 8, rows), f32),
            like((count, pack_rows, deep)),
        ),
        scatter_scratch(
            count,
            cores,
            rows,
            part,
            [(left_forward.shape[1], True), (left_backward.shape[1], True)],
        )
        + [pltpu.SemaphoreType.REGULAR((count * (cores - 1),))],
        vmem=60 * 2**20,
    )
    output = (hidden + mixture.astype(f32)).astype(bf16)

    gate_total = jnp.sum(dots_all[:, :, 0, :], axis=0).T
    weighted_dots = jnp.sum(gates * gate_total, axis=1, keepdims=True)
    grad_logits = gates * (gate_total - weighted_dots)

    down_grad = mm("rf,rd->fd", exp_act, gated_grad)
    gate_grad = mm("rd,rf->df", received, gate_back)
    up_grad = mm("rd,rf->df", received, up_back)
    cotangent = out_grad.astype(f32)
    grad_two = summed_back.astype(f32) + jnp.einsum(
        "te,ed->td", grad_logits, router_full.astype(f32), precision=highest
    )
    scaled = grad_two * ffn_gain
    inner = jnp.mean(scaled * hidden, axis=-1, keepdims=True)
    grad_hidden = cotangent + rstd_two * scaled - hidden * (rstd_two * rstd_two * rstd_two) * inner
    ffn_gain_part = jnp.sum(grad_two * hidden * rstd_two, axis=0)
    grad_branch = grad_hidden.astype(bf16)
    grad_heads = mm("td,cd->tc", grad_branch, out_full).astype(bf16)
    out_proj_part = mm("tc,td->cd", heads_out, grad_branch).astype(bf16)

    turns = count // heads

    def spread(vector):
        return jnp.pad(vector.reshape(count, 1, deep), ((0, 0), (0, 7), (0, 0)))

    if strips.direct:

        def back_body(place, given, made, room):
            gh, gl, op, fg, qkv_s, pr, ct, st, xn, wt = given
            one, qg_all, op_sum, ag_all, fg_all, logit_all = made
            qkv_v, pr_v, ct_v, st_v, gh_v, held, sums, grad_qkv, right, gains, blocks = room[14:]
            own = lax.rem(place.e, heads)
            moves = [place.keep(x, y) for x, y in ((qkv_s, qkv_v), (pr, pr_v), (ct, ct_v), (st, st_v), (wt, right))]
            arrived, finish = start_exchange(
                place, heads, lambda s: gh.at[:, lanes(s, HEAD_DIM)], lambda s: gh_v.at[s]
            )
            one_view = part_view(one, rows, part)

            def fetch(d):
                slot = lax.rem(own + d, heads)
                source = xn.at[pl.ds(pl.multiple_of(slot * rows, rows), rows), :]
                return place.keep(source, held.at[d % 2])

            def main():
                coming = fetch(0)
                for move in moves:
                    move.wait()
                for d in range(heads):
                    now, slot = coming, lax.rem(own + d, heads)
                    if d + 1 < heads:
                        coming = fetch(d + 1)
                    if d > 0:
                        arrived(slot)
                    now.wait()
                    attend_back(
                        held.at[d % 2], (qkv_v, pr_v, ct_v, st_v, gh_v, grad_qkv, sums), slot, rows, d == 0
                    )
                    yield
                tail()
                yield
                kept = Kept(grad_qkv, right, rows)
                yield from scatter(place, heads, [kept], room[:7], [lambda c: one_view(0, c)], (rows, part), True)

            def tail():
                ones = jnp.ones((8, 3 * HEAD_DIM), f32)

                def body(at, carry):
                    block = sums[:, lanes(at, deep)].T
                    blocks[at] = block.astype(bf16)
                    weights = right[pl.ds(pl.multiple_of(at * deep, deep), deep), :].astype(f32)
                    gains[:, lanes(at, deep)] = dot(ones, block * weights, ((1,), (1,)), highest)
                    return carry

                lax.fori_loop(0, count, body, 0)
                for which in range(3):

                    def landing(slot, which=which):
                        return qg_all.at[which, lax.div(slot, heads), :, lanes(lax.rem(slot, heads), HEAD_DIM)]

                    def block(slot, which=which):
                        return blocks.at[slot, :, pl.ds(which * HEAD_DIM, HEAD_DIM)]

                    tasks.append(exchange(place, count, block, landing))
                tasks.append(
                    both(
                        place,
                        count,
                        lambda s: gains.at[:, lanes(s, deep)],
                        lambda c, s: ag_all.at[c, s],
                        lambda c: ag_all.at[c],
                    )
                )

            projection = scatter(
                place, count, [lambda s: strips.at(op, s)], room[7:14], [lambda c: op_sum], (out_rows, deep), False
            )
            tasks = [
                main(),
                twice(projection),
                exchange(place, count, lambda s: gl, lambda s: logit_all.at[s]),
                exchange(place, count, lambda s: fg.at[s], lambda s: fg_all.at[s]),
            ]
            yield tasks
            finish()

        grad_one, qkv_all, out_proj_sum, attn_gains, ffn_gains, logits_all = transfer(
            "attention_back",
            4,
            mesh,
            back_body,
            (
                grad_heads,
                grad_logits.T,
                out_proj_part,
                spread(ffn_gain_part),
                qkv_saved,
                probs_saved,
                cosine_wide,
                sine_wide,
                xn_chunk,
                w_qkv,
            ),
            (
                like((rows, width)),
                like((3, turns, deep, heads * HEAD_DIM)),
                like((out_rows, deep)),
                like((cores, count, 8, deep), f32),
                like((count, 8, deep), f32),
                like((count, experts, rows), f32),
            ),
            scatter_scratch(heads, cores, rows, part)
            + scatter_scratch(count, 1, out_rows, deep)
            + [
                pltpu.VMEM((chunk, 3 * HEAD_DIM), bf16),
                pltpu.VMEM((chunk, rows), f32),
                pltpu.VMEM((chunk, HEAD_DIM), f32),
                pltpu.VMEM((chunk, HEAD_DIM), f32),
                pltpu.VMEM((heads, rows, HEAD_DIM), bf16),
                pltpu.VMEM((2, rows, width), bf16),
                pltpu.VMEM((3 * HEAD_DIM, width), f32),
                pltpu.VMEM((chunk, 3 * HEAD_DIM), bf16),
                pltpu.VMEM((width, 3 * HEAD_DIM), bf16),
                pltpu.VMEM((8, width), f32),
                pltpu.VMEM((count, deep, 3 * HEAD_DIM), bf16),
            ],
            semaphores=640,
            vmem=56 * 2**20,
        )
    else:
        def fifth_body(place, given, made, room):
            gl, logit_all = given[1], made[1]
            yield exchange(place, count, lambda s: gl, lambda s: logit_all.at[s])
            yield exchange(place, heads, lambda s: given[0].at[:, lanes(s, HEAD_DIM)], lambda s: made[0].at[s])

        grad_head, logits_all = transfer(
            "exchange_heads",
            4,
            mesh,
            fifth_body,
            (grad_heads, grad_logits.T),
            (like((heads, rows, HEAD_DIM)), like((count, experts, rows), f32)),
        )
        grad_value = mm("gqk,gqd->gkd", probs_low, grad_head)
        grad_probs = mm("gqd,gkd->gqk", grad_head, valued)
        weighted = jnp.sum(probs * grad_probs, axis=-1, keepdims=True)
        grad_scores = (probs * (grad_probs - weighted)).astype(bf16)
        grad_query = mm("gqk,gkd->gqd", grad_scores, keyed) * scale
        grad_key = mm("gqk,gqd->gkd", grad_scores, query) * scale
        grad_qkv = jnp.concatenate(
            [
                rotary_back(grad_query, cosine, sine).astype(bf16),
                rotary_back(grad_key, cosine, sine).astype(bf16),
                grad_value.astype(bf16),
            ],
            axis=2,
        ).reshape(chunk, 3 * HEAD_DIM)
        qkv_grad = mm("td,tc->dc", xn_chunk, grad_qkv)
        attn_gain_part = jnp.sum(qkv_grad * w_qkv.astype(f32), axis=1)
        qkv_grad = qkv_grad.astype(bf16)

        def sixth_body(place, given, made, room):
            gq, wq, qg, op, ag, fg = given
            one, qg_all, op_sum, ag_all, fg_all = made
            one_view = part_view(one, rows, part)
            made_here = Product(place, gq, None, wq, room[7:9], heads, rows, part)
            yield scatter(place, heads, [made_here], room[:7], [lambda c: one_view(0, c)], (rows, part), True)
            yield scatter(
                place, count, [lambda s: strips.at(op, s)], room[9:], [lambda c: op_sum], (out_rows, deep), False
            )
            yield both(place, count, lambda s: ag.at[s], lambda c, s: ag_all.at[c, s], lambda c: ag_all.at[c])
            yield exchange(place, count, lambda s: fg.at[s], lambda s: fg_all.at[s])
            for which in range(3):

                def source(slot, which=which):
                    at = pl.ds(pl.multiple_of(slot * deep, deep), deep)
                    return qg.at[at, pl.ds(which * HEAD_DIM, HEAD_DIM)]

                def landing(slot, which=which):
                    return qg_all.at[which, lax.div(slot, heads), :, lanes(lax.rem(slot, heads), HEAD_DIM)]

                yield later(exchange(place, count, source, landing), 6)

        grad_one, qkv_all, out_proj_sum, attn_gains, ffn_gains = transfer(
            "scatter_grads",
            5,
            mesh,
            sixth_body,
            (
                grad_qkv,
                w_qkv.T,
                qkv_grad,
                strips.cut(out_proj_part),
                spread(attn_gain_part),
                spread(ffn_gain_part),
            ),
            (
                like((rows, width)),
                like((3, turns, deep, heads * HEAD_DIM)),
                like((out_rows, deep)),
                like((cores, count, 8, deep), f32),
                like((count, 8, deep), f32),
            ),
            scatter_scratch(heads, cores, rows, part, [(3 * HEAD_DIM, False)])
            + scatter_scratch(count, 1, out_rows, deep),
            semaphores=600,
            vmem=56 * 2**20,
        )

    xn_columns = lax.dynamic_slice_in_dim(xn_all, e * deep, deep, axis=1).astype(f32).reshape(count, rows, deep)
    router_grad = jnp.einsum("gtd,get->de", xn_columns, logits_all, precision=highest)
    grad_one = grad_one.astype(f32)
    rstd_one = lax.rsqrt(jnp.mean(inputs * inputs, axis=-1, keepdims=True) + eps)
    scaled_one = grad_one * attn_gain
    inner_one = jnp.mean(scaled_one * inputs, axis=-1, keepdims=True)
    input_grad = (
        grad_hidden + rstd_one * scaled_one - inputs * (rstd_one * rstd_one * rstd_one) * inner_one
    ).astype(bf16)

    def of_heads(which):
        return jnp.sum(qkv_all[which].astype(f32), axis=0)

    def of_shared(which):
        return shared_back[:, which * hidden_units : (which + 1) * hidden_units].reshape(-1, deep).astype(f32)

    return (
        output,
        input_grad,
        jnp.sum(attn_gains[:, :, 0, :], axis=(0, 1)) / gain_attn.astype(f32),
        of_heads(0),
        of_heads(1),
        of_heads(2),
        out_proj_sum.astype(f32),
        jnp.sum(ffn_gains[:, 0, :], axis=0),
        router_grad,
        gate_grad[None],
        up_grad[None],
        down_grad[None],
        of_shared(0).T,
        of_shared(1).T,
        of_shared(2),
    )


def solution(mesh):
    in_specs = (
        P("expert", None),
        P("expert", None),
        P("expert", None),
        P("expert"),
        P("expert", "tensor"),
        P("expert", "tensor"),
        P("expert", "tensor"),
        P("tensor", "expert"),
        P("expert"),
        P("expert", None),
        P("expert", None, "tensor"),
        P("expert", None, "tensor"),
        P("expert", "tensor", None),
        P("expert", "tensor"),
        P("expert", "tensor"),
        P("tensor", "expert"),
        P("expert", None),
    )
    out_specs = (
        P("expert", None),
        P("expert", None),
        P("expert"),
        P("expert", "tensor"),
        P("expert", "tensor"),
        P("expert", "tensor"),
        P("tensor", "expert"),
        P("expert"),
        P("expert", None),
        P("expert", None, "tensor"),
        P("expert", None, "tensor"),
        P("expert", "tensor", None),
        P("expert", "tensor"),
        P("expert", "tensor"),
        P("tensor", "expert"),
    )
    return jax.shard_map(
        functools.partial(local, mesh), mesh=mesh, in_specs=in_specs, out_specs=out_specs, check_vma=False
    )
```

```python
import functools

import jax
import jax.numpy as jnp
from jax import lax
from jax.experimental import pallas as pl
from jax.experimental.pallas import tpu as pltpu
from jax.sharding import PartitionSpec as P

HEAD_DIM = 128
TOP = 6
MESH = pl.DeviceIdType.MESH
ANY = pl.BlockSpec(memory_space=pl.ANY)

bf16 = jnp.bfloat16
f32 = jnp.float32
eps = 1e-06
highest = lax.Precision.HIGHEST
floor_score = -1e30


class Place:
    def __init__(self, sems, count, cores):
        self.sems, self.used = sems, 0
        self.count, self.cores = count, cores
        self.e = lax.axis_index("expert")
        self.t = lax.axis_index("tensor")
        self.quad = lax.rem(self.e, 4)
        self.far = lax.div(self.e, 4)

    def take(self, number):
        first = self.used
        self.used = first + number
        return first

    def ring(self, distance):
        return lax.rem(self.t + distance, self.cores)

    def copy(self, src, dst, out_sem, in_sem, e, t):
        return pltpu.make_async_remote_copy(
            src_ref=src,
            dst_ref=dst,
            send_sem=self.sems.at[out_sem],
            recv_sem=self.sems.at[in_sem],
            device_id={"expert": e, "tensor": t},
            device_id_type=MESH,
        )

    def send(self, src, dst, out_sem, in_sem, e, t):
        move = self.copy(src, dst, out_sem, in_sem, e, t)
        move.start()
        return move

    def arrived(self, landing, in_sem):
        self.copy(landing, landing, in_sem, in_sem, self.e, self.t).wait_recv()

    def keep(self, src, dst):
        move = pltpu.make_async_copy(src, dst, self.sems.at[self.take(1)])
        move.start()
        return move

    def local(self, src, dst, sem):
        return pltpu.make_async_copy(src, dst, self.sems.at[sem])

    def meet(self):
        barrier = pltpu.get_barrier_semaphore()
        for step in range(1, self.count):
            pl.semaphore_signal(
                barrier,
                inc=1,
                device_id={"expert": lax.rem(self.e + step, self.count), "tensor": self.t},
                device_id_type=MESH,
            )
        for step in range(1, self.cores):
            pl.semaphore_signal(
                barrier,
                inc=1,
                device_id={"expert": self.e, "tensor": self.ring(step)},
                device_id_type=MESH,
            )
        pl.semaphore_wait(barrier, self.count + self.cores - 2)


class Block:
    def __init__(self, place, members):
        self.place, self.deep = place, members // 4
        self.rank = lax.rem(place.far, self.deep)
        self.start = place.far - self.rank

    def flips(self, order):
        high, low = lax.div(self.place.quad, 2), lax.rem(self.place.quad, 2)
        one = high + (low - high) * order
        two = low + (high - low) * order
        return (2 - order) * (1 - 2 * one), (1 + order) * (1 - 2 * two)

    def slot(self, k, i, j, order):
        one, two = self.flips(order)
        return lax.rem(self.rank + k, self.deep) * 4 + self.place.quad + i * one + j * two

    def own(self):
        return self.rank * 4 + self.place.quad

    def device(self, slot):
        return self.start * 4 + slot


class Gather:
    def __init__(self, place, members, mine, whole, view, halves, pieces=1):
        self.place, self.block = place, Block(place, members)
        self.mine, self.whole, self.view, self.pieces = mine, whole, view, pieces
        self.deep, self.order = self.block.deep, lax.rem(place.t, 2)
        self.cores = place.cores if halves else 1
        self.zs, self.zr = self.lots(2), self.lots(1)
        self.s2, self.r2 = self.lots(1), self.lots(1)
        self.s3, self.r3 = self.lots(2), self.lots(2)
        self.s4, self.r4 = self.lots(4 * (self.cores - 1)), self.lots(4 * (self.cores - 1))
        self.sent, self.closing = [], False

    def lots(self, number):
        return self.place.take(number * self.deep * self.pieces)

    def near(self, n):
        rank, deep = self.block.rank, self.deep
        if isinstance(n, int) and n == 0:
            return rank
        low = jnp.minimum(rank, deep - 1 - rank)
        if isinstance(n, int):
            paired = rank - (n + 1) // 2 if n % 2 else rank + n // 2
        else:
            paired = rank + jnp.where(lax.rem(n, 2) == 1, -lax.div(n + 1, 2), lax.div(n, 2))
        single = jnp.where(rank < deep - 1 - rank, rank + (n - low), rank - (n - low))
        return jnp.where(n <= 2 * low, paired, single)

    def slot(self, n, i, j, order=None):
        one, two = self.block.flips(self.order if order is None else order)
        return self.near(n) * 4 + self.place.quad + i * one + j * two

    def index(self, n, kind, kinds, p):
        return (self.near(n) * kinds + kind) * self.pieces + p

    def pass_on(self, source, landing, out, into, at, e, t, condition=None):
        move = self.place.copy(source, landing, out + at[0], into + at[1], e, t)
        if self.closing:
            when(condition, move.wait_send)
            return
        self.sent.append((condition, move))
        when(condition, move.start)

    def along(self, n, p, source, landing):
        rank, e = self.block.rank, self.place.e
        near = self.near(n)
        for way in (1, -1):
            fits = rank < self.deep - 1 if way > 0 else rank >= 1
            if not isinstance(n, int) or n > 0:
                fits = jnp.logical_and(fits, near < rank if way > 0 else near > rank)
            out = self.index(n, 0 if way > 0 else 1, 2, p)
            into = self.index(n, 0, 1, p)
            self.pass_on(source, landing, self.zs, self.zr, (out, into), e + 4 * way, self.place.t, fits)

    def across(self, n, i, p, source, landing):
        one, two = self.block.flips(self.order)
        e, t = self.place.e, self.place.t
        if i == 0:
            at = self.index(n, 0, 1, p)
            self.pass_on(source, landing, self.s2, self.r2, (at, at), e + one, t)
        at = self.index(n, i, 2, p)
        self.pass_on(source, landing, self.s3, self.r3, (at, at), e + two, t)

    def share(self, n, i, j, p):
        ref = self.view(self.slot(n, i, j), self.place.t, p)
        for far in range(1, self.cores):
            kind = (far - 1) * 4 + i * 2 + j
            at = self.index(n, kind, 4 * (self.cores - 1), p)
            self.pass_on(ref, ref, self.s4, self.r4, (at, at), self.place.e, self.place.ring(far))

    def start(self, p):
        if p == 0:
            self.kept = self.place.keep(self.whole[0], self.whole[1](self.block.own()))
        source, landing = self.mine(p), self.view(self.block.own(), self.place.t, p)
        if self.deep > 1:
            self.along(0, p, source, landing)
        self.across(0, 0, p, source, landing)

    def from_line(self, n, p):
        ref = self.view(self.slot(n, 0, 0), self.place.t, p)
        self.place.arrived(ref, self.zr + self.index(n, 0, 1, p))
        if self.deep > 2:
            self.along(n, p, ref, ref)
        self.across(n, 0, p, ref, ref)
        self.share(n, 0, 0, p)

    def from_one(self, n, p):
        ref = self.view(self.slot(n, 1, 0), self.place.t, p)
        self.place.arrived(ref, self.r2 + self.index(n, 0, 1, p))
        self.across(n, 1, p, ref, ref)
        self.share(n, 1, 0, p)

    def from_two(self, n, i, p):
        ref = self.view(self.slot(n, i, 1), self.place.t, p)
        self.place.arrived(ref, self.r3 + self.index(n, i, 2, p))
        self.share(n, i, 1, p)

    def from_cores(self, n, i, j):
        if i + j == 0 and isinstance(n, int) and n == 0:
            return
        if i + j == 0 and not isinstance(n, int):
            pl.when(n > 0)(lambda: self.of_cores(n, i, j))
        else:
            self.of_cores(n, i, j)

    def of_cores(self, n, i, j):
        for far in range(1, self.cores):
            source = self.place.ring(self.cores - far)
            first, second = (j, i) if far % 2 else (i, j)
            kind = (far - 1) * 4 + first * 2 + second
            for p in range(self.pieces):
                ref = self.view(self.slot(n, i, j), source, p)
                self.place.arrived(ref, self.r4 + self.index(n, kind, 4 * (self.cores - 1), p))

    def finish(self):
        for condition, move in self.sent:
            when(condition, move.wait_send)

    def close(self):
        self.closing = True
        for p in range(self.pieces):
            source, landing = self.mine(p), self.view(self.block.own(), self.place.t, p)
            self.along(0, p, source, landing)
            self.across(0, 0, p, source, landing)
            for n in range(self.deep):
                if n > 0:
                    ref = self.view(self.slot(n, 0, 0), self.place.t, p)
                    self.along(n, p, ref, ref)
                    self.across(n, 0, p, ref, ref)
                    self.share(n, 0, 0, p)
                ref = self.view(self.slot(n, 1, 0), self.place.t, p)
                self.across(n, 1, p, ref, ref)
                self.share(n, 1, 0, p)
                self.share(n, 0, 1, p)
                self.share(n, 1, 1, p)

    def links(self):
        for p in range(self.pieces):
            self.start(p)
            yield
        for n in range(1, self.deep + 1):
            for p in range(self.pieces):
                self.from_one(n - 1, p)
                yield
                if n < self.deep:
                    self.from_line(n, p)
                    yield

    def last(self, n):
        for i in range(2):
            for p in range(self.pieces):
                self.from_two(n, i, p)

    def all(self):
        yield from self.links()
        for n in range(self.deep):
            self.last(n)
            yield
        for n in range(self.deep):
            for i in range(2):
                for j in range(2):
                    self.from_cores(n, i, j)
        self.finish()
        self.kept.wait()


def when(condition, action):
    if condition is None:
        action()
    else:
        pl.when(condition)(action)


def gather(place, members, mine, whole, view, halves, pieces=1):
    return Gather(place, members, mine, whole, view, halves, pieces).all()


class Kept:
    def __init__(self, left, right, rows):
        self.left, self.right, self.rows, self.slots = left, right, rows, {}

    def fetch(self, turn, slot):
        self.slots[turn] = pl.ds(pl.multiple_of(slot * self.rows, self.rows), self.rows)

    def ready(self, turn):
        pass

    def make(self, turn, core, target):
        columns = target.shape[1]
        wide = min(columns, 512)

        def body(tile, carry):
            source = pl.ds(pl.multiple_of(core * columns + tile * wide, wide), wide)
            into = pl.ds(pl.multiple_of(tile * wide, wide), wide)
            target[:, into] = dot(self.left[self.slots[turn], :], self.right[source, :], ((1,), (1,))).astype(bf16)
            return carry

        lax.fori_loop(0, columns // wide, body, 0)


def dot(left, right, sides=((1,), (0,)), precision=None):
    return lax.dot_general(left, right, (sides, ((), ())), precision=precision, preferred_element_type=f32)


def attend(tokens, gain, weights, first, position_rows, rooms, at, slot, rows):
    normed, qkv, probs, cosines, sines, out, inverse = rooms
    own = pl.ds(pl.multiple_of(slot * rows, rows), rows)

    def norm(piece_at, carry):
        source = pl.ds(pl.multiple_of(slot * rows + piece_at * 16, 16), 16)
        values = tokens[source, :].astype(f32)
        rstd = lax.rsqrt(jnp.mean(values * values, axis=1, keepdims=True) + eps)
        normed[at, pl.ds(pl.multiple_of(piece_at * 16, 16), 16), :] = (values * rstd * gain).astype(bf16)
        return carry

    lax.fori_loop(0, rows // 16, norm, 0)
    half = HEAD_DIM // 2
    angles = (position_rows - first) * inverse[...]
    lane = lax.broadcasted_iota(jnp.int32, (rows, HEAD_DIM), 1)
    cosine, sine = jnp.cos(angles), jnp.sin(angles)
    sine = jnp.where(lane < half, -sine, sine)
    cosines[own, :] = cosine
    sines[own, :] = sine
    lin = dot(normed[at], weights[...])

    def turn(values):
        return (values * cosine + pltpu.roll(values, half, 1) * sine).astype(bf16)

    query, keyed = turn(lin[:, :HEAD_DIM]), turn(lin[:, HEAD_DIM : 2 * HEAD_DIM])
    valued = lin[:, 2 * HEAD_DIM :].astype(bf16)
    qkv[own, :HEAD_DIM] = query
    qkv[own, HEAD_DIM : 2 * HEAD_DIM] = keyed
    qkv[own, 2 * HEAD_DIM :] = valued
    key_at = lax.broadcasted_iota(jnp.int32, (rows, rows), 1).astype(f32)
    query_at = lax.broadcasted_iota(jnp.int32, (rows, rows), 0).astype(f32)
    allowed = (key_at <= query_at) & (key_at >= first[:, :1])
    scores = jnp.where(allowed, dot(query, keyed, ((1,), (1,))) * (HEAD_DIM ** (-0.5)), floor_score)
    raised = jnp.exp(scores - jnp.max(scores, axis=1, keepdims=True))
    chances = raised / jnp.sum(raised, axis=1, keepdims=True)
    probs[own, :] = chances
    out[slot] = dot(chances.astype(bf16), valued).astype(bf16)


def attend_back(normed, rooms, slot, rows, start):
    qkv, probs, cosines, sines, grads, grad_qkv, sums = rooms
    own = pl.ds(pl.multiple_of(slot * rows, rows), rows)
    query = qkv[own, :HEAD_DIM]
    keyed = qkv[own, HEAD_DIM : 2 * HEAD_DIM]
    valued = qkv[own, 2 * HEAD_DIM :]
    cosine, sine = cosines[own, :], sines[own, :]
    chances, grad = probs[own, :], grads[slot]
    scale = HEAD_DIM ** (-0.5)

    def turn_back(values):
        return (values * cosine - pltpu.roll(values, HEAD_DIM // 2, 1) * sine).astype(bf16)

    grad_qkv[own, 2 * HEAD_DIM :] = dot(chances.astype(bf16), grad, ((0,), (0,))).astype(bf16)
    grad_chances = dot(grad, valued, ((1,), (1,)))
    weighted = jnp.sum(chances * grad_chances, axis=1, keepdims=True)
    grad_scores = (chances * (grad_chances - weighted)).astype(bf16)
    grad_qkv[own, :HEAD_DIM] = turn_back(dot(grad_scores, keyed) * scale)
    grad_qkv[own, HEAD_DIM : 2 * HEAD_DIM] = turn_back(dot(grad_scores, query, ((0,), (0,))) * scale)
    wide = 512

    def body(tile, carry):
        into = pl.ds(pl.multiple_of(tile * wide, wide), wide)
        product = dot(grad_qkv[own, :], normed[:, into], ((0,), (0,)))
        sums[:, into] = product if start else sums[:, into] + product
        return carry

    lax.fori_loop(0, sums.shape[1] // wide, body, 0)


def add_up(target, sources, rows, columns):
    step = max(16, min(rows, 16384 // columns // 16 * 16))

    def body(at, carry):
        piece = pl.ds(pl.multiple_of(at * step, step), step)
        total = sources[0][piece, :].astype(f32)
        for other in sources[1:]:
            total = total + other[piece, :].astype(f32)
        target[piece, :] = total.astype(target.dtype)
        return carry

    lax.fori_loop(0, rows // step, body, 0)


class Product:
    def __init__(self, place, left, varied, fixed, rooms, members, rows, columns):
        self.place, self.left, self.varied = place, left, varied
        self.lhs, self.rhs = rooms
        self.rows, self.columns = rows, columns
        self.lead = 0 if varied is None else varied.shape[0] // members
        self.waits, self.turn = {}, 0
        self.setup = []
        for buffer in range(self.rhs.shape[0]):
            self.setup.append(place.keep(fixed, self.rhs.at[buffer, pl.ds(self.lead, fixed.shape[0]), :]))

    def fetch(self, turn, slot):
        buffer = turn % 2
        rows = pl.ds(pl.multiple_of(slot * self.rows, self.rows), self.rows)
        moves = [self.place.keep(self.left.at[rows, :], self.lhs.at[buffer])]
        if self.lead:
            lead = pl.ds(pl.multiple_of(slot * self.lead, self.lead), self.lead)
            moves.append(self.place.keep(self.varied.at[lead, :], self.rhs.at[buffer, pl.ds(0, self.lead), :]))
        self.waits[turn] = moves

    def ready(self, turn):
        for move in self.setup:
            move.wait()
        self.setup = []
        for move in self.waits.pop(turn):
            move.wait()

    def make(self, turn, core, target):
        buffer = turn % 2
        right = self.rhs.at[buffer if self.lead else 0]
        wide = min(self.columns, 512)

        def body(at, carry):
            source = pl.ds(pl.multiple_of(core * self.columns + at * wide, wide), wide)
            into = pl.ds(pl.multiple_of(at * wide, wide), wide)
            target[:, into] = jnp.dot(
                self.lhs[buffer], right[:, source], preferred_element_type=f32
            ).astype(bf16)
            return carry

        lax.fori_loop(0, self.columns // wide, body, 0)


def scatter(place, members, sources, room, views, shape, halves, credit=None):
    block = Block(place, members)
    deep, e, t = block.deep, place.e, place.t
    rows, columns = shape
    order = 1 - lax.rem(t, 2)
    cores = place.cores if halves else 1
    count = len(sources)
    mine, outgoing, land0, land1s, land2s, land3s, finals = room
    s0, r0 = place.take(4 * deep * cores * count), place.take(4 * deep * cores * count)
    s1, r1 = place.take(2 * deep * count), place.take(2 * deep * count)
    s2, r2 = place.take(deep * count), place.take(deep * count)
    s3, r3 = place.take(deep * count), place.take(deep * count)
    s4, r4 = place.take(cores * count), place.take(cores * count)
    walk = [(f, k) for f in range(count) for k in list(range(1, deep)) + [0]]
    one, two = block.flips(order)
    sent, loads, last, kept = [], {}, {}, []
    quads = [(1, 1), (1, 0), (0, 1), (0, 0)]
    turns = [(f, k, i, j) for f, k in walk for i, j in quads]
    ring = outgoing.shape[0]
    leaving = []

    def slot_of(k, i, j):
        return block.slot(k, i, j, order)

    def land_index(d, k, i, j):
        return (d - 1) * deep * 4 + k * 4 + i * 2 + j

    def produce(number):
        f, k, i, j = turns[number]
        source = sources[f]
        if (k, i, j) in last:
            last.pop((k, i, j)).wait_send()
        if not isinstance(source, (Product, Kept)):
            loads[f, k, i, j] = place.keep(source(slot_of(k, i, j)), mine.at[slot_of(k, i, j)])
            return
        local_number = number - f * 4 * deep
        if local_number == 0:
            source.fetch(0, slot_of(k, i, j))
        source.ready(local_number)
        if local_number + 1 < 4 * deep:
            source.fetch(local_number + 1, slot_of(*turns[number + 1][1:]))
        if number >= ring:
            for move in leaving[number - ring]:
                move.wait_send()
        moves = []
        for d in range(1, cores):
            target = place.ring(d)
            buffer = outgoing.at[number % ring, d - 1]
            source.make(local_number, target, buffer)
            at = land_index(d, k, *((j, i) if d % 2 else (i, j)))
            if f > 0:
                pl.semaphore_wait(credit.at[at], 1)
            sem = f * 4 * deep * cores + at
            moves.append(place.send(buffer, land0.at[at], s0 + sem, r0 + sem, e, target))
        leaving.append(moves)
        source.make(local_number, t, mine.at[slot_of(k, i, j)])

    def terms_of(f, k, i, j):
        if (f, k, i, j) in loads:
            loads[f, k, i, j].wait()
        terms = [mine.at[slot_of(k, i, j)]]
        for d in range(1, cores):
            at = land_index(d, k, i, j)
            place.arrived(land0.at[at], r0 + f * 4 * deep * cores + at)
            terms.append(land0.at[at])
        if i == 0:
            at = (f * deep + k) * 2 + j
            place.arrived(land1s.at[at], r1 + at)
            terms.append(land1s.at[at])
            if j == 0:
                at = f * deep + k
                place.arrived(land2s.at[at], r2 + at)
                terms.append(land2s.at[at])
        return terms

    def give_back(f, k, i, j):
        if f + 1 < count:
            for d in range(1, cores):
                pl.semaphore_signal(
                    credit.at[land_index(d, k, i, j)],
                    inc=1,
                    device_id={"expert": e, "tensor": place.ring(cores - d)},
                    device_id_type=MESH,
                )

    def leave(f, k, i, j, landing, out, into, at, target):
        move = place.send(mine.at[slot_of(k, i, j)], landing.at[at], out + at, into + at, target, t)
        last[k, i, j] = move

    def first_flip(f, k, j):
        terms, ref = terms_of(f, k, 1, j), mine.at[slot_of(k, 1, j)]
        if len(terms) > 1:
            add_up(ref, terms, rows, columns)
        give_back(f, k, 1, j)
        leave(f, k, 1, j, land1s, s1, r1, (f * deep + k) * 2 + j, e + one)

    def second_flip(f, k):
        add_up(mine.at[slot_of(k, 0, 1)], terms_of(f, k, 0, 1), rows, columns)
        give_back(f, k, 0, 1)
        leave(f, k, 0, 1, land2s, s2, r2, f * deep + k, e + two)

    def line(f, k):
        terms, ref = terms_of(f, k, 0, 0), mine.at[slot_of(k, 0, 0)]
        if k > 0:
            add_up(ref, terms, rows, columns)
            give_back(f, k, 0, 0)
            peer = block.device(lax.rem(block.rank + k, deep) * 4 + place.quad)
            leave(f, k, 0, 0, land3s, s3, r3, f * deep + k, peer)
            return
        for far in range(1, deep):
            place.arrived(land3s.at[f * deep + far], r3 + f * deep + far)
            terms.append(land3s.at[f * deep + far])
        final = finals.at[f]
        add_up(final, terms, rows, columns)
        give_back(f, k, 0, 0)
        kept.append(place.keep(final, views[f](t)))
        for d in range(1, cores):
            at = f * cores + d
            sent.append(place.send(final, views[f](t), s4 + at, r4 + at, e, place.ring(d)))

    for step in range(len(walk) + 2):
        fresh = step < len(walk)
        if fresh:
            produce(4 * step)
            yield
            produce(4 * step + 1)
            yield
            first_flip(*walk[step], 1)
            yield
            produce(4 * step + 2)
            yield
        if 0 <= step - 1 < len(walk):
            second_flip(*walk[step - 1])
            yield
        if fresh:
            produce(4 * step + 3)
            yield
            first_flip(*walk[step], 0)
            yield
        if 0 <= step - 2 < len(walk):
            line(*walk[step - 2])
            yield
    for f in range(count):
        for d in range(1, cores):
            place.arrived(views[f](place.ring(cores - d)), r4 + f * cores + d)
    for moves in leaving[-ring:]:
        for move in moves:
            move.wait_send()
    for move in list(last.values()) + sent:
        move.wait_send()
    for move in kept:
        move.wait()


def scatter_scratch(members, cores, rows, columns, products=(), ring=4):
    deep = members // 4
    count = max(1, len(products))
    short = rows if cores > 1 else 16
    rooms = [
        pltpu.VMEM((members, rows, columns), bf16),
        pltpu.VMEM((ring, max(1, cores - 1), short, columns), bf16),
        pltpu.VMEM((max(1, (cores - 1) * members), short, columns), bf16),
        pltpu.VMEM((2 * deep * count, rows, columns), bf16),
        pltpu.VMEM((deep * count, rows, columns), bf16),
        pltpu.VMEM((deep * count, rows, columns), bf16),
        pltpu.VMEM((count, rows, columns), bf16),
    ]
    for depth, varied in products:
        rooms.append(pltpu.VMEM((2, rows, depth), bf16))
        rooms.append(pltpu.VMEM((2 if varied else 1, depth, columns * cores), bf16))
    return rooms


def exchange(place, members, source, landing):
    e, t = place.e, place.t
    own = lax.rem(e, members)
    base = e - own
    sends, arrivals = place.take(members), place.take(members)
    sent = []
    for d in range(1, members):
        target = lax.rem(own + d, members)
        sent.append(place.send(source(target), landing(own), sends + d, arrivals + d, base + target, t))
    kept = place.keep(source(own), landing(own))
    yield
    for d in range(1, members):
        place.arrived(landing(lax.rem(own + members - d, members)), arrivals + d)
    for move in sent:
        move.wait_send()
    kept.wait()


def start_exchange(place, members, source, landing):
    e, t = place.e, place.t
    own = lax.rem(e, members)
    base = e - own
    sends, arrivals = place.take(members), place.take(members)
    sent = []
    for d in range(1, members):
        target = lax.rem(own + d, members)
        sent.append(place.send(source(target), landing(own), sends + target, arrivals + own, base + target, t))
    place.keep(source(own), landing(own)).wait()

    def arrived(slot):
        pl.when(slot != own)(lambda: place.arrived(landing(slot), arrivals + slot))

    def finish():
        for move in sent:
            move.wait_send()

    return arrived, finish


def both(place, members, source, landing, part):
    yield from exchange(place, members, source, lambda slot: landing(place.t, slot))
    sends, arrivals = place.take(place.cores), place.take(place.cores)
    sent = []
    for d in range(1, place.cores):
        mine = part(place.t)
        sent.append(place.send(mine, mine, sends + d, arrivals + d, place.e, place.ring(d)))
    yield
    for d in range(1, place.cores):
        place.arrived(part(place.ring(place.cores - d)), arrivals + d)
    for move in sent:
        move.wait_send()


def twice(task):
    for _ in task:
        next(task, None)
        yield


def later(task, rounds):
    for _ in range(rounds):
        yield
    yield from task


def run(tasks):
    while tasks:
        for task in list(tasks):
            try:
                next(task)
            except StopIteration:
                tasks.remove(task)


def transfer(name, number, mesh, body, ins, outs, scratch=(), semaphores=400, vmem=None):
    count, cores = mesh.shape["expert"], mesh.shape["tensor"]
    semaphores = semaphores * max(1, count * cores // 32)

    def kernel(*refs):
        given = refs[: len(ins)]
        made = refs[len(ins) : len(ins) + len(outs)]
        room = refs[len(ins) + len(outs) : -1]
        place = Place(refs[-1], count, cores)
        place.meet()
        tasks = []
        for task in body(place, given, made, room):
            if isinstance(task, list):
                run(task)
            else:
                tasks.append(task)
        run(tasks)
        assert place.used <= semaphores, place.used

    size = sum(x.size * x.dtype.itemsize for x in list(ins) + list(outs))
    return pl.pallas_call(
        kernel,
        name=name,
        out_shape=[jax.ShapeDtypeStruct(shape, dtype) for shape, dtype in outs_of(outs)],
        in_specs=[ANY] * len(ins),
        out_specs=[ANY] * len(outs),
        scratch_shapes=list(scratch) + [pltpu.SemaphoreType.DMA((semaphores,))],
        cost_estimate=pl.CostEstimate(flops=0, bytes_accessed=size, transcendentals=0),
        compiler_params=pltpu.CompilerParams(
            collective_id=number, has_side_effects=True, vmem_limit_bytes=vmem
        ),
    )(*ins)


def outs_of(outs):
    return [(x.shape, x.dtype) for x in outs]


def like(shape, dtype=bf16):
    return jax.ShapeDtypeStruct(shape, dtype)


def part_view(ref, rows, columns, pieces=1):
    height = rows // pieces

    def view(slot, core, piece=0):
        at = 0 if isinstance(slot, int) else pl.multiple_of(slot * rows, rows)
        return ref.at[
            pl.ds(at + piece * height, height), pl.ds(pl.multiple_of(core * columns, columns), columns)
        ]

    return view


PIECES = 2


def lanes(at, columns):
    return pl.ds(pl.multiple_of(at * columns, columns), columns)


class Strips:
    def __init__(self, count, columns):
        self.count, self.columns = count, columns
        self.direct = columns % 128 == 0

    def shape(self, rows):
        return (rows, self.count * self.columns) if self.direct else (self.count, rows, self.columns)

    def at(self, ref, slot):
        return ref.at[:, lanes(slot, self.columns)] if self.direct else ref.at[slot]

    def cut(self, array):
        rows = array.shape[0]
        return array if self.direct else array.reshape(rows, self.count, self.columns).transpose(1, 0, 2)

    def join(self, array):
        rows = array.shape[0 if self.direct else 1]
        return array if self.direct else array.transpose(1, 0, 2).reshape(rows, self.count * self.columns)


def row_gather(place, members, source, landing, rows, part):
    def mine(piece):
        height = rows // PIECES
        return source.at[pl.ds(piece * height, height), lanes(place.t, part)]

    whole = (source, lambda slot: landing.at[pl.ds(pl.multiple_of(slot * rows, rows), rows), :])
    return Gather(place, members, mine, whole, part_view(landing, rows, part, PIECES), True, PIECES)


def rotary(values, cosine, sine):
    half = values.shape[-1] // 2
    first = values[..., :half]
    second = values[..., half:]
    return jnp.concatenate([first * cosine - second * sine, second * cosine + first * sine], axis=-1)


def rotary_back(grads, cosine, sine):
    half = grads.shape[-1] // 2
    first = grads[..., :half]
    second = grads[..., half:]
    return jnp.concatenate([first * cosine + second * sine, second * cosine - first * sine], axis=-1)


def sequence_tables(lengths_rows, tok_rows):
    ends = jnp.cumsum(lengths_rows, axis=1)
    starts = ends - lengths_rows
    places = jnp.arange(tok_rows, dtype=jnp.int32)
    segment = jnp.sum((places[None, :, None] >= ends[:, None, :]).astype(jnp.int32), axis=2)
    member = segment[:, :, None] == jnp.arange(lengths_rows.shape[1], dtype=jnp.int32)[None, None, :]
    first = jnp.sum(jnp.where(member, starts[:, None, :], 0), axis=2)
    return segment, places[None, :] - first


def silu_parts(values):
    sigmoid_value = jax.nn.sigmoid(values)
    return values * sigmoid_value, sigmoid_value * (1.0 + values * (1.0 - sigmoid_value))


def mm(form, left, right):
    return jnp.einsum(form, left, right, preferred_element_type=f32)


def up_to(value, step):
    return -(-value // step) * step


def second_norm(place, cores, rows, given, hid_out, room):
    ap, tok, gn, rt, mk = given
    parts, tok_v, gn_v, rt_v, mk_v, hid, xn, _ = room
    t = place.t
    sends, arrivals = place.take(cores), place.take(cores)
    sent = [place.send(ap, parts.at[t], sends + d, arrivals + d, place.e, place.ring(d)) for d in range(1, cores)]
    kept = [place.keep(ap, parts.at[t])]
    kept += [place.keep(a, b) for a, b in ((tok, tok_v), (gn, gn_v), (rt, rt_v), (mk, mk_v))]
    for move in kept:
        move.wait()
    for d in range(1, cores):
        place.arrived(parts.at[place.ring(cores - d)], arrivals + d)

    def body(at, carry):
        piece = pl.ds(pl.multiple_of(at * 16, 16), 16)
        total = parts[0, piece, :].astype(f32)
        for core in range(1, cores):
            total = total + parts[core, piece, :].astype(f32)
        values = tok_v[piece, :].astype(f32) + total
        hid[piece, :] = values
        rstd = lax.rsqrt(jnp.mean(values * values, axis=1, keepdims=True) + eps)
        xn[piece, :] = (values * rstd * gn_v[...]).astype(bf16)
        return carry

    lax.fori_loop(0, rows // 16, body, 0)
    saved = place.keep(hid, hid_out)
    return sent, saved


def route(room):
    _, _, _, rt_v, mk_v, _, xn, gt = room
    logits = lax.dot_general(rt_v[...], xn[...], (((1,), (1,)), ((), ())), preferred_element_type=f32)
    picked = mk_v[...] > 0.5
    top_logit = jnp.max(jnp.where(picked, logits, floor_score), axis=0, keepdims=True)
    lifted = jnp.where(picked, jnp.exp(jnp.where(picked, logits - top_logit, 0.0)), 0.0)
    gt[...] = lifted / jnp.sum(lifted, axis=0, keepdims=True)


class Out:
    def __init__(self, place, buffer, array, unit):
        self.place, self.buffer, self.array, self.unit = place, buffer, array, unit
        self.sem = place.take(2)

    def moves(self, slots):
        for at, slot in enumerate(slots):
            if self.unit is None:
                yield self.place.local(self.buffer.at[at], self.array.at[slot], self.sem + at)
            else:
                into = pl.ds(pl.multiple_of(slot * self.unit, self.unit), self.unit)
                source = self.buffer.at[pl.ds(at * self.unit, self.unit), :]
                yield self.place.local(source, self.array.at[into, :], self.sem + at)

    def go(self, slots):
        for move in self.moves(slots):
            move.start()

    def free(self, condition=None):
        for move in self.moves((jnp.int32(0), jnp.int32(0))):
            when(condition, move.wait)


def experts_pair(slots, used, capacity, rows, rows_in, grads_in, position, gate_of, weights, outs):
    wg, wu, wd, sh_in, sh_down = weights
    received, gated, low, back, acts, gate_backs, up_backs, dots_out, left_forward, left_backward = outs
    wide = sh_down.shape[0]
    places = lax.broadcasted_iota(jnp.int32, (capacity, rows), 0).astype(f32)
    gates, onehots = [], []
    for out in (received, gated, low, left_forward, left_backward):
        out.free(used)
    for at, slot in enumerate(slots):
        token, own = pl.ds(pl.multiple_of(slot * rows, rows), rows), pl.ds(at * capacity, capacity)
        mine = pl.ds(at * rows, rows)
        chosen = (position[slot] == places).astype(f32)
        onehot = chosen.astype(bf16)
        onehots.append(chosen)
        received.buffer[own, :] = dot(onehot, rows_in[token, :]).astype(bf16)
        gate = jnp.sum(chosen * gate_of(slot), axis=1, keepdims=True)
        row_grads = dot(onehot, grads_in[mine, :])
        gated.buffer[own, :] = (gate * row_grads).astype(bf16)
        low.buffer[own, :] = row_grads.astype(bf16)
        gates.append(gate)
        turned = chosen.T.astype(bf16)
        left_forward.buffer[mine, :capacity] = turned
        left_backward.buffer[mine, :capacity] = turned
    received.go(slots)
    gated.go(slots)
    gate = jnp.concatenate(gates, axis=0)
    rows_now = received.buffer[...]
    exp_gate = dot(rows_now, wg[...], ((1,), (1,)))
    exp_up = dot(rows_now, wu[...], ((1,), (1,)))
    silu, slope = silu_parts(exp_gate)
    act = (silu * exp_up).astype(bf16)
    acts.free(used)
    acts.buffer[...] = act
    acts.go(slots)
    out = dot(act, wd[...])
    dots = jnp.sum(low.buffer[...].astype(f32) * out, axis=1, keepdims=True)
    low.buffer[...] = (gate * out).astype(bf16)
    low.go(slots)
    dots_out.free(used)
    for at in range(2):
        column = dots[at * capacity : (at + 1) * capacity]
        token_dots = jnp.sum(onehots[at] * column, axis=0, keepdims=True)
        dots_out.buffer[at] = jnp.broadcast_to(token_dots, (8, rows))
    dots_out.go(slots)
    act_grad = dot(gated.buffer[...], wd[...], ((1,), (1,)))
    gate_back = (act_grad * exp_up * slope).astype(bf16)
    up_back = (act_grad * silu).astype(bf16)
    gate_backs.free(used)
    up_backs.free(used)
    gate_backs.buffer[...] = gate_back
    up_backs.buffer[...] = up_back
    gate_backs.go(slots)
    up_backs.go(slots)
    back.free(used)
    back.buffer[...] = (dot(gate_back, wg[...]) + dot(up_back, wu[...])).astype(bf16)
    back.go(slots)
    for at, slot in enumerate(slots):
        token, mine = pl.ds(pl.multiple_of(slot * rows, rows), rows), pl.ds(at * rows, rows)
        both_sides = dot(rows_in[token, :], sh_in[...], ((1,), (1,)))
        sh_gate, sh_up = both_sides[:, :wide], both_sides[:, wide:]
        sh_silu, sh_slope = silu_parts(sh_gate)
        left_forward.buffer[mine, capacity:] = (sh_silu * sh_up).astype(bf16)
        sh_grad = dot(grads_in[mine, :], sh_down[...], ((1,), (1,)))
        left_backward.buffer[mine, capacity : capacity + wide] = (sh_grad * sh_up * sh_slope).astype(bf16)
        left_backward.buffer[mine, capacity + wide :] = (sh_grad * sh_silu).astype(bf16)
    left_forward.go(slots)
    left_backward.go(slots)


def experts_kernel(
    groups,
    capacity,
    rows,
    xn_ref,
    grad_ref,
    position_ref,
    gate_ref,
    wg_ref,
    wu_ref,
    wd_ref,
    sh_in_ref,
    sh_down_ref,
    received_ref,
    gated_ref,
    low_ref,
    back_ref,
    act_ref,
    gate_back_ref,
    up_back_ref,
    dots_ref,
    left_forward_ref,
    left_backward_ref,
):
    places = lax.broadcasted_iota(jnp.int32, (capacity, rows), 0).astype(f32)
    gates, grads, onehots = [], [], []
    for g in range(groups):
        token = pl.ds(g * rows, rows)
        slot = pl.ds(g * capacity, capacity)
        chosen = (position_ref[g] == places).astype(f32)
        onehot = chosen.astype(bf16)
        onehots.append(chosen)
        received_ref[slot, :] = dot(onehot, xn_ref[token, :]).astype(bf16)
        gate = jnp.sum(chosen * gate_ref[g], axis=1, keepdims=True)
        row_grads = dot(onehot, grad_ref[token, :])
        gated_ref[slot, :] = (gate * row_grads).astype(bf16)
        low_ref[slot, :] = row_grads.astype(bf16)
        gates.append(gate)
        turned = chosen.T.astype(bf16)
        left_forward_ref[token, :capacity] = turned
        left_backward_ref[token, :capacity] = turned
    gate = jnp.concatenate(gates, axis=0)
    received = received_ref[...]
    exp_gate = dot(received, wg_ref[...], ((1,), (1,)))
    exp_up = dot(received, wu_ref[...], ((1,), (1,)))
    silu, slope = silu_parts(exp_gate)
    act = (silu * exp_up).astype(bf16)
    act_ref[...] = act
    out = dot(act, wd_ref[...])
    dots = jnp.sum(low_ref[...].astype(f32) * out, axis=1, keepdims=True)
    low_ref[...] = (gate * out).astype(bf16)
    for g in range(groups):
        column = dots[g * capacity : (g + 1) * capacity]
        token_dots = jnp.sum(onehots[g] * column, axis=0, keepdims=True)
        dots_ref[g] = jnp.broadcast_to(token_dots, (8, rows))
    act_grad = dot(gated_ref[...], wd_ref[...], ((1,), (1,)))
    gate_back = (act_grad * exp_up * slope).astype(bf16)
    up_back = (act_grad * silu).astype(bf16)
    gate_back_ref[...] = gate_back
    up_back_ref[...] = up_back
    back_ref[...] = (
        dot(gate_back, wg_ref[...]) + dot(up_back, wu_ref[...])
    ).astype(bf16)
    wide = sh_down_ref.shape[0]
    both = dot(xn_ref[...], sh_in_ref[...], ((1,), (1,)))
    sh_gate, sh_up = both[:, :wide], both[:, wide:]
    sh_silu, sh_slope = silu_parts(sh_gate)
    left_forward_ref[:, capacity:] = (sh_silu * sh_up).astype(bf16)
    sh_grad = dot(grad_ref[...], sh_down_ref[...], ((1,), (1,)))
    left_backward_ref[:, capacity : capacity + wide] = (sh_grad * sh_up * sh_slope).astype(bf16)
    left_backward_ref[:, capacity + wide :] = (sh_grad * sh_silu).astype(bf16)


def experts_pass(count, capacity, rows, xn_all, grad_all, position, gate, wg, wu, wd, sh_in, sh_down):
    groups = 2
    units, width = wg.shape
    wide = sh_down.shape[0]

    def along(*shape):
        return pl.BlockSpec(shape, lambda i: (i,) + (0,) * (len(shape) - 1))

    def whole(array):
        return pl.BlockSpec(array.shape, lambda i: (0,) * array.ndim, pipeline_mode=pl.Buffered(1))

    slots = groups * capacity
    tokens = groups * rows
    flops = 2 * count * capacity * width * units * 6
    return pl.pallas_call(
        functools.partial(experts_kernel, groups, capacity, rows),
        name="experts_pass",
        grid=(count // groups,),
        in_specs=[
            along(tokens, width),
            along(tokens, width),
            along(groups, 1, rows),
            along(groups, 1, rows),
            whole(wg),
            whole(wu),
            whole(wd),
            whole(sh_in),
            whole(sh_down),
        ],
        out_specs=[
            along(slots, width),
            along(slots, width),
            along(slots, width),
            along(slots, width),
            along(slots, units),
            along(slots, units),
            along(slots, units),
            along(groups, 8, rows),
            along(tokens, capacity + wide),
            along(tokens, capacity + 2 * wide),
        ],
        out_shape=[like((count * capacity, width))] * 4
        + [like((count * capacity, units))] * 3
        + [
            like((count, 8, rows), f32),
            like((count * rows, capacity + wide)),
            like((count * rows, capacity + 2 * wide)),
        ],
        cost_estimate=pl.CostEstimate(
            flops=flops, bytes_accessed=4 * count * (rows + 2 * capacity) * width, transcendentals=0
        ),
        compiler_params=pltpu.CompilerParams(vmem_limit_bytes=58 * 2**20),
    )(xn_all, grad_all, position, gate, wg, wu, wd, sh_in, sh_down)


def local(
    mesh,
    tokens,
    lengths,
    routes,
    gain_attn,
    w_query,
    w_key,
    w_value,
    w_out,
    gain_ffn,
    w_router,
    routed_gate_weight,
    routed_up_weight,
    w_down,
    w_shared_gate,
    w_shared_up,
    w_shared_down,
    out_grad,
):
    count, cores = mesh.shape["expert"], mesh.shape["tensor"]
    rows, width = tokens.shape
    part = width // cores
    deep = w_query.shape[0]
    experts = w_router.shape[1]
    heads = w_query.shape[1] // HEAD_DIM
    capacity = up_to(min(rows, rows * TOP * 4 // (3 * count)), 128)
    hidden_units = w_shared_gate.shape[1] // count
    scale = HEAD_DIM ** (-0.5)
    e = lax.axis_index("expert")
    t = lax.axis_index("tensor")
    chunk = heads * rows
    strips = Strips(count, deep)

    expert_ids = jnp.arange(experts, dtype=jnp.int32)
    choose = jnp.any(routes[:, :, None] == expert_ids[None, None, :], axis=1)
    mask_t = choose.T.astype(bf16)
    vectors = jnp.concatenate(
        [
            w_router.T,
            gain_attn[None],
            gain_ffn[None],
            jnp.pad(lengths.astype(bf16), ((0, 0), (0, deep - lengths.shape[1]))),
        ],
        axis=0,
    )
    head_rows = up_to(vectors.shape[0], 16)
    vectors = jnp.pad(vectors, ((0, head_rows - vectors.shape[0]), (0, 0)))
    pieces = rows // deep
    mask_rows = mask_t.reshape(experts * pieces, deep)
    small = jnp.concatenate([vectors, mask_rows], axis=0)
    small_rows = up_to(small.shape[0], 16)
    small = jnp.pad(small, ((0, small_rows - small.shape[0]), (0, 0)))

    def unpack(gathered):
        router = gathered[:experts]
        attn_gain, ffn_gain = gathered[experts].astype(f32), gathered[experts + 1].astype(f32)
        rows_of = gathered[experts + 2].reshape(count, deep)[:, : lengths.shape[1]].astype(f32).astype(jnp.int32)
        masks = gathered[head_rows : head_rows + experts * pieces].reshape(experts, pieces, count, deep)
        return router, attn_gain, ffn_gain, rows_of, masks.transpose(2, 0, 1, 3).reshape(count, experts, rows)

    shared_pack = jnp.concatenate(
        [
            w_shared_gate.T.reshape(count, hidden_units, deep),
            w_shared_up.T.reshape(count, hidden_units, deep),
            w_shared_down.reshape(count, hidden_units, deep),
        ],
        axis=1,
    )
    pack_rows = up_to(3 * hidden_units, 16)
    shared_pack = jnp.pad(shared_pack, ((0, 0), (0, pack_rows - 3 * hidden_units), (0, 0)))
    out_rows = w_out.shape[0]

    if strips.direct:

        def front_body(place, given, made, room):
            tok, sm, wq, wk, wv, wo, sp, inv = given
            sm_all, w_all, xn_all, qkv_all, pr_all, ct_all, st_all, ho_all, wo_all, sp_all = made
            sm_v, tok_v, w_v, normed, qkv, probs, cosines, sines, out, inverse = room
            own = lax.rem(place.e, heads)
            base = place.e - own
            ready = place.keep(inv, inverse)
            small_in, small_out = start_exchange(place, count, lambda s: sm, lambda s: sm_v.at[:, lanes(s, deep)])
            tokens_in = row_gather(place, heads, tok, tok_v, rows, part)
            sends, arrivals = place.take(heads), place.take(heads)

            def wo_view(slot, core=0, piece=0):
                return strips.at(wo_all, slot)

            def attention():
                links = tokens_in.links()
                for _ in range(PIECES):
                    next(links)
                pulls = []
                for which, weight in enumerate((wq, wk, wv)):

                    def landing(slot, which=which):
                        at = pl.ds(pl.multiple_of(slot * deep, deep), deep)
                        return w_v.at[at, pl.ds(which * HEAD_DIM, HEAD_DIM)]

                    pulls.append(
                        start_exchange(
                            place, count, lambda s, w=weight: w.at[:, lanes(lax.rem(s, heads), HEAD_DIM)], landing
                        )
                    )
                yield
                yield from links
                for d in range(1, count):
                    slot = lax.rem(place.e + d, count)
                    for arrived in [small_in] + [pull[0] for pull in pulls]:
                        arrived(slot)
                ready.wait()
                saved = [place.keep(sm_v, sm_all), place.keep(w_v, w_all)]
                head = experts - experts % 16
                vectors = sm_v[pl.ds(head, 16), :].astype(f32)
                gain = vectors[experts - head : experts - head + 1, :]
                position = lax.broadcasted_iota(jnp.int32, (rows, HEAD_DIM), 0).astype(f32)
                gave, stored = [], []

                def group(n, i, j):
                    tokens_in.from_cores(n, i, j)
                    slot = tokens_in.slot(n, i, j)
                    at = len(stored) % 2
                    if len(stored) >= 2:
                        stored[-2].wait()
                    row = sm_v[pl.ds(head, 16), lanes(tokens_in.block.device(slot), deep)].astype(f32)
                    row = row[experts + 2 - head : experts + 3 - head, :]
                    end, first = jnp.zeros((1, 1), f32), jnp.zeros((rows, HEAD_DIM), f32)
                    for place_in in range(lengths.shape[1]):
                        end = end + row[:, place_in : place_in + 1]
                        first = jnp.where(position >= end, end, first)
                    attend(
                        tok_v,
                        gain,
                        w_v,
                        first,
                        position,
                        (normed, qkv, probs, cosines, sines, out, inverse),
                        at,
                        slot,
                        rows,
                    )
                    stored.append(
                        place.keep(
                            normed.at[at], xn_all.at[pl.ds(pl.multiple_of(slot * rows, rows), rows), :]
                        )
                    )
                    landing = ho_all.at[:, lanes(own, HEAD_DIM)]
                    if n + i + j == 0:
                        saved.append(place.keep(out.at[slot], landing))
                    else:
                        gave.append(
                            place.send(out.at[slot], landing, sends + slot, arrivals + own, base + slot, place.t)
                        )

                for n in range(tokens_in.deep):
                    if n == 0:
                        tokens_in.kept.wait()
                    group(n, 0, 0)
                    yield
                for n in range(tokens_in.deep):
                    tokens_in.last(n)
                    for i, j in ((1, 0), (0, 1), (1, 1)):
                        group(n, i, j)
                        yield
                for source, target in ((qkv, qkv_all), (probs, pr_all), (cosines, ct_all), (sines, st_all)):
                    saved.append(place.keep(source, target))
                yield
                for d in range(1, heads):
                    slot = lax.rem(own + d, heads)
                    place.arrived(ho_all.at[:, lanes(slot, HEAD_DIM)], arrivals + slot)
                for move in gave:
                    move.wait_send()
                for move in stored[-2:] + saved:
                    move.wait()
                for pull in pulls:
                    pull[1]()
                small_out()
                tokens_in.finish()

            yield attention()
            yield later(gather(place, count, lambda p: wo, (wo, wo_view), wo_view, False), 3)
            yield later(exchange(place, count, lambda s: sp.at[s], lambda s: strips.at(sp_all, s)), 6)

        half = HEAD_DIM // 2
        inverse = 10000.0 ** (-2.0 * jnp.arange(half, dtype=f32) / HEAD_DIM)
        (
            small_all,
            w_qkv,
            xn_chunk,
            qkv_saved,
            probs_saved,
            cosine_wide,
            sine_wide,
            heads_out,
            out_full,
            shared_all,
        ) = transfer(
            "attention_front",
            0,
            mesh,
            front_body,
            (
                tokens,
                small,
                w_query,
                w_key,
                w_value,
                w_out,
                shared_pack,
                jnp.concatenate([inverse, inverse])[None],
            ),
            (
                like((small_rows, width)),
                like((width, 3 * HEAD_DIM)),
                like((chunk, width)),
                like((chunk, 3 * HEAD_DIM)),
                like((chunk, rows), f32),
                like((chunk, HEAD_DIM), f32),
                like((chunk, HEAD_DIM), f32),
                like((rows, heads * HEAD_DIM)),
                like((out_rows, width)),
                like((pack_rows, width)),
            ),
            [
                pltpu.VMEM((small_rows, width), bf16),
                pltpu.VMEM((chunk, width), bf16),
                pltpu.VMEM((width, 3 * HEAD_DIM), bf16),
                pltpu.VMEM((2, rows, width), bf16),
                pltpu.VMEM((chunk, 3 * HEAD_DIM), bf16),
                pltpu.VMEM((chunk, rows), f32),
                pltpu.VMEM((chunk, HEAD_DIM), f32),
                pltpu.VMEM((chunk, HEAD_DIM), f32),
                pltpu.VMEM((heads, rows, HEAD_DIM), bf16),
                pltpu.VMEM((1, HEAD_DIM), f32),
            ],
            semaphores=640,
            vmem=56 * 2**20,
        )
        router_full, attn_gain, ffn_gain, _, masks = unpack(small_all)
    else:
        def first_body(place, given, made, room):
            tok, sm, *weights = given
            tok_all, sm_all, w_all = made
            yield exchange(place, count, lambda s: sm, lambda s: sm_all.at[s])
            yield row_gather(place, heads, tok, tok_all, rows, part).all()
            for which, weight in enumerate(weights):

                def landing(slot, which=which):
                    at = pl.ds(pl.multiple_of(slot * deep, deep), deep)
                    return w_all.at[at, pl.ds(which * HEAD_DIM, HEAD_DIM)]

                yield exchange(
                    place, count, lambda s, w=weight: w.at[:, lanes(lax.rem(s, heads), HEAD_DIM)], landing
                )

        tok_chunk, small_all, w_qkv = transfer(
            "gather_tokens",
            0,
            mesh,
            first_body,
            (tokens, small, w_query, w_key, w_value),
            (like((chunk, width)), like((count, small_rows, deep)), like((width, 3 * HEAD_DIM))),
        )

        router_full, attn_gain, ffn_gain, lengths_all, masks = unpack(strips.join(small_all))

        member = e % heads
        lengths_chunk = lax.dynamic_slice_in_dim(lengths_all, e - member, heads, axis=0)
        segment, positions = sequence_tables(lengths_chunk, rows)
        half = HEAD_DIM // 2
        inverse = 10000.0 ** (-2.0 * jnp.arange(half, dtype=f32) / HEAD_DIM)
        angles = positions.astype(f32)[:, :, None] * inverse[None, None, :]
        cosine, sine = jnp.cos(angles), jnp.sin(angles)

        tok32 = tok_chunk.astype(f32)
        rstd_chunk = lax.rsqrt(jnp.mean(tok32 * tok32, axis=-1, keepdims=True) + eps)
        xn_chunk = (tok32 * rstd_chunk * attn_gain).astype(bf16)
        qkv = jnp.dot(xn_chunk, w_qkv, preferred_element_type=f32).reshape(heads, rows, 3 * HEAD_DIM)
        query = rotary(qkv[..., :HEAD_DIM], cosine, sine).astype(bf16)
        keyed = rotary(qkv[..., HEAD_DIM : 2 * HEAD_DIM], cosine, sine).astype(bf16)
        valued = qkv[..., 2 * HEAD_DIM :].astype(bf16)
        places = jnp.arange(rows, dtype=jnp.int32)
        allowed = (segment[:, :, None] == segment[:, None, :]) & (places[None, :] <= places[:, None])[None]
        scores = jnp.where(allowed, mm("gqd,gkd->gqk", query, keyed) * scale, floor_score)
        top_score = jnp.max(scores, axis=-1, keepdims=True)
        raised = jnp.exp(scores - top_score)
        probs = raised / jnp.sum(raised, axis=-1, keepdims=True)
        probs_low = probs.astype(bf16)
        head_out = mm("gqk,gkd->gqd", probs_low, valued).astype(bf16)

        def second_body(place, given, made, room):
            ho, og, wo, sp = given
            ho_all, og_all, wo_all, sp_all = made
            yield exchange(place, heads, lambda s: ho.at[s], lambda s: ho_all.at[:, lanes(s, HEAD_DIM)])
            yield row_gather(place, count, og, og_all, rows, part).all()

            def wo_view(slot, core=0, piece=0):
                return strips.at(wo_all, slot)

            yield gather(place, count, lambda p: wo, (wo, wo_view), wo_view, False)
            yield exchange(place, count, lambda s: sp.at[s], lambda s: strips.at(sp_all, s))

        heads_out, grad_all, out_full, shared_all = transfer(
            "gather_inputs",
            1,
            mesh,
            second_body,
            (head_out, out_grad, w_out, shared_pack),
            (
                like((rows, heads * HEAD_DIM)),
                like((count * rows, width)),
                like(strips.shape(out_rows)),
                like(strips.shape(pack_rows)),
            ),
            semaphores=640,
        )
        out_full, shared_all = strips.join(out_full), strips.join(shared_all)
    attention_part = jnp.dot(heads_out, out_full, preferred_element_type=f32).astype(bf16)

    own_mask = lax.dynamic_index_in_dim(masks, e, axis=1, keepdims=False).astype(f32)
    at_row = jnp.arange(rows, dtype=jnp.int32)
    earlier = (at_row[:, None] < at_row[None, :]).astype(bf16)
    position = jnp.where(own_mask > 0.5, jnp.dot(own_mask.astype(bf16), earlier, preferred_element_type=f32), -1.0)
    gate_weight, up_weight, down_weight = routed_gate_weight[0].T, routed_up_weight[0].T, w_down[0]
    sh_wide = up_to(hidden_units, 128)

    def widened(which):
        piece = shared_all[which * hidden_units : (which + 1) * hidden_units]
        return jnp.pad(piece, ((0, sh_wide - hidden_units), (0, 0)))

    fixed_backward = jnp.concatenate([widened(0), widened(1)], axis=0)
    fixed_forward = widened(2)
    units = gate_weight.shape[0]
    norm_rooms = [
        pltpu.VMEM((cores, rows, width), bf16),
        pltpu.VMEM((rows, width), bf16),
        pltpu.VMEM((1, width), f32),
        pltpu.VMEM((experts, width), bf16),
        pltpu.VMEM((experts, rows), f32),
        pltpu.VMEM((rows, width), f32),
        pltpu.VMEM((rows, width), bf16),
        pltpu.VMEM((experts, rows), f32),
    ]
    if strips.direct:

        def rows_body(place, given, made, room):
            og, pos, *weights = given[5:]
            hid_out, xn_all, og_all, gt_out, *arrays = made
            xn, gt = room[6:8]
            gates_v, xn_v, og_v, pos_v = room[8:12]
            weights_v, buffers = room[12:17], room[17:]
            grads_moving = row_gather(place, count, og, og_all, rows, part)
            for p in range(PIECES):
                grads_moving.start(p)
            loads = [place.keep(pos, pos_v)] + [place.keep(x, y) for x, y in zip(weights, weights_v)]
            sent, saved = second_norm(place, cores, rows, given[:5], hid_out, room[:8])
            moving = row_gather(place, count, xn, xn_v, rows, part)
            for p in range(PIECES):
                moving.start(p)
            route(room[:8])
            saved_gates = place.keep(gt, gt_out)
            gate_in, gate_out = start_exchange(place, count, lambda s: gt, lambda s: gates_v.at[s])
            sizes = [capacity] * 7 + [None] + [rows] * 2
            outs = [
                [Out(place, buffer.at[pair], array, unit) for buffer, array, unit in zip(buffers, arrays, sizes)]
                for pair in range(2)
            ]
            grad_sems, row_sems = place.take(4), place.take(4)
            quads = (((0, 0), (1, 0)), ((0, 1), (1, 1)))
            expert = lax.broadcasted_iota(jnp.int32, (experts, rows), 0)

            def gate_of(slot):
                return jnp.sum(jnp.where(expert == place.e, gates_v[slot], 0.0), axis=0, keepdims=True)

            def of_rows(slot):
                return pl.ds(pl.multiple_of(slot * rows, rows), rows)

            def grads(m, pair):
                for at, (i, j) in enumerate(quads[pair]):
                    source = og_all.at[of_rows(moving.slot(m, i, j)), :]
                    yield place.local(
                        source, og_v.at[pair, pl.ds(at * rows, rows), :], grad_sems + 2 * pair + at
                    )

            def keep_rows(m):
                for at, (i, j) in enumerate(quads[0] + quads[1]):
                    own = of_rows(moving.slot(m, i, j))
                    yield place.local(xn_v.at[own, :], xn_all.at[own, :], row_sems + at)

            def link(c):
                for gathered in (moving, grads_moving):
                    for p in range(PIECES):
                        gathered.from_one(c, p)
                        pl.when(c + 1 < moving.deep)(lambda: gathered.from_line(c + 1, p))

            def complete(gathered, m):
                gathered.last(m)
                for i, j in quads[0] + quads[1]:
                    gathered.from_cores(m, i, j)

            def work(m):
                pl.when(2 * m + 1 < moving.deep)(lambda: link(2 * m + 1))
                complete(moving, m)
                complete(grads_moving, m)
                for i, j in quads[0] + quads[1]:
                    gate_in(moving.slot(m, i, j))
                for move in keep_rows(m):
                    when(m > 0, move.wait)
                    move.start()
                for pair in range(2):
                    for move in grads(m, pair):
                        move.start()
                for pair in range(2):
                    for move in grads(m, pair):
                        move.wait()
                    slots = [moving.slot(m, i, j) for i, j in quads[pair]]
                    experts_pair(
                        slots,
                        m > 0,
                        capacity,
                        rows,
                        xn_v,
                        og_v.at[pair],
                        pos_v,
                        gate_of,
                        weights_v,
                        outs[pair],
                    )
                    if pair == 0:
                        pl.when(2 * m + 2 < moving.deep)(lambda: link(2 * m + 2))

            for move in loads:
                move.wait()
            moving.kept.wait()
            grads_moving.kept.wait()
            link(0)

            def stage(m, carry):
                work(m)
                return carry

            lax.fori_loop(0, moving.deep, stage, 0)
            for out in outs[0] + outs[1]:
                out.free()
            for move in keep_rows(0):
                move.wait()
            gate_out()
            moving.close()
            grads_moving.close()
            for move in sent:
                move.wait_send()
            saved.wait()
            saved_gates.wait()
            yield from ()

        shapes = [(count * capacity, width)] * 4 + [(count * capacity, units)] * 3
        shapes += [(count, 8, rows), (count * rows, capacity + sh_wide), (count * rows, capacity + 2 * sh_wide)]
        pair_shapes = [(2 * capacity, width)] * 4 + [(2 * capacity, units)] * 3
        pair_shapes += [(2, 8, rows), (2 * rows, capacity + sh_wide), (2 * rows, capacity + 2 * sh_wide)]
        kinds = [bf16] * 7 + [f32] + [bf16] * 2
        (
            hidden,
            xn_all,
            grad_all,
            gates_t,
            received,
            gated_grad,
            exp_low,
            back_rows,
            exp_act,
            gate_back,
            up_back,
            token_dots,
            left_forward,
            left_backward,
        ) = transfer(
            "rows_and_experts",
            2,
            mesh,
            rows_body,
            (
                attention_part,
                tokens,
                ffn_gain[None],
                router_full,
                mask_t.astype(f32),
                out_grad,
                position[:, None],
                gate_weight,
                up_weight,
                down_weight,
                fixed_backward,
                fixed_forward,
            ),
            (
                like((rows, width), f32),
                like((count * rows, width)),
                like((count * rows, width)),
                like((experts, rows), f32),
            )
            + tuple(like(shape, kind) for shape, kind in zip(shapes, kinds)),
            norm_rooms
            + [
                pltpu.VMEM((count, experts, rows), f32),
                pltpu.VMEM((count * rows, width), bf16),
                pltpu.VMEM((2, 2 * rows, width), bf16),
                pltpu.VMEM((count, 1, rows), f32),
                pltpu.VMEM((units, width), bf16),
                pltpu.VMEM((units, width), bf16),
                pltpu.VMEM((units, width), bf16),
                pltpu.VMEM((2 * sh_wide, width), bf16),
                pltpu.VMEM((sh_wide, width), bf16),
            ]
            + [pltpu.VMEM((2,) + shape, kind) for shape, kind in zip(pair_shapes, kinds)],
            semaphores=480,
            vmem=62 * 2**20,
        )
        gates = gates_t.T
    else:
        def third_body(place, given, made, room):
            ap, tok, gn, rt, mk = given
            hid_out, xn_all, gt_all = made
            xn, gt = room[6:]
            sent, saved = second_norm(place, cores, rows, given, hid_out, room)
            yield row_gather(place, count, xn, xn_all, rows, part).all()
            route(room)
            yield exchange(place, count, lambda s: gt, lambda s: gt_all.at[s])
            for move in sent:
                move.wait_send()
            saved.wait()

        hidden, xn_all, gates_all = transfer(
            "gather_rows",
            2,
            mesh,
            third_body,
            (attention_part, tokens, ffn_gain[None], router_full, mask_t.astype(f32)),
            (like((rows, width), f32), like((count * rows, width)), like((count, experts, rows), f32)),
            norm_rooms,
            semaphores=400,
            vmem=40 * 2**20,
        )
        gates = lax.dynamic_index_in_dim(gates_all, e, axis=0, keepdims=False).T
        own_gate = lax.dynamic_index_in_dim(gates_all, e, axis=1, keepdims=False)
        (
            received,
            gated_grad,
            exp_low,
            back_rows,
            exp_act,
            gate_back,
            up_back,
            token_dots,
            left_forward,
            left_backward,
        ) = experts_pass(
            count,
            capacity,
            rows,
            xn_all,
            grad_all,
            position[:, None],
            own_gate[:, None],
            gate_weight,
            up_weight,
            down_weight,
            fixed_backward,
            fixed_forward,
        )

    inputs = tokens.astype(f32)
    rstd_two = lax.rsqrt(jnp.mean(hidden * hidden, axis=-1, keepdims=True) + eps)

    sh_grads = mm("tf,td->fd", left_backward[:, capacity:], xn_all).astype(bf16)
    shared_grads = jnp.concatenate(
        [
            sh_grads[:hidden_units],
            sh_grads[sh_wide : sh_wide + hidden_units],
            mm("tf,td->fd", left_forward[:, capacity:], grad_all).astype(bf16)[:hidden_units],
        ],
        axis=0,
    )
    shared_grads = jnp.pad(shared_grads, ((0, pack_rows - 3 * hidden_units), (0, 0)))

    def fourth_body(place, given, made, room):
        lf, el, ff, lb, br, fb, td, sg = given
        mixed, summed, dots, sg_all = made
        mixed_view, summed_view = part_view(mixed, rows, part), part_view(summed, rows, part)
        forward = Product(place, lf, el, ff, room[7:9], count, rows, part)
        backward = Product(place, lb, br, fb, room[9:11], count, rows, part)
        yield scatter(
            place,
            count,
            [forward, backward],
            room[:7],
            [lambda c: mixed_view(0, c), lambda c: summed_view(0, c)],
            (rows, part),
            True,
            room[11],
        )
        yield both(place, count, lambda s: td.at[s], lambda c, s: dots.at[c, s], lambda c: dots.at[c])
        yield later(exchange(place, count, lambda s: strips.at(sg, s), lambda s: sg_all.at[s]), 8)

    mixture, summed_back, dots_all, shared_back = transfer(
        "scatter_both",
        3,
        mesh,
        fourth_body,
        (
            left_forward,
            exp_low,
            fixed_forward,
            left_backward,
            back_rows,
            fixed_backward,
            token_dots,
            strips.cut(shared_grads),
        ),
        (
            like((rows, width)),
            like((rows, width)),
            like((cores, count, 8, rows), f32),
            like((count, pack_rows, deep)),
        ),
        scatter_scratch(
            count,
            cores,
            rows,
            part,
            [(left_forward.shape[1], True), (left_backward.shape[1], True)],
        )
        + [pltpu.SemaphoreType.REGULAR((count * (cores - 1),))],
        vmem=60 * 2**20,
    )
    output = (hidden + mixture.astype(f32)).astype(bf16)

    gate_total = jnp.sum(dots_all[:, :, 0, :], axis=0).T
    weighted_dots = jnp.sum(gates * gate_total, axis=1, keepdims=True)
    grad_logits = gates * (gate_total - weighted_dots)

    down_grad = mm("rf,rd->fd", exp_act, gated_grad)
    gate_grad = mm("rd,rf->df", received, gate_back)
    up_grad = mm("rd,rf->df", received, up_back)
    cotangent = out_grad.astype(f32)
    grad_two = summed_back.astype(f32) + jnp.einsum(
        "te,ed->td", grad_logits, router_full.astype(f32), precision=highest
    )
    scaled = grad_two * ffn_gain
    inner = jnp.mean(scaled * hidden, axis=-1, keepdims=True)
    grad_hidden = cotangent + rstd_two * scaled - hidden * (rstd_two * rstd_two * rstd_two) * inner
    ffn_gain_part = jnp.sum(grad_two * hidden * rstd_two, axis=0)
    grad_branch = grad_hidden.astype(bf16)
    grad_heads = mm("td,cd->tc", grad_branch, out_full).astype(bf16)
    out_proj_part = mm("tc,td->cd", heads_out, grad_branch).astype(bf16)

    turns = count // heads

    def spread(vector):
        return jnp.pad(vector.reshape(count, 1, deep), ((0, 0), (0, 7), (0, 0)))

    if strips.direct:

        def back_body(place, given, made, room):
            gh, gl, op, fg, qkv_s, pr, ct, st, xn, wt = given
            one, qg_all, op_sum, ag_all, fg_all, logit_all = made
            qkv_v, pr_v, ct_v, st_v, gh_v, held, sums, grad_qkv, right, gains, blocks = room[14:]
            own = lax.rem(place.e, heads)
            moves = [place.keep(x, y) for x, y in ((qkv_s, qkv_v), (pr, pr_v), (ct, ct_v), (st, st_v), (wt, right))]
            arrived, finish = start_exchange(
                place, heads, lambda s: gh.at[:, lanes(s, HEAD_DIM)], lambda s: gh_v.at[s]
            )
            one_view = part_view(one, rows, part)

            def fetch(d):
                slot = lax.rem(own + d, heads)
                source = xn.at[pl.ds(pl.multiple_of(slot * rows, rows), rows), :]
                return place.keep(source, held.at[d % 2])

            def main():
                coming = fetch(0)
                for move in moves:
                    move.wait()
                for d in range(heads):
                    now, slot = coming, lax.rem(own + d, heads)
                    if d + 1 < heads:
                        coming = fetch(d + 1)
                    if d > 0:
                        arrived(slot)
                    now.wait()
                    attend_back(
                        held.at[d % 2], (qkv_v, pr_v, ct_v, st_v, gh_v, grad_qkv, sums), slot, rows, d == 0
                    )
                    yield
                tail()
                yield
                kept = Kept(grad_qkv, right, rows)
                yield from scatter(place, heads, [kept], room[:7], [lambda c: one_view(0, c)], (rows, part), True)

            def tail():
                ones = jnp.ones((8, 3 * HEAD_DIM), f32)

                def body(at, carry):
                    block = sums[:, lanes(at, deep)].T
                    blocks[at] = block.astype(bf16)
                    weights = right[pl.ds(pl.multiple_of(at * deep, deep), deep), :].astype(f32)
                    gains[:, lanes(at, deep)] = dot(ones, block * weights, ((1,), (1,)), highest)
                    return carry

                lax.fori_loop(0, count, body, 0)
                for which in range(3):

                    def landing(slot, which=which):
                        return qg_all.at[which, lax.div(slot, heads), :, lanes(lax.rem(slot, heads), HEAD_DIM)]

                    def block(slot, which=which):
                        return blocks.at[slot, :, pl.ds(which * HEAD_DIM, HEAD_DIM)]

                    tasks.append(exchange(place, count, block, landing))
                tasks.append(
                    both(
                        place,
                        count,
                        lambda s: gains.at[:, lanes(s, deep)],
                        lambda c, s: ag_all.at[c, s],
                        lambda c: ag_all.at[c],
                    )
                )

            projection = scatter(
                place, count, [lambda s: strips.at(op, s)], room[7:14], [lambda c: op_sum], (out_rows, deep), False
            )
            tasks = [
                main(),
                twice(projection),
                exchange(place, count, lambda s: gl, lambda s: logit_all.at[s]),
                exchange(place, count, lambda s: fg.at[s], lambda s: fg_all.at[s]),
            ]
            yield tasks
            finish()

        grad_one, qkv_all, out_proj_sum, attn_gains, ffn_gains, logits_all = transfer(
            "attention_back",
            4,
            mesh,
            back_body,
            (
                grad_heads,
                grad_logits.T,
                out_proj_part,
                spread(ffn_gain_part),
                qkv_saved,
                probs_saved,
                cosine_wide,
                sine_wide,
                xn_chunk,
                w_qkv,
            ),
            (
                like((rows, width)),
                like((3, turns, deep, heads * HEAD_DIM)),
                like((out_rows, deep)),
                like((cores, count, 8, deep), f32),
                like((count, 8, deep), f32),
                like((count, experts, rows), f32),
            ),
            scatter_scratch(heads, cores, rows, part)
            + scatter_scratch(count, 1, out_rows, deep)
            + [
                pltpu.VMEM((chunk, 3 * HEAD_DIM), bf16),
                pltpu.VMEM((chunk, rows), f32),
                pltpu.VMEM((chunk, HEAD_DIM), f32),
                pltpu.VMEM((chunk, HEAD_DIM), f32),
                pltpu.VMEM((heads, rows, HEAD_DIM), bf16),
                pltpu.VMEM((2, rows, width), bf16),
                pltpu.VMEM((3 * HEAD_DIM, width), f32),
                pltpu.VMEM((chunk, 3 * HEAD_DIM), bf16),
                pltpu.VMEM((width, 3 * HEAD_DIM), bf16),
                pltpu.VMEM((8, width), f32),
                pltpu.VMEM((count, deep, 3 * HEAD_DIM), bf16),
            ],
            semaphores=640,
            vmem=56 * 2**20,
        )
    else:
        def fifth_body(place, given, made, room):
            gl, logit_all = given[1], made[1]
            yield exchange(place, count, lambda s: gl, lambda s: logit_all.at[s])
            yield exchange(place, heads, lambda s: given[0].at[:, lanes(s, HEAD_DIM)], lambda s: made[0].at[s])

        grad_head, logits_all = transfer(
            "exchange_heads",
            4,
            mesh,
            fifth_body,
            (grad_heads, grad_logits.T),
            (like((heads, rows, HEAD_DIM)), like((count, experts, rows), f32)),
        )
        grad_value = mm("gqk,gqd->gkd", probs_low, grad_head)
        grad_probs = mm("gqd,gkd->gqk", grad_head, valued)
        weighted = jnp.sum(probs * grad_probs, axis=-1, keepdims=True)
        grad_scores = (probs * (grad_probs - weighted)).astype(bf16)
        grad_query = mm("gqk,gkd->gqd", grad_scores, keyed) * scale
        grad_key = mm("gqk,gqd->gkd", grad_scores, query) * scale
        grad_qkv = jnp.concatenate(
            [
                rotary_back(grad_query, cosine, sine).astype(bf16),
                rotary_back(grad_key, cosine, sine).astype(bf16),
                grad_value.astype(bf16),
            ],
            axis=2,
        ).reshape(chunk, 3 * HEAD_DIM)
        qkv_grad = mm("td,tc->dc", xn_chunk, grad_qkv)
        attn_gain_part = jnp.sum(qkv_grad * w_qkv.astype(f32), axis=1)
        qkv_grad = qkv_grad.astype(bf16)

        def sixth_body(place, given, made, room):
            gq, wq, qg, op, ag, fg = given
            one, qg_all, op_sum, ag_all, fg_all = made
            one_view = part_view(one, rows, part)
            made_here = Product(place, gq, None, wq, room[7:9], heads, rows, part)
            yield scatter(place, heads, [made_here], room[:7], [lambda c: one_view(0, c)], (rows, part), True)
            yield scatter(
                place, count, [lambda s: strips.at(op, s)], room[9:], [lambda c: op_sum], (out_rows, deep), False
            )
            yield both(place, count, lambda s: ag.at[s], lambda c, s: ag_all.at[c, s], lambda c: ag_all.at[c])
            yield exchange(place, count, lambda s: fg.at[s], lambda s: fg_all.at[s])
            for which in range(3):

                def source(slot, which=which):
                    at = pl.ds(pl.multiple_of(slot * deep, deep), deep)
                    return qg.at[at, pl.ds(which * HEAD_DIM, HEAD_DIM)]

                def landing(slot, which=which):
                    return qg_all.at[which, lax.div(slot, heads), :, lanes(lax.rem(slot, heads), HEAD_DIM)]

                yield later(exchange(place, count, source, landing), 6)

        grad_one, qkv_all, out_proj_sum, attn_gains, ffn_gains = transfer(
            "scatter_grads",
            5,
            mesh,
            sixth_body,
            (
                grad_qkv,
                w_qkv.T,
                qkv_grad,
                strips.cut(out_proj_part),
                spread(attn_gain_part),
                spread(ffn_gain_part),
            ),
            (
                like((rows, width)),
                like((3, turns, deep, heads * HEAD_DIM)),
                like((out_rows, deep)),
                like((cores, count, 8, deep), f32),
                like((count, 8, deep), f32),
            ),
            scatter_scratch(heads, cores, rows, part, [(3 * HEAD_DIM, False)])
            + scatter_scratch(count, 1, out_rows, deep),
            semaphores=600,
            vmem=56 * 2**20,
        )

    xn_columns = lax.dynamic_slice_in_dim(xn_all, e * deep, deep, axis=1).astype(f32).reshape(count, rows, deep)
    router_grad = jnp.einsum("gtd,get->de", xn_columns, logits_all, precision=highest)
    grad_one = grad_one.astype(f32)
    rstd_one = lax.rsqrt(jnp.mean(inputs * inputs, axis=-1, keepdims=True) + eps)
    scaled_one = grad_one * attn_gain
    inner_one = jnp.mean(scaled_one * inputs, axis=-1, keepdims=True)
    input_grad = (
        grad_hidden + rstd_one * scaled_one - inputs * (rstd_one * rstd_one * rstd_one) * inner_one
    ).astype(bf16)

    def of_heads(which):
        return jnp.sum(qkv_all[which].astype(f32), axis=0)

    def of_shared(which):
        return shared_back[:, which * hidden_units : (which + 1) * hidden_units].reshape(-1, deep).astype(f32)

    return (
        output,
        input_grad,
        jnp.sum(attn_gains[:, :, 0, :], axis=(0, 1)) / gain_attn.astype(f32),
        of_heads(0),
        of_heads(1),
        of_heads(2),
        out_proj_sum.astype(f32),
        jnp.sum(ffn_gains[:, 0, :], axis=0),
        router_grad,
        gate_grad[None],
        up_grad[None],
        down_grad[None],
        of_shared(0).T,
        of_shared(1).T,
        of_shared(2),
    )


def solution(mesh):
    in_specs = (
        P("expert", None),
        P("expert", None),
        P("expert", None),
        P("expert"),
        P("expert", "tensor"),
        P("expert", "tensor"),
        P("expert", "tensor"),
        P("tensor", "expert"),
        P("expert"),
        P("expert", None),
        P("expert", None, "tensor"),
        P("expert", None, "tensor"),
        P("expert", "tensor", None),
        P("expert", "tensor"),
        P("expert", "tensor"),
        P("tensor", "expert"),
        P("expert", None),
    )
    out_specs = (
        P("expert", None),
        P("expert", None),
        P("expert"),
        P("expert", "tensor"),
        P("expert", "tensor"),
        P("expert", "tensor"),
        P("tensor", "expert"),
        P("expert"),
        P("expert", None),
        P("expert", None, "tensor"),
        P("expert", None, "tensor"),
        P("expert", "tensor", None),
        P("expert", "tensor"),
        P("expert", "tensor"),
        P("tensor", "expert"),
    )
    return jax.shard_map(
        functools.partial(local, mesh), mesh=mesh, in_specs=in_specs, out_specs=out_specs, check_vma=False
    )
```

```python
import functools

import jax
import jax.numpy as jnp
from jax import lax
from jax.experimental import pallas as pl
from jax.experimental.pallas import tpu as pltpu
from jax.sharding import PartitionSpec as P

HEAD_DIM = 128
TOP = 6
MESH = pl.DeviceIdType.MESH
ANY = pl.BlockSpec(memory_space=pl.ANY)

bf16 = jnp.bfloat16
f32 = jnp.float32
eps = 1e-06
highest = lax.Precision.HIGHEST
floor_score = -1e30


class Place:
    def __init__(self, sems, count, cores):
        self.sems, self.used = sems, 0
        self.count, self.cores = count, cores
        self.e = lax.axis_index("expert")
        self.t = lax.axis_index("tensor")
        self.quad = lax.rem(self.e, 4)
        self.far = lax.div(self.e, 4)

    def take(self, number):
        first = self.used
        self.used = first + number
        return first

    def ring(self, distance):
        return lax.rem(self.t + distance, self.cores)

    def copy(self, src, dst, out_sem, in_sem, e, t):
        return pltpu.make_async_remote_copy(
            src_ref=src,
            dst_ref=dst,
            send_sem=self.sems.at[out_sem],
            recv_sem=self.sems.at[in_sem],
            device_id={"expert": e, "tensor": t},
            device_id_type=MESH,
        )

    def send(self, src, dst, out_sem, in_sem, e, t):
        move = self.copy(src, dst, out_sem, in_sem, e, t)
        move.start()
        return move

    def arrived(self, landing, in_sem):
        self.copy(landing, landing, in_sem, in_sem, self.e, self.t).wait_recv()

    def keep(self, src, dst):
        move = pltpu.make_async_copy(src, dst, self.sems.at[self.take(1)])
        move.start()
        return move

    def local(self, src, dst, sem):
        return pltpu.make_async_copy(src, dst, self.sems.at[sem])

    def meet(self):
        barrier = pltpu.get_barrier_semaphore()
        for step in range(1, self.count):
            pl.semaphore_signal(
                barrier,
                inc=1,
                device_id={"expert": lax.rem(self.e + step, self.count), "tensor": self.t},
                device_id_type=MESH,
            )
        for step in range(1, self.cores):
            pl.semaphore_signal(
                barrier,
                inc=1,
                device_id={"expert": self.e, "tensor": self.ring(step)},
                device_id_type=MESH,
            )
        pl.semaphore_wait(barrier, self.count + self.cores - 2)


class Block:
    def __init__(self, place, members):
        self.place, self.deep = place, members // 4
        self.rank = lax.rem(place.far, self.deep)
        self.start = place.far - self.rank

    def flips(self, order):
        high, low = lax.div(self.place.quad, 2), lax.rem(self.place.quad, 2)
        one = high + (low - high) * order
        two = low + (high - low) * order
        return (2 - order) * (1 - 2 * one), (1 + order) * (1 - 2 * two)

    def slot(self, k, i, j, order):
        one, two = self.flips(order)
        return lax.rem(self.rank + k, self.deep) * 4 + self.place.quad + i * one + j * two

    def own(self):
        return self.rank * 4 + self.place.quad

    def device(self, slot):
        return self.start * 4 + slot


class Gather:
    def __init__(self, place, members, mine, whole, view, halves, pieces=1):
        self.place, self.block = place, Block(place, members)
        self.mine, self.whole, self.view, self.pieces = mine, whole, view, pieces
        self.deep, self.order = self.block.deep, lax.rem(place.t, 2)
        self.cores = place.cores if halves else 1
        self.zs, self.zr = self.lots(2), self.lots(1)
        self.s2, self.r2 = self.lots(1), self.lots(1)
        self.s3, self.r3 = self.lots(2), self.lots(2)
        self.s4, self.r4 = self.lots(4 * (self.cores - 1)), self.lots(4 * (self.cores - 1))
        self.sent, self.closing = [], False

    def lots(self, number):
        return self.place.take(number * self.deep * self.pieces)

    def near(self, n):
        rank, deep = self.block.rank, self.deep
        if isinstance(n, int) and n == 0:
            return rank
        low = jnp.minimum(rank, deep - 1 - rank)
        if isinstance(n, int):
            paired = rank - (n + 1) // 2 if n % 2 else rank + n // 2
        else:
            paired = rank + jnp.where(lax.rem(n, 2) == 1, -lax.div(n + 1, 2), lax.div(n, 2))
        single = jnp.where(rank < deep - 1 - rank, rank + (n - low), rank - (n - low))
        return jnp.where(n <= 2 * low, paired, single)

    def slot(self, n, i, j, order=None):
        one, two = self.block.flips(self.order if order is None else order)
        return self.near(n) * 4 + self.place.quad + i * one + j * two

    def index(self, n, kind, kinds, p):
        return (self.near(n) * kinds + kind) * self.pieces + p

    def pass_on(self, source, landing, out, into, at, e, t, condition=None):
        move = self.place.copy(source, landing, out + at[0], into + at[1], e, t)
        if self.closing:
            when(condition, move.wait_send)
            return
        self.sent.append((condition, move))
        when(condition, move.start)

    def along(self, n, p, source, landing):
        rank, e = self.block.rank, self.place.e
        near = self.near(n)
        for way in (1, -1):
            fits = rank < self.deep - 1 if way > 0 else rank >= 1
            if not isinstance(n, int) or n > 0:
                fits = jnp.logical_and(fits, near < rank if way > 0 else near > rank)
            out = self.index(n, 0 if way > 0 else 1, 2, p)
            into = self.index(n, 0, 1, p)
            self.pass_on(source, landing, self.zs, self.zr, (out, into), e + 4 * way, self.place.t, fits)

    def across(self, n, i, p, source, landing):
        one, two = self.block.flips(self.order)
        e, t = self.place.e, self.place.t
        if i == 0:
            at = self.index(n, 0, 1, p)
            self.pass_on(source, landing, self.s2, self.r2, (at, at), e + one, t)
        at = self.index(n, i, 2, p)
        self.pass_on(source, landing, self.s3, self.r3, (at, at), e + two, t)

    def share(self, n, i, j, p):
        ref = self.view(self.slot(n, i, j), self.place.t, p)
        for far in range(1, self.cores):
            kind = (far - 1) * 4 + i * 2 + j
            at = self.index(n, kind, 4 * (self.cores - 1), p)
            self.pass_on(ref, ref, self.s4, self.r4, (at, at), self.place.e, self.place.ring(far))

    def start(self, p):
        if p == 0:
            self.kept = self.place.keep(self.whole[0], self.whole[1](self.block.own()))
        source, landing = self.mine(p), self.view(self.block.own(), self.place.t, p)
        if self.deep > 1:
            self.along(0, p, source, landing)
        self.across(0, 0, p, source, landing)

    def from_line(self, n, p):
        ref = self.view(self.slot(n, 0, 0), self.place.t, p)
        self.place.arrived(ref, self.zr + self.index(n, 0, 1, p))
        if self.deep > 2:
            self.along(n, p, ref, ref)
        self.across(n, 0, p, ref, ref)
        self.share(n, 0, 0, p)

    def from_one(self, n, p):
        ref = self.view(self.slot(n, 1, 0), self.place.t, p)
        self.place.arrived(ref, self.r2 + self.index(n, 0, 1, p))
        self.across(n, 1, p, ref, ref)
        self.share(n, 1, 0, p)

    def from_two(self, n, i, p):
        ref = self.view(self.slot(n, i, 1), self.place.t, p)
        self.place.arrived(ref, self.r3 + self.index(n, i, 2, p))
        self.share(n, i, 1, p)

    def from_cores(self, n, i, j):
        if i + j == 0 and isinstance(n, int) and n == 0:
            return
        if i + j == 0 and not isinstance(n, int):
            pl.when(n > 0)(lambda: self.of_cores(n, i, j))
        else:
            self.of_cores(n, i, j)

    def of_cores(self, n, i, j):
        for far in range(1, self.cores):
            source = self.place.ring(self.cores - far)
            first, second = (j, i) if far % 2 else (i, j)
            kind = (far - 1) * 4 + first * 2 + second
            for p in range(self.pieces):
                ref = self.view(self.slot(n, i, j), source, p)
                self.place.arrived(ref, self.r4 + self.index(n, kind, 4 * (self.cores - 1), p))

    def finish(self):
        for condition, move in self.sent:
            when(condition, move.wait_send)

    def close(self):
        self.closing = True
        for p in range(self.pieces):
            source, landing = self.mine(p), self.view(self.block.own(), self.place.t, p)
            self.along(0, p, source, landing)
            self.across(0, 0, p, source, landing)
            for n in range(self.deep):
                if n > 0:
                    ref = self.view(self.slot(n, 0, 0), self.place.t, p)
                    self.along(n, p, ref, ref)
                    self.across(n, 0, p, ref, ref)
                    self.share(n, 0, 0, p)
                ref = self.view(self.slot(n, 1, 0), self.place.t, p)
                self.across(n, 1, p, ref, ref)
                self.share(n, 1, 0, p)
                self.share(n, 0, 1, p)
                self.share(n, 1, 1, p)

    def links(self):
        for p in range(self.pieces):
            self.start(p)
            yield
        for n in range(1, self.deep + 1):
            for p in range(self.pieces):
                self.from_one(n - 1, p)
                yield
                if n < self.deep:
                    self.from_line(n, p)
                    yield

    def last(self, n):
        for i in range(2):
            for p in range(self.pieces):
                self.from_two(n, i, p)

    def all(self):
        yield from self.links()
        for n in range(self.deep):
            self.last(n)
            yield
        for n in range(self.deep):
            for i in range(2):
                for j in range(2):
                    self.from_cores(n, i, j)
        self.finish()
        self.kept.wait()


def when(condition, action):
    if condition is None:
        action()
    else:
        pl.when(condition)(action)


def gather(place, members, mine, whole, view, halves, pieces=1):
    return Gather(place, members, mine, whole, view, halves, pieces).all()


class Kept:
    def __init__(self, left, right, rows):
        self.left, self.right, self.rows, self.slots = left, right, rows, {}

    def fetch(self, turn, slot):
        self.slots[turn] = pl.ds(pl.multiple_of(slot * self.rows, self.rows), self.rows)

    def ready(self, turn):
        pass

    def make(self, turn, core, target):
        columns = target.shape[1]
        wide = min(columns, 512)

        def body(tile, carry):
            source = pl.ds(pl.multiple_of(core * columns + tile * wide, wide), wide)
            into = pl.ds(pl.multiple_of(tile * wide, wide), wide)
            target[:, into] = dot(self.left[self.slots[turn], :], self.right[source, :], ((1,), (1,))).astype(bf16)
            return carry

        lax.fori_loop(0, columns // wide, body, 0)


def dot(left, right, sides=((1,), (0,)), precision=None):
    return lax.dot_general(left, right, (sides, ((), ())), precision=precision, preferred_element_type=f32)


def attend(tokens, gain, weights, first, cosine, sine, rooms, at, slot, rows):
    normed, qkv, probs, cosines, sines, out = rooms
    own = pl.ds(pl.multiple_of(slot * rows, rows), rows)

    def norm(piece_at, carry):
        for part in range(4):
            row = piece_at * 64 + part * 16
            values = tokens[pl.ds(pl.multiple_of(slot * rows + row, 16), 16), :].astype(f32)
            rstd = lax.rsqrt(jnp.mean(values * values, axis=1, keepdims=True) + eps)
            normed[at, pl.ds(pl.multiple_of(row, 16), 16), :] = (values * rstd * gain).astype(bf16)
        return carry

    lax.fori_loop(0, rows // 64, norm, 0)
    half = HEAD_DIM // 2
    lane = lax.broadcasted_iota(jnp.int32, (rows, HEAD_DIM), 1)
    sine = jnp.where(lane < half, -sine, sine)
    cosines[own, :] = cosine
    sines[own, :] = sine
    lin = dot(normed[at], weights[...])

    def turn(values):
        return (values * cosine + pltpu.roll(values, half, 1) * sine).astype(bf16)

    query, keyed = turn(lin[:, :HEAD_DIM]), turn(lin[:, HEAD_DIM : 2 * HEAD_DIM])
    valued = lin[:, 2 * HEAD_DIM :].astype(bf16)
    qkv[own, :HEAD_DIM] = query
    qkv[own, HEAD_DIM : 2 * HEAD_DIM] = keyed
    qkv[own, 2 * HEAD_DIM :] = valued
    key_at = lax.broadcasted_iota(jnp.int32, (rows, rows), 1).astype(f32)
    query_at = lax.broadcasted_iota(jnp.int32, (rows, rows), 0).astype(f32)
    allowed = (key_at <= query_at) & (key_at >= first[:, :1])
    scores = jnp.where(allowed, dot(query, keyed, ((1,), (1,))) * (HEAD_DIM ** (-0.5)), floor_score)
    raised = jnp.exp(scores - jnp.max(scores, axis=1, keepdims=True))
    chances = raised / jnp.sum(raised, axis=1, keepdims=True)
    probs[own, :] = chances
    out[slot] = dot(chances.astype(bf16), valued).astype(bf16)


def attend_back(rooms, slot, rows):
    qkv, probs, cosines, sines, grads, grad_qkv, turned = rooms
    own = pl.ds(pl.multiple_of(slot * rows, rows), rows)
    query = qkv[own, :HEAD_DIM]
    keyed = qkv[own, HEAD_DIM : 2 * HEAD_DIM]
    valued = qkv[own, 2 * HEAD_DIM :]
    cosine, sine = cosines[own, :], sines[own, :]
    chances, grad = probs[own, :], grads[slot]
    scale = HEAD_DIM ** (-0.5)

    def turn_back(values):
        return (values * cosine - pltpu.roll(values, HEAD_DIM // 2, 1) * sine).astype(bf16)

    grad_qkv[own, 2 * HEAD_DIM :] = dot(chances.astype(bf16), grad, ((0,), (0,))).astype(bf16)
    grad_chances = dot(grad, valued, ((1,), (1,)))
    weighted = jnp.sum(chances * grad_chances, axis=1, keepdims=True)
    grad_scores = (chances * (grad_chances - weighted)).astype(bf16)
    grad_qkv[own, :HEAD_DIM] = turn_back(dot(grad_scores, keyed) * scale)
    grad_qkv[own, HEAD_DIM : 2 * HEAD_DIM] = turn_back(dot(grad_scores, query, ((0,), (0,))) * scale)
    turned[:, own] = grad_qkv[own, :].T


def add_up(target, sources, rows, columns):
    step = max(16, min(rows, 16384 // columns // 16 * 16))

    def body(at, carry):
        piece = pl.ds(pl.multiple_of(at * step, step), step)
        total = sources[0][piece, :].astype(f32)
        for other in sources[1:]:
            total = total + other[piece, :].astype(f32)
        target[piece, :] = total.astype(target.dtype)
        return carry

    lax.fori_loop(0, rows // step, body, 0)


class Product:
    def __init__(self, place, left, varied, fixed, rooms, members, rows, columns):
        self.place, self.left, self.varied = place, left, varied
        self.lhs, self.rhs = rooms
        self.rows, self.columns = rows, columns
        self.lead = 0 if varied is None else varied.shape[0] // members
        self.waits, self.turn = {}, 0
        self.setup = []
        for buffer in range(self.rhs.shape[0]):
            self.setup.append(place.keep(fixed, self.rhs.at[buffer, pl.ds(self.lead, fixed.shape[0]), :]))

    def fetch(self, turn, slot):
        buffer = turn % 2
        rows = pl.ds(pl.multiple_of(slot * self.rows, self.rows), self.rows)
        moves = [self.place.keep(self.left.at[rows, :], self.lhs.at[buffer])]
        if self.lead:
            lead = pl.ds(pl.multiple_of(slot * self.lead, self.lead), self.lead)
            moves.append(self.place.keep(self.varied.at[lead, :], self.rhs.at[buffer, pl.ds(0, self.lead), :]))
        self.waits[turn] = moves

    def ready(self, turn):
        for move in self.setup:
            move.wait()
        self.setup = []
        for move in self.waits.pop(turn):
            move.wait()

    def make(self, turn, core, target):
        buffer = turn % 2
        right = self.rhs.at[buffer if self.lead else 0]
        wide = min(self.columns, 512)

        def body(at, carry):
            source = pl.ds(pl.multiple_of(core * self.columns + at * wide, wide), wide)
            into = pl.ds(pl.multiple_of(at * wide, wide), wide)
            target[:, into] = jnp.dot(
                self.lhs[buffer], right[:, source], preferred_element_type=f32
            ).astype(bf16)
            return carry

        lax.fori_loop(0, self.columns // wide, body, 0)


def scatter(place, members, sources, room, views, shape, halves, credit=None):
    block = Block(place, members)
    deep, e, t = block.deep, place.e, place.t
    rows, columns = shape
    order = 1 - lax.rem(t, 2)
    cores = place.cores if halves else 1
    count = len(sources)
    mine, outgoing, land0, land1s, land2s, land3s, finals = room
    s0, r0 = place.take(4 * deep * cores * count), place.take(4 * deep * cores * count)
    s1, r1 = place.take(2 * deep * count), place.take(2 * deep * count)
    s2, r2 = place.take(deep * count), place.take(deep * count)
    s3, r3 = place.take(deep * count), place.take(deep * count)
    s4, r4 = place.take(cores * count), place.take(cores * count)
    walk = [(f, k) for f in range(count) for k in list(range(1, deep)) + [0]]
    one, two = block.flips(order)
    sent, loads, last, kept = [], {}, {}, []
    quads = [(1, 1), (1, 0), (0, 1), (0, 0)]
    turns = [(f, k, i, j) for f, k in walk for i, j in quads]
    ring = outgoing.shape[0]
    leaving = []

    def slot_of(k, i, j):
        return block.slot(k, i, j, order)

    def land_index(d, k, i, j):
        return (d - 1) * deep * 4 + k * 4 + i * 2 + j

    def produce(number):
        f, k, i, j = turns[number]
        source = sources[f]
        if (k, i, j) in last:
            last.pop((k, i, j)).wait_send()
        if not isinstance(source, (Product, Kept)):
            loads[f, k, i, j] = place.keep(source(slot_of(k, i, j)), mine.at[slot_of(k, i, j)])
            return
        local_number = number - f * 4 * deep
        if local_number == 0:
            source.fetch(0, slot_of(k, i, j))
        source.ready(local_number)
        if local_number + 1 < 4 * deep:
            source.fetch(local_number + 1, slot_of(*turns[number + 1][1:]))
        if number >= ring:
            for move in leaving[number - ring]:
                move.wait_send()
        moves = []
        for d in range(1, cores):
            target = place.ring(d)
            buffer = outgoing.at[number % ring, d - 1]
            source.make(local_number, target, buffer)
            at = land_index(d, k, *((j, i) if d % 2 else (i, j)))
            if f > 0:
                pl.semaphore_wait(credit.at[at], 1)
            sem = f * 4 * deep * cores + at
            moves.append(place.send(buffer, land0.at[at], s0 + sem, r0 + sem, e, target))
        leaving.append(moves)
        source.make(local_number, t, mine.at[slot_of(k, i, j)])

    def terms_of(f, k, i, j):
        if (f, k, i, j) in loads:
            loads[f, k, i, j].wait()
        terms = [mine.at[slot_of(k, i, j)]]
        for d in range(1, cores):
            at = land_index(d, k, i, j)
            place.arrived(land0.at[at], r0 + f * 4 * deep * cores + at)
            terms.append(land0.at[at])
        if i == 0:
            at = (f * deep + k) * 2 + j
            place.arrived(land1s.at[at], r1 + at)
            terms.append(land1s.at[at])
            if j == 0:
                at = f * deep + k
                place.arrived(land2s.at[at], r2 + at)
                terms.append(land2s.at[at])
        return terms

    def give_back(f, k, i, j):
        if f + 1 < count:
            for d in range(1, cores):
                pl.semaphore_signal(
                    credit.at[land_index(d, k, i, j)],
                    inc=1,
                    device_id={"expert": e, "tensor": place.ring(cores - d)},
                    device_id_type=MESH,
                )

    def leave(f, k, i, j, landing, out, into, at, target):
        move = place.send(mine.at[slot_of(k, i, j)], landing.at[at], out + at, into + at, target, t)
        last[k, i, j] = move

    def first_flip(f, k, j):
        terms, ref = terms_of(f, k, 1, j), mine.at[slot_of(k, 1, j)]
        if len(terms) > 1:
            add_up(ref, terms, rows, columns)
        give_back(f, k, 1, j)
        leave(f, k, 1, j, land1s, s1, r1, (f * deep + k) * 2 + j, e + one)

    def second_flip(f, k):
        add_up(mine.at[slot_of(k, 0, 1)], terms_of(f, k, 0, 1), rows, columns)
        give_back(f, k, 0, 1)
        leave(f, k, 0, 1, land2s, s2, r2, f * deep + k, e + two)

    def line(f, k):
        terms, ref = terms_of(f, k, 0, 0), mine.at[slot_of(k, 0, 0)]
        if k > 0:
            add_up(ref, terms, rows, columns)
            give_back(f, k, 0, 0)
            peer = block.device(lax.rem(block.rank + k, deep) * 4 + place.quad)
            leave(f, k, 0, 0, land3s, s3, r3, f * deep + k, peer)
            return
        for far in range(1, deep):
            place.arrived(land3s.at[f * deep + far], r3 + f * deep + far)
            terms.append(land3s.at[f * deep + far])
        final = finals.at[f]
        add_up(final, terms, rows, columns)
        give_back(f, k, 0, 0)
        kept.append(place.keep(final, views[f](t)))
        for d in range(1, cores):
            at = f * cores + d
            sent.append(place.send(final, views[f](t), s4 + at, r4 + at, e, place.ring(d)))

    for step in range(len(walk) + 2):
        fresh = step < len(walk)
        if fresh:
            produce(4 * step)
            yield
            produce(4 * step + 1)
            yield
            first_flip(*walk[step], 1)
            yield
            produce(4 * step + 2)
            yield
        if 0 <= step - 1 < len(walk):
            second_flip(*walk[step - 1])
            yield
        if fresh:
            produce(4 * step + 3)
            yield
            first_flip(*walk[step], 0)
            yield
        if 0 <= step - 2 < len(walk):
            line(*walk[step - 2])
            yield
    for f in range(count):
        for d in range(1, cores):
            place.arrived(views[f](place.ring(cores - d)), r4 + f * cores + d)
    for moves in leaving[-ring:]:
        for move in moves:
            move.wait_send()
    for move in list(last.values()) + sent:
        move.wait_send()
    for move in kept:
        move.wait()


def scatter_scratch(members, cores, rows, columns, products=(), ring=4):
    deep = members // 4
    count = max(1, len(products))
    short = rows if cores > 1 else 16
    rooms = [
        pltpu.VMEM((members, rows, columns), bf16),
        pltpu.VMEM((ring, max(1, cores - 1), short, columns), bf16),
        pltpu.VMEM((max(1, (cores - 1) * members), short, columns), bf16),
        pltpu.VMEM((2 * deep * count, rows, columns), bf16),
        pltpu.VMEM((deep * count, rows, columns), bf16),
        pltpu.VMEM((deep * count, rows, columns), bf16),
        pltpu.VMEM((count, rows, columns), bf16),
    ]
    for depth, varied in products:
        rooms.append(pltpu.VMEM((2, rows, depth), bf16))
        rooms.append(pltpu.VMEM((2 if varied else 1, depth, columns * cores), bf16))
    return rooms


def exchange(place, members, source, landing):
    e, t = place.e, place.t
    own = lax.rem(e, members)
    base = e - own
    sends, arrivals = place.take(members), place.take(members)
    sent = []
    for d in range(1, members):
        target = lax.rem(own + d, members)
        sent.append(place.send(source(target), landing(own), sends + d, arrivals + d, base + target, t))
    kept = place.keep(source(own), landing(own))
    yield
    for d in range(1, members):
        place.arrived(landing(lax.rem(own + members - d, members)), arrivals + d)
    for move in sent:
        move.wait_send()
    kept.wait()


def start_exchange(place, members, source, landing):
    e, t = place.e, place.t
    own = lax.rem(e, members)
    base = e - own
    sends, arrivals = place.take(members), place.take(members)
    sent = []
    for d in range(1, members):
        target = lax.rem(own + d, members)
        sent.append(place.send(source(target), landing(own), sends + target, arrivals + own, base + target, t))
    place.keep(source(own), landing(own)).wait()

    def arrived(slot):
        pl.when(slot != own)(lambda: place.arrived(landing(slot), arrivals + slot))

    def finish():
        for move in sent:
            move.wait_send()

    return arrived, finish


def both(place, members, source, landing, part):
    yield from exchange(place, members, source, lambda slot: landing(place.t, slot))
    sends, arrivals = place.take(place.cores), place.take(place.cores)
    sent = []
    for d in range(1, place.cores):
        mine = part(place.t)
        sent.append(place.send(mine, mine, sends + d, arrivals + d, place.e, place.ring(d)))
    yield
    for d in range(1, place.cores):
        place.arrived(part(place.ring(place.cores - d)), arrivals + d)
    for move in sent:
        move.wait_send()


def twice(task):
    for _ in task:
        next(task, None)
        yield


def later(task, rounds):
    for _ in range(rounds):
        yield
    yield from task


def run(tasks):
    while tasks:
        for task in list(tasks):
            try:
                next(task)
            except StopIteration:
                tasks.remove(task)


def transfer(name, number, mesh, body, ins, outs, scratch=(), semaphores=400, vmem=None):
    count, cores = mesh.shape["expert"], mesh.shape["tensor"]
    semaphores = semaphores * max(1, count * cores // 32)

    def kernel(*refs):
        given = refs[: len(ins)]
        made = refs[len(ins) : len(ins) + len(outs)]
        room = refs[len(ins) + len(outs) : -1]
        place = Place(refs[-1], count, cores)
        place.meet()
        tasks = []
        for task in body(place, given, made, room):
            if isinstance(task, list):
                run(task)
            else:
                tasks.append(task)
        run(tasks)
        assert place.used <= semaphores, place.used

    size = sum(x.size * x.dtype.itemsize for x in list(ins) + list(outs))
    return pl.pallas_call(
        kernel,
        name=name,
        out_shape=[jax.ShapeDtypeStruct(shape, dtype) for shape, dtype in outs_of(outs)],
        in_specs=[ANY] * len(ins),
        out_specs=[ANY] * len(outs),
        scratch_shapes=list(scratch) + [pltpu.SemaphoreType.DMA((semaphores,))],
        cost_estimate=pl.CostEstimate(flops=0, bytes_accessed=size, transcendentals=0),
        compiler_params=pltpu.CompilerParams(
            collective_id=number, has_side_effects=True, vmem_limit_bytes=vmem
        ),
    )(*ins)


def outs_of(outs):
    return [(x.shape, x.dtype) for x in outs]


def like(shape, dtype=bf16):
    return jax.ShapeDtypeStruct(shape, dtype)


def part_view(ref, rows, columns, pieces=1):
    height = rows // pieces

    def view(slot, core, piece=0):
        at = 0 if isinstance(slot, int) else pl.multiple_of(slot * rows, rows)
        return ref.at[
            pl.ds(at + piece * height, height), pl.ds(pl.multiple_of(core * columns, columns), columns)
        ]

    return view


PIECES = 2


def lanes(at, columns):
    return pl.ds(pl.multiple_of(at * columns, columns), columns)


class Strips:
    def __init__(self, count, columns):
        self.count, self.columns = count, columns
        self.direct = columns % 128 == 0

    def shape(self, rows):
        return (rows, self.count * self.columns) if self.direct else (self.count, rows, self.columns)

    def at(self, ref, slot):
        return ref.at[:, lanes(slot, self.columns)] if self.direct else ref.at[slot]

    def cut(self, array):
        rows = array.shape[0]
        return array if self.direct else array.reshape(rows, self.count, self.columns).transpose(1, 0, 2)

    def join(self, array):
        rows = array.shape[0 if self.direct else 1]
        return array if self.direct else array.transpose(1, 0, 2).reshape(rows, self.count * self.columns)


def row_gather(place, members, source, landing, rows, part):
    def mine(piece):
        height = rows // PIECES
        return source.at[pl.ds(piece * height, height), lanes(place.t, part)]

    whole = (source, lambda slot: landing.at[pl.ds(pl.multiple_of(slot * rows, rows), rows), :])
    return Gather(place, members, mine, whole, part_view(landing, rows, part, PIECES), True, PIECES)


def rotary(values, cosine, sine):
    half = values.shape[-1] // 2
    first = values[..., :half]
    second = values[..., half:]
    return jnp.concatenate([first * cosine - second * sine, second * cosine + first * sine], axis=-1)


def rotary_back(grads, cosine, sine):
    half = grads.shape[-1] // 2
    first = grads[..., :half]
    second = grads[..., half:]
    return jnp.concatenate([first * cosine + second * sine, second * cosine - first * sine], axis=-1)


def sequence_tables(lengths_rows, tok_rows):
    ends = jnp.cumsum(lengths_rows, axis=1)
    starts = ends - lengths_rows
    places = jnp.arange(tok_rows, dtype=jnp.int32)
    segment = jnp.sum((places[None, :, None] >= ends[:, None, :]).astype(jnp.int32), axis=2)
    member = segment[:, :, None] == jnp.arange(lengths_rows.shape[1], dtype=jnp.int32)[None, None, :]
    first = jnp.sum(jnp.where(member, starts[:, None, :], 0), axis=2)
    return segment, places[None, :] - first


def silu_parts(values):
    sigmoid_value = jax.nn.sigmoid(values)
    return values * sigmoid_value, sigmoid_value * (1.0 + values * (1.0 - sigmoid_value))


def mm(form, left, right):
    return jnp.einsum(form, left, right, preferred_element_type=f32)


def up_to(value, step):
    return -(-value // step) * step


def second_norm(place, cores, rows, given, hid_out, room):
    ap, tok, gn, rt, mk = given
    parts, tok_v, gn_v, rt_v, mk_v, hid, xn, _ = room
    t = place.t
    sends, arrivals = place.take(cores), place.take(cores)
    sent = [place.send(ap, parts.at[t], sends + d, arrivals + d, place.e, place.ring(d)) for d in range(1, cores)]
    kept = [place.keep(ap, parts.at[t])]
    kept += [place.keep(a, b) for a, b in ((tok, tok_v), (gn, gn_v), (rt, rt_v), (mk, mk_v))]
    for move in kept:
        move.wait()
    for d in range(1, cores):
        place.arrived(parts.at[place.ring(cores - d)], arrivals + d)

    def body(at, carry):
        for step in range(4):
            piece = pl.ds(pl.multiple_of(at * 64 + step * 16, 16), 16)
            total = parts[0, piece, :].astype(f32)
            for core in range(1, cores):
                total = total + parts[core, piece, :].astype(f32)
            values = tok_v[piece, :].astype(f32) + total
            hid[piece, :] = values
            rstd = lax.rsqrt(jnp.mean(values * values, axis=1, keepdims=True) + eps)
            xn[piece, :] = (values * rstd * gn_v[...]).astype(bf16)
        return carry

    lax.fori_loop(0, rows // 64, body, 0)
    saved = place.keep(hid, hid_out)
    return sent, saved


def route(room):
    _, _, _, rt_v, mk_v, _, xn, gt = room
    logits = lax.dot_general(rt_v[...], xn[...], (((1,), (1,)), ((), ())), preferred_element_type=f32)
    picked = mk_v[...] > 0.5
    top_logit = jnp.max(jnp.where(picked, logits, floor_score), axis=0, keepdims=True)
    lifted = jnp.where(picked, jnp.exp(jnp.where(picked, logits - top_logit, 0.0)), 0.0)
    gt[...] = lifted / jnp.sum(lifted, axis=0, keepdims=True)


class Out:
    def __init__(self, place, buffer, array, unit):
        self.place, self.buffer, self.array, self.unit = place, buffer, array, unit
        self.sem = place.take(2)

    def moves(self, slots):
        for at, slot in enumerate(slots):
            if self.unit is None:
                yield self.place.local(self.buffer.at[at], self.array.at[slot], self.sem + at)
            else:
                into = pl.ds(pl.multiple_of(slot * self.unit, self.unit), self.unit)
                source = self.buffer.at[pl.ds(at * self.unit, self.unit), :]
                yield self.place.local(source, self.array.at[into, :], self.sem + at)

    def go(self, slots):
        for move in self.moves(slots):
            move.start()

    def free(self, condition=None):
        for move in self.moves((jnp.int32(0), jnp.int32(0))):
            when(condition, move.wait)


def experts_pair(slots, used, capacity, rows, rows_in, grads_in, position, gate_of, weights, outs):
    wg, wu, wd, sh_in, sh_down = weights
    received, gated, low, back, acts, gate_backs, up_backs, dots_out, left_forward, left_backward = outs
    wide = sh_down.shape[0]
    places = lax.broadcasted_iota(jnp.int32, (capacity, rows), 0).astype(f32)
    gates, onehots = [], []
    for out in (received, gated, low, left_forward, left_backward):
        out.free(used)
    for at, slot in enumerate(slots):
        token, own = pl.ds(pl.multiple_of(slot * rows, rows), rows), pl.ds(at * capacity, capacity)
        mine = pl.ds(at * rows, rows)
        chosen = (position[slot] == places).astype(f32)
        onehot = chosen.astype(bf16)
        onehots.append(chosen)
        received.buffer[own, :] = dot(onehot, rows_in[token, :]).astype(bf16)
        gate = jnp.sum(chosen * gate_of(slot), axis=1, keepdims=True)
        row_grads = dot(onehot, grads_in[mine, :])
        gated.buffer[own, :] = (gate * row_grads).astype(bf16)
        low.buffer[own, :] = row_grads.astype(bf16)
        gates.append(gate)
        turned = chosen.T.astype(bf16)
        left_forward.buffer[mine, :capacity] = turned
        left_backward.buffer[mine, :capacity] = turned
    received.go(slots)
    gated.go(slots)
    gate = jnp.concatenate(gates, axis=0)
    rows_now = received.buffer[...]
    exp_gate = dot(rows_now, wg[...], ((1,), (1,)))
    exp_up = dot(rows_now, wu[...], ((1,), (1,)))
    silu, slope = silu_parts(exp_gate)
    act = (silu * exp_up).astype(bf16)
    acts.free(used)
    acts.buffer[...] = act
    acts.go(slots)
    out = dot(act, wd[...])
    dots = jnp.sum(low.buffer[...].astype(f32) * out, axis=1, keepdims=True)
    low.buffer[...] = (gate * out).astype(bf16)
    low.go(slots)
    dots_out.free(used)
    for at in range(2):
        column = dots[at * capacity : (at + 1) * capacity]
        token_dots = jnp.sum(onehots[at] * column, axis=0, keepdims=True)
        dots_out.buffer[at] = jnp.broadcast_to(token_dots, (8, rows))
    dots_out.go(slots)
    act_grad = dot(gated.buffer[...], wd[...], ((1,), (1,)))
    gate_back = (act_grad * exp_up * slope).astype(bf16)
    up_back = (act_grad * silu).astype(bf16)
    gate_backs.free(used)
    up_backs.free(used)
    gate_backs.buffer[...] = gate_back
    up_backs.buffer[...] = up_back
    gate_backs.go(slots)
    up_backs.go(slots)
    back.free(used)
    back.buffer[...] = (dot(gate_back, wg[...]) + dot(up_back, wu[...])).astype(bf16)
    back.go(slots)
    for at, slot in enumerate(slots):
        token, mine = pl.ds(pl.multiple_of(slot * rows, rows), rows), pl.ds(at * rows, rows)
        both_sides = dot(rows_in[token, :], sh_in[...], ((1,), (1,)))
        sh_gate, sh_up = both_sides[:, :wide], both_sides[:, wide:]
        sh_silu, sh_slope = silu_parts(sh_gate)
        left_forward.buffer[mine, capacity:] = (sh_silu * sh_up).astype(bf16)
        sh_grad = dot(grads_in[mine, :], sh_down[...], ((1,), (1,)))
        left_backward.buffer[mine, capacity : capacity + wide] = (sh_grad * sh_up * sh_slope).astype(bf16)
        left_backward.buffer[mine, capacity + wide :] = (sh_grad * sh_silu).astype(bf16)
    left_forward.go(slots)
    left_backward.go(slots)


def experts_kernel(
    groups,
    capacity,
    rows,
    xn_ref,
    grad_ref,
    position_ref,
    gate_ref,
    wg_ref,
    wu_ref,
    wd_ref,
    sh_in_ref,
    sh_down_ref,
    received_ref,
    gated_ref,
    low_ref,
    back_ref,
    act_ref,
    gate_back_ref,
    up_back_ref,
    dots_ref,
    left_forward_ref,
    left_backward_ref,
):
    places = lax.broadcasted_iota(jnp.int32, (capacity, rows), 0).astype(f32)
    gates, grads, onehots = [], [], []
    for g in range(groups):
        token = pl.ds(g * rows, rows)
        slot = pl.ds(g * capacity, capacity)
        chosen = (position_ref[g] == places).astype(f32)
        onehot = chosen.astype(bf16)
        onehots.append(chosen)
        received_ref[slot, :] = dot(onehot, xn_ref[token, :]).astype(bf16)
        gate = jnp.sum(chosen * gate_ref[g], axis=1, keepdims=True)
        row_grads = dot(onehot, grad_ref[token, :])
        gated_ref[slot, :] = (gate * row_grads).astype(bf16)
        low_ref[slot, :] = row_grads.astype(bf16)
        gates.append(gate)
        turned = chosen.T.astype(bf16)
        left_forward_ref[token, :capacity] = turned
        left_backward_ref[token, :capacity] = turned
    gate = jnp.concatenate(gates, axis=0)
    received = received_ref[...]
    exp_gate = dot(received, wg_ref[...], ((1,), (1,)))
    exp_up = dot(received, wu_ref[...], ((1,), (1,)))
    silu, slope = silu_parts(exp_gate)
    act = (silu * exp_up).astype(bf16)
    act_ref[...] = act
    out = dot(act, wd_ref[...])
    dots = jnp.sum(low_ref[...].astype(f32) * out, axis=1, keepdims=True)
    low_ref[...] = (gate * out).astype(bf16)
    for g in range(groups):
        column = dots[g * capacity : (g + 1) * capacity]
        token_dots = jnp.sum(onehots[g] * column, axis=0, keepdims=True)
        dots_ref[g] = jnp.broadcast_to(token_dots, (8, rows))
    act_grad = dot(gated_ref[...], wd_ref[...], ((1,), (1,)))
    gate_back = (act_grad * exp_up * slope).astype(bf16)
    up_back = (act_grad * silu).astype(bf16)
    gate_back_ref[...] = gate_back
    up_back_ref[...] = up_back
    back_ref[...] = (
        dot(gate_back, wg_ref[...]) + dot(up_back, wu_ref[...])
    ).astype(bf16)
    wide = sh_down_ref.shape[0]
    both = dot(xn_ref[...], sh_in_ref[...], ((1,), (1,)))
    sh_gate, sh_up = both[:, :wide], both[:, wide:]
    sh_silu, sh_slope = silu_parts(sh_gate)
    left_forward_ref[:, capacity:] = (sh_silu * sh_up).astype(bf16)
    sh_grad = dot(grad_ref[...], sh_down_ref[...], ((1,), (1,)))
    left_backward_ref[:, capacity : capacity + wide] = (sh_grad * sh_up * sh_slope).astype(bf16)
    left_backward_ref[:, capacity + wide :] = (sh_grad * sh_silu).astype(bf16)


def experts_pass(count, capacity, rows, xn_all, grad_all, position, gate, wg, wu, wd, sh_in, sh_down):
    groups = 2
    units, width = wg.shape
    wide = sh_down.shape[0]

    def along(*shape):
        return pl.BlockSpec(shape, lambda i: (i,) + (0,) * (len(shape) - 1))

    def whole(array):
        return pl.BlockSpec(array.shape, lambda i: (0,) * array.ndim, pipeline_mode=pl.Buffered(1))

    slots = groups * capacity
    tokens = groups * rows
    flops = 2 * count * capacity * width * units * 6
    return pl.pallas_call(
        functools.partial(experts_kernel, groups, capacity, rows),
        name="experts_pass",
        grid=(count // groups,),
        in_specs=[
            along(tokens, width),
            along(tokens, width),
            along(groups, 1, rows),
            along(groups, 1, rows),
            whole(wg),
            whole(wu),
            whole(wd),
            whole(sh_in),
            whole(sh_down),
        ],
        out_specs=[
            along(slots, width),
            along(slots, width),
            along(slots, width),
            along(slots, width),
            along(slots, units),
            along(slots, units),
            along(slots, units),
            along(groups, 8, rows),
            along(tokens, capacity + wide),
            along(tokens, capacity + 2 * wide),
        ],
        out_shape=[like((count * capacity, width))] * 4
        + [like((count * capacity, units))] * 3
        + [
            like((count, 8, rows), f32),
            like((count * rows, capacity + wide)),
            like((count * rows, capacity + 2 * wide)),
        ],
        cost_estimate=pl.CostEstimate(
            flops=flops, bytes_accessed=4 * count * (rows + 2 * capacity) * width, transcendentals=0
        ),
        compiler_params=pltpu.CompilerParams(vmem_limit_bytes=58 * 2**20),
    )(xn_all, grad_all, position, gate, wg, wu, wd, sh_in, sh_down)


def local(
    mesh,
    tokens,
    lengths,
    routes,
    gain_attn,
    w_query,
    w_key,
    w_value,
    w_out,
    gain_ffn,
    w_router,
    routed_gate_weight,
    routed_up_weight,
    w_down,
    w_shared_gate,
    w_shared_up,
    w_shared_down,
    out_grad,
):
    count, cores = mesh.shape["expert"], mesh.shape["tensor"]
    rows, width = tokens.shape
    part = width // cores
    deep = w_query.shape[0]
    experts = w_router.shape[1]
    heads = w_query.shape[1] // HEAD_DIM
    capacity = up_to(min(rows, rows * TOP * 4 // (3 * count)), 128)
    hidden_units = w_shared_gate.shape[1] // count
    scale = HEAD_DIM ** (-0.5)
    e = lax.axis_index("expert")
    t = lax.axis_index("tensor")
    chunk = heads * rows
    strips = Strips(count, deep)

    expert_ids = jnp.arange(experts, dtype=jnp.int32)
    choose = jnp.any(routes[:, :, None] == expert_ids[None, None, :], axis=1)
    mask_t = choose.T.astype(bf16)
    vectors = jnp.concatenate(
        [
            w_router.T,
            gain_attn[None],
            gain_ffn[None],
            jnp.pad(lengths.astype(bf16), ((0, 0), (0, deep - lengths.shape[1]))),
        ],
        axis=0,
    )
    head_rows = up_to(vectors.shape[0], 16)
    vectors = jnp.pad(vectors, ((0, head_rows - vectors.shape[0]), (0, 0)))
    pieces = rows // deep
    mask_rows = mask_t.reshape(experts * pieces, deep)
    small = jnp.concatenate([vectors, mask_rows], axis=0)
    small_rows = up_to(small.shape[0], 16)
    small = jnp.pad(small, ((0, small_rows - small.shape[0]), (0, 0)))

    def unpack(gathered):
        router = gathered[:experts]
        attn_gain, ffn_gain = gathered[experts].astype(f32), gathered[experts + 1].astype(f32)
        rows_of = gathered[experts + 2].reshape(count, deep)[:, : lengths.shape[1]].astype(f32).astype(jnp.int32)
        masks = gathered[head_rows : head_rows + experts * pieces].reshape(experts, pieces, count, deep)
        return router, attn_gain, ffn_gain, rows_of, masks.transpose(2, 0, 1, 3).reshape(count, experts, rows)

    shared_pack = jnp.concatenate(
        [
            w_shared_gate.T.reshape(count, hidden_units, deep),
            w_shared_up.T.reshape(count, hidden_units, deep),
            w_shared_down.reshape(count, hidden_units, deep),
        ],
        axis=1,
    )
    pack_rows = up_to(3 * hidden_units, 16)
    shared_pack = jnp.pad(shared_pack, ((0, 0), (0, pack_rows - 3 * hidden_units), (0, 0)))
    out_rows = w_out.shape[0]

    if strips.direct:

        def front_body(place, given, made, room):
            tok, sm, wq, wk, wv, wo, sp, inv, cos_in, sin_in = given
            sm_all, w_all, xn_all, qkv_all, pr_all, ct_all, st_all, ho_all, wo_all, sp_all = made
            sm_v, tok_v, w_v, normed, qkv, probs, cosines, sines, out, inverse, cos_v, sin_v = room
            own = lax.rem(place.e, heads)
            base = place.e - own
            ready = [place.keep(x, y) for x, y in ((inv, inverse), (cos_in, cos_v), (sin_in, sin_v))]
            small_in, small_out = start_exchange(place, count, lambda s: sm, lambda s: sm_v.at[:, lanes(s, deep)])
            tokens_in = row_gather(place, heads, tok, tok_v, rows, part)
            sends, arrivals = place.take(heads), place.take(heads)

            def wo_view(slot, core=0, piece=0):
                return strips.at(wo_all, slot)

            def attention():
                links = tokens_in.links()
                for _ in range(PIECES):
                    next(links)
                pulls = []
                for which, weight in enumerate((wq, wk, wv)):

                    def landing(slot, which=which):
                        at = pl.ds(pl.multiple_of(slot * deep, deep), deep)
                        return w_v.at[at, pl.ds(which * HEAD_DIM, HEAD_DIM)]

                    pulls.append(
                        start_exchange(
                            place, count, lambda s, w=weight: w.at[:, lanes(lax.rem(s, heads), HEAD_DIM)], landing
                        )
                    )
                yield
                yield from links
                for d in range(1, count):
                    slot = lax.rem(place.e + d, count)
                    for arrived in [small_in] + [pull[0] for pull in pulls]:
                        arrived(slot)
                for move in ready:
                    move.wait()
                saved = [place.keep(sm_v, sm_all), place.keep(w_v, w_all)]
                head = experts - experts % 16
                vectors = sm_v[pl.ds(head, 16), :].astype(f32)
                gain = vectors[experts - head : experts - head + 1, :]
                position = lax.broadcasted_iota(jnp.int32, (rows, HEAD_DIM), 0).astype(f32)
                gave, stored = [], []

                def group(n, i, j):
                    tokens_in.from_cores(n, i, j)
                    slot = tokens_in.slot(n, i, j)
                    at = len(stored) % 2
                    if len(stored) >= 2:
                        stored[-2].wait()
                    row = sm_v[pl.ds(head, 16), lanes(tokens_in.block.device(slot), deep)].astype(f32)
                    row = row[experts + 2 - head : experts + 3 - head, :]
                    sequences = lengths.shape[1]
                    ends, end = [], jnp.zeros((1, 1), f32)
                    for place_in in range(sequences - 1):
                        end = end + row[:, place_in : place_in + 1]
                        ends.append(end)
                    line = lax.broadcasted_iota(jnp.int32, (up_to(sequences, 8), HEAD_DIM), 0)
                    starts = jnp.zeros(line.shape, f32)
                    for which, end in enumerate(ends):
                        starts = jnp.where(line == which, end, starts)
                    angles = starts * inverse[...]
                    cos_starts, sin_starts = jnp.cos(angles), jnp.sin(angles)
                    first = jnp.zeros((rows, HEAD_DIM), f32)
                    cos_first, sin_first = jnp.ones((rows, HEAD_DIM), f32), jnp.zeros((rows, HEAD_DIM), f32)
                    for which, end in enumerate(ends):
                        after = position >= end
                        first = jnp.where(after, end, first)
                        cos_first = jnp.where(after, cos_starts[which : which + 1, :], cos_first)
                        sin_first = jnp.where(after, sin_starts[which : which + 1, :], sin_first)
                    cosine = cos_v[...] * cos_first + sin_v[...] * sin_first
                    sine = sin_v[...] * cos_first - cos_v[...] * sin_first
                    attend(
                        tok_v,
                        gain,
                        w_v,
                        first,
                        cosine,
                        sine,
                        (normed, qkv, probs, cosines, sines, out),
                        at,
                        slot,
                        rows,
                    )
                    stored.append(
                        place.keep(
                            normed.at[at], xn_all.at[pl.ds(pl.multiple_of(slot * rows, rows), rows), :]
                        )
                    )
                    landing = ho_all.at[:, lanes(own, HEAD_DIM)]
                    if n + i + j == 0:
                        saved.append(place.keep(out.at[slot], landing))
                    else:
                        gave.append(
                            place.send(out.at[slot], landing, sends + slot, arrivals + own, base + slot, place.t)
                        )

                for n in range(tokens_in.deep):
                    if n == 0:
                        tokens_in.kept.wait()
                    group(n, 0, 0)
                    yield
                for n in range(tokens_in.deep):
                    tokens_in.last(n)
                    for i, j in ((1, 0), (0, 1), (1, 1)):
                        group(n, i, j)
                        yield
                for source, target in ((qkv, qkv_all), (probs, pr_all), (cosines, ct_all), (sines, st_all)):
                    saved.append(place.keep(source, target))
                yield
                for d in range(1, heads):
                    slot = lax.rem(own + d, heads)
                    place.arrived(ho_all.at[:, lanes(slot, HEAD_DIM)], arrivals + slot)
                for move in gave:
                    move.wait_send()
                for move in stored[-2:] + saved:
                    move.wait()
                for pull in pulls:
                    pull[1]()
                small_out()
                tokens_in.finish()

            yield attention()
            yield later(gather(place, count, lambda p: wo, (wo, wo_view), wo_view, False), 3)
            yield later(exchange(place, count, lambda s: sp.at[s], lambda s: strips.at(sp_all, s)), 6)

        half = HEAD_DIM // 2
        inverse = 10000.0 ** (-2.0 * jnp.arange(half, dtype=f32) / HEAD_DIM)
        inverse = jnp.concatenate([inverse, inverse])[None]
        row_angles = jnp.arange(rows, dtype=f32)[:, None] * inverse
        (
            small_all,
            w_qkv,
            xn_chunk,
            qkv_saved,
            probs_saved,
            cosine_wide,
            sine_wide,
            heads_out,
            out_full,
            shared_all,
        ) = transfer(
            "attention_front",
            0,
            mesh,
            front_body,
            (
                tokens,
                small,
                w_query,
                w_key,
                w_value,
                w_out,
                shared_pack,
                inverse,
                jnp.cos(row_angles),
                jnp.sin(row_angles),
            ),
            (
                like((small_rows, width)),
                like((width, 3 * HEAD_DIM)),
                like((chunk, width)),
                like((chunk, 3 * HEAD_DIM)),
                like((chunk, rows), f32),
                like((chunk, HEAD_DIM), f32),
                like((chunk, HEAD_DIM), f32),
                like((rows, heads * HEAD_DIM)),
                like((out_rows, width)),
                like((pack_rows, width)),
            ),
            [
                pltpu.VMEM((small_rows, width), bf16),
                pltpu.VMEM((chunk, width), bf16),
                pltpu.VMEM((width, 3 * HEAD_DIM), bf16),
                pltpu.VMEM((2, rows, width), bf16),
                pltpu.VMEM((chunk, 3 * HEAD_DIM), bf16),
                pltpu.VMEM((chunk, rows), f32),
                pltpu.VMEM((chunk, HEAD_DIM), f32),
                pltpu.VMEM((chunk, HEAD_DIM), f32),
                pltpu.VMEM((heads, rows, HEAD_DIM), bf16),
                pltpu.VMEM((1, HEAD_DIM), f32),
                pltpu.VMEM((rows, HEAD_DIM), f32),
                pltpu.VMEM((rows, HEAD_DIM), f32),
            ],
            semaphores=640,
            vmem=56 * 2**20,
        )
        router_full, attn_gain, ffn_gain, _, masks = unpack(small_all)
    else:
        def first_body(place, given, made, room):
            tok, sm, *weights = given
            tok_all, sm_all, w_all = made
            yield exchange(place, count, lambda s: sm, lambda s: sm_all.at[s])
            yield row_gather(place, heads, tok, tok_all, rows, part).all()
            for which, weight in enumerate(weights):

                def landing(slot, which=which):
                    at = pl.ds(pl.multiple_of(slot * deep, deep), deep)
                    return w_all.at[at, pl.ds(which * HEAD_DIM, HEAD_DIM)]

                yield exchange(
                    place, count, lambda s, w=weight: w.at[:, lanes(lax.rem(s, heads), HEAD_DIM)], landing
                )

        tok_chunk, small_all, w_qkv = transfer(
            "gather_tokens",
            0,
            mesh,
            first_body,
            (tokens, small, w_query, w_key, w_value),
            (like((chunk, width)), like((count, small_rows, deep)), like((width, 3 * HEAD_DIM))),
        )

        router_full, attn_gain, ffn_gain, lengths_all, masks = unpack(strips.join(small_all))

        member = e % heads
        lengths_chunk = lax.dynamic_slice_in_dim(lengths_all, e - member, heads, axis=0)
        segment, positions = sequence_tables(lengths_chunk, rows)
        half = HEAD_DIM // 2
        inverse = 10000.0 ** (-2.0 * jnp.arange(half, dtype=f32) / HEAD_DIM)
        angles = positions.astype(f32)[:, :, None] * inverse[None, None, :]
        cosine, sine = jnp.cos(angles), jnp.sin(angles)

        tok32 = tok_chunk.astype(f32)
        rstd_chunk = lax.rsqrt(jnp.mean(tok32 * tok32, axis=-1, keepdims=True) + eps)
        xn_chunk = (tok32 * rstd_chunk * attn_gain).astype(bf16)
        qkv = jnp.dot(xn_chunk, w_qkv, preferred_element_type=f32).reshape(heads, rows, 3 * HEAD_DIM)
        query = rotary(qkv[..., :HEAD_DIM], cosine, sine).astype(bf16)
        keyed = rotary(qkv[..., HEAD_DIM : 2 * HEAD_DIM], cosine, sine).astype(bf16)
        valued = qkv[..., 2 * HEAD_DIM :].astype(bf16)
        places = jnp.arange(rows, dtype=jnp.int32)
        allowed = (segment[:, :, None] == segment[:, None, :]) & (places[None, :] <= places[:, None])[None]
        scores = jnp.where(allowed, mm("gqd,gkd->gqk", query, keyed) * scale, floor_score)
        top_score = jnp.max(scores, axis=-1, keepdims=True)
        raised = jnp.exp(scores - top_score)
        probs = raised / jnp.sum(raised, axis=-1, keepdims=True)
        probs_low = probs.astype(bf16)
        head_out = mm("gqk,gkd->gqd", probs_low, valued).astype(bf16)

        def second_body(place, given, made, room):
            ho, og, wo, sp = given
            ho_all, og_all, wo_all, sp_all = made
            yield exchange(place, heads, lambda s: ho.at[s], lambda s: ho_all.at[:, lanes(s, HEAD_DIM)])
            yield row_gather(place, count, og, og_all, rows, part).all()

            def wo_view(slot, core=0, piece=0):
                return strips.at(wo_all, slot)

            yield gather(place, count, lambda p: wo, (wo, wo_view), wo_view, False)
            yield exchange(place, count, lambda s: sp.at[s], lambda s: strips.at(sp_all, s))

        heads_out, grad_all, out_full, shared_all = transfer(
            "gather_inputs",
            1,
            mesh,
            second_body,
            (head_out, out_grad, w_out, shared_pack),
            (
                like((rows, heads * HEAD_DIM)),
                like((count * rows, width)),
                like(strips.shape(out_rows)),
                like(strips.shape(pack_rows)),
            ),
            semaphores=640,
        )
        out_full, shared_all = strips.join(out_full), strips.join(shared_all)
    attention_part = jnp.dot(heads_out, out_full, preferred_element_type=f32).astype(bf16)

    own_mask = lax.dynamic_index_in_dim(masks, e, axis=1, keepdims=False).astype(f32)
    at_row = jnp.arange(rows, dtype=jnp.int32)
    earlier = (at_row[:, None] < at_row[None, :]).astype(bf16)
    position = jnp.where(own_mask > 0.5, jnp.dot(own_mask.astype(bf16), earlier, preferred_element_type=f32), -1.0)
    gate_weight, up_weight, down_weight = routed_gate_weight[0].T, routed_up_weight[0].T, w_down[0]
    sh_wide = up_to(hidden_units, 128)

    def widened(which):
        piece = shared_all[which * hidden_units : (which + 1) * hidden_units]
        return jnp.pad(piece, ((0, sh_wide - hidden_units), (0, 0)))

    fixed_backward = jnp.concatenate([widened(0), widened(1)], axis=0)
    fixed_forward = widened(2)
    units = gate_weight.shape[0]
    norm_rooms = [
        pltpu.VMEM((cores, rows, width), bf16),
        pltpu.VMEM((rows, width), bf16),
        pltpu.VMEM((1, width), f32),
        pltpu.VMEM((experts, width), bf16),
        pltpu.VMEM((experts, rows), f32),
        pltpu.VMEM((rows, width), f32),
        pltpu.VMEM((rows, width), bf16),
        pltpu.VMEM((experts, rows), f32),
    ]
    if strips.direct:

        def rows_body(place, given, made, room):
            og, pos, *weights = given[5:]
            hid_out, xn_all, og_all, gt_out, *arrays = made
            xn, gt = room[6:8]
            gates_v, xn_v, og_v, pos_v = room[8:12]
            weights_v, buffers = room[12:17], room[17:]
            grads_moving = row_gather(place, count, og, og_all, rows, part)
            for p in range(PIECES):
                grads_moving.start(p)
            loads = [place.keep(pos, pos_v)] + [place.keep(x, y) for x, y in zip(weights, weights_v)]
            sent, saved = second_norm(place, cores, rows, given[:5], hid_out, room[:8])
            moving = row_gather(place, count, xn, xn_v, rows, part)
            for p in range(PIECES):
                moving.start(p)
            route(room[:8])
            saved_gates = place.keep(gt, gt_out)
            gate_in, gate_out = start_exchange(place, count, lambda s: gt, lambda s: gates_v.at[s])
            sizes = [capacity] * 7 + [None] + [rows] * 2
            outs = [
                [Out(place, buffer.at[pair], array, unit) for buffer, array, unit in zip(buffers, arrays, sizes)]
                for pair in range(2)
            ]
            grad_sems, row_sems = place.take(4), place.take(4)
            quads = (((0, 0), (1, 0)), ((0, 1), (1, 1)))
            expert = lax.broadcasted_iota(jnp.int32, (experts, rows), 0)

            def gate_of(slot):
                return jnp.sum(jnp.where(expert == place.e, gates_v[slot], 0.0), axis=0, keepdims=True)

            def of_rows(slot):
                return pl.ds(pl.multiple_of(slot * rows, rows), rows)

            def grads(m, pair):
                for at, (i, j) in enumerate(quads[pair]):
                    source = og_all.at[of_rows(moving.slot(m, i, j)), :]
                    yield place.local(
                        source, og_v.at[pair, pl.ds(at * rows, rows), :], grad_sems + 2 * pair + at
                    )

            def keep_rows(m):
                for at, (i, j) in enumerate(quads[0] + quads[1]):
                    own = of_rows(moving.slot(m, i, j))
                    yield place.local(xn_v.at[own, :], xn_all.at[own, :], row_sems + at)

            def link(c):
                for gathered in (moving, grads_moving):
                    for p in range(PIECES):
                        gathered.from_one(c, p)
                        pl.when(c + 1 < moving.deep)(lambda: gathered.from_line(c + 1, p))

            def complete(gathered, m):
                gathered.last(m)
                for i, j in quads[0] + quads[1]:
                    gathered.from_cores(m, i, j)

            def work(m):
                pl.when(2 * m + 1 < moving.deep)(lambda: link(2 * m + 1))
                complete(moving, m)
                complete(grads_moving, m)
                for i, j in quads[0] + quads[1]:
                    gate_in(moving.slot(m, i, j))
                for move in keep_rows(m):
                    when(m > 0, move.wait)
                    move.start()
                for pair in range(2):
                    for move in grads(m, pair):
                        move.start()
                for pair in range(2):
                    for move in grads(m, pair):
                        move.wait()
                    slots = [moving.slot(m, i, j) for i, j in quads[pair]]
                    experts_pair(
                        slots,
                        m > 0,
                        capacity,
                        rows,
                        xn_v,
                        og_v.at[pair],
                        pos_v,
                        gate_of,
                        weights_v,
                        outs[pair],
                    )
                    if pair == 0:
                        pl.when(2 * m + 2 < moving.deep)(lambda: link(2 * m + 2))

            for move in loads:
                move.wait()
            moving.kept.wait()
            grads_moving.kept.wait()
            link(0)

            def stage(m, carry):
                work(m)
                return carry

            lax.fori_loop(0, moving.deep, stage, 0)
            for out in outs[0] + outs[1]:
                out.free()
            for move in keep_rows(0):
                move.wait()
            gate_out()
            moving.close()
            grads_moving.close()
            for move in sent:
                move.wait_send()
            saved.wait()
            saved_gates.wait()
            yield from ()

        shapes = [(count * capacity, width)] * 4 + [(count * capacity, units)] * 3
        shapes += [(count, 8, rows), (count * rows, capacity + sh_wide), (count * rows, capacity + 2 * sh_wide)]
        pair_shapes = [(2 * capacity, width)] * 4 + [(2 * capacity, units)] * 3
        pair_shapes += [(2, 8, rows), (2 * rows, capacity + sh_wide), (2 * rows, capacity + 2 * sh_wide)]
        kinds = [bf16] * 7 + [f32] + [bf16] * 2
        (
            hidden,
            xn_all,
            grad_all,
            gates_t,
            received,
            gated_grad,
            exp_low,
            back_rows,
            exp_act,
            gate_back,
            up_back,
            token_dots,
            left_forward,
            left_backward,
        ) = transfer(
            "rows_and_experts",
            2,
            mesh,
            rows_body,
            (
                attention_part,
                tokens,
                ffn_gain[None],
                router_full,
                mask_t.astype(f32),
                out_grad,
                position[:, None],
                gate_weight,
                up_weight,
                down_weight,
                fixed_backward,
                fixed_forward,
            ),
            (
                like((rows, width), f32),
                like((count * rows, width)),
                like((count * rows, width)),
                like((experts, rows), f32),
            )
            + tuple(like(shape, kind) for shape, kind in zip(shapes, kinds)),
            norm_rooms
            + [
                pltpu.VMEM((count, experts, rows), f32),
                pltpu.VMEM((count * rows, width), bf16),
                pltpu.VMEM((2, 2 * rows, width), bf16),
                pltpu.VMEM((count, 1, rows), f32),
                pltpu.VMEM((units, width), bf16),
                pltpu.VMEM((units, width), bf16),
                pltpu.VMEM((units, width), bf16),
                pltpu.VMEM((2 * sh_wide, width), bf16),
                pltpu.VMEM((sh_wide, width), bf16),
            ]
            + [pltpu.VMEM((2,) + shape, kind) for shape, kind in zip(pair_shapes, kinds)],
            semaphores=480,
            vmem=62 * 2**20,
        )
        gates = gates_t.T
    else:
        def third_body(place, given, made, room):
            ap, tok, gn, rt, mk = given
            hid_out, xn_all, gt_all = made
            xn, gt = room[6:]
            sent, saved = second_norm(place, cores, rows, given, hid_out, room)
            yield row_gather(place, count, xn, xn_all, rows, part).all()
            route(room)
            yield exchange(place, count, lambda s: gt, lambda s: gt_all.at[s])
            for move in sent:
                move.wait_send()
            saved.wait()

        hidden, xn_all, gates_all = transfer(
            "gather_rows",
            2,
            mesh,
            third_body,
            (attention_part, tokens, ffn_gain[None], router_full, mask_t.astype(f32)),
            (like((rows, width), f32), like((count * rows, width)), like((count, experts, rows), f32)),
            norm_rooms,
            semaphores=400,
            vmem=40 * 2**20,
        )
        gates = lax.dynamic_index_in_dim(gates_all, e, axis=0, keepdims=False).T
        own_gate = lax.dynamic_index_in_dim(gates_all, e, axis=1, keepdims=False)
        (
            received,
            gated_grad,
            exp_low,
            back_rows,
            exp_act,
            gate_back,
            up_back,
            token_dots,
            left_forward,
            left_backward,
        ) = experts_pass(
            count,
            capacity,
            rows,
            xn_all,
            grad_all,
            position[:, None],
            own_gate[:, None],
            gate_weight,
            up_weight,
            down_weight,
            fixed_backward,
            fixed_forward,
        )

    inputs = tokens.astype(f32)
    rstd_two = lax.rsqrt(jnp.mean(hidden * hidden, axis=-1, keepdims=True) + eps)

    sh_grads = mm("tf,td->fd", left_backward[:, capacity:], xn_all).astype(bf16)
    shared_grads = jnp.concatenate(
        [
            sh_grads[:hidden_units],
            sh_grads[sh_wide : sh_wide + hidden_units],
            mm("tf,td->fd", left_forward[:, capacity:], grad_all).astype(bf16)[:hidden_units],
        ],
        axis=0,
    )
    shared_grads = jnp.pad(shared_grads, ((0, pack_rows - 3 * hidden_units), (0, 0)))

    def fourth_body(place, given, made, room):
        lf, el, ff, lb, br, fb, td, sg = given
        mixed, summed, dots, sg_all = made
        mixed_view, summed_view = part_view(mixed, rows, part), part_view(summed, rows, part)
        forward = Product(place, lf, el, ff, room[7:9], count, rows, part)
        backward = Product(place, lb, br, fb, room[9:11], count, rows, part)
        yield scatter(
            place,
            count,
            [forward, backward],
            room[:7],
            [lambda c: mixed_view(0, c), lambda c: summed_view(0, c)],
            (rows, part),
            True,
            room[11],
        )
        yield both(place, count, lambda s: td.at[s], lambda c, s: dots.at[c, s], lambda c: dots.at[c])
        yield later(exchange(place, count, lambda s: strips.at(sg, s), lambda s: sg_all.at[s]), 8)

    mixture, summed_back, dots_all, shared_back = transfer(
        "scatter_both",
        3,
        mesh,
        fourth_body,
        (
            left_forward,
            exp_low,
            fixed_forward,
            left_backward,
            back_rows,
            fixed_backward,
            token_dots,
            strips.cut(shared_grads),
        ),
        (
            like((rows, width)),
            like((rows, width)),
            like((cores, count, 8, rows), f32),
            like((count, pack_rows, deep)),
        ),
        scatter_scratch(
            count,
            cores,
            rows,
            part,
            [(left_forward.shape[1], True), (left_backward.shape[1], True)],
        )
        + [pltpu.SemaphoreType.REGULAR((count * (cores - 1),))],
        vmem=60 * 2**20,
    )
    output = (hidden + mixture.astype(f32)).astype(bf16)

    gate_total = jnp.sum(dots_all[:, :, 0, :], axis=0).T
    weighted_dots = jnp.sum(gates * gate_total, axis=1, keepdims=True)
    grad_logits = gates * (gate_total - weighted_dots)

    down_grad = mm("rf,rd->fd", exp_act, gated_grad)
    gate_grad = mm("rd,rf->df", received, gate_back)
    up_grad = mm("rd,rf->df", received, up_back)
    cotangent = out_grad.astype(f32)
    grad_two = summed_back.astype(f32) + jnp.einsum(
        "te,ed->td", grad_logits, router_full.astype(f32), precision=highest
    )
    scaled = grad_two * ffn_gain
    inner = jnp.mean(scaled * hidden, axis=-1, keepdims=True)
    grad_hidden = cotangent + rstd_two * scaled - hidden * (rstd_two * rstd_two * rstd_two) * inner
    ffn_gain_part = jnp.sum(grad_two * hidden * rstd_two, axis=0)
    grad_branch = grad_hidden.astype(bf16)
    grad_heads = mm("td,cd->tc", grad_branch, out_full).astype(bf16)
    out_proj_part = mm("tc,td->cd", heads_out, grad_branch).astype(bf16)

    turns = count // heads

    def spread(vector):
        return jnp.pad(vector.reshape(count, 1, deep), ((0, 0), (0, 7), (0, 0)))

    if strips.direct:

        def back_body(place, given, made, room):
            gh, gl, op, fg, qkv_s, pr, ct, st, xn, wt = given
            one, qg_all, op_sum, ag_all, fg_all, logit_all = made
            qkv_v, pr_v, ct_v, st_v, gh_v, normed, turned, sums, grad_qkv, right, gains, blocks = room[14:]
            own = lax.rem(place.e, heads)
            moves = [place.keep(x, y) for x, y in ((qkv_s, qkv_v), (pr, pr_v), (ct, ct_v), (st, st_v))]
            lasts = [place.keep(xn, normed), place.keep(wt, right)]
            arrived, finish = start_exchange(
                place, heads, lambda s: gh.at[:, lanes(s, HEAD_DIM)], lambda s: gh_v.at[s]
            )
            one_view = part_view(one, rows, part)

            def main():
                for move in moves:
                    move.wait()
                for d in range(heads):
                    slot = lax.rem(own + d, heads)
                    if d > 0:
                        arrived(slot)
                    attend_back((qkv_v, pr_v, ct_v, st_v, gh_v, grad_qkv, turned), slot, rows)
                    yield
                for move in lasts:
                    move.wait()
                tail()
                yield
                kept = Kept(grad_qkv, right, rows)
                yield from scatter(place, heads, [kept], room[:7], [lambda c: one_view(0, c)], (rows, part), True)

            def tail():
                wide = 2 * deep

                def product(at, carry):
                    sums[:, lanes(at, wide)] = dot(turned[...], normed[:, lanes(at, wide)])
                    return carry

                lax.fori_loop(0, width // wide, product, 0)

                def body(at, carry):
                    block = sums[:, lanes(at, deep)]
                    blocks[at] = block.astype(bf16).T
                    weights = right[pl.ds(pl.multiple_of(at * deep, deep), deep), :].T.astype(f32)
                    gain_row = jnp.sum(block * weights, axis=0, keepdims=True)
                    gains[:, lanes(at, deep)] = jnp.broadcast_to(gain_row, (8, deep))
                    return carry

                lax.fori_loop(0, count, body, 0)
                for which in range(3):

                    def landing(slot, which=which):
                        return qg_all.at[which, lax.div(slot, heads), :, lanes(lax.rem(slot, heads), HEAD_DIM)]

                    def block(slot, which=which):
                        return blocks.at[slot, :, pl.ds(which * HEAD_DIM, HEAD_DIM)]

                    tasks.append(exchange(place, count, block, landing))
                tasks.append(
                    both(
                        place,
                        count,
                        lambda s: gains.at[:, lanes(s, deep)],
                        lambda c, s: ag_all.at[c, s],
                        lambda c: ag_all.at[c],
                    )
                )

            projection = scatter(
                place, count, [lambda s: strips.at(op, s)], room[7:14], [lambda c: op_sum], (out_rows, deep), False
            )
            tasks = [
                main(),
                twice(projection),
                exchange(place, count, lambda s: gl, lambda s: logit_all.at[s]),
                exchange(place, count, lambda s: fg.at[s], lambda s: fg_all.at[s]),
            ]
            yield tasks
            finish()

        grad_one, qkv_all, out_proj_sum, attn_gains, ffn_gains, logits_all = transfer(
            "attention_back",
            4,
            mesh,
            back_body,
            (
                grad_heads,
                grad_logits.T,
                out_proj_part,
                spread(ffn_gain_part),
                qkv_saved,
                probs_saved,
                cosine_wide,
                sine_wide,
                xn_chunk,
                w_qkv,
            ),
            (
                like((rows, width)),
                like((3, turns, deep, heads * HEAD_DIM)),
                like((out_rows, deep)),
                like((cores, count, 8, deep), f32),
                like((count, 8, deep), f32),
                like((count, experts, rows), f32),
            ),
            scatter_scratch(heads, cores, rows, part)
            + scatter_scratch(count, 1, out_rows, deep)
            + [
                pltpu.VMEM((chunk, 3 * HEAD_DIM), bf16),
                pltpu.VMEM((chunk, rows), f32),
                pltpu.VMEM((chunk, HEAD_DIM), f32),
                pltpu.VMEM((chunk, HEAD_DIM), f32),
                pltpu.VMEM((heads, rows, HEAD_DIM), bf16),
                pltpu.VMEM((chunk, width), bf16),
                pltpu.VMEM((3 * HEAD_DIM, chunk), bf16),
                pltpu.VMEM((3 * HEAD_DIM, width), f32),
                pltpu.VMEM((chunk, 3 * HEAD_DIM), bf16),
                pltpu.VMEM((width, 3 * HEAD_DIM), bf16),
                pltpu.VMEM((8, width), f32),
                pltpu.VMEM((count, deep, 3 * HEAD_DIM), bf16),
            ],
            semaphores=640,
            vmem=56 * 2**20,
        )
    else:
        def fifth_body(place, given, made, room):
            gl, logit_all = given[1], made[1]
            yield exchange(place, count, lambda s: gl, lambda s: logit_all.at[s])
            yield exchange(place, heads, lambda s: given[0].at[:, lanes(s, HEAD_DIM)], lambda s: made[0].at[s])

        grad_head, logits_all = transfer(
            "exchange_heads",
            4,
            mesh,
            fifth_body,
            (grad_heads, grad_logits.T),
            (like((heads, rows, HEAD_DIM)), like((count, experts, rows), f32)),
        )
        grad_value = mm("gqk,gqd->gkd", probs_low, grad_head)
        grad_probs = mm("gqd,gkd->gqk", grad_head, valued)
        weighted = jnp.sum(probs * grad_probs, axis=-1, keepdims=True)
        grad_scores = (probs * (grad_probs - weighted)).astype(bf16)
        grad_query = mm("gqk,gkd->gqd", grad_scores, keyed) * scale
        grad_key = mm("gqk,gqd->gkd", grad_scores, query) * scale
        grad_qkv = jnp.concatenate(
            [
                rotary_back(grad_query, cosine, sine).astype(bf16),
                rotary_back(grad_key, cosine, sine).astype(bf16),
                grad_value.astype(bf16),
            ],
            axis=2,
        ).reshape(chunk, 3 * HEAD_DIM)
        qkv_grad = mm("td,tc->dc", xn_chunk, grad_qkv)
        attn_gain_part = jnp.sum(qkv_grad * w_qkv.astype(f32), axis=1)
        qkv_grad = qkv_grad.astype(bf16)

        def sixth_body(place, given, made, room):
            gq, wq, qg, op, ag, fg = given
            one, qg_all, op_sum, ag_all, fg_all = made
            one_view = part_view(one, rows, part)
            made_here = Product(place, gq, None, wq, room[7:9], heads, rows, part)
            yield scatter(place, heads, [made_here], room[:7], [lambda c: one_view(0, c)], (rows, part), True)
            yield scatter(
                place, count, [lambda s: strips.at(op, s)], room[9:], [lambda c: op_sum], (out_rows, deep), False
            )
            yield both(place, count, lambda s: ag.at[s], lambda c, s: ag_all.at[c, s], lambda c: ag_all.at[c])
            yield exchange(place, count, lambda s: fg.at[s], lambda s: fg_all.at[s])
            for which in range(3):

                def source(slot, which=which):
                    at = pl.ds(pl.multiple_of(slot * deep, deep), deep)
                    return qg.at[at, pl.ds(which * HEAD_DIM, HEAD_DIM)]

                def landing(slot, which=which):
                    return qg_all.at[which, lax.div(slot, heads), :, lanes(lax.rem(slot, heads), HEAD_DIM)]

                yield later(exchange(place, count, source, landing), 6)

        grad_one, qkv_all, out_proj_sum, attn_gains, ffn_gains = transfer(
            "scatter_grads",
            5,
            mesh,
            sixth_body,
            (
                grad_qkv,
                w_qkv.T,
                qkv_grad,
                strips.cut(out_proj_part),
                spread(attn_gain_part),
                spread(ffn_gain_part),
            ),
            (
                like((rows, width)),
                like((3, turns, deep, heads * HEAD_DIM)),
                like((out_rows, deep)),
                like((cores, count, 8, deep), f32),
                like((count, 8, deep), f32),
            ),
            scatter_scratch(heads, cores, rows, part, [(3 * HEAD_DIM, False)])
            + scatter_scratch(count, 1, out_rows, deep),
            semaphores=600,
            vmem=56 * 2**20,
        )

    xn_columns = lax.dynamic_slice_in_dim(xn_all, e * deep, deep, axis=1).astype(f32).reshape(count, rows, deep)
    router_grad = jnp.einsum("gtd,get->de", xn_columns, logits_all, precision=highest)
    grad_one = grad_one.astype(f32)
    rstd_one = lax.rsqrt(jnp.mean(inputs * inputs, axis=-1, keepdims=True) + eps)
    scaled_one = grad_one * attn_gain
    inner_one = jnp.mean(scaled_one * inputs, axis=-1, keepdims=True)
    input_grad = (
        grad_hidden + rstd_one * scaled_one - inputs * (rstd_one * rstd_one * rstd_one) * inner_one
    ).astype(bf16)

    def of_heads(which):
        return jnp.sum(qkv_all[which].astype(f32), axis=0)

    def of_shared(which):
        return shared_back[:, which * hidden_units : (which + 1) * hidden_units].reshape(-1, deep).astype(f32)

    return (
        output,
        input_grad,
        jnp.sum(attn_gains[:, :, 0, :], axis=(0, 1)) / gain_attn.astype(f32),
        of_heads(0),
        of_heads(1),
        of_heads(2),
        out_proj_sum.astype(f32),
        jnp.sum(ffn_gains[:, 0, :], axis=0),
        router_grad,
        gate_grad[None],
        up_grad[None],
        down_grad[None],
        of_shared(0).T,
        of_shared(1).T,
        of_shared(2),
    )


def solution(mesh):
    in_specs = (
        P("expert", None),
        P("expert", None),
        P("expert", None),
        P("expert"),
        P("expert", "tensor"),
        P("expert", "tensor"),
        P("expert", "tensor"),
        P("tensor", "expert"),
        P("expert"),
        P("expert", None),
        P("expert", None, "tensor"),
        P("expert", None, "tensor"),
        P("expert", "tensor", None),
        P("expert", "tensor"),
        P("expert", "tensor"),
        P("tensor", "expert"),
        P("expert", None),
    )
    out_specs = (
        P("expert", None),
        P("expert", None),
        P("expert"),
        P("expert", "tensor"),
        P("expert", "tensor"),
        P("expert", "tensor"),
        P("tensor", "expert"),
        P("expert"),
        P("expert", None),
        P("expert", None, "tensor"),
        P("expert", None, "tensor"),
        P("expert", "tensor", None),
        P("expert", "tensor"),
        P("expert", "tensor"),
        P("tensor", "expert"),
    )
    return jax.shard_map(
        functools.partial(local, mesh), mesh=mesh, in_specs=in_specs, out_specs=out_specs, check_vma=False
    )
```

```python
import functools

import jax
import jax.numpy as jnp
from jax import lax
from jax.experimental import pallas as pl
from jax.experimental.pallas import tpu as pltpu
from jax.sharding import PartitionSpec as P

HEAD_DIM = 128
TOP = 6
MESH = pl.DeviceIdType.MESH
ANY = pl.BlockSpec(memory_space=pl.ANY)

bf16 = jnp.bfloat16
f32 = jnp.float32
eps = 1e-06
highest = lax.Precision.HIGHEST
floor_score = -1e30


class Place:
    def __init__(self, sems, count, cores):
        self.sems, self.used = sems, 0
        self.count, self.cores = count, cores
        self.e = lax.axis_index("expert")
        self.t = lax.axis_index("tensor")
        self.quad = lax.rem(self.e, 4)
        self.far = lax.div(self.e, 4)

    def take(self, number):
        first = self.used
        self.used = first + number
        return first

    def ring(self, distance):
        return lax.rem(self.t + distance, self.cores)

    def copy(self, src, dst, out_sem, in_sem, e, t):
        return pltpu.make_async_remote_copy(
            src_ref=src,
            dst_ref=dst,
            send_sem=self.sems.at[out_sem],
            recv_sem=self.sems.at[in_sem],
            device_id={"expert": e, "tensor": t},
            device_id_type=MESH,
        )

    def send(self, src, dst, out_sem, in_sem, e, t):
        move = self.copy(src, dst, out_sem, in_sem, e, t)
        move.start()
        return move

    def arrived(self, landing, in_sem):
        self.copy(landing, landing, in_sem, in_sem, self.e, self.t).wait_recv()

    def keep(self, src, dst):
        move = pltpu.make_async_copy(src, dst, self.sems.at[self.take(1)])
        move.start()
        return move

    def local(self, src, dst, sem):
        return pltpu.make_async_copy(src, dst, self.sems.at[sem])

    def meet(self):
        barrier = pltpu.get_barrier_semaphore()
        for step in range(1, self.count):
            pl.semaphore_signal(
                barrier,
                inc=1,
                device_id={"expert": lax.rem(self.e + step, self.count), "tensor": self.t},
                device_id_type=MESH,
            )
        for step in range(1, self.cores):
            pl.semaphore_signal(
                barrier,
                inc=1,
                device_id={"expert": self.e, "tensor": self.ring(step)},
                device_id_type=MESH,
            )
        pl.semaphore_wait(barrier, self.count + self.cores - 2)


class Block:
    def __init__(self, place, members):
        self.place, self.deep = place, members // 4
        self.rank = lax.rem(place.far, self.deep)
        self.start = place.far - self.rank

    def flips(self, order):
        high, low = lax.div(self.place.quad, 2), lax.rem(self.place.quad, 2)
        one = high + (low - high) * order
        two = low + (high - low) * order
        return (2 - order) * (1 - 2 * one), (1 + order) * (1 - 2 * two)

    def slot(self, k, i, j, order):
        one, two = self.flips(order)
        return lax.rem(self.rank + k, self.deep) * 4 + self.place.quad + i * one + j * two

    def own(self):
        return self.rank * 4 + self.place.quad

    def device(self, slot):
        return self.start * 4 + slot


class Gather:
    def __init__(self, place, members, mine, whole, view, halves, pieces=1):
        self.place, self.block = place, Block(place, members)
        self.mine, self.whole, self.view, self.pieces = mine, whole, view, pieces
        self.deep, self.order = self.block.deep, lax.rem(place.t, 2)
        self.cores = place.cores if halves else 1
        self.zs, self.zr = self.lots(2), self.lots(1)
        self.s2, self.r2 = self.lots(1), self.lots(1)
        self.s3, self.r3 = self.lots(2), self.lots(2)
        self.s4, self.r4 = self.lots(4 * (self.cores - 1)), self.lots(4 * (self.cores - 1))
        self.sent, self.closing = [], False

    def lots(self, number):
        return self.place.take(number * self.deep * self.pieces)

    def near(self, n):
        rank, deep = self.block.rank, self.deep
        if isinstance(n, int) and n == 0:
            return rank
        low = jnp.minimum(rank, deep - 1 - rank)
        if isinstance(n, int):
            paired = rank - (n + 1) // 2 if n % 2 else rank + n // 2
        else:
            paired = rank + jnp.where(lax.rem(n, 2) == 1, -lax.div(n + 1, 2), lax.div(n, 2))
        single = jnp.where(rank < deep - 1 - rank, rank + (n - low), rank - (n - low))
        return jnp.where(n <= 2 * low, paired, single)

    def slot(self, n, i, j, order=None):
        one, two = self.block.flips(self.order if order is None else order)
        return self.near(n) * 4 + self.place.quad + i * one + j * two

    def index(self, n, kind, kinds, p):
        return (self.near(n) * kinds + kind) * self.pieces + p

    def pass_on(self, source, landing, out, into, at, e, t, condition=None):
        move = self.place.copy(source, landing, out + at[0], into + at[1], e, t)
        if self.closing:
            when(condition, move.wait_send)
            return
        self.sent.append((condition, move))
        when(condition, move.start)

    def along(self, n, p, source, landing):
        rank, e = self.block.rank, self.place.e
        near = self.near(n)
        for way in (1, -1):
            fits = rank < self.deep - 1 if way > 0 else rank >= 1
            if not isinstance(n, int) or n > 0:
                fits = jnp.logical_and(fits, near < rank if way > 0 else near > rank)
            out = self.index(n, 0 if way > 0 else 1, 2, p)
            into = self.index(n, 0, 1, p)
            self.pass_on(source, landing, self.zs, self.zr, (out, into), e + 4 * way, self.place.t, fits)

    def across(self, n, i, p, source, landing):
        one, two = self.block.flips(self.order)
        e, t = self.place.e, self.place.t
        if i == 0:
            at = self.index(n, 0, 1, p)
            self.pass_on(source, landing, self.s2, self.r2, (at, at), e + one, t)
        at = self.index(n, i, 2, p)
        self.pass_on(source, landing, self.s3, self.r3, (at, at), e + two, t)

    def share(self, n, i, j, p):
        ref = self.view(self.slot(n, i, j), self.place.t, p)
        for far in range(1, self.cores):
            kind = (far - 1) * 4 + i * 2 + j
            at = self.index(n, kind, 4 * (self.cores - 1), p)
            self.pass_on(ref, ref, self.s4, self.r4, (at, at), self.place.e, self.place.ring(far))

    def start(self, p):
        if p == 0:
            self.kept = self.place.keep(self.whole[0], self.whole[1](self.block.own()))
        source, landing = self.mine(p), self.view(self.block.own(), self.place.t, p)
        if self.deep > 1:
            self.along(0, p, source, landing)
        self.across(0, 0, p, source, landing)

    def from_line(self, n, p):
        ref = self.view(self.slot(n, 0, 0), self.place.t, p)
        self.place.arrived(ref, self.zr + self.index(n, 0, 1, p))
        if self.deep > 2:
            self.along(n, p, ref, ref)
        self.across(n, 0, p, ref, ref)
        self.share(n, 0, 0, p)

    def from_one(self, n, p):
        ref = self.view(self.slot(n, 1, 0), self.place.t, p)
        self.place.arrived(ref, self.r2 + self.index(n, 0, 1, p))
        self.across(n, 1, p, ref, ref)
        self.share(n, 1, 0, p)

    def from_two(self, n, i, p):
        ref = self.view(self.slot(n, i, 1), self.place.t, p)
        self.place.arrived(ref, self.r3 + self.index(n, i, 2, p))
        self.share(n, i, 1, p)

    def from_cores(self, n, i, j):
        if i + j == 0 and isinstance(n, int) and n == 0:
            return
        if i + j == 0 and not isinstance(n, int):
            pl.when(n > 0)(lambda: self.of_cores(n, i, j))
        else:
            self.of_cores(n, i, j)

    def of_cores(self, n, i, j):
        for far in range(1, self.cores):
            source = self.place.ring(self.cores - far)
            first, second = (j, i) if far % 2 else (i, j)
            kind = (far - 1) * 4 + first * 2 + second
            for p in range(self.pieces):
                ref = self.view(self.slot(n, i, j), source, p)
                self.place.arrived(ref, self.r4 + self.index(n, kind, 4 * (self.cores - 1), p))

    def finish(self):
        for condition, move in self.sent:
            when(condition, move.wait_send)

    def close(self):
        self.closing = True
        for p in range(self.pieces):
            source, landing = self.mine(p), self.view(self.block.own(), self.place.t, p)
            self.along(0, p, source, landing)
            self.across(0, 0, p, source, landing)
            for n in range(self.deep):
                if n > 0:
                    ref = self.view(self.slot(n, 0, 0), self.place.t, p)
                    self.along(n, p, ref, ref)
                    self.across(n, 0, p, ref, ref)
                    self.share(n, 0, 0, p)
                ref = self.view(self.slot(n, 1, 0), self.place.t, p)
                self.across(n, 1, p, ref, ref)
                self.share(n, 1, 0, p)
                self.share(n, 0, 1, p)
                self.share(n, 1, 1, p)

    def links(self):
        for p in range(self.pieces):
            self.start(p)
            yield
        for n in range(1, self.deep + 1):
            for p in range(self.pieces):
                self.from_one(n - 1, p)
                yield
                if n < self.deep:
                    self.from_line(n, p)
                    yield

    def last(self, n):
        for i in range(2):
            for p in range(self.pieces):
                self.from_two(n, i, p)

    def all(self):
        yield from self.links()
        for n in range(self.deep):
            self.last(n)
            yield
        for n in range(self.deep):
            for i in range(2):
                for j in range(2):
                    self.from_cores(n, i, j)
        self.finish()
        self.kept.wait()


def when(condition, action):
    if condition is None:
        action()
    else:
        pl.when(condition)(action)


def gather(place, members, mine, whole, view, halves, pieces=1):
    return Gather(place, members, mine, whole, view, halves, pieces).all()


class Kept:
    def __init__(self, left, right, rows):
        self.left, self.right, self.rows, self.slots = left, right, rows, {}

    def fetch(self, turn, slot):
        self.slots[turn] = pl.ds(pl.multiple_of(slot * self.rows, self.rows), self.rows)

    def ready(self, turn):
        pass

    def make(self, turn, core, target):
        columns = target.shape[1]
        wide = min(columns, 512)

        def body(tile, carry):
            source = pl.ds(pl.multiple_of(core * columns + tile * wide, wide), wide)
            into = pl.ds(pl.multiple_of(tile * wide, wide), wide)
            target[:, into] = dot(self.left[self.slots[turn], :], self.right[source, :], ((1,), (1,))).astype(bf16)
            return carry

        lax.fori_loop(0, columns // wide, body, 0)


def dot(left, right, sides=((1,), (0,)), precision=None):
    return lax.dot_general(left, right, (sides, ((), ())), precision=precision, preferred_element_type=f32)


def attend(tokens, gain, weights, first, cosine, sine, rooms, at, slot, rows):
    normed, qkv, probs, cosines, sines, out = rooms
    own = pl.ds(pl.multiple_of(slot * rows, rows), rows)

    def norm(piece_at, carry):
        for part in range(4):
            row = piece_at * 64 + part * 16
            values = tokens[pl.ds(pl.multiple_of(slot * rows + row, 16), 16), :].astype(f32)
            rstd = lax.rsqrt(jnp.mean(values * values, axis=1, keepdims=True) + eps)
            normed[at, pl.ds(pl.multiple_of(row, 16), 16), :] = (values * rstd * gain).astype(bf16)
        return carry

    lax.fori_loop(0, rows // 64, norm, 0)
    half = HEAD_DIM // 2
    lane = lax.broadcasted_iota(jnp.int32, (rows, HEAD_DIM), 1)
    sine = jnp.where(lane < half, -sine, sine)
    cosines[own, :] = cosine
    sines[own, :] = sine
    lin = dot(normed[at], weights[...])

    def turn(values):
        return (values * cosine + pltpu.roll(values, half, 1) * sine).astype(bf16)

    query, keyed = turn(lin[:, :HEAD_DIM]), turn(lin[:, HEAD_DIM : 2 * HEAD_DIM])
    valued = lin[:, 2 * HEAD_DIM :].astype(bf16)
    qkv[own, :HEAD_DIM] = query
    qkv[own, HEAD_DIM : 2 * HEAD_DIM] = keyed
    qkv[own, 2 * HEAD_DIM :] = valued
    key_at = lax.broadcasted_iota(jnp.int32, (rows, rows), 1).astype(f32)
    query_at = lax.broadcasted_iota(jnp.int32, (rows, rows), 0).astype(f32)
    allowed = (key_at <= query_at) & (key_at >= first[:, :1])
    scores = jnp.where(allowed, dot(query, keyed, ((1,), (1,))) * (HEAD_DIM ** (-0.5)), floor_score)
    raised = jnp.exp(scores - jnp.max(scores, axis=1, keepdims=True))
    chances = raised / jnp.sum(raised, axis=1, keepdims=True)
    probs[own, :] = chances
    out[slot] = dot(chances.astype(bf16), valued).astype(bf16)


def attend_back(rooms, slot, rows):
    qkv, probs, cosines, sines, grads, grad_qkv, turned = rooms
    own = pl.ds(pl.multiple_of(slot * rows, rows), rows)
    query = qkv[own, :HEAD_DIM]
    keyed = qkv[own, HEAD_DIM : 2 * HEAD_DIM]
    valued = qkv[own, 2 * HEAD_DIM :]
    cosine, sine = cosines[own, :], sines[own, :]
    chances, grad = probs[own, :], grads[slot]
    scale = HEAD_DIM ** (-0.5)

    def turn_back(values):
        return (values * cosine - pltpu.roll(values, HEAD_DIM // 2, 1) * sine).astype(bf16)

    grad_qkv[own, 2 * HEAD_DIM :] = dot(chances.astype(bf16), grad, ((0,), (0,))).astype(bf16)
    grad_chances = dot(grad, valued, ((1,), (1,)))
    weighted = jnp.sum(chances * grad_chances, axis=1, keepdims=True)
    grad_scores = (chances * (grad_chances - weighted)).astype(bf16)
    grad_qkv[own, :HEAD_DIM] = turn_back(dot(grad_scores, keyed) * scale)
    grad_qkv[own, HEAD_DIM : 2 * HEAD_DIM] = turn_back(dot(grad_scores, query, ((0,), (0,))) * scale)
    turned[:, own] = grad_qkv[own, :].T


def add_up(target, sources, rows, columns):
    step = max(16, min(rows, 16384 // columns // 16 * 16))

    def body(at, carry):
        piece = pl.ds(pl.multiple_of(at * step, step), step)
        total = sources[0][piece, :].astype(f32)
        for other in sources[1:]:
            total = total + other[piece, :].astype(f32)
        target[piece, :] = total.astype(target.dtype)
        return carry

    lax.fori_loop(0, rows // step, body, 0)


class Product:
    def __init__(self, place, left, varied, fixed, rooms, members, rows, columns):
        self.place, self.left, self.varied = place, left, varied
        self.lhs, self.rhs = rooms
        self.rows, self.columns = rows, columns
        self.lead = 0 if varied is None else varied.shape[0] // members
        self.waits, self.turn = {}, 0
        self.setup = []
        for buffer in range(self.rhs.shape[0]):
            self.setup.append(place.keep(fixed, self.rhs.at[buffer, pl.ds(self.lead, fixed.shape[0]), :]))

    def fetch(self, turn, slot):
        buffer = turn % 2
        rows = pl.ds(pl.multiple_of(slot * self.rows, self.rows), self.rows)
        moves = [self.place.keep(self.left.at[rows, :], self.lhs.at[buffer])]
        if self.lead:
            lead = pl.ds(pl.multiple_of(slot * self.lead, self.lead), self.lead)
            moves.append(self.place.keep(self.varied.at[lead, :], self.rhs.at[buffer, pl.ds(0, self.lead), :]))
        self.waits[turn] = moves

    def ready(self, turn):
        for move in self.setup:
            move.wait()
        self.setup = []
        for move in self.waits.pop(turn):
            move.wait()

    def make(self, turn, core, target):
        buffer = turn % 2
        right = self.rhs.at[buffer if self.lead else 0]
        wide = min(self.columns, 512)

        def body(at, carry):
            source = pl.ds(pl.multiple_of(core * self.columns + at * wide, wide), wide)
            into = pl.ds(pl.multiple_of(at * wide, wide), wide)
            target[:, into] = jnp.dot(
                self.lhs[buffer], right[:, source], preferred_element_type=f32
            ).astype(bf16)
            return carry

        lax.fori_loop(0, self.columns // wide, body, 0)


def scatter(place, members, sources, room, views, shape, halves, credit=None):
    block = Block(place, members)
    deep, e, t = block.deep, place.e, place.t
    rows, columns = shape
    order = 1 - lax.rem(t, 2)
    cores = place.cores if halves else 1
    count = len(sources)
    mine, outgoing, land0, land1s, land2s, land3s, finals = room
    s0, r0 = place.take(4 * deep * cores * count), place.take(4 * deep * cores * count)
    s1, r1 = place.take(2 * deep * count), place.take(2 * deep * count)
    s2, r2 = place.take(deep * count), place.take(deep * count)
    s3, r3 = place.take(deep * count), place.take(deep * count)
    s4, r4 = place.take(cores * count), place.take(cores * count)
    walk = [(f, k) for f in range(count) for k in list(range(1, deep)) + [0]]
    one, two = block.flips(order)
    sent, loads, last, kept = [], {}, {}, []
    quads = [(1, 1), (1, 0), (0, 1), (0, 0)]
    turns = [(f, k, i, j) for f, k in walk for i, j in quads]
    ring = outgoing.shape[0]
    leaving = []

    def slot_of(k, i, j):
        return block.slot(k, i, j, order)

    def land_index(d, k, i, j):
        return (d - 1) * deep * 4 + k * 4 + i * 2 + j

    def produce(number):
        f, k, i, j = turns[number]
        source = sources[f]
        if (k, i, j) in last:
            last.pop((k, i, j)).wait_send()
        if not isinstance(source, (Product, Kept)):
            loads[f, k, i, j] = place.keep(source(slot_of(k, i, j)), mine.at[slot_of(k, i, j)])
            return
        local_number = number - f * 4 * deep
        if local_number == 0:
            source.fetch(0, slot_of(k, i, j))
        source.ready(local_number)
        if local_number + 1 < 4 * deep:
            source.fetch(local_number + 1, slot_of(*turns[number + 1][1:]))
        if number >= ring:
            for move in leaving[number - ring]:
                move.wait_send()
        moves = []
        for d in range(1, cores):
            target = place.ring(d)
            buffer = outgoing.at[number % ring, d - 1]
            source.make(local_number, target, buffer)
            at = land_index(d, k, *((j, i) if d % 2 else (i, j)))
            if f > 0:
                pl.semaphore_wait(credit.at[at], 1)
            sem = f * 4 * deep * cores + at
            moves.append(place.send(buffer, land0.at[at], s0 + sem, r0 + sem, e, target))
        leaving.append(moves)
        source.make(local_number, t, mine.at[slot_of(k, i, j)])

    def terms_of(f, k, i, j):
        if (f, k, i, j) in loads:
            loads[f, k, i, j].wait()
        terms = [mine.at[slot_of(k, i, j)]]
        for d in range(1, cores):
            at = land_index(d, k, i, j)
            place.arrived(land0.at[at], r0 + f * 4 * deep * cores + at)
            terms.append(land0.at[at])
        if i == 0:
            at = (f * deep + k) * 2 + j
            place.arrived(land1s.at[at], r1 + at)
            terms.append(land1s.at[at])
            if j == 0:
                at = f * deep + k
                place.arrived(land2s.at[at], r2 + at)
                terms.append(land2s.at[at])
        return terms

    def give_back(f, k, i, j):
        if f + 1 < count:
            for d in range(1, cores):
                pl.semaphore_signal(
                    credit.at[land_index(d, k, i, j)],
                    inc=1,
                    device_id={"expert": e, "tensor": place.ring(cores - d)},
                    device_id_type=MESH,
                )

    def leave(f, k, i, j, landing, out, into, at, target):
        move = place.send(mine.at[slot_of(k, i, j)], landing.at[at], out + at, into + at, target, t)
        last[k, i, j] = move

    def first_flip(f, k, j):
        terms, ref = terms_of(f, k, 1, j), mine.at[slot_of(k, 1, j)]
        if len(terms) > 1:
            add_up(ref, terms, rows, columns)
        give_back(f, k, 1, j)
        leave(f, k, 1, j, land1s, s1, r1, (f * deep + k) * 2 + j, e + one)

    def second_flip(f, k):
        add_up(mine.at[slot_of(k, 0, 1)], terms_of(f, k, 0, 1), rows, columns)
        give_back(f, k, 0, 1)
        leave(f, k, 0, 1, land2s, s2, r2, f * deep + k, e + two)

    def line(f, k):
        terms, ref = terms_of(f, k, 0, 0), mine.at[slot_of(k, 0, 0)]
        if k > 0:
            add_up(ref, terms, rows, columns)
            give_back(f, k, 0, 0)
            peer = block.device(lax.rem(block.rank + k, deep) * 4 + place.quad)
            leave(f, k, 0, 0, land3s, s3, r3, f * deep + k, peer)
            return
        for far in range(1, deep):
            place.arrived(land3s.at[f * deep + far], r3 + f * deep + far)
            terms.append(land3s.at[f * deep + far])
        final = finals.at[f]
        add_up(final, terms, rows, columns)
        give_back(f, k, 0, 0)
        kept.append(place.keep(final, views[f](t)))
        for d in range(1, cores):
            at = f * cores + d
            sent.append(place.send(final, views[f](t), s4 + at, r4 + at, e, place.ring(d)))

    for step in range(len(walk) + 2):
        fresh = step < len(walk)
        if fresh:
            produce(4 * step)
            yield
            produce(4 * step + 1)
            yield
            first_flip(*walk[step], 1)
            yield
            produce(4 * step + 2)
            yield
        if 0 <= step - 1 < len(walk):
            second_flip(*walk[step - 1])
            yield
        if fresh:
            produce(4 * step + 3)
            yield
            first_flip(*walk[step], 0)
            yield
        if 0 <= step - 2 < len(walk):
            line(*walk[step - 2])
            yield
    for f in range(count):
        for d in range(1, cores):
            place.arrived(views[f](place.ring(cores - d)), r4 + f * cores + d)
    for moves in leaving[-ring:]:
        for move in moves:
            move.wait_send()
    for move in list(last.values()) + sent:
        move.wait_send()
    for move in kept:
        move.wait()


def scatter_scratch(members, cores, rows, columns, products=(), ring=4):
    deep = members // 4
    count = max(1, len(products))
    short = rows if cores > 1 else 16
    rooms = [
        pltpu.VMEM((members, rows, columns), bf16),
        pltpu.VMEM((ring, max(1, cores - 1), short, columns), bf16),
        pltpu.VMEM((max(1, (cores - 1) * members), short, columns), bf16),
        pltpu.VMEM((2 * deep * count, rows, columns), bf16),
        pltpu.VMEM((deep * count, rows, columns), bf16),
        pltpu.VMEM((deep * count, rows, columns), bf16),
        pltpu.VMEM((count, rows, columns), bf16),
    ]
    for depth, varied in products:
        rooms.append(pltpu.VMEM((2, rows, depth), bf16))
        rooms.append(pltpu.VMEM((2 if varied else 1, depth, columns * cores), bf16))
    return rooms


def exchange(place, members, source, landing):
    e, t = place.e, place.t
    own = lax.rem(e, members)
    base = e - own
    sends, arrivals = place.take(members), place.take(members)
    sent = []
    for d in range(1, members):
        target = lax.rem(own + d, members)
        sent.append(place.send(source(target), landing(own), sends + d, arrivals + d, base + target, t))
    kept = place.keep(source(own), landing(own))
    yield
    for d in range(1, members):
        place.arrived(landing(lax.rem(own + members - d, members)), arrivals + d)
    for move in sent:
        move.wait_send()
    kept.wait()


def start_exchange(place, members, source, landing):
    e, t = place.e, place.t
    own = lax.rem(e, members)
    base = e - own
    sends, arrivals = place.take(members), place.take(members)
    sent = []
    for d in range(1, members):
        target = lax.rem(own + d, members)
        sent.append(place.send(source(target), landing(own), sends + target, arrivals + own, base + target, t))
    place.keep(source(own), landing(own)).wait()

    def arrived(slot):
        pl.when(slot != own)(lambda: place.arrived(landing(slot), arrivals + slot))

    def finish():
        for move in sent:
            move.wait_send()

    return arrived, finish


def both(place, members, source, landing, part):
    yield from exchange(place, members, source, lambda slot: landing(place.t, slot))
    sends, arrivals = place.take(place.cores), place.take(place.cores)
    sent = []
    for d in range(1, place.cores):
        mine = part(place.t)
        sent.append(place.send(mine, mine, sends + d, arrivals + d, place.e, place.ring(d)))
    yield
    for d in range(1, place.cores):
        place.arrived(part(place.ring(place.cores - d)), arrivals + d)
    for move in sent:
        move.wait_send()


def twice(task):
    for _ in task:
        next(task, None)
        yield


def later(task, rounds):
    for _ in range(rounds):
        yield
    yield from task


def run(tasks):
    while tasks:
        for task in list(tasks):
            try:
                next(task)
            except StopIteration:
                tasks.remove(task)


def transfer(name, number, mesh, body, ins, outs, scratch=(), semaphores=400, vmem=None):
    count, cores = mesh.shape["expert"], mesh.shape["tensor"]
    semaphores = semaphores * max(1, count * cores // 32)

    def kernel(*refs):
        given = refs[: len(ins)]
        made = refs[len(ins) : len(ins) + len(outs)]
        room = refs[len(ins) + len(outs) : -1]
        place = Place(refs[-1], count, cores)
        place.meet()
        tasks = []
        for task in body(place, given, made, room):
            if isinstance(task, list):
                run(task)
            else:
                tasks.append(task)
        run(tasks)
        assert place.used <= semaphores, place.used

    size = sum(x.size * x.dtype.itemsize for x in list(ins) + list(outs))
    return pl.pallas_call(
        kernel,
        name=name,
        out_shape=[jax.ShapeDtypeStruct(shape, dtype) for shape, dtype in outs_of(outs)],
        in_specs=[ANY] * len(ins),
        out_specs=[ANY] * len(outs),
        scratch_shapes=list(scratch) + [pltpu.SemaphoreType.DMA((semaphores,))],
        cost_estimate=pl.CostEstimate(flops=0, bytes_accessed=size, transcendentals=0),
        compiler_params=pltpu.CompilerParams(
            collective_id=number, has_side_effects=True, vmem_limit_bytes=vmem
        ),
    )(*ins)


def outs_of(outs):
    return [(x.shape, x.dtype) for x in outs]


def like(shape, dtype=bf16):
    return jax.ShapeDtypeStruct(shape, dtype)


def part_view(ref, rows, columns, pieces=1):
    height = rows // pieces

    def view(slot, core, piece=0):
        at = 0 if isinstance(slot, int) else pl.multiple_of(slot * rows, rows)
        return ref.at[
            pl.ds(at + piece * height, height), pl.ds(pl.multiple_of(core * columns, columns), columns)
        ]

    return view


PIECES = 2


def lanes(at, columns):
    return pl.ds(pl.multiple_of(at * columns, columns), columns)


class Strips:
    def __init__(self, count, columns):
        self.count, self.columns = count, columns
        self.direct = columns % 128 == 0

    def shape(self, rows):
        return (rows, self.count * self.columns) if self.direct else (self.count, rows, self.columns)

    def at(self, ref, slot):
        return ref.at[:, lanes(slot, self.columns)] if self.direct else ref.at[slot]

    def cut(self, array):
        rows = array.shape[0]
        return array if self.direct else array.reshape(rows, self.count, self.columns).transpose(1, 0, 2)

    def join(self, array):
        rows = array.shape[0 if self.direct else 1]
        return array if self.direct else array.transpose(1, 0, 2).reshape(rows, self.count * self.columns)


def row_gather(place, members, source, landing, rows, part):
    def mine(piece):
        height = rows // PIECES
        return source.at[pl.ds(piece * height, height), lanes(place.t, part)]

    whole = (source, lambda slot: landing.at[pl.ds(pl.multiple_of(slot * rows, rows), rows), :])
    return Gather(place, members, mine, whole, part_view(landing, rows, part, PIECES), True, PIECES)


def rotary(values, cosine, sine):
    half = values.shape[-1] // 2
    first = values[..., :half]
    second = values[..., half:]
    return jnp.concatenate([first * cosine - second * sine, second * cosine + first * sine], axis=-1)


def rotary_back(grads, cosine, sine):
    half = grads.shape[-1] // 2
    first = grads[..., :half]
    second = grads[..., half:]
    return jnp.concatenate([first * cosine + second * sine, second * cosine - first * sine], axis=-1)


def sequence_tables(lengths_rows, tok_rows):
    ends = jnp.cumsum(lengths_rows, axis=1)
    starts = ends - lengths_rows
    places = jnp.arange(tok_rows, dtype=jnp.int32)
    segment = jnp.sum((places[None, :, None] >= ends[:, None, :]).astype(jnp.int32), axis=2)
    member = segment[:, :, None] == jnp.arange(lengths_rows.shape[1], dtype=jnp.int32)[None, None, :]
    first = jnp.sum(jnp.where(member, starts[:, None, :], 0), axis=2)
    return segment, places[None, :] - first


def silu_parts(values):
    sigmoid_value = jax.nn.sigmoid(values)
    return values * sigmoid_value, sigmoid_value * (1.0 + values * (1.0 - sigmoid_value))


def mm(form, left, right):
    return jnp.einsum(form, left, right, preferred_element_type=f32)


def up_to(value, step):
    return -(-value // step) * step


def second_norm(place, cores, rows, given, hid_out, room):
    ap, tok, gn, rt, mk = given
    parts, tok_v, gn_v, rt_v, mk_v, hid, xn, _ = room
    t = place.t
    sends, arrivals = place.take(cores), place.take(cores)
    sent = [place.send(ap, parts.at[t], sends + d, arrivals + d, place.e, place.ring(d)) for d in range(1, cores)]
    kept = [place.keep(ap, parts.at[t])]
    kept += [place.keep(a, b) for a, b in ((tok, tok_v), (gn, gn_v), (rt, rt_v), (mk, mk_v))]
    for move in kept:
        move.wait()
    for d in range(1, cores):
        place.arrived(parts.at[place.ring(cores - d)], arrivals + d)

    def body(at, carry):
        for step in range(4):
            piece = pl.ds(pl.multiple_of(at * 64 + step * 16, 16), 16)
            total = parts[0, piece, :].astype(f32)
            for core in range(1, cores):
                total = total + parts[core, piece, :].astype(f32)
            values = tok_v[piece, :].astype(f32) + total
            hid[piece, :] = values
            rstd = lax.rsqrt(jnp.mean(values * values, axis=1, keepdims=True) + eps)
            xn[piece, :] = (values * rstd * gn_v[...]).astype(bf16)
        return carry

    lax.fori_loop(0, rows // 64, body, 0)
    saved = place.keep(hid, hid_out)
    return sent, saved


def route(room):
    _, _, _, rt_v, mk_v, _, xn, gt = room
    logits = lax.dot_general(rt_v[...], xn[...], (((1,), (1,)), ((), ())), preferred_element_type=f32)
    picked = mk_v[...] > 0.5
    top_logit = jnp.max(jnp.where(picked, logits, floor_score), axis=0, keepdims=True)
    lifted = jnp.where(picked, jnp.exp(jnp.where(picked, logits - top_logit, 0.0)), 0.0)
    gt[...] = lifted / jnp.sum(lifted, axis=0, keepdims=True)


class Out:
    def __init__(self, place, buffer, array, unit):
        self.place, self.buffer, self.array, self.unit = place, buffer, array, unit
        self.sem = place.take(2)

    def moves(self, slots):
        for at, slot in enumerate(slots):
            if self.unit is None:
                yield self.place.local(self.buffer.at[at], self.array.at[slot], self.sem + at)
            else:
                into = pl.ds(pl.multiple_of(slot * self.unit, self.unit), self.unit)
                source = self.buffer.at[pl.ds(at * self.unit, self.unit), :]
                yield self.place.local(source, self.array.at[into, :], self.sem + at)

    def go(self, slots):
        for move in self.moves(slots):
            move.start()

    def free(self, condition=None):
        for move in self.moves((jnp.int32(0), jnp.int32(0))):
            when(condition, move.wait)


def experts_pair(slots, used, capacity, rows, rows_in, grads_in, position, gate_of, weights, outs):
    wg, wu, wd, sh_in, sh_down = weights
    received, gated, low, back, acts, gate_backs, up_backs, dots_out, left_forward, left_backward = outs
    wide = sh_down.shape[0]
    places = lax.broadcasted_iota(jnp.int32, (capacity, rows), 0).astype(f32)
    gates, onehots = [], []
    for out in (received, gated, low, left_forward, left_backward):
        out.free(used)
    for at, slot in enumerate(slots):
        token, own = pl.ds(pl.multiple_of(slot * rows, rows), rows), pl.ds(at * capacity, capacity)
        mine = pl.ds(at * rows, rows)
        chosen = (position[slot] == places).astype(f32)
        onehot = chosen.astype(bf16)
        onehots.append(chosen)
        received.buffer[own, :] = dot(onehot, rows_in[token, :]).astype(bf16)
        gate = jnp.sum(chosen * gate_of(slot), axis=1, keepdims=True)
        row_grads = dot(onehot, grads_in[mine, :])
        gated.buffer[own, :] = (gate * row_grads).astype(bf16)
        low.buffer[own, :] = row_grads.astype(bf16)
        gates.append(gate)
        turned = chosen.T.astype(bf16)
        left_forward.buffer[mine, :capacity] = turned
        left_backward.buffer[mine, :capacity] = turned
    received.go(slots)
    gated.go(slots)
    gate = jnp.concatenate(gates, axis=0)
    rows_now = received.buffer[...]
    exp_gate = dot(rows_now, wg[...], ((1,), (1,)))
    exp_up = dot(rows_now, wu[...], ((1,), (1,)))
    silu, slope = silu_parts(exp_gate)
    act = (silu * exp_up).astype(bf16)
    acts.free(used)
    acts.buffer[...] = act
    acts.go(slots)
    out = dot(act, wd[...])
    dots = jnp.sum(low.buffer[...].astype(f32) * out, axis=1, keepdims=True)
    low.buffer[...] = (gate * out).astype(bf16)
    low.go(slots)
    dots_out.free(used)
    for at in range(2):
        column = dots[at * capacity : (at + 1) * capacity]
        token_dots = jnp.sum(onehots[at] * column, axis=0, keepdims=True)
        dots_out.buffer[at] = jnp.broadcast_to(token_dots, (8, rows))
    dots_out.go(slots)
    act_grad = dot(gated.buffer[...], wd[...], ((1,), (1,)))
    gate_back = (act_grad * exp_up * slope).astype(bf16)
    up_back = (act_grad * silu).astype(bf16)
    gate_backs.free(used)
    up_backs.free(used)
    gate_backs.buffer[...] = gate_back
    up_backs.buffer[...] = up_back
    gate_backs.go(slots)
    up_backs.go(slots)
    back.free(used)
    back.buffer[...] = (dot(gate_back, wg[...]) + dot(up_back, wu[...])).astype(bf16)
    back.go(slots)
    for at, slot in enumerate(slots):
        token, mine = pl.ds(pl.multiple_of(slot * rows, rows), rows), pl.ds(at * rows, rows)
        both_sides = dot(rows_in[token, :], sh_in[...], ((1,), (1,)))
        sh_gate, sh_up = both_sides[:, :wide], both_sides[:, wide:]
        sh_silu, sh_slope = silu_parts(sh_gate)
        left_forward.buffer[mine, capacity:] = (sh_silu * sh_up).astype(bf16)
        sh_grad = dot(grads_in[mine, :], sh_down[...], ((1,), (1,)))
        left_backward.buffer[mine, capacity : capacity + wide] = (sh_grad * sh_up * sh_slope).astype(bf16)
        left_backward.buffer[mine, capacity + wide :] = (sh_grad * sh_silu).astype(bf16)
    left_forward.go(slots)
    left_backward.go(slots)


def experts_kernel(
    groups,
    capacity,
    rows,
    xn_ref,
    grad_ref,
    position_ref,
    gate_ref,
    wg_ref,
    wu_ref,
    wd_ref,
    sh_in_ref,
    sh_down_ref,
    received_ref,
    gated_ref,
    low_ref,
    back_ref,
    act_ref,
    gate_back_ref,
    up_back_ref,
    dots_ref,
    left_forward_ref,
    left_backward_ref,
):
    places = lax.broadcasted_iota(jnp.int32, (capacity, rows), 0).astype(f32)
    gates, grads, onehots = [], [], []
    for g in range(groups):
        token = pl.ds(g * rows, rows)
        slot = pl.ds(g * capacity, capacity)
        chosen = (position_ref[g] == places).astype(f32)
        onehot = chosen.astype(bf16)
        onehots.append(chosen)
        received_ref[slot, :] = dot(onehot, xn_ref[token, :]).astype(bf16)
        gate = jnp.sum(chosen * gate_ref[g], axis=1, keepdims=True)
        row_grads = dot(onehot, grad_ref[token, :])
        gated_ref[slot, :] = (gate * row_grads).astype(bf16)
        low_ref[slot, :] = row_grads.astype(bf16)
        gates.append(gate)
        turned = chosen.T.astype(bf16)
        left_forward_ref[token, :capacity] = turned
        left_backward_ref[token, :capacity] = turned
    gate = jnp.concatenate(gates, axis=0)
    received = received_ref[...]
    exp_gate = dot(received, wg_ref[...], ((1,), (1,)))
    exp_up = dot(received, wu_ref[...], ((1,), (1,)))
    silu, slope = silu_parts(exp_gate)
    act = (silu * exp_up).astype(bf16)
    act_ref[...] = act
    out = dot(act, wd_ref[...])
    dots = jnp.sum(low_ref[...].astype(f32) * out, axis=1, keepdims=True)
    low_ref[...] = (gate * out).astype(bf16)
    for g in range(groups):
        column = dots[g * capacity : (g + 1) * capacity]
        token_dots = jnp.sum(onehots[g] * column, axis=0, keepdims=True)
        dots_ref[g] = jnp.broadcast_to(token_dots, (8, rows))
    act_grad = dot(gated_ref[...], wd_ref[...], ((1,), (1,)))
    gate_back = (act_grad * exp_up * slope).astype(bf16)
    up_back = (act_grad * silu).astype(bf16)
    gate_back_ref[...] = gate_back
    up_back_ref[...] = up_back
    back_ref[...] = (
        dot(gate_back, wg_ref[...]) + dot(up_back, wu_ref[...])
    ).astype(bf16)
    wide = sh_down_ref.shape[0]
    both = dot(xn_ref[...], sh_in_ref[...], ((1,), (1,)))
    sh_gate, sh_up = both[:, :wide], both[:, wide:]
    sh_silu, sh_slope = silu_parts(sh_gate)
    left_forward_ref[:, capacity:] = (sh_silu * sh_up).astype(bf16)
    sh_grad = dot(grad_ref[...], sh_down_ref[...], ((1,), (1,)))
    left_backward_ref[:, capacity : capacity + wide] = (sh_grad * sh_up * sh_slope).astype(bf16)
    left_backward_ref[:, capacity + wide :] = (sh_grad * sh_silu).astype(bf16)


def experts_pass(count, capacity, rows, xn_all, grad_all, position, gate, wg, wu, wd, sh_in, sh_down):
    groups = 2
    units, width = wg.shape
    wide = sh_down.shape[0]

    def along(*shape):
        return pl.BlockSpec(shape, lambda i: (i,) + (0,) * (len(shape) - 1))

    def whole(array):
        return pl.BlockSpec(array.shape, lambda i: (0,) * array.ndim, pipeline_mode=pl.Buffered(1))

    slots = groups * capacity
    tokens = groups * rows
    flops = 2 * count * capacity * width * units * 6
    return pl.pallas_call(
        functools.partial(experts_kernel, groups, capacity, rows),
        name="experts_pass",
        grid=(count // groups,),
        in_specs=[
            along(tokens, width),
            along(tokens, width),
            along(groups, 1, rows),
            along(groups, 1, rows),
            whole(wg),
            whole(wu),
            whole(wd),
            whole(sh_in),
            whole(sh_down),
        ],
        out_specs=[
            along(slots, width),
            along(slots, width),
            along(slots, width),
            along(slots, width),
            along(slots, units),
            along(slots, units),
            along(slots, units),
            along(groups, 8, rows),
            along(tokens, capacity + wide),
            along(tokens, capacity + 2 * wide),
        ],
        out_shape=[like((count * capacity, width))] * 4
        + [like((count * capacity, units))] * 3
        + [
            like((count, 8, rows), f32),
            like((count * rows, capacity + wide)),
            like((count * rows, capacity + 2 * wide)),
        ],
        cost_estimate=pl.CostEstimate(
            flops=flops, bytes_accessed=4 * count * (rows + 2 * capacity) * width, transcendentals=0
        ),
        compiler_params=pltpu.CompilerParams(vmem_limit_bytes=58 * 2**20),
    )(xn_all, grad_all, position, gate, wg, wu, wd, sh_in, sh_down)


def local(
    mesh,
    tokens,
    lengths,
    routes,
    gain_attn,
    w_query,
    w_key,
    w_value,
    w_out,
    gain_ffn,
    w_router,
    routed_gate_weight,
    routed_up_weight,
    w_down,
    w_shared_gate,
    w_shared_up,
    w_shared_down,
    out_grad,
):
    count, cores = mesh.shape["expert"], mesh.shape["tensor"]
    rows, width = tokens.shape
    part = width // cores
    deep = w_query.shape[0]
    experts = w_router.shape[1]
    heads = w_query.shape[1] // HEAD_DIM
    capacity = up_to(min(rows, rows * TOP * 4 // (3 * count)), 128)
    hidden_units = w_shared_gate.shape[1] // count
    scale = HEAD_DIM ** (-0.5)
    e = lax.axis_index("expert")
    t = lax.axis_index("tensor")
    chunk = heads * rows
    strips = Strips(count, deep)

    expert_ids = jnp.arange(experts, dtype=jnp.int32)
    choose = jnp.any(routes[:, :, None] == expert_ids[None, None, :], axis=1)
    mask_t = choose.T.astype(bf16)
    vectors = jnp.concatenate(
        [
            w_router.T,
            gain_attn[None],
            gain_ffn[None],
            jnp.pad(lengths.astype(bf16), ((0, 0), (0, deep - lengths.shape[1]))),
        ],
        axis=0,
    )
    head_rows = up_to(vectors.shape[0], 16)
    vectors = jnp.pad(vectors, ((0, head_rows - vectors.shape[0]), (0, 0)))
    pieces = rows // deep
    mask_rows = mask_t.reshape(experts * pieces, deep)
    small = jnp.concatenate([vectors, mask_rows], axis=0)
    small_rows = up_to(small.shape[0], 16)
    small = jnp.pad(small, ((0, small_rows - small.shape[0]), (0, 0)))

    def unpack(gathered):
        router = gathered[:experts]
        attn_gain, ffn_gain = gathered[experts].astype(f32), gathered[experts + 1].astype(f32)
        rows_of = gathered[experts + 2].reshape(count, deep)[:, : lengths.shape[1]].astype(f32).astype(jnp.int32)
        masks = gathered[head_rows : head_rows + experts * pieces].reshape(experts, pieces, count, deep)
        return router, attn_gain, ffn_gain, rows_of, masks.transpose(2, 0, 1, 3).reshape(count, experts, rows)

    shared_pack = jnp.concatenate(
        [
            w_shared_gate.T.reshape(count, hidden_units, deep),
            w_shared_up.T.reshape(count, hidden_units, deep),
            w_shared_down.reshape(count, hidden_units, deep),
        ],
        axis=1,
    )
    pack_rows = up_to(3 * hidden_units, 16)
    shared_pack = jnp.pad(shared_pack, ((0, 0), (0, pack_rows - 3 * hidden_units), (0, 0)))
    out_rows = w_out.shape[0]

    if strips.direct:

        def front_body(place, given, made, room):
            tok, sm, wq, wk, wv, og, wo, sp, inv, cos_in, sin_in = given
            sm_all, w_all, xn_all, qkv_all, pr_all, ct_all, st_all, ho_all, og_all, wo_all, sp_all = made
            sm_v, tok_v, w_v, normed, qkv, probs, cosines, sines, out, inverse, cos_v, sin_v = room
            own = lax.rem(place.e, heads)
            base = place.e - own
            ready = [place.keep(x, y) for x, y in ((inv, inverse), (cos_in, cos_v), (sin_in, sin_v))]
            small_in, small_out = start_exchange(place, count, lambda s: sm, lambda s: sm_v.at[:, lanes(s, deep)])
            tokens_in = row_gather(place, heads, tok, tok_v, rows, part)
            sends, arrivals = place.take(heads), place.take(heads)

            def wo_view(slot, core=0, piece=0):
                return strips.at(wo_all, slot)

            def attention():
                links = tokens_in.links()
                for _ in range(PIECES):
                    next(links)
                pulls = []
                for which, weight in enumerate((wq, wk, wv)):

                    def landing(slot, which=which):
                        at = pl.ds(pl.multiple_of(slot * deep, deep), deep)
                        return w_v.at[at, pl.ds(which * HEAD_DIM, HEAD_DIM)]

                    pulls.append(
                        start_exchange(
                            place, count, lambda s, w=weight: w.at[:, lanes(lax.rem(s, heads), HEAD_DIM)], landing
                        )
                    )
                yield
                yield from links
                for d in range(1, count):
                    slot = lax.rem(place.e + d, count)
                    for arrived in [small_in] + [pull[0] for pull in pulls]:
                        arrived(slot)
                for move in ready:
                    move.wait()
                saved = [place.keep(sm_v, sm_all), place.keep(w_v, w_all)]
                head = experts - experts % 16
                vectors = sm_v[pl.ds(head, 16), :].astype(f32)
                gain = vectors[experts - head : experts - head + 1, :]
                position = lax.broadcasted_iota(jnp.int32, (rows, HEAD_DIM), 0).astype(f32)
                gave, stored = [], []

                def group(n, i, j):
                    tokens_in.from_cores(n, i, j)
                    slot = tokens_in.slot(n, i, j)
                    at = len(stored) % 2
                    if len(stored) >= 2:
                        stored[-2].wait()
                    row = sm_v[pl.ds(head, 16), lanes(tokens_in.block.device(slot), deep)].astype(f32)
                    row = row[experts + 2 - head : experts + 3 - head, :]
                    sequences = lengths.shape[1]
                    ends, end = [], jnp.zeros((1, 1), f32)
                    for place_in in range(sequences - 1):
                        end = end + row[:, place_in : place_in + 1]
                        ends.append(end)
                    line = lax.broadcasted_iota(jnp.int32, (up_to(sequences, 8), HEAD_DIM), 0)
                    starts = jnp.zeros(line.shape, f32)
                    for which, end in enumerate(ends):
                        starts = jnp.where(line == which, end, starts)
                    angles = starts * inverse[...]
                    cos_starts, sin_starts = jnp.cos(angles), jnp.sin(angles)
                    first = jnp.zeros((rows, HEAD_DIM), f32)
                    cos_first, sin_first = jnp.ones((rows, HEAD_DIM), f32), jnp.zeros((rows, HEAD_DIM), f32)
                    for which, end in enumerate(ends):
                        after = position >= end
                        first = jnp.where(after, end, first)
                        cos_first = jnp.where(after, cos_starts[which : which + 1, :], cos_first)
                        sin_first = jnp.where(after, sin_starts[which : which + 1, :], sin_first)
                    cosine = cos_v[...] * cos_first + sin_v[...] * sin_first
                    sine = sin_v[...] * cos_first - cos_v[...] * sin_first
                    attend(
                        tok_v,
                        gain,
                        w_v,
                        first,
                        cosine,
                        sine,
                        (normed, qkv, probs, cosines, sines, out),
                        at,
                        slot,
                        rows,
                    )
                    stored.append(
                        place.keep(
                            normed.at[at], xn_all.at[pl.ds(pl.multiple_of(slot * rows, rows), rows), :]
                        )
                    )
                    landing = ho_all.at[:, lanes(own, HEAD_DIM)]
                    if n + i + j == 0:
                        saved.append(place.keep(out.at[slot], landing))
                    else:
                        gave.append(
                            place.send(out.at[slot], landing, sends + slot, arrivals + own, base + slot, place.t)
                        )

                for n in range(tokens_in.deep):
                    if n == 0:
                        tokens_in.kept.wait()
                    group(n, 0, 0)
                    yield
                for n in range(tokens_in.deep):
                    tokens_in.last(n)
                    for i, j in ((1, 0), (0, 1), (1, 1)):
                        group(n, i, j)
                        yield
                for source, target in ((qkv, qkv_all), (probs, pr_all), (cosines, ct_all), (sines, st_all)):
                    saved.append(place.keep(source, target))
                yield
                for d in range(1, heads):
                    slot = lax.rem(own + d, heads)
                    place.arrived(ho_all.at[:, lanes(slot, HEAD_DIM)], arrivals + slot)
                for move in gave:
                    move.wait_send()
                for move in stored[-2:] + saved:
                    move.wait()
                for pull in pulls:
                    pull[1]()
                small_out()
                tokens_in.finish()

            yield attention()
            yield later(row_gather(place, count, og, og_all, rows, part).all(), 3)
            yield later(gather(place, count, lambda p: wo, (wo, wo_view), wo_view, False), 3)
            yield later(exchange(place, count, lambda s: sp.at[s], lambda s: strips.at(sp_all, s)), 6)

        half = HEAD_DIM // 2
        inverse = 10000.0 ** (-2.0 * jnp.arange(half, dtype=f32) / HEAD_DIM)
        inverse = jnp.concatenate([inverse, inverse])[None]
        row_angles = jnp.arange(rows, dtype=f32)[:, None] * inverse
        (
            small_all,
            w_qkv,
            xn_chunk,
            qkv_saved,
            probs_saved,
            cosine_wide,
            sine_wide,
            heads_out,
            grad_all,
            out_full,
            shared_all,
        ) = transfer(
            "attention_front",
            0,
            mesh,
            front_body,
            (
                tokens,
                small,
                w_query,
                w_key,
                w_value,
                out_grad,
                w_out,
                shared_pack,
                inverse,
                jnp.cos(row_angles),
                jnp.sin(row_angles),
            ),
            (
                like((small_rows, width)),
                like((width, 3 * HEAD_DIM)),
                like((chunk, width)),
                like((chunk, 3 * HEAD_DIM)),
                like((chunk, rows), f32),
                like((chunk, HEAD_DIM), f32),
                like((chunk, HEAD_DIM), f32),
                like((rows, heads * HEAD_DIM)),
                like((count * rows, width)),
                like((out_rows, width)),
                like((pack_rows, width)),
            ),
            [
                pltpu.VMEM((small_rows, width), bf16),
                pltpu.VMEM((chunk, width), bf16),
                pltpu.VMEM((width, 3 * HEAD_DIM), bf16),
                pltpu.VMEM((2, rows, width), bf16),
                pltpu.VMEM((chunk, 3 * HEAD_DIM), bf16),
                pltpu.VMEM((chunk, rows), f32),
                pltpu.VMEM((chunk, HEAD_DIM), f32),
                pltpu.VMEM((chunk, HEAD_DIM), f32),
                pltpu.VMEM((heads, rows, HEAD_DIM), bf16),
                pltpu.VMEM((1, HEAD_DIM), f32),
                pltpu.VMEM((rows, HEAD_DIM), f32),
                pltpu.VMEM((rows, HEAD_DIM), f32),
            ],
            semaphores=640,
            vmem=56 * 2**20,
        )
        router_full, attn_gain, ffn_gain, _, masks = unpack(small_all)
    else:
        def first_body(place, given, made, room):
            tok, sm, *weights = given
            tok_all, sm_all, w_all = made
            yield exchange(place, count, lambda s: sm, lambda s: sm_all.at[s])
            yield row_gather(place, heads, tok, tok_all, rows, part).all()
            for which, weight in enumerate(weights):

                def landing(slot, which=which):
                    at = pl.ds(pl.multiple_of(slot * deep, deep), deep)
                    return w_all.at[at, pl.ds(which * HEAD_DIM, HEAD_DIM)]

                yield exchange(
                    place, count, lambda s, w=weight: w.at[:, lanes(lax.rem(s, heads), HEAD_DIM)], landing
                )

        tok_chunk, small_all, w_qkv = transfer(
            "gather_tokens",
            0,
            mesh,
            first_body,
            (tokens, small, w_query, w_key, w_value),
            (like((chunk, width)), like((count, small_rows, deep)), like((width, 3 * HEAD_DIM))),
        )

        router_full, attn_gain, ffn_gain, lengths_all, masks = unpack(strips.join(small_all))

        member = e % heads
        lengths_chunk = lax.dynamic_slice_in_dim(lengths_all, e - member, heads, axis=0)
        segment, positions = sequence_tables(lengths_chunk, rows)
        half = HEAD_DIM // 2
        inverse = 10000.0 ** (-2.0 * jnp.arange(half, dtype=f32) / HEAD_DIM)
        angles = positions.astype(f32)[:, :, None] * inverse[None, None, :]
        cosine, sine = jnp.cos(angles), jnp.sin(angles)

        tok32 = tok_chunk.astype(f32)
        rstd_chunk = lax.rsqrt(jnp.mean(tok32 * tok32, axis=-1, keepdims=True) + eps)
        xn_chunk = (tok32 * rstd_chunk * attn_gain).astype(bf16)
        qkv = jnp.dot(xn_chunk, w_qkv, preferred_element_type=f32).reshape(heads, rows, 3 * HEAD_DIM)
        query = rotary(qkv[..., :HEAD_DIM], cosine, sine).astype(bf16)
        keyed = rotary(qkv[..., HEAD_DIM : 2 * HEAD_DIM], cosine, sine).astype(bf16)
        valued = qkv[..., 2 * HEAD_DIM :].astype(bf16)
        places = jnp.arange(rows, dtype=jnp.int32)
        allowed = (segment[:, :, None] == segment[:, None, :]) & (places[None, :] <= places[:, None])[None]
        scores = jnp.where(allowed, mm("gqd,gkd->gqk", query, keyed) * scale, floor_score)
        top_score = jnp.max(scores, axis=-1, keepdims=True)
        raised = jnp.exp(scores - top_score)
        probs = raised / jnp.sum(raised, axis=-1, keepdims=True)
        probs_low = probs.astype(bf16)
        head_out = mm("gqk,gkd->gqd", probs_low, valued).astype(bf16)

        def second_body(place, given, made, room):
            ho, og, wo, sp = given
            ho_all, og_all, wo_all, sp_all = made
            yield exchange(place, heads, lambda s: ho.at[s], lambda s: ho_all.at[:, lanes(s, HEAD_DIM)])
            yield row_gather(place, count, og, og_all, rows, part).all()

            def wo_view(slot, core=0, piece=0):
                return strips.at(wo_all, slot)

            yield gather(place, count, lambda p: wo, (wo, wo_view), wo_view, False)
            yield exchange(place, count, lambda s: sp.at[s], lambda s: strips.at(sp_all, s))

        heads_out, grad_all, out_full, shared_all = transfer(
            "gather_inputs",
            1,
            mesh,
            second_body,
            (head_out, out_grad, w_out, shared_pack),
            (
                like((rows, heads * HEAD_DIM)),
                like((count * rows, width)),
                like(strips.shape(out_rows)),
                like(strips.shape(pack_rows)),
            ),
            semaphores=640,
        )
        out_full, shared_all = strips.join(out_full), strips.join(shared_all)
    attention_part = jnp.dot(heads_out, out_full, preferred_element_type=f32).astype(bf16)

    own_mask = lax.dynamic_index_in_dim(masks, e, axis=1, keepdims=False).astype(f32)
    at_row = jnp.arange(rows, dtype=jnp.int32)
    earlier = (at_row[:, None] < at_row[None, :]).astype(bf16)
    position = jnp.where(own_mask > 0.5, jnp.dot(own_mask.astype(bf16), earlier, preferred_element_type=f32), -1.0)
    gate_weight, up_weight, down_weight = routed_gate_weight[0].T, routed_up_weight[0].T, w_down[0]
    sh_wide = up_to(hidden_units, 128)

    def widened(which):
        piece = shared_all[which * hidden_units : (which + 1) * hidden_units]
        return jnp.pad(piece, ((0, sh_wide - hidden_units), (0, 0)))

    fixed_backward = jnp.concatenate([widened(0), widened(1)], axis=0)
    fixed_forward = widened(2)
    units = gate_weight.shape[0]
    norm_rooms = [
        pltpu.VMEM((cores, rows, width), bf16),
        pltpu.VMEM((rows, width), bf16),
        pltpu.VMEM((1, width), f32),
        pltpu.VMEM((experts, width), bf16),
        pltpu.VMEM((experts, rows), f32),
        pltpu.VMEM((rows, width), f32),
        pltpu.VMEM((rows, width), bf16),
        pltpu.VMEM((experts, rows), f32),
    ]
    if strips.direct:

        def rows_body(place, given, made, room):
            og, pos, *weights = given[5:]
            hid_out, xn_all, gt_out, *arrays = made
            xn, gt = room[6:8]
            gates_v, xn_v, og_v, pos_v = room[8:12]
            weights_v, buffers = room[12:17], room[17:]
            loads = [place.keep(pos, pos_v)] + [place.keep(x, y) for x, y in zip(weights, weights_v)]
            sent, saved = second_norm(place, cores, rows, given[:5], hid_out, room[:8])
            moving = row_gather(place, count, xn, xn_v, rows, part)
            for p in range(PIECES):
                moving.start(p)
            route(room[:8])
            saved_gates = place.keep(gt, gt_out)
            gate_in, gate_out = start_exchange(place, count, lambda s: gt, lambda s: gates_v.at[s])
            sizes = [capacity] * 7 + [None] + [rows] * 2
            outs = [
                [Out(place, buffer.at[pair], array, unit) for buffer, array, unit in zip(buffers, arrays, sizes)]
                for pair in range(2)
            ]
            grad_sems, row_sems = place.take(4), place.take(4)
            quads = (((0, 0), (1, 0)), ((0, 1), (1, 1)))
            expert = lax.broadcasted_iota(jnp.int32, (experts, rows), 0)

            def gate_of(slot):
                return jnp.sum(jnp.where(expert == place.e, gates_v[slot], 0.0), axis=0, keepdims=True)

            def of_rows(slot):
                return pl.ds(pl.multiple_of(slot * rows, rows), rows)

            def grads(m, pair):
                for at, (i, j) in enumerate(quads[pair]):
                    source = og.at[of_rows(moving.slot(m, i, j)), :]
                    yield place.local(
                        source, og_v.at[pair, pl.ds(at * rows, rows), :], grad_sems + 2 * pair + at
                    )

            def keep_rows(m):
                for at, (i, j) in enumerate(quads[0] + quads[1]):
                    own = of_rows(moving.slot(m, i, j))
                    yield place.local(xn_v.at[own, :], xn_all.at[own, :], row_sems + at)

            def link(c):
                for p in range(PIECES):
                    moving.from_one(c, p)
                    pl.when(c + 1 < moving.deep)(lambda: moving.from_line(c + 1, p))

            def complete(gathered, m):
                gathered.last(m)
                for i, j in quads[0] + quads[1]:
                    gathered.from_cores(m, i, j)

            def work(m):
                pl.when(2 * m + 1 < moving.deep)(lambda: link(2 * m + 1))
                for move in grads(m, 1):
                    move.start()
                complete(moving, m)
                for i, j in quads[0] + quads[1]:
                    gate_in(moving.slot(m, i, j))
                for move in keep_rows(m):
                    when(m > 0, move.wait)
                    move.start()
                for pair in range(2):
                    for move in grads(m, pair):
                        move.wait()
                    slots = [moving.slot(m, i, j) for i, j in quads[pair]]
                    experts_pair(
                        slots,
                        m > 0,
                        capacity,
                        rows,
                        xn_v,
                        og_v.at[pair],
                        pos_v,
                        gate_of,
                        weights_v,
                        outs[pair],
                    )
                    if pair == 0:
                        pl.when(2 * m + 2 < moving.deep)(lambda: link(2 * m + 2))
                        for move in grads(m + 1, 0):
                            when(m + 1 < moving.deep, move.start)

            for move in grads(0, 0):
                move.start()
            link(0)
            for move in loads:
                move.wait()
            moving.kept.wait()

            def stage(m, carry):
                work(m)
                return carry

            lax.fori_loop(0, moving.deep, stage, 0)
            for out in outs[0] + outs[1]:
                out.free()
            for move in keep_rows(0):
                move.wait()
            gate_out()
            moving.close()
            for move in sent:
                move.wait_send()
            saved.wait()
            saved_gates.wait()
            yield from ()

        shapes = [(count * capacity, width)] * 4 + [(count * capacity, units)] * 3
        shapes += [(count, 8, rows), (count * rows, capacity + sh_wide), (count * rows, capacity + 2 * sh_wide)]
        pair_shapes = [(2 * capacity, width)] * 4 + [(2 * capacity, units)] * 3
        pair_shapes += [(2, 8, rows), (2 * rows, capacity + sh_wide), (2 * rows, capacity + 2 * sh_wide)]
        kinds = [bf16] * 7 + [f32] + [bf16] * 2
        (
            hidden,
            xn_all,
            gates_t,
            received,
            gated_grad,
            exp_low,
            back_rows,
            exp_act,
            gate_back,
            up_back,
            token_dots,
            left_forward,
            left_backward,
        ) = transfer(
            "rows_and_experts",
            2,
            mesh,
            rows_body,
            (
                attention_part,
                tokens,
                ffn_gain[None],
                router_full,
                mask_t.astype(f32),
                grad_all,
                position[:, None],
                gate_weight,
                up_weight,
                down_weight,
                fixed_backward,
                fixed_forward,
            ),
            (
                like((rows, width), f32),
                like((count * rows, width)),
                like((experts, rows), f32),
            )
            + tuple(like(shape, kind) for shape, kind in zip(shapes, kinds)),
            norm_rooms
            + [
                pltpu.VMEM((count, experts, rows), f32),
                pltpu.VMEM((count * rows, width), bf16),
                pltpu.VMEM((2, 2 * rows, width), bf16),
                pltpu.VMEM((count, 1, rows), f32),
                pltpu.VMEM((units, width), bf16),
                pltpu.VMEM((units, width), bf16),
                pltpu.VMEM((units, width), bf16),
                pltpu.VMEM((2 * sh_wide, width), bf16),
                pltpu.VMEM((sh_wide, width), bf16),
            ]
            + [pltpu.VMEM((2,) + shape, kind) for shape, kind in zip(pair_shapes, kinds)],
            semaphores=480,
            vmem=62 * 2**20,
        )
        gates = gates_t.T
    else:
        def third_body(place, given, made, room):
            ap, tok, gn, rt, mk = given
            hid_out, xn_all, gt_all = made
            xn, gt = room[6:]
            sent, saved = second_norm(place, cores, rows, given, hid_out, room)
            yield row_gather(place, count, xn, xn_all, rows, part).all()
            route(room)
            yield exchange(place, count, lambda s: gt, lambda s: gt_all.at[s])
            for move in sent:
                move.wait_send()
            saved.wait()

        hidden, xn_all, gates_all = transfer(
            "gather_rows",
            2,
            mesh,
            third_body,
            (attention_part, tokens, ffn_gain[None], router_full, mask_t.astype(f32)),
            (like((rows, width), f32), like((count * rows, width)), like((count, experts, rows), f32)),
            norm_rooms,
            semaphores=400,
            vmem=40 * 2**20,
        )
        gates = lax.dynamic_index_in_dim(gates_all, e, axis=0, keepdims=False).T
        own_gate = lax.dynamic_index_in_dim(gates_all, e, axis=1, keepdims=False)
        (
            received,
            gated_grad,
            exp_low,
            back_rows,
            exp_act,
            gate_back,
            up_back,
            token_dots,
            left_forward,
            left_backward,
        ) = experts_pass(
            count,
            capacity,
            rows,
            xn_all,
            grad_all,
            position[:, None],
            own_gate[:, None],
            gate_weight,
            up_weight,
            down_weight,
            fixed_backward,
            fixed_forward,
        )

    inputs = tokens.astype(f32)
    rstd_two = lax.rsqrt(jnp.mean(hidden * hidden, axis=-1, keepdims=True) + eps)

    sh_grads = mm("tf,td->fd", left_backward[:, capacity:], xn_all).astype(bf16)
    shared_grads = jnp.concatenate(
        [
            sh_grads[:hidden_units],
            sh_grads[sh_wide : sh_wide + hidden_units],
            mm("tf,td->fd", left_forward[:, capacity:], grad_all).astype(bf16)[:hidden_units],
        ],
        axis=0,
    )
    shared_grads = jnp.pad(shared_grads, ((0, pack_rows - 3 * hidden_units), (0, 0)))

    def fourth_body(place, given, made, room):
        lf, el, ff, lb, br, fb, td, sg = given
        mixed, summed, dots, sg_all = made
        mixed_view, summed_view = part_view(mixed, rows, part), part_view(summed, rows, part)
        forward = Product(place, lf, el, ff, room[7:9], count, rows, part)
        backward = Product(place, lb, br, fb, room[9:11], count, rows, part)
        yield scatter(
            place,
            count,
            [forward, backward],
            room[:7],
            [lambda c: mixed_view(0, c), lambda c: summed_view(0, c)],
            (rows, part),
            True,
            room[11],
        )
        yield both(place, count, lambda s: td.at[s], lambda c, s: dots.at[c, s], lambda c: dots.at[c])
        yield later(exchange(place, count, lambda s: strips.at(sg, s), lambda s: sg_all.at[s]), 8)

    mixture, summed_back, dots_all, shared_back = transfer(
        "scatter_both",
        3,
        mesh,
        fourth_body,
        (
            left_forward,
            exp_low,
            fixed_forward,
            left_backward,
            back_rows,
            fixed_backward,
            token_dots,
            strips.cut(shared_grads),
        ),
        (
            like((rows, width)),
            like((rows, width)),
            like((cores, count, 8, rows), f32),
            like((count, pack_rows, deep)),
        ),
        scatter_scratch(
            count,
            cores,
            rows,
            part,
            [(left_forward.shape[1], True), (left_backward.shape[1], True)],
        )
        + [pltpu.SemaphoreType.REGULAR((count * (cores - 1),))],
        vmem=60 * 2**20,
    )
    output = (hidden + mixture.astype(f32)).astype(bf16)

    gate_total = jnp.sum(dots_all[:, :, 0, :], axis=0).T
    weighted_dots = jnp.sum(gates * gate_total, axis=1, keepdims=True)
    grad_logits = gates * (gate_total - weighted_dots)

    down_grad = mm("rf,rd->fd", exp_act, gated_grad)
    gate_grad = mm("rd,rf->df", received, gate_back)
    up_grad = mm("rd,rf->df", received, up_back)
    cotangent = out_grad.astype(f32)
    grad_two = summed_back.astype(f32) + jnp.einsum(
        "te,ed->td", grad_logits, router_full.astype(f32), precision=highest
    )
    scaled = grad_two * ffn_gain
    inner = jnp.mean(scaled * hidden, axis=-1, keepdims=True)
    grad_hidden = cotangent + rstd_two * scaled - hidden * (rstd_two * rstd_two * rstd_two) * inner
    ffn_gain_part = jnp.sum(grad_two * hidden * rstd_two, axis=0)
    grad_branch = grad_hidden.astype(bf16)
    grad_heads = mm("td,cd->tc", grad_branch, out_full).astype(bf16)
    out_proj_part = mm("tc,td->cd", heads_out, grad_branch).astype(bf16)

    turns = count // heads

    def spread(vector):
        return jnp.pad(vector.reshape(count, 1, deep), ((0, 0), (0, 7), (0, 0)))

    if strips.direct:

        def back_body(place, given, made, room):
            gh, gl, op, fg, qkv_s, pr, ct, st, xn, wt = given
            one, qg_all, op_sum, ag_all, fg_all, logit_all = made
            qkv_v, pr_v, ct_v, st_v, gh_v, normed, turned, sums, grad_qkv, right, gains, blocks = room[14:]
            own = lax.rem(place.e, heads)
            moves = [place.keep(x, y) for x, y in ((qkv_s, qkv_v), (pr, pr_v), (ct, ct_v), (st, st_v))]
            lasts = [place.keep(xn, normed), place.keep(wt, right)]
            arrived, finish = start_exchange(
                place, heads, lambda s: gh.at[:, lanes(s, HEAD_DIM)], lambda s: gh_v.at[s]
            )
            one_view = part_view(one, rows, part)

            def main():
                for move in moves:
                    move.wait()
                for d in range(heads):
                    slot = lax.rem(own + d, heads)
                    if d > 0:
                        arrived(slot)
                    attend_back((qkv_v, pr_v, ct_v, st_v, gh_v, grad_qkv, turned), slot, rows)
                    yield
                for move in lasts:
                    move.wait()
                tail()
                yield
                kept = Kept(grad_qkv, right, rows)
                yield from scatter(place, heads, [kept], room[:7], [lambda c: one_view(0, c)], (rows, part), True)

            def tail():
                wide = 2 * deep

                def product(at, carry):
                    sums[:, lanes(at, wide)] = dot(turned[...], normed[:, lanes(at, wide)])
                    return carry

                lax.fori_loop(0, width // wide, product, 0)

                def body(at, carry):
                    block = sums[:, lanes(at, deep)]
                    blocks[at] = block.astype(bf16).T
                    weights = right[pl.ds(pl.multiple_of(at * deep, deep), deep), :].T.astype(f32)
                    gain_row = jnp.sum(block * weights, axis=0, keepdims=True)
                    gains[:, lanes(at, deep)] = jnp.broadcast_to(gain_row, (8, deep))
                    return carry

                lax.fori_loop(0, count, body, 0)
                for which in range(3):

                    def landing(slot, which=which):
                        return qg_all.at[which, lax.div(slot, heads), :, lanes(lax.rem(slot, heads), HEAD_DIM)]

                    def block(slot, which=which):
                        return blocks.at[slot, :, pl.ds(which * HEAD_DIM, HEAD_DIM)]

                    tasks.append(exchange(place, count, block, landing))
                tasks.append(
                    both(
                        place,
                        count,
                        lambda s: gains.at[:, lanes(s, deep)],
                        lambda c, s: ag_all.at[c, s],
                        lambda c: ag_all.at[c],
                    )
                )

            projection = scatter(
                place, count, [lambda s: strips.at(op, s)], room[7:14], [lambda c: op_sum], (out_rows, deep), False
            )
            tasks = [
                main(),
                twice(projection),
                exchange(place, count, lambda s: gl, lambda s: logit_all.at[s]),
                exchange(place, count, lambda s: fg.at[s], lambda s: fg_all.at[s]),
            ]
            yield tasks
            finish()

        grad_one, qkv_all, out_proj_sum, attn_gains, ffn_gains, logits_all = transfer(
            "attention_back",
            4,
            mesh,
            back_body,
            (
                grad_heads,
                grad_logits.T,
                out_proj_part,
                spread(ffn_gain_part),
                qkv_saved,
                probs_saved,
                cosine_wide,
                sine_wide,
                xn_chunk,
                w_qkv,
            ),
            (
                like((rows, width)),
                like((3, turns, deep, heads * HEAD_DIM)),
                like((out_rows, deep)),
                like((cores, count, 8, deep), f32),
                like((count, 8, deep), f32),
                like((count, experts, rows), f32),
            ),
            scatter_scratch(heads, cores, rows, part)
            + scatter_scratch(count, 1, out_rows, deep)
            + [
                pltpu.VMEM((chunk, 3 * HEAD_DIM), bf16),
                pltpu.VMEM((chunk, rows), f32),
                pltpu.VMEM((chunk, HEAD_DIM), f32),
                pltpu.VMEM((chunk, HEAD_DIM), f32),
                pltpu.VMEM((heads, rows, HEAD_DIM), bf16),
                pltpu.VMEM((chunk, width), bf16),
                pltpu.VMEM((3 * HEAD_DIM, chunk), bf16),
                pltpu.VMEM((3 * HEAD_DIM, width), f32),
                pltpu.VMEM((chunk, 3 * HEAD_DIM), bf16),
                pltpu.VMEM((width, 3 * HEAD_DIM), bf16),
                pltpu.VMEM((8, width), f32),
                pltpu.VMEM((count, deep, 3 * HEAD_DIM), bf16),
            ],
            semaphores=640,
            vmem=56 * 2**20,
        )
    else:
        def fifth_body(place, given, made, room):
            gl, logit_all = given[1], made[1]
            yield exchange(place, count, lambda s: gl, lambda s: logit_all.at[s])
            yield exchange(place, heads, lambda s: given[0].at[:, lanes(s, HEAD_DIM)], lambda s: made[0].at[s])

        grad_head, logits_all = transfer(
            "exchange_heads",
            4,
            mesh,
            fifth_body,
            (grad_heads, grad_logits.T),
            (like((heads, rows, HEAD_DIM)), like((count, experts, rows), f32)),
        )
        grad_value = mm("gqk,gqd->gkd", probs_low, grad_head)
        grad_probs = mm("gqd,gkd->gqk", grad_head, valued)
        weighted = jnp.sum(probs * grad_probs, axis=-1, keepdims=True)
        grad_scores = (probs * (grad_probs - weighted)).astype(bf16)
        grad_query = mm("gqk,gkd->gqd", grad_scores, keyed) * scale
        grad_key = mm("gqk,gqd->gkd", grad_scores, query) * scale
        grad_qkv = jnp.concatenate(
            [
                rotary_back(grad_query, cosine, sine).astype(bf16),
                rotary_back(grad_key, cosine, sine).astype(bf16),
                grad_value.astype(bf16),
            ],
            axis=2,
        ).reshape(chunk, 3 * HEAD_DIM)
        qkv_grad = mm("td,tc->dc", xn_chunk, grad_qkv)
        attn_gain_part = jnp.sum(qkv_grad * w_qkv.astype(f32), axis=1)
        qkv_grad = qkv_grad.astype(bf16)

        def sixth_body(place, given, made, room):
            gq, wq, qg, op, ag, fg = given
            one, qg_all, op_sum, ag_all, fg_all = made
            one_view = part_view(one, rows, part)
            made_here = Product(place, gq, None, wq, room[7:9], heads, rows, part)
            yield scatter(place, heads, [made_here], room[:7], [lambda c: one_view(0, c)], (rows, part), True)
            yield scatter(
                place, count, [lambda s: strips.at(op, s)], room[9:], [lambda c: op_sum], (out_rows, deep), False
            )
            yield both(place, count, lambda s: ag.at[s], lambda c, s: ag_all.at[c, s], lambda c: ag_all.at[c])
            yield exchange(place, count, lambda s: fg.at[s], lambda s: fg_all.at[s])
            for which in range(3):

                def source(slot, which=which):
                    at = pl.ds(pl.multiple_of(slot * deep, deep), deep)
                    return qg.at[at, pl.ds(which * HEAD_DIM, HEAD_DIM)]

                def landing(slot, which=which):
                    return qg_all.at[which, lax.div(slot, heads), :, lanes(lax.rem(slot, heads), HEAD_DIM)]

                yield later(exchange(place, count, source, landing), 6)

        grad_one, qkv_all, out_proj_sum, attn_gains, ffn_gains = transfer(
            "scatter_grads",
            5,
            mesh,
            sixth_body,
            (
                grad_qkv,
                w_qkv.T,
                qkv_grad,
                strips.cut(out_proj_part),
                spread(attn_gain_part),
                spread(ffn_gain_part),
            ),
            (
                like((rows, width)),
                like((3, turns, deep, heads * HEAD_DIM)),
                like((out_rows, deep)),
                like((cores, count, 8, deep), f32),
                like((count, 8, deep), f32),
            ),
            scatter_scratch(heads, cores, rows, part, [(3 * HEAD_DIM, False)])
            + scatter_scratch(count, 1, out_rows, deep),
            semaphores=600,
            vmem=56 * 2**20,
        )

    xn_columns = lax.dynamic_slice_in_dim(xn_all, e * deep, deep, axis=1).astype(f32).reshape(count, rows, deep)
    router_grad = jnp.einsum("gtd,get->de", xn_columns, logits_all, precision=highest)
    grad_one = grad_one.astype(f32)
    rstd_one = lax.rsqrt(jnp.mean(inputs * inputs, axis=-1, keepdims=True) + eps)
    scaled_one = grad_one * attn_gain
    inner_one = jnp.mean(scaled_one * inputs, axis=-1, keepdims=True)
    input_grad = (
        grad_hidden + rstd_one * scaled_one - inputs * (rstd_one * rstd_one * rstd_one) * inner_one
    ).astype(bf16)

    def of_heads(which):
        return jnp.sum(qkv_all[which].astype(f32), axis=0)

    def of_shared(which):
        return shared_back[:, which * hidden_units : (which + 1) * hidden_units].reshape(-1, deep).astype(f32)

    return (
        output,
        input_grad,
        jnp.sum(attn_gains[:, :, 0, :], axis=(0, 1)) / gain_attn.astype(f32),
        of_heads(0),
        of_heads(1),
        of_heads(2),
        out_proj_sum.astype(f32),
        jnp.sum(ffn_gains[:, 0, :], axis=0),
        router_grad,
        gate_grad[None],
        up_grad[None],
        down_grad[None],
        of_shared(0).T,
        of_shared(1).T,
        of_shared(2),
    )


def solution(mesh):
    in_specs = (
        P("expert", None),
        P("expert", None),
        P("expert", None),
        P("expert"),
        P("expert", "tensor"),
        P("expert", "tensor"),
        P("expert", "tensor"),
        P("tensor", "expert"),
        P("expert"),
        P("expert", None),
        P("expert", None, "tensor"),
        P("expert", None, "tensor"),
        P("expert", "tensor", None),
        P("expert", "tensor"),
        P("expert", "tensor"),
        P("tensor", "expert"),
        P("expert", None),
    )
    out_specs = (
        P("expert", None),
        P("expert", None),
        P("expert"),
        P("expert", "tensor"),
        P("expert", "tensor"),
        P("expert", "tensor"),
        P("tensor", "expert"),
        P("expert"),
        P("expert", None),
        P("expert", None, "tensor"),
        P("expert", None, "tensor"),
        P("expert", "tensor", None),
        P("expert", "tensor"),
        P("expert", "tensor"),
        P("tensor", "expert"),
    )
    return jax.shard_map(
        functools.partial(local, mesh), mesh=mesh, in_specs=in_specs, out_specs=out_specs, check_vma=False
    )
```
